128 devices in a mesh: expert: 32 (over y, z, core), shard: 4 (over x).
Axes of the slice: x: 4, y: 4, z: 4, core: 2. Of those that a mesh axis runs over, the one named last changes fastest.
Arguments:
- tokens: bfloat16 [32768, 1536], P(('expert', 'shard')), may hold values from -6 to 6
- lengths: int32 [32, 4], P('expert'), may hold values from 1 to 896, 1024 in all within a row
- top_experts: int32 [32768, 4], P(('expert', 'shard')), may hold values from 0 to 31, all different within a row; in each aligned block of 256 rows (0 to 255, 256 to 511, ...) at most 48 rows name the same one
- w_qkv: bfloat16 [1536, 2048], P(('expert', 'shard')), may hold values from -0.15625 to 0.15625
- w_out: bfloat16 [1536, 1536], P(None, ('expert', 'shard')), may hold values from -0.875 to 0.875
- gain_attn: bfloat16 [1536], P(('expert', 'shard')), may hold values from 0.5 to 1.5
- gain_ffn: bfloat16 [1536], P(('expert', 'shard')), may hold values from 0.5 to 1.5
- router: bfloat16 [1536, 32], P(('expert', 'shard')), may hold values from -0.078125 to 0.078125
- gate_up: bfloat16 [32, 1536, 1536], P('expert'), may hold values from -0.15625 to 0.15625
- down_proj: bfloat16 [32, 768, 1536], P('expert'), may hold values from -0.4375 to 0.4375
- cotangent: bfloat16 [32768, 1536], P(('expert', 'shard')), may hold values from -6 to 6
Outputs:
- output: bfloat16 [32768, 1536], P(('expert', 'shard'))
- grad_tokens: bfloat16 [32768, 1536], P(('expert', 'shard'))
- grad_qkv: float32 [1536, 2048], P(('expert', 'shard'))
- grad_out: float32 [1536, 1536], P(None, ('expert', 'shard'))
- grad_gain_attn: float32 [1536], P(('expert', 'shard'))
- grad_gain_ffn: float32 [1536], P(('expert', 'shard'))
- grad_router: float32 [1536, 32], P(('expert', 'shard'))
- grad_gate_up: float32 [32, 1536, 1536], P('expert', 'shard')
- grad_down: float32 [32, 768, 1536], P('expert', None, 'shard')
The draws below stay inside these ranges and needn't reach their ends.
Inputs may be any that keep to these rules, and one draw needn't show every extreme that they name: The 4 lengths of a group sum to 1024; the longest is 896. `top_experts`: each row names 4 different experts. Among the rows of one device no expert is named more than 48 times; in some devices' rows one expert is named exactly 48 times.
All inputs are finite; a program needn't handle non-finite values.
Results may differ from the reference program's by a relative error of at most 0.02.
Values may be sent and summed in bfloat16 or wider, within the bound.
A program may use at most 192 MiB of HBM per device.

```python
import math
import jax
import jax.numpy as jnp
import numpy as np
from jax import lax

D = 1536
HEADS_Q = 12
HEADS_KV = 2
HEAD_DIM = 128
FF = 768
TOP = 4
TOK_DEV = 256
SEQS = 4
EXPERTS = 32
GROUP = 1024
TOKENS = 32768
CAP = 48
QKV_W = 2048
N_EXPERT = 32
N_SHARD = 4


def steps_of(stream_key, extent, shards, low, largest):
    factor_of = 1.0
    for axis_at, parts in shards:
        steps = jax.random.uniform(jax.random.fold_in(jax.random.fold_in(stream_key, 6), axis_at), (parts,), jnp.float32, low / len(shards), largest / len(shards))
        factor_of = factor_of * jnp.repeat(jnp.exp(steps), extent[axis_at] // parts).reshape((-1,) + (1,) * (len(extent) - 1 - axis_at))
    return factor_of


def length_profile(amount, total, reach, skew):
    portions = [(1 << 20) // math.isqrt(standing ** skew) + 1 for standing in range(2, amount + 1)]
    surplus, given = total - reach - (amount - 1), [1] * (amount - 1)
    while surplus > 0:
        candidates = [i for i in range(amount - 1) if given[i] < reach]
        whole, budget = sum([portions[i] for i in candidates]), surplus
        for i in candidates:
            extra = min(reach - given[i], max(1, budget * portions[i] // whole), surplus)
            given[i] = given[i] + extra
            surplus = surplus - extra
    return np.array([reach] + given)


def uneven_parts(rng, number_of, total, limit, skew):
    if number_of == 2:
        one = jax.random.randint(rng, (), max(1, total - limit), min(limit, total - 1) + 1)
        return jnp.stack([one, total - one])
    tallies = jnp.asarray(length_profile(number_of, total, limit, skew), jnp.int32)
    twos = (number_of - 1) // 2
    source_of, taker = tallies[1:1 + 2 * twos:2], tallies[2:2 + 2 * twos:2]
    margin = jnp.minimum(source_of - 1, limit - taker)
    moved = jax.random.randint(jax.random.fold_in(rng, 1), (twos,), 0, 1 << 20) % (margin + 1)
    tallies = tallies.at[1:1 + 2 * twos:2].set(source_of - moved).at[2:2 + 2 * twos:2].set(taker + moved)
    return tallies[jax.random.permutation(jax.random.fold_in(rng, 2), number_of)]


def assign_block(key, own, number, rows, count, top, bound, slope):
    order = jax.random.permutation(key, count)
    packed, usual = shares(count, rows * top, bound, slope, True), shares(count, rows * top, bound, slope, False)
    places = jnp.arange(count)

    def named(tallies, rotation):
        used = int((tallies > 0).sum())
        fixed = max(1, used // 4)
        moved = fixed + (places - fixed + rotation * (used - fixed)) % max(1, count - fixed)
        return jnp.zeros((count,), jnp.int32).at[order[jnp.where(places < fixed, places, moved)]].set(jnp.asarray(tallies, jnp.int32))

    tallies = jnp.where(number % 4 == 0, named(packed, number // 4), named(usual, number - number // 4 - 1))
    mixed = jax.random.permutation(jax.random.fold_in(own, 3), count)
    giver, taker = mixed[0:count // 2 * 2:2], mixed[1:count // 2 * 2:2]
    room = jnp.minimum(tallies[giver] - 1, bound - tallies[taker]) // 2
    room = jnp.where((giver == order[0]) | (taker == order[0]) | (tallies[taker] == 0), 0, jnp.maximum(room, 0))
    moved = jax.random.randint(jax.random.fold_in(own, 4), (count // 2,), 0, 1 << 20) % (room + 1)
    tallies = tallies.at[giver].add(-moved).at[taker].add(moved)
    members = jnp.searchsorted(jnp.cumsum(tallies), jnp.arange(rows * top), side="right").astype(jnp.int32)
    grid = members.reshape(top, rows).T
    grid = grid[jax.random.permutation(jax.random.fold_in(own, 1), rows)]
    rotation = jax.random.randint(jax.random.fold_in(own, 2), (rows, 1), 0, top)
    return jnp.take_along_axis(grid, (jnp.arange(top)[None, :] + rotation) % top, axis=1)


def shares(number_of, total, limit, skew, full):
    loads = [(1 << 20) // math.isqrt(rank ** skew) + 1 for rank in range(1, number_of + 1)]
    largest = limit if full else min(limit, max(-(-total // number_of), total * loads[0] // sum(loads)))
    least = 1 if total - largest >= number_of - 1 else 0
    given, surplus = [largest] + [least] * (number_of - 1), total - largest - least * (number_of - 1)
    while surplus > 0:
        free = [i for i in range(1, number_of) if given[i] < largest] or [i for i in range(1, number_of) if given[i] < limit]
        pool, remaining = sum([loads[i] for i in free]), surplus
        for i in free:
            extra = min(limit - given[i], max(1, remaining * loads[i] // pool), surplus)
            given[i] = given[i] + extra
            surplus = surplus - extra
    return np.array(given)


def normal_values(key, extent, spread, reach, cuts=(), held_as=jnp.bfloat16):
    array = spread * jax.random.normal(key, extent, jnp.float32)
    if cuts:
        array = array * steps_of(key, extent, cuts, -0.22, 0.18)
    return jnp.clip(array, -reach, reach).astype(held_as)


def setup_inputs(seed: int = 0) -> dict:
    seeds = jax.random.split(jax.random.key(seed), 12)
    tokens = normal_values(seeds[0], (TOKENS, D), 1.0, 6.0, ((0, 128),))
    lengths = jax.vmap(lambda own: uneven_parts(own, SEQS, GROUP, GROUP - GROUP // 8, 2))(jax.random.split(seeds[1], N_EXPERT)).reshape((N_EXPERT, SEQS)).astype(jnp.int32)
    top_experts_keys = jax.random.split(jax.random.fold_in(seeds[2], 1), TOKENS // TOK_DEV)
    top_experts_turns = jax.random.permutation(jax.random.fold_in(seeds[2], 3), TOKENS // TOK_DEV)
    top_experts = jax.vmap(lambda own, number: assign_block(jax.random.fold_in(seeds[2], 2), own, number, TOK_DEV, EXPERTS, TOP, CAP, 1))(top_experts_keys, top_experts_turns).reshape((TOKENS, TOP))
    w_qkv = normal_values(seeds[3], (D, QKV_W), D ** -0.5, 0.15625, ((0, 128),))
    w_out = normal_values(seeds[4], (HEADS_Q * HEAD_DIM, D), (HEADS_Q * HEAD_DIM // 32) ** -0.5, 0.875, ((1, 128),))
    gain_attn = jnp.clip(1.0 + 0.1 * jax.random.normal(seeds[5], (D,), jnp.float32), 0.5, 1.5).astype(jnp.bfloat16)
    gain_ffn = jnp.clip(1.0 + 0.1 * jax.random.normal(seeds[6], (D,), jnp.float32), 0.5, 1.5).astype(jnp.bfloat16)
    router = normal_values(seeds[7], (D, EXPERTS), (4 * D) ** -0.5, 0.078125, ((0, 128),))
    gate_up = normal_values(seeds[8], (EXPERTS, D, 2 * FF), D ** -0.5, 0.15625, ((0, 32),))
    down_proj = normal_values(seeds[9], (EXPERTS, FF, D), (FF // 4) ** -0.5, 0.4375, ((0, 32),))
    cotangent = normal_values(seeds[10], (TOKENS, D), 1.0, 6.0, ((0, 128),))
    return {"tokens": tokens, "lengths": lengths, "top_experts": top_experts, "w_qkv": w_qkv, "w_out": w_out, "gain_attn": gain_attn, "gain_ffn": gain_ffn, "router": router, "gate_up": gate_up, "down_proj": down_proj, "cotangent": cotangent}


@jax.custom_vjp
def low(v):
    return lax.optimization_barrier(v.astype(jnp.bfloat16)).astype(jnp.float32)

@jax.custom_vjp
def low_back(v):
    return v

def low_keep(v):
    return (low(v), None)

def low_pass(kept, grad):
    return (grad,)

def back_keep(v):
    return (v, None)

def back_low(kept, grad):
    return (low(grad),)
low.defvjp(low_keep, low_pass)
low_back.defvjp(back_keep, back_low)
norm_eps = 1e-06
rope_base = 1000000.0
precise = lax.Precision.HIGHEST

def rms_scale(values, gain_vec):
    return values * lax.rsqrt(lax.optimization_barrier(jnp.mean(values * values, axis=-1, keepdims=True)) + norm_eps) * gain_vec

def rope_tables(position, half_dim):
    frequency = rope_base ** (-jnp.arange(half_dim, dtype=jnp.float32) / half_dim)
    angles = position.astype(jnp.float32)[:, None] * frequency[None, :]
    return (jnp.cos(angles)[:, None, :], jnp.sin(angles)[:, None, :])

def rotate(values, cosine, sine_tab):
    half_dim = values.shape[-1] // 2
    lower_half = values[..., :half_dim]
    upper_half = values[..., half_dim:]
    return jnp.concatenate([lower_half * cosine - upper_half * sine_tab, lower_half * sine_tab + upper_half * cosine], axis=-1)

def seq_layout(seq_lens, row_ids):
    seq_ends = jnp.cumsum(seq_lens)
    segment = lax.optimization_barrier(jnp.sum((row_ids[:, None] >= seq_ends[None, :]).astype(jnp.int32), axis=1))
    seq_start = lax.optimization_barrier(jnp.sum(jnp.where(seq_ends[None, :] <= row_ids[:, None], seq_lens[None, :], 0), axis=1))
    return (segment, (row_ids - seq_start).astype(jnp.int32))

def slot_table(top_block, experts, capacity):
    flat_ids = top_block.reshape(-1)
    onehot = (flat_ids[:, None] == jnp.arange(experts, dtype=jnp.int32)[None, :]).astype(jnp.int32)
    before = jnp.cumsum(onehot, axis=0) - onehot
    target = lax.optimization_barrier(jnp.sum(onehot * (before + jnp.arange(experts, dtype=jnp.int32)[None, :] * capacity), axis=1))
    slot_hits = target[:, None] == jnp.arange(experts * capacity, dtype=jnp.int32)[None, :]
    return slot_hits.reshape(top_block.shape[0], top_block.shape[1], experts * capacity)

def group_layer(group_x, group_top, seq_lens, qkv_f, out_f, attn_g, ffn_g, router_f, gate_f, down_f):
    row_ids = jnp.arange(GROUP, dtype=jnp.int32)
    segment, position = seq_layout(seq_lens, row_ids)
    width_q = HEADS_Q * HEAD_DIM
    width_kv = HEADS_KV * HEAD_DIM
    normed = low(rms_scale(group_x, attn_g))
    projected = low_back(jnp.dot(normed, qkv_f, precision=precise))
    cosine, sine_tab = rope_tables(position, HEAD_DIM // 2)
    queries = low(rotate(projected[:, :width_q].reshape(GROUP, HEADS_Q, HEAD_DIM), cosine, sine_tab))
    keys_rot = low(rotate(projected[:, width_q:width_q + width_kv].reshape(GROUP, HEADS_KV, HEAD_DIM), cosine, sine_tab))
    values = low(projected[:, width_q + width_kv:].reshape(GROUP, HEADS_KV, HEAD_DIM))
    grouped = queries.reshape(GROUP, HEADS_KV, HEADS_Q // HEADS_KV, HEAD_DIM)
    scores = low_back(jnp.einsum('qgrd,kgd->grqk', grouped, keys_rot, precision=precise) * HEAD_DIM ** (-0.5))
    allowed = (segment[:, None] == segment[None, :]) & (row_ids[None, :] <= row_ids[:, None])
    attn_probs = low(jax.nn.softmax(jnp.where(allowed, scores, -1e+30), axis=-1))
    attended = jnp.einsum('grqk,kgd->qgrd', attn_probs, values, precision=precise).reshape(GROUP, width_q)
    attended = low_back(low(attended))
    branch = low_back(jnp.dot(attended, out_f, precision=precise))
    middle = group_x + branch
    logits = jnp.dot(group_x, router_f, precision=precise)
    onehot = (group_top[:, :, None] == jnp.arange(EXPERTS, dtype=jnp.int32)[None, None, :]).astype(jnp.float32)
    gate_vals = jax.nn.softmax(lax.optimization_barrier(jnp.sum(onehot * logits[:, None, :], axis=-1)), axis=-1)
    normed_ffn = low(rms_scale(middle, ffn_g))
    slot_hits = jax.vmap(lambda block_top: slot_table(block_top, EXPERTS, CAP))(group_top.reshape(N_SHARD, TOK_DEV, TOP)).astype(jnp.float32)
    dispatched = low_back(jnp.einsum('stkp,std->spd', slot_hits, normed_ffn.reshape(N_SHARD, TOK_DEV, D), precision=precise))
    by_expert = dispatched.reshape(N_SHARD, EXPERTS, CAP, D).transpose(1, 0, 2, 3).reshape(EXPERTS, N_SHARD * CAP, D)
    hidden = low_back(jnp.einsum('erd,edf->erf', by_expert, gate_f, precision=precise))
    mixed_hidden = low(jax.nn.gelu(hidden[..., :FF], approximate=True) * hidden[..., FF:])
    expert_out = low_back(low(jnp.einsum('erf,efd->erd', mixed_hidden, down_f, precision=precise)))
    returned = expert_out.reshape(EXPERTS, N_SHARD, CAP, D).transpose(1, 0, 2, 3).reshape(N_SHARD, EXPERTS * CAP, D)
    picked = jnp.einsum('stkp,spd->stkd', slot_hits, returned, precision=precise)
    combined = lax.optimization_barrier(jnp.sum(gate_vals.reshape(N_SHARD, TOK_DEV, TOP)[..., None] * picked, axis=2)).reshape(GROUP, D)
    return middle + combined

def reference(tokens, lengths, top_experts, w_qkv, w_out, gain_attn, gain_ffn, router, gate_up, down_proj, cotangent):
    floats = tuple((array_in.astype(jnp.float32) for array_in in (tokens, w_qkv, w_out, gain_attn, gain_ffn, router, gate_up, down_proj)))

    def forward(tok_f, qkv_f, out_f, attn_g, ffn_g, router_f, gate_f, down_f):

        def one_group(pieces):
            group_x, group_top, seq_lens = pieces
            return group_layer(group_x, group_top, seq_lens, qkv_f, out_f, attn_g, ffn_g, router_f, gate_f, down_f)
        result = lax.map(jax.checkpoint(one_group), (tok_f.reshape(N_EXPERT, GROUP, D), top_experts.reshape(N_EXPERT, GROUP, TOP), lengths))
        return result.reshape(TOKENS, D)
    output, pullback = jax.vjp(forward, *floats)
    grads = pullback(cotangent.astype(jnp.float32))
    return (output.astype(jnp.bfloat16), grads[0].astype(jnp.bfloat16), grads[1], grads[2], grads[3], grads[4], grads[5], grads[6], grads[7])
```

```python
import functools

import jax
import jax.numpy as jnp
from jax import lax
from jax.experimental import pallas as pl
from jax.experimental.pallas import tpu as pltpu
from jax.sharding import PartitionSpec as P

D = 1536
HEADS_Q = 12
HEADS_KV = 2
HEAD_DIM = 128
FF = 768
TOP = 4
EXPERTS = 32
CAP = 48
WIDTH_Q = HEADS_Q * HEAD_DIM
WIDTH_KV = HEADS_KV * HEAD_DIM
REPEAT = HEADS_Q // HEADS_KV

norm_eps = 1e-06
rope_base = 1000000.0
precise = lax.Precision.HIGHEST
MESH = pl.DeviceIdType.MESH
F32 = jnp.float32
BF16 = jnp.bfloat16

PIECE = 12
PADDED = 16
BLOCK = 48
WA = 2048
WB = 1664
SMALL = WB - D


def place():
    e = lax.axis_index("expert")
    return e // 8, (e // 2) % 4, e % 2, lax.axis_index("shard")


def device(y, z, c, x):
    return ((y * 4 + z) * 2 + c, x)


def greet(devices):
    barrier = pltpu.get_barrier_semaphore()
    for d in devices:
        pl.semaphore_signal(barrier, inc=1, device_id=d, device_id_type=MESH)
    pl.semaphore_wait(barrier, len(devices))


class Links:
    def __init__(self, send, recv):
        self.send, self.recv, self.made = send, recv, []

    def push(self, src, dst, where):
        i = len(self.made)
        copy = pltpu.make_async_remote_copy(
            src_ref=src,
            dst_ref=dst,
            send_sem=self.send.at[i],
            recv_sem=self.recv.at[i],
            device_id=where,
            device_id_type=MESH,
        )
        copy.start()
        self.made.append(copy)
        return copy

    def drain(self):
        for copy in self.made:
            copy.wait_send()


def neighbours(y, z, c, x):
    other = 1 - c
    return dict(
        x=[device(y, z, c, (x + d) % 4) for d in (1, 2, 3)],
        y=(device((y + 1) % 4, z, c, x), device((y + 3) % 4, z, c, x)),
        z=(device(y, (z + 1) % 4, c, x), device(y, (z + 3) % 4, c, x)),
        core=device(y, z, other, x),
    )


def everyone_near(near):
    return list(near["x"]) + list(near["y"]) + list(near["z"]) + [near["core"]]


def pick_rows(rows, columns, row_block, column_block):
    r = lax.broadcasted_iota(jnp.int32, (rows, columns), 0)
    q = lax.broadcasted_iota(jnp.int32, (rows, columns), 1)
    same = (r // row_block == q // column_block) & (r % row_block == q % column_block)
    return jnp.where(same, 1.0, 0.0).astype(BF16)


def gather_kernel(pack, full_a, full_b, xbuf, own_a, own_b, send, recv, local):
    y, z, c, x = place()
    near = neighbours(y, z, c, x)
    greet(everyone_near(near))
    link = Links(send, recv)
    first = [link.push(pack, xbuf.at[x], near["x"][d]) for d in range(3)]
    xbuf[pl.ds(x, 1)] = pack[...][None]
    for copy in first:
        copy.wait_recv()
    select = pick_rows(BLOCK, 4 * PADDED, PIECE, PADDED)
    pieces = xbuf[...].reshape(4 * PADDED, WA + WB)
    own_a[...] = jnp.dot(select, pieces[:, :WA], preferred_element_type=F32).astype(BF16)
    own_b[...] = jnp.dot(select, pieces[:, WA:], preferred_element_type=F32).astype(BF16)

    def at_a(far, close, columns=None):
        view = full_a.at[far, close, c]
        return view if columns is None else view.at[:, columns]

    def at_b(far, close, columns=None):
        view = full_b.at[close, far, c]
        return view if columns is None else view.at[:, columns]

    def line_a(far, part=slice(None)):
        return full_a.at[far, part, c]

    def line_b(far, part=slice(None)):
        return full_b.at[part, far, c]

    jobs = [
        dict(own=own_a, at=at_a, line=line_a, close="z", far="y", p=z, q=y, half=1024, i=0),
        dict(own=own_b, at=at_b, line=line_b, close="y", far="z", p=y, q=z, half=896, i=1),
    ]
    for j in jobs:
        here = j["at"](j["q"], j["p"])
        plus, minus = near[j["close"]]
        j["up"] = link.push(j["own"], here, plus)
        j["down"] = link.push(j["own"], here, minus)
        j["core"] = [link.push(j["own"], here, near["core"])]
        j["local"] = pltpu.make_async_copy(j["own"], here, local.at[j["i"]])
        j["local"].start()
    for j in jobs:
        plus, minus = near[j["close"]]
        left, right = (j["p"] + 3) % 4, (j["p"] + 1) % 4
        j["up"].wait_recv()
        part = j["at"](j["q"], left, pl.ds(0, j["half"]))
        j["up2"] = link.push(part, part, plus)
        j["down"].wait_recv()
        part = j["at"](j["q"], right, pl.ds(j["half"], j["own"].shape[1] - j["half"]))
        j["down2"] = link.push(part, part, minus)
        for side in (left, right):
            block = j["at"](j["q"], side)
            j["core"].append(link.push(block, block, near["core"]))
    for j in jobs:
        j["up2"].wait_recv()
        j["down2"].wait_recv()
        block = j["at"](j["q"], (j["p"] + 2) % 4)
        j["local"].wait()
        plus, minus = near[j["far"]]
        line = j["line"](j["q"])
        j["up"] = link.push(line, line, plus)
        j["down"] = link.push(line, line, minus)
        j["core"].append(link.push(block, block, near["core"]))
    for j in jobs:
        plus, minus = near[j["far"]]
        left, right = (j["q"] + 3) % 4, (j["q"] + 1) % 4
        j["up"].wait_recv()
        part = j["line"](left, pl.ds(0, 2))
        j["up2"] = link.push(part, part, plus)
        j["down"].wait_recv()
        part = j["line"](right, pl.ds(2, 2))
        j["down2"] = link.push(part, part, minus)
        for side in (left, right):
            block = j["line"](side)
            j["core"].append(link.push(block, block, near["core"]))
    for j in jobs:
        opposite = (j["q"] + 2) % 4
        j["up2"].wait_recv()
        part = j["line"](opposite, pl.ds(0, 2))
        j["core"].append(link.push(part, part, near["core"]))
        j["down2"].wait_recv()
        part = j["line"](opposite, pl.ds(2, 2))
        j["core"].append(link.push(part, part, near["core"]))
    for j in jobs:
        for copy in j["core"]:
            copy.wait_recv()
    link.drain()


def gather_weights(pack):
    copies = 3 + 2 * 16
    return pl.pallas_call(
        gather_kernel,
        name="gather_weights",
        out_shape=(
            jax.ShapeDtypeStruct((4, 4, 2, BLOCK, WA), BF16),
            jax.ShapeDtypeStruct((4, 4, 2, BLOCK, WB), BF16),
        ),
        in_specs=[pl.BlockSpec(memory_space=pltpu.VMEM)],
        out_specs=(pl.BlockSpec(memory_space=pl.ANY), pl.BlockSpec(memory_space=pl.ANY)),
        scratch_shapes=[
            pltpu.VMEM((4, PADDED, WA + WB), BF16),
            pltpu.VMEM((BLOCK, WA), BF16),
            pltpu.VMEM((BLOCK, WB), BF16),
            pltpu.SemaphoreType.DMA((copies,)),
            pltpu.SemaphoreType.DMA((copies,)),
            pltpu.SemaphoreType.DMA((2,)),
        ],
        compiler_params=pltpu.CompilerParams(
            collective_id=0, has_side_effects=True, vmem_limit_bytes=16 * 1024 * 1024
        ),
        cost_estimate=pl.CostEstimate(flops=0, bytes_accessed=24_000_000, transcendentals=0),
    )(pack)


def add_blocks(dst, far, start, count, sources):
    def step(i, carry):
        total = dst[far, start + i].astype(F32)
        for source in sources:
            total = total + source(i).astype(F32)
        dst[far, start + i] = total.astype(BF16)
        return carry

    lax.fori_loop(0, count, step, 0)


def scatter_kernel(
    ga, gb, gs, out_a, out_b,
    core_a, core_b, mine_a, mine_b, one_a, one_b, two_a, two_b,
    half_a0, half_a1, half_b0, half_b1, last_a, last_b, xout, xin,
    send, recv, local,
):
    y, z, c, x = place()
    near = neighbours(y, z, c, x)
    greet(everyone_near(near))
    link = Links(send, recv)
    other = 1 - c
    jobs = [
        dict(src=[(lambda f, s: ga.at[f, :, s], 0, WA)], core=core_a, mine=mine_a, one=one_a, two=two_a,
             halves=(half_a0, half_a1), last=last_a, far="y", close="z", q=y, p=z,
             width=WA, half=1024, lane=0, i=0),
        dict(src=[(lambda f, s: gb.at[:, f, s], 0, D), (lambda f, s: gs.at[:, f, s], D, SMALL)],
             core=core_b, mine=mine_b, one=one_b, two=two_b,
             halves=(half_b0, half_b1), last=last_b, far="z", close="y", q=z, p=y,
             width=WB, half=896, lane=WA, i=1),
    ]
    slots = 0
    for step in (2, 3, 1, 0):
        for j in jobs:
            f = (j["q"] + step) % 4
            j[step] = []
            for source, lane, width in j["src"]:
                lanes = pl.ds(lane, width)
                pushed = link.push(
                    source(f, other), j["core"].at[f, :, :, lanes], near["core"]
                )
                kept = pltpu.make_async_copy(
                    source(f, c), j["mine"].at[f, :, :, lanes], local.at[slots]
                )
                slots += 1
                kept.start()
                j[step].append((pushed, kept))

    def ready(j, step):
        for pushed, kept in j[step]:
            pushed.wait_recv()
            kept.wait()

    for j in jobs:
        f = (j["q"] + 2) % 4
        ready(j, 2)
        mine = j["mine"]
        add_blocks(j["core"], f, 0, 4, [lambda i, f=f, m=mine: m[f, i]])
        plus, minus = near[j["far"]]
        j["down"] = link.push(j["core"].at[f, pl.ds(0, 2)], j["one"].at[0], minus)
        j["up"] = link.push(j["core"].at[f, pl.ds(2, 2)], j["one"].at[1], plus)
    for j in jobs:
        plus, minus = near[j["far"]]
        mine, one = j["mine"], j["one"]
        f = (j["q"] + 3) % 4
        ready(j, 3)
        add_blocks(j["core"], f, 2, 2, [lambda i, f=f, m=mine: m[f, i + 2]])
        j["down"].wait_recv()
        add_blocks(
            j["core"], f, 0, 2, [lambda i, f=f, m=mine: m[f, i], lambda i, o=one: o[0, i]]
        )
        j["down2"] = link.push(j["core"].at[f], j["two"].at[0], minus)
        f = (j["q"] + 1) % 4
        ready(j, 1)
        add_blocks(j["core"], f, 0, 2, [lambda i, f=f, m=mine: m[f, i]])
        j["up"].wait_recv()
        add_blocks(
            j["core"], f, 2, 2, [lambda i, f=f, m=mine: m[f, i + 2], lambda i, o=one: o[1, i]]
        )
        j["up2"] = link.push(j["core"].at[f], j["two"].at[1], plus)
    for j in jobs:
        mine, two = j["mine"], j["two"]
        f = j["q"]
        ready(j, 0)
        j["down2"].wait_recv()
        j["up2"].wait_recv()
        add_blocks(
            j["core"], f, 0, 4,
            [lambda i, f=f, m=mine: m[f, i], lambda i, t=two: t[0, i], lambda i, t=two: t[1, i]],
        )
        plus, minus = near[j["close"]]
        g = (j["p"] + 2) % 4
        h, w = j["half"], j["width"]
        j["down"] = link.push(j["core"].at[f, g, :, pl.ds(0, h)], j["halves"][0], minus)
        j["up"] = link.push(j["core"].at[f, g, :, pl.ds(h, w - h)], j["halves"][1], plus)
    for j in jobs:
        plus, minus = near[j["close"]]
        f, h, w, core = j["q"], j["half"], j["width"], j["core"]
        g = (j["p"] + 3) % 4
        j["down"].wait_recv()
        core[f, g, :, 0:h] = (
            core[f, g, :, 0:h].astype(F32) + j["halves"][0][...].astype(F32)
        ).astype(BF16)
        j["down2"] = link.push(core.at[f, g], j["last"].at[0], minus)
        g = (j["p"] + 1) % 4
        j["up"].wait_recv()
        core[f, g, :, h:w] = (
            core[f, g, :, h:w].astype(F32) + j["halves"][1][...].astype(F32)
        ).astype(BF16)
        j["up2"] = link.push(core.at[f, g], j["last"].at[1], plus)
    select = pick_rows(4 * PADDED, BLOCK, PADDED, PIECE)
    for j in jobs:
        f, g = j["q"], j["p"]
        j["down2"].wait_recv()
        j["up2"].wait_recv()
        total = (
            j["core"][f, g].astype(F32)
            + j["last"][0].astype(F32)
            + j["last"][1].astype(F32)
        ).astype(BF16)
        spread = jnp.dot(select, total, preferred_element_type=F32).astype(BF16)
        xout[:, :, j["lane"] : j["lane"] + j["width"]] = spread.reshape(4, PADDED, j["width"])
    final = [
        link.push(xout.at[(x + d) % 4], xin.at[d - 1], near["x"][d - 1]) for d in (1, 2, 3)
    ]
    for copy in final:
        copy.wait_recv()
    mine = xout[x].astype(F32)
    for d in range(3):
        mine = mine + xin[d].astype(F32)
    out_a[...] = mine[:, :WA]
    out_b[...] = mine[:, WA:]
    link.drain()


def scatter_sums(ga, gb, gs):
    copies = 2 * (4 + 4 + 4) + 4 + 3
    vmem = pltpu.VMEM
    scratch = []
    for shape in ((4, 4), (4, 4), (2, 2), (2, 4)):
        scratch += [vmem((*shape, BLOCK, WA), BF16), vmem((*shape, BLOCK, WB), BF16)]
    scratch += [
        vmem((BLOCK, 1024), BF16),
        vmem((BLOCK, 1024), BF16),
        vmem((BLOCK, 896), BF16),
        vmem((BLOCK, WB - 896), BF16),
        vmem((2, BLOCK, WA), BF16),
        vmem((2, BLOCK, WB), BF16),
        vmem((4, PADDED, WA + WB), BF16),
        vmem((3, PADDED, WA + WB), BF16),
        pltpu.SemaphoreType.DMA((copies,)),
        pltpu.SemaphoreType.DMA((copies,)),
        pltpu.SemaphoreType.DMA((12,)),
    ]
    return pl.pallas_call(
        scatter_kernel,
        name="scatter_sums",
        out_shape=(
            jax.ShapeDtypeStruct((PADDED, WA), F32),
            jax.ShapeDtypeStruct((PADDED, WB), F32),
        ),
        in_specs=[pl.BlockSpec(memory_space=pl.ANY)] * 3,
        out_specs=(pl.BlockSpec(memory_space=pltpu.VMEM), pl.BlockSpec(memory_space=pltpu.VMEM)),
        scratch_shapes=scratch,
        compiler_params=pltpu.CompilerParams(
            collective_id=1, has_side_effects=True, vmem_limit_bytes=40 * 1024 * 1024
        ),
        cost_estimate=pl.CostEstimate(flops=0, bytes_accessed=24_000_000, transcendentals=0),
    )(ga, gb, gs)


def rms_scale(values, gain_vec):
    return (
        values * lax.rsqrt(jnp.mean(values * values, axis=-1, keepdims=True) + norm_eps) * gain_vec
    )


def rope_tables(position, half_dim):
    frequency = rope_base ** (-jnp.arange(half_dim, dtype=jnp.float32) / half_dim)
    angles = position.astype(jnp.float32)[:, None] * frequency[None, :]
    return (jnp.cos(angles)[:, None, :], jnp.sin(angles)[:, None, :])


def rotate(values, cosine, sine_tab):
    half_dim = values.shape[-1] // 2
    lower_half = values[..., :half_dim]
    upper_half = values[..., half_dim:]
    return jnp.concatenate(
        [lower_half * cosine - upper_half * sine_tab, lower_half * sine_tab + upper_half * cosine],
        axis=-1,
    )


def unrotate(grads_in, cosine, sine_tab):
    half_dim = grads_in.shape[-1] // 2
    lower_half = grads_in[..., :half_dim]
    upper_half = grads_in[..., half_dim:]
    return jnp.concatenate(
        [lower_half * cosine + upper_half * sine_tab, upper_half * cosine - lower_half * sine_tab],
        axis=-1,
    )


def seq_layout(seq_lens, row_ids):
    seq_ends = jnp.cumsum(seq_lens)
    segment = jnp.sum((row_ids[:, None] >= seq_ends[None, :]).astype(jnp.int32), axis=1)
    seq_start = jnp.sum(
        jnp.where(seq_ends[None, :] <= row_ids[:, None], seq_lens[None, :], 0), axis=1
    )
    return (segment, row_ids - seq_start)


def exchange(rows):
    return lax.all_to_all(
        rows.reshape(EXPERTS, CAP, D), "expert", split_axis=0, concat_axis=0, tiled=True
    ).reshape(EXPERTS * CAP, D)


def body(
    tokens, lengths, top_experts, w_qkv, w_out, gain_attn, gain_ffn, router, gate_up, down_proj, cotangent,
):
    count = tokens.shape[0]
    scale = HEAD_DIM ** (-0.5)
    pack = jnp.concatenate(
        [
            w_qkv,
            w_out.T,
            router,
            gain_attn[:, None],
            gain_ffn[:, None],
            jnp.zeros((PIECE, SMALL - EXPERTS - 2), BF16),
        ],
        axis=1,
    )
    pack = jnp.pad(pack, ((0, PADDED - PIECE), (0, 0)))
    full_a, full_b = gather_weights(pack)
    full_qkv = full_a.reshape(D, WA)
    full_b = full_b.reshape(D, WB)
    out_t = full_b[:, :D]
    full_router = full_b[:, D : D + EXPERTS]
    gains = full_b[:, D + EXPERTS : D + EXPERTS + 2].astype(F32).T
    attn_g, ffn_g = gains[0], gains[1]

    named = jnp.sum(
        (top_experts[:, :, None] == jnp.arange(EXPERTS, dtype=jnp.int32)).astype(F32), axis=1
    )
    row_ids = jnp.arange(count, dtype=jnp.int32)
    earlier = (row_ids[None, :] < row_ids[:, None]).astype(BF16)
    slot_of = jnp.dot(earlier, named.astype(BF16), preferred_element_type=F32)
    slot_of = jnp.where(named > 0, slot_of, -1.0)
    hits = slot_of[:, :, None] == jnp.arange(CAP, dtype=F32)
    any_slot = hits.reshape(count, EXPERTS * CAP).astype(BF16)
    logits = jnp.dot(tokens, full_router, preferred_element_type=F32)
    masked_logits = jnp.where(named > 0, logits, -jnp.inf)
    gates = jax.nn.softmax(masked_logits, axis=-1)
    slot_gates = jnp.sum(jnp.where(hits, gates[:, :, None], 0.0), axis=0).reshape(-1)
    row_grads = (
        jnp.dot(any_slot.T, cotangent, preferred_element_type=F32) * slot_gates[:, None]
    ).astype(BF16)
    arrived_grads = exchange(row_grads)

    tok_f = tokens.astype(F32)
    normed = rms_scale(tok_f, attn_g).astype(BF16)
    projected = jnp.dot(normed, full_qkv, preferred_element_type=F32)
    shard_pos = lax.axis_index("shard")
    group_rows = lax.axis_size("shard") * count
    all_ids = jnp.arange(group_rows, dtype=jnp.int32)
    key_segment, key_position = seq_layout(lengths[0], all_ids)
    own_ids = shard_pos * count + row_ids
    own_segment = lax.dynamic_slice_in_dim(key_segment, shard_pos * count, count)
    own_position = lax.dynamic_slice_in_dim(key_position, shard_pos * count, count)
    cosine, sine_tab = rope_tables(own_position, HEAD_DIM // 2)
    queries = rotate(
        projected[:, :WIDTH_Q].reshape(count, HEADS_Q, HEAD_DIM), cosine, sine_tab
    ).astype(BF16)
    keys_rot = rotate(
        projected[:, WIDTH_Q : WIDTH_Q + WIDTH_KV].reshape(count, HEADS_KV, HEAD_DIM),
        cosine,
        sine_tab,
    ).astype(BF16)
    values = projected[:, WIDTH_Q + WIDTH_KV :].astype(BF16)
    local_kv = jnp.concatenate([keys_rot.reshape(count, WIDTH_KV), values], axis=1)
    group_kv = lax.all_gather(local_kv, "shard", axis=0, tiled=True)
    keys_all = group_kv[:, :WIDTH_KV].reshape(group_rows, HEADS_KV, HEAD_DIM)
    values_all = group_kv[:, WIDTH_KV:].reshape(group_rows, HEADS_KV, HEAD_DIM)
    grouped = queries.reshape(count, HEADS_KV, REPEAT, HEAD_DIM)
    allowed = (own_segment[:, None] == key_segment[None, :]) & (
        all_ids[None, :] <= own_ids[:, None]
    )

    def attn_scores():
        raw_scores = (
            jnp.einsum("tgrd,kgd->grtk", grouped, keys_all, preferred_element_type=F32) * scale
        )
        return jnp.where(allowed, raw_scores, -1e30)

    masked = attn_scores()
    top_score = jnp.max(masked, axis=-1, keepdims=True)
    expo_vals = jnp.exp(masked - top_score)
    total_weight = jnp.sum(expo_vals, axis=-1, keepdims=True)
    probs_low = (expo_vals / total_weight).astype(BF16)
    attended = (
        jnp.einsum("grtk,kgd->tgrd", probs_low, values_all, preferred_element_type=F32)
        .reshape(count, WIDTH_Q)
        .astype(BF16)
    )
    branch = lax.dot_general(
        attended, out_t, (((1,), (1,)), ((), ())), preferred_element_type=F32
    )
    middle = tok_f + branch
    normed_ffn = rms_scale(middle, ffn_g).astype(BF16)
    dispatch = jnp.dot(any_slot.T, normed_ffn, preferred_element_type=F32).astype(BF16)
    dispatch, arrived_grads = lax.optimization_barrier((dispatch, arrived_grads))
    arrived = exchange(dispatch)
    hidden = jnp.dot(arrived, gate_up[0], preferred_element_type=F32)

    def activate(hidden_in):
        return jax.nn.gelu(hidden_in[:, :FF], approximate=True) * hidden_in[:, FF:]

    mixed_hidden, act_pull = jax.vjp(activate, hidden)
    mixed_low = mixed_hidden.astype(BF16)
    grad_mixed = jnp.dot(arrived_grads, down_proj[0].T, preferred_element_type=F32)
    grad_hidden = act_pull(grad_mixed)[0].astype(BF16)
    grad_rows = jnp.dot(grad_hidden, gate_up[0].T, preferred_element_type=F32).astype(BF16)
    back_rows = exchange(grad_rows)
    expert_out = jnp.dot(mixed_low, down_proj[0], preferred_element_type=F32).astype(BF16)
    expert_out, back_rows = lax.optimization_barrier((expert_out, back_rows))
    returned = exchange(expert_out)
    grad_down_local = jnp.dot(mixed_low.T, arrived_grads, preferred_element_type=F32)
    grad_up_local = jnp.dot(arrived.T, grad_hidden, preferred_element_type=F32)

    upstream = cotangent.astype(F32)
    grad_normed_ffn = jnp.dot(any_slot, back_rows, preferred_element_type=F32)
    ffn_value, ffn_pull = jax.vjp(rms_scale, middle, ffn_g)
    grad_mid_norm, grad_ffn_gain = ffn_pull(grad_normed_ffn)
    grad_middle = upstream + grad_mid_norm
    grad_branch = grad_middle.astype(BF16)
    grad_out_t = jnp.dot(grad_branch.T, attended, preferred_element_type=F32).astype(BF16)
    grad_attended = (
        jnp.dot(grad_branch, out_t, preferred_element_type=F32)
        .astype(BF16)
        .reshape(count, HEADS_KV, REPEAT, HEAD_DIM)
    )
    probs_again = jnp.exp(attn_scores() - top_score) / total_weight
    grad_probs = jnp.einsum(
        "tgrd,kgd->grtk", grad_attended, values_all, preferred_element_type=F32
    )
    grad_scores = (
        probs_again * (grad_probs - jnp.sum(probs_again * grad_probs, axis=-1, keepdims=True))
    ).astype(BF16)
    grad_queries = (
        jnp.einsum("grtk,kgd->tgrd", grad_scores, keys_all, preferred_element_type=F32) * scale
    )
    grad_keys = (
        jnp.einsum("grtk,tgrd->kgd", grad_scores, grouped, preferred_element_type=F32) * scale
    )
    grad_values = jnp.einsum(
        "grtk,tgrd->kgd", probs_low, grad_attended, preferred_element_type=F32
    )
    group_grads = jnp.concatenate(
        [grad_keys.reshape(group_rows, WIDTH_KV), grad_values.reshape(group_rows, WIDTH_KV)], axis=1
    )
    own_kv_grads = lax.psum_scatter(
        group_grads.astype(BF16), "shard", scatter_dimension=0, tiled=True
    ).astype(F32)
    grad_projected = jnp.concatenate(
        [
            unrotate(grad_queries.reshape(count, HEADS_Q, HEAD_DIM), cosine, sine_tab).reshape(
                count, WIDTH_Q
            ),
            unrotate(
                own_kv_grads[:, :WIDTH_KV].reshape(count, HEADS_KV, HEAD_DIM), cosine, sine_tab
            ).reshape(count, WIDTH_KV),
            own_kv_grads[:, WIDTH_KV:],
        ],
        axis=1,
    ).astype(BF16)
    grad_qkv_local = jnp.dot(normed.T, grad_projected, preferred_element_type=F32).astype(BF16)
    grad_normed = lax.dot_general(
        grad_projected, full_qkv, (((1,), (1,)), ((), ())), preferred_element_type=F32
    )
    attn_value, attn_pull = jax.vjp(rms_scale, tok_f, attn_g)
    grad_tok_norm, grad_attn_gain = attn_pull(grad_normed)

    mix = jnp.where(hits, gates[:, :, None], 0.0).reshape(count, EXPERTS * CAP)
    mix_high = mix.astype(BF16)
    mix_low = (mix - mix_high.astype(F32)).astype(BF16)
    combined = jnp.dot(mix_high, returned, preferred_element_type=F32) + jnp.dot(
        mix_low, returned, preferred_element_type=F32
    )
    output = (middle + combined).astype(BF16)
    products = lax.dot_general(
        cotangent, returned, (((1,), (1,)), ((), ())), preferred_element_type=F32
    ).reshape(count, EXPERTS, CAP)
    gate_grad = jnp.sum(jnp.where(hits, products, 0.0), axis=-1)
    logit_grad = gates * (gate_grad - jnp.sum(gates * gate_grad, axis=-1, keepdims=True))
    router_f = full_router.astype(F32)
    grad_router_local = jnp.dot(tok_f.T, logit_grad, precision=precise)
    grad_from_router = jnp.dot(logit_grad, router_f.T, precision=precise)
    grad_tokens = (grad_middle + grad_tok_norm + grad_from_router).astype(BF16)

    grad_small = jnp.concatenate(
        [
            grad_router_local,
            grad_attn_gain[:, None],
            grad_ffn_gain[:, None],
            jnp.zeros((D, SMALL - EXPERTS - 2), F32),
        ],
        axis=1,
    ).astype(BF16)
    sum_a, sum_b = scatter_sums(
        grad_qkv_local.reshape(4, 4, 2, BLOCK, WA),
        grad_out_t.reshape(4, 4, 2, BLOCK, D),
        grad_small.reshape(4, 4, 2, BLOCK, SMALL),
    )
    sum_b = sum_b[:PIECE]
    up_sum = lax.psum_scatter(
        grad_up_local[None].astype(BF16), "shard", scatter_dimension=1, tiled=True
    ).astype(F32)
    down_sum = lax.psum_scatter(
        grad_down_local[None].astype(BF16), "shard", scatter_dimension=2, tiled=True
    ).astype(F32)
    return (
        output,
        grad_tokens,
        sum_a[:PIECE],
        sum_b[:, :D].T,
        sum_b[:, D + EXPERTS],
        sum_b[:, D + EXPERTS + 1],
        sum_b[:, D : D + EXPERTS],
        up_sum,
        down_sum,
    )


def solution(mesh):
    return jax.shard_map(
        body,
        mesh=mesh,
        in_specs=(
            P(("expert", "shard"), None),
            P("expert", None),
            P(("expert", "shard"), None),
            P(("expert", "shard"), None),
            P(None, ("expert", "shard")),
            P(("expert", "shard")),
            P(("expert", "shard")),
            P(("expert", "shard"), None),
            P("expert", None, None),
            P("expert", None, None),
            P(("expert", "shard"), None),
        ),
        out_specs=(
            P(("expert", "shard"), None),
            P(("expert", "shard"), None),
            P(("expert", "shard"), None),
            P(None, ("expert", "shard")),
            P(("expert", "shard")),
            P(("expert", "shard")),
            P(("expert", "shard"), None),
            P("expert", "shard", None),
            P("expert", None, "shard"),
        ),
        check_vma=False,
    )
```

```python
import functools

import jax
import jax.numpy as jnp
from jax import lax
from jax.experimental import pallas as pl
from jax.experimental.pallas import tpu as pltpu
from jax.sharding import PartitionSpec as P

D = 1536
HEADS_Q = 12
HEADS_KV = 2
HEAD_DIM = 128
FF = 768
TOP = 4
EXPERTS = 32
CAP = 48
WIDTH_Q = HEADS_Q * HEAD_DIM
WIDTH_KV = HEADS_KV * HEAD_DIM
REPEAT = HEADS_Q // HEADS_KV

norm_eps = 1e-06
rope_base = 1000000.0
precise = lax.Precision.HIGHEST
MESH = pl.DeviceIdType.MESH
F32 = jnp.float32
BF16 = jnp.bfloat16

PIECE = 12
PADDED = 16
BLOCK = 48
WA = 2048
WB = 1664
SMALL = WB - D


def place():
    e = lax.axis_index("expert")
    return e // 8, (e // 2) % 4, e % 2, lax.axis_index("shard")


def device(y, z, c, x):
    return ((y * 4 + z) * 2 + c, x)


def greet(devices):
    barrier = pltpu.get_barrier_semaphore()
    for d in devices:
        pl.semaphore_signal(barrier, inc=1, device_id=d, device_id_type=MESH)
    pl.semaphore_wait(barrier, len(devices))


class Links:
    def __init__(self, send, recv):
        self.send, self.recv, self.made = send, recv, []

    def push(self, src, dst, where):
        i = len(self.made)
        copy = pltpu.make_async_remote_copy(
            src_ref=src,
            dst_ref=dst,
            send_sem=self.send.at[i],
            recv_sem=self.recv.at[i],
            device_id=where,
            device_id_type=MESH,
        )
        copy.start()
        self.made.append(copy)
        return copy

    def drain(self):
        for copy in self.made:
            copy.wait_send()


def neighbours(y, z, c, x):
    other = 1 - c
    return dict(
        x=[device(y, z, c, (x + d) % 4) for d in (1, 2, 3)],
        y=(device((y + 1) % 4, z, c, x), device((y + 3) % 4, z, c, x)),
        z=(device(y, (z + 1) % 4, c, x), device(y, (z + 3) % 4, c, x)),
        core=device(y, z, other, x),
    )


def everyone_near(near):
    return list(near["x"]) + list(near["y"]) + list(near["z"]) + [near["core"]]


def pick_rows(rows, columns, row_block, column_block):
    r = lax.broadcasted_iota(jnp.int32, (rows, columns), 0)
    q = lax.broadcasted_iota(jnp.int32, (rows, columns), 1)
    same = (r // row_block == q // column_block) & (r % row_block == q % column_block)
    return jnp.where(same, 1.0, 0.0).astype(BF16)


def gather_kernel(pack, full_a, full_b, xbuf, own_a, own_b, send, recv, local):
    y, z, c, x = place()
    near = neighbours(y, z, c, x)
    greet(everyone_near(near))
    link = Links(send, recv)
    first = [link.push(pack, xbuf.at[x], near["x"][d]) for d in range(3)]
    xbuf[pl.ds(x, 1)] = pack[...][None]
    for copy in first:
        copy.wait_recv()
    select = pick_rows(BLOCK, 4 * PADDED, PIECE, PADDED)
    pieces = xbuf[...].reshape(4 * PADDED, WA + WB)
    own_a[...] = jnp.dot(select, pieces[:, :WA], preferred_element_type=F32).astype(BF16)
    own_b[...] = jnp.dot(select, pieces[:, WA:], preferred_element_type=F32).astype(BF16)

    def at_a(far, close, columns=None):
        view = full_a.at[far, close, c]
        return view if columns is None else view.at[:, columns]

    def at_b(far, close, columns=None):
        view = full_b.at[close, far, c]
        return view if columns is None else view.at[:, columns]

    def line_a(far, part=slice(None)):
        return full_a.at[far, part, c]

    def line_b(far, part=slice(None)):
        return full_b.at[part, far, c]

    jobs = [
        dict(own=own_a, at=at_a, line=line_a, close="z", far="y", p=z, q=y, half=1024, i=0),
        dict(own=own_b, at=at_b, line=line_b, close="y", far="z", p=y, q=z, half=896, i=1),
    ]
    for j in jobs:
        here = j["at"](j["q"], j["p"])
        plus, minus = near[j["close"]]
        j["up"] = link.push(j["own"], here, plus)
        j["down"] = link.push(j["own"], here, minus)
        j["core"] = [link.push(j["own"], here, near["core"])]
        j["local"] = pltpu.make_async_copy(j["own"], here, local.at[j["i"]])
        j["local"].start()
    for j in jobs:
        plus, minus = near[j["close"]]
        left, right = (j["p"] + 3) % 4, (j["p"] + 1) % 4
        j["up"].wait_recv()
        part = j["at"](j["q"], left, pl.ds(0, j["half"]))
        j["up2"] = link.push(part, part, plus)
        j["down"].wait_recv()
        part = j["at"](j["q"], right, pl.ds(j["half"], j["own"].shape[1] - j["half"]))
        j["down2"] = link.push(part, part, minus)
        for side in (left, right):
            block = j["at"](j["q"], side)
            j["core"].append(link.push(block, block, near["core"]))
    for j in jobs:
        j["up2"].wait_recv()
        j["down2"].wait_recv()
        block = j["at"](j["q"], (j["p"] + 2) % 4)
        j["local"].wait()
        plus, minus = near[j["far"]]
        line = j["line"](j["q"])
        j["up"] = link.push(line, line, plus)
        j["down"] = link.push(line, line, minus)
        j["core"].append(link.push(block, block, near["core"]))
    for j in jobs:
        plus, minus = near[j["far"]]
        left, right = (j["q"] + 3) % 4, (j["q"] + 1) % 4
        j["up"].wait_recv()
        part = j["line"](left, pl.ds(0, 2))
        j["up2"] = link.push(part, part, plus)
        j["down"].wait_recv()
        part = j["line"](right, pl.ds(2, 2))
        j["down2"] = link.push(part, part, minus)
        for side in (left, right):
            block = j["line"](side)
            j["core"].append(link.push(block, block, near["core"]))
    for j in jobs:
        opposite = (j["q"] + 2) % 4
        j["up2"].wait_recv()
        part = j["line"](opposite, pl.ds(0, 2))
        j["core"].append(link.push(part, part, near["core"]))
        j["down2"].wait_recv()
        part = j["line"](opposite, pl.ds(2, 2))
        j["core"].append(link.push(part, part, near["core"]))
    for j in jobs:
        for copy in j["core"]:
            copy.wait_recv()
    link.drain()


def gather_weights(pack):
    copies = 3 + 2 * 16
    return pl.pallas_call(
        gather_kernel,
        name="gather_weights",
        out_shape=(
            jax.ShapeDtypeStruct((4, 4, 2, BLOCK, WA), BF16),
            jax.ShapeDtypeStruct((4, 4, 2, BLOCK, WB), BF16),
        ),
        in_specs=[pl.BlockSpec(memory_space=pltpu.VMEM)],
        out_specs=(pl.BlockSpec(memory_space=pl.ANY), pl.BlockSpec(memory_space=pl.ANY)),
        scratch_shapes=[
            pltpu.VMEM((4, PADDED, WA + WB), BF16),
            pltpu.VMEM((BLOCK, WA), BF16),
            pltpu.VMEM((BLOCK, WB), BF16),
            pltpu.SemaphoreType.DMA((copies,)),
            pltpu.SemaphoreType.DMA((copies,)),
            pltpu.SemaphoreType.DMA((2,)),
        ],
        compiler_params=pltpu.CompilerParams(
            collective_id=0, has_side_effects=True, vmem_limit_bytes=16 * 1024 * 1024
        ),
        cost_estimate=pl.CostEstimate(flops=0, bytes_accessed=24_000_000, transcendentals=0),
    )(pack)


def add_blocks(dst, far, start, count, sources):
    def step(i, carry):
        total = dst[far, start + i].astype(F32)
        for source in sources:
            total = total + source(i).astype(F32)
        dst[far, start + i] = total.astype(BF16)
        return carry

    lax.fori_loop(0, count, step, 0)


def scatter_kernel(
    ga, gb, gs, out_a, out_b,
    core_a, core_b, mine_a, mine_b, one_a, one_b, two_a, two_b,
    half_a0, half_a1, half_b0, half_b1, last_a, last_b, xout, xin,
    send, recv, local,
):
    y, z, c, x = place()
    near = neighbours(y, z, c, x)
    greet(everyone_near(near))
    link = Links(send, recv)
    other = 1 - c
    jobs = [
        dict(src=[(lambda f, s: ga.at[f, :, s], 0, WA)], core=core_a, mine=mine_a, one=one_a, two=two_a,
             halves=(half_a0, half_a1), last=last_a, far="y", close="z", q=y, p=z,
             width=WA, half=1024, lane=0, i=0),
        dict(src=[(lambda f, s: gb.at[:, f, s], 0, D), (lambda f, s: gs.at[:, f, s], D, SMALL)],
             core=core_b, mine=mine_b, one=one_b, two=two_b,
             halves=(half_b0, half_b1), last=last_b, far="z", close="y", q=z, p=y,
             width=WB, half=896, lane=WA, i=1),
    ]
    slots = 0
    for step in (2, 3, 1, 0):
        for j in jobs:
            f = (j["q"] + step) % 4
            j[step] = []
            for source, lane, width in j["src"]:
                lanes = pl.ds(lane, width)
                pushed = link.push(
                    source(f, other), j["core"].at[f, :, :, lanes], near["core"]
                )
                kept = pltpu.make_async_copy(
                    source(f, c), j["mine"].at[f, :, :, lanes], local.at[slots]
                )
                slots += 1
                kept.start()
                j[step].append((pushed, kept))

    def ready(j, step):
        for pushed, kept in j[step]:
            pushed.wait_recv()
            kept.wait()

    for j in jobs:
        f = (j["q"] + 2) % 4
        ready(j, 2)
        mine = j["mine"]
        add_blocks(j["core"], f, 0, 4, [lambda i, f=f, m=mine: m[f, i]])
        plus, minus = near[j["far"]]
        j["down"] = link.push(j["core"].at[f, pl.ds(0, 2)], j["one"].at[0], minus)
        j["up"] = link.push(j["core"].at[f, pl.ds(2, 2)], j["one"].at[1], plus)
    for j in jobs:
        plus, minus = near[j["far"]]
        mine, one = j["mine"], j["one"]
        f = (j["q"] + 3) % 4
        ready(j, 3)
        add_blocks(j["core"], f, 2, 2, [lambda i, f=f, m=mine: m[f, i + 2]])
        j["down"].wait_recv()
        add_blocks(
            j["core"], f, 0, 2, [lambda i, f=f, m=mine: m[f, i], lambda i, o=one: o[0, i]]
        )
        j["down2"] = link.push(j["core"].at[f], j["two"].at[0], minus)
        f = (j["q"] + 1) % 4
        ready(j, 1)
        add_blocks(j["core"], f, 0, 2, [lambda i, f=f, m=mine: m[f, i]])
        j["up"].wait_recv()
        add_blocks(
            j["core"], f, 2, 2, [lambda i, f=f, m=mine: m[f, i + 2], lambda i, o=one: o[1, i]]
        )
        j["up2"] = link.push(j["core"].at[f], j["two"].at[1], plus)
    for j in jobs:
        mine, two = j["mine"], j["two"]
        f = j["q"]
        ready(j, 0)
        j["down2"].wait_recv()
        j["up2"].wait_recv()
        add_blocks(
            j["core"], f, 0, 4,
            [lambda i, f=f, m=mine: m[f, i], lambda i, t=two: t[0, i], lambda i, t=two: t[1, i]],
        )
        plus, minus = near[j["close"]]
        g = (j["p"] + 2) % 4
        h, w = j["half"], j["width"]
        j["down"] = link.push(j["core"].at[f, g, :, pl.ds(0, h)], j["halves"][0], minus)
        j["up"] = link.push(j["core"].at[f, g, :, pl.ds(h, w - h)], j["halves"][1], plus)
    for j in jobs:
        plus, minus = near[j["close"]]
        f, h, w, core = j["q"], j["half"], j["width"], j["core"]
        g = (j["p"] + 3) % 4
        j["down"].wait_recv()
        core[f, g, :, 0:h] = (
            core[f, g, :, 0:h].astype(F32) + j["halves"][0][...].astype(F32)
        ).astype(BF16)
        j["down2"] = link.push(core.at[f, g], j["last"].at[0], minus)
        g = (j["p"] + 1) % 4
        j["up"].wait_recv()
        core[f, g, :, h:w] = (
            core[f, g, :, h:w].astype(F32) + j["halves"][1][...].astype(F32)
        ).astype(BF16)
        j["up2"] = link.push(core.at[f, g], j["last"].at[1], plus)
    select = pick_rows(4 * PADDED, BLOCK, PADDED, PIECE)
    for j in jobs:
        f, g = j["q"], j["p"]
        j["down2"].wait_recv()
        j["up2"].wait_recv()
        total = (
            j["core"][f, g].astype(F32)
            + j["last"][0].astype(F32)
            + j["last"][1].astype(F32)
        ).astype(BF16)
        spread = jnp.dot(select, total, preferred_element_type=F32).astype(BF16)
        xout[:, :, j["lane"] : j["lane"] + j["width"]] = spread.reshape(4, PADDED, j["width"])
    final = [
        link.push(xout.at[(x + d) % 4], xin.at[d - 1], near["x"][d - 1]) for d in (1, 2, 3)
    ]
    for copy in final:
        copy.wait_recv()
    mine = xout[x].astype(F32)
    for d in range(3):
        mine = mine + xin[d].astype(F32)
    out_a[...] = mine[:, :WA]
    out_b[...] = mine[:, WA:]
    link.drain()


def scatter_sums(ga, gb, gs):
    copies = 2 * (4 + 4 + 4) + 4 + 3
    vmem = pltpu.VMEM
    scratch = []
    for shape in ((4, 4), (4, 4), (2, 2), (2, 4)):
        scratch += [vmem((*shape, BLOCK, WA), BF16), vmem((*shape, BLOCK, WB), BF16)]
    scratch += [
        vmem((BLOCK, 1024), BF16),
        vmem((BLOCK, 1024), BF16),
        vmem((BLOCK, 896), BF16),
        vmem((BLOCK, WB - 896), BF16),
        vmem((2, BLOCK, WA), BF16),
        vmem((2, BLOCK, WB), BF16),
        vmem((4, PADDED, WA + WB), BF16),
        vmem((3, PADDED, WA + WB), BF16),
        pltpu.SemaphoreType.DMA((copies,)),
        pltpu.SemaphoreType.DMA((copies,)),
        pltpu.SemaphoreType.DMA((12,)),
    ]
    return pl.pallas_call(
        scatter_kernel,
        name="scatter_sums",
        out_shape=(
            jax.ShapeDtypeStruct((PADDED, WA), F32),
            jax.ShapeDtypeStruct((PADDED, WB), F32),
        ),
        in_specs=[pl.BlockSpec(memory_space=pl.ANY)] * 3,
        out_specs=(pl.BlockSpec(memory_space=pltpu.VMEM), pl.BlockSpec(memory_space=pltpu.VMEM)),
        scratch_shapes=scratch,
        compiler_params=pltpu.CompilerParams(
            collective_id=1, has_side_effects=True, vmem_limit_bytes=40 * 1024 * 1024
        ),
        cost_estimate=pl.CostEstimate(flops=0, bytes_accessed=24_000_000, transcendentals=0),
    )(ga, gb, gs)


NEAREST = (
    (0, 0), (0, 1), (1, 0), (0, 3),
    (3, 0), (1, 1), (3, 3), (1, 3),
    (3, 1), (0, 2), (2, 0), (1, 2),
    (2, 1), (3, 2), (2, 3), (2, 2),
)
ROWS = EXPERTS * CAP
CHUNKS = 4
CHUNK = ROWS // CHUNKS
TILE = 256


def gelu_parts(g):
    inner = 0.7978845608 * (g + 0.044715 * g * g * g)
    th = jnp.tanh(inner)
    half = 0.5 * (1.0 + th)
    slope = half + 0.5 * g * (1.0 - th * th) * (0.7978845608 * (1.0 + 0.134145 * g * g))
    return g * half, slope


def experts_kernel(
    sent, grads_in, gate_up, down, back, outs, up_grad, down_grad,
    rows, grads, gu, dn, mixed, ghid, grow, eout,
    send, recv, bsend, brecv, gsem, wsem, osem, own,
):
    y, z, c, x = place()
    me = (y * 4 + z) * 2 + c
    weights = [
        pltpu.make_async_copy(gate_up.at[0], gu, wsem.at[0]),
        pltpu.make_async_copy(down.at[0], dn, wsem.at[1]),
    ]
    slots = []
    for s, (dy, dz) in enumerate(NEAREST):
        for b in (0, 1):
            core = c if b == 0 else 1 - c
            source = device((y + dy) % 4, (z + dz) % 4, core, x)
            target = device((y + 4 - dy) % 4, (z + 4 - dz) % 4, core, x)
            slots.append((2 * s + b, source, target))
    greet([source for _, source, _ in slots[1:]])
    links, back_links = [], []
    for i, source, target in slots:
        here = rows.at[pl.ds(i * CAP, CAP)]
        if i == 0:
            copy = pltpu.make_async_copy(sent.at[me], here, own.at[0])
        else:
            copy = pltpu.make_async_remote_copy(
                src_ref=sent.at[target[0]], dst_ref=here, send_sem=send.at[i],
                recv_sem=recv.at[i], device_id=target, device_id_type=MESH,
            )
        copy.start()
        links.append(copy)
    incoming = []
    for copy in weights:
        copy.start()
    for i, source, target in slots:
        copy = pltpu.make_async_copy(
            grads_in.at[source[0]], grads.at[pl.ds(i * CAP, CAP)], gsem.at[i]
        )
        copy.start()
        incoming.append(copy)
    for copy in weights:
        copy.wait()
    leaving = []
    per = len(slots) // CHUNKS
    for k in range(CHUNKS):
        part = slots[k * per : (k + 1) * per]
        for i, source, target in part:
            incoming[i].wait()
            if i == 0:
                links[0].wait()
            else:
                links[i].wait_recv()
        base = k * CHUNK
        block = pl.ds(base, CHUNK)

        def hidden_tile(j, carry, block=block):
            lanes = pl.ds(pl.multiple_of(j * TILE, TILE), TILE)
            upper = pl.ds(pl.multiple_of(FF + j * TILE, TILE), TILE)
            g = jnp.dot(rows[block, :], gu[:, lanes], preferred_element_type=F32)
            act, slope = gelu_parts(g)
            u = jnp.dot(rows[block, :], gu[:, upper], preferred_element_type=F32)
            mixed[block, lanes] = (act * u).astype(BF16)
            m = lax.dot_general(
                grads[block, :], dn[lanes, :], (((1,), (1,)), ((), ())),
                preferred_element_type=F32,
            )
            ghid[block, lanes] = (m * u * slope).astype(BF16)
            ghid[block, upper] = (m * act).astype(BF16)
            return carry

        lax.fori_loop(0, FF // TILE, hidden_tile, 0)

        def rows_tile(j, carry, block=block):
            lanes = pl.ds(pl.multiple_of(j * TILE, TILE), TILE)
            grow[block, lanes] = lax.dot_general(
                ghid[block, :], gu[lanes, :], (((1,), (1,)), ((), ())),
                preferred_element_type=F32,
            ).astype(BF16)
            return carry

        lax.fori_loop(0, D // TILE, rows_tile, 0)
        for i, source, target in part:
            here = grow.at[pl.ds(i * CAP, CAP)]
            if i == 0:
                copy = pltpu.make_async_copy(here, back.at[me], own.at[1])
            else:
                copy = pltpu.make_async_remote_copy(
                    src_ref=here, dst_ref=back.at[me], send_sem=bsend.at[i],
                    recv_sem=brecv.at[i], device_id=source, device_id_type=MESH,
                )
            copy.start()
            back_links.append(copy)

        def out_tile(j, carry, block=block):
            lanes = pl.ds(pl.multiple_of(j * TILE, TILE), TILE)
            eout[block, lanes] = jnp.dot(
                mixed[block, :], dn[:, lanes], preferred_element_type=F32
            ).astype(BF16)
            return carry

        lax.fori_loop(0, D // TILE, out_tile, 0)
        for i, source, target in part:
            copy = pltpu.make_async_copy(
                eout.at[pl.ds(i * CAP, CAP)], outs.at[source[0]], osem.at[i]
            )
            copy.start()
            leaving.append(copy)

    def up_tile(j, carry):
        lanes = pl.ds(pl.multiple_of(j * TILE, TILE), TILE)
        up_grad[lanes, :] = lax.dot_general(
            rows[:, lanes], ghid[...], (((0,), (0,)), ((), ())), preferred_element_type=F32
        ).astype(BF16)
        return carry

    lax.fori_loop(0, D // TILE, up_tile, 0)

    def down_tile(j, carry):
        lanes = pl.ds(pl.multiple_of(j * TILE, TILE), TILE)
        down_grad[lanes, :] = lax.dot_general(
            mixed[:, lanes], grads[...], (((0,), (0,)), ((), ())), preferred_element_type=F32
        ).astype(BF16)
        return carry

    lax.fori_loop(0, FF // TILE, down_tile, 0)
    for copy in leaving:
        copy.wait()
    back_links[0].wait()
    for copy in back_links[1:]:
        copy.wait_recv()
    for copy in links[1:]:
        copy.wait_send()
    for copy in back_links[1:]:
        copy.wait_send()


def run_experts(sent, grads_in, gate_up, down):
    anywhere = pl.BlockSpec(memory_space=pl.ANY)
    inside = pl.BlockSpec(memory_space=pltpu.VMEM)
    blocks = jax.ShapeDtypeStruct((EXPERTS, CAP, D), BF16)
    vmem, dma = pltpu.VMEM, pltpu.SemaphoreType.DMA
    return pl.pallas_call(
        experts_kernel,
        name="experts",
        out_shape=(
            blocks,
            blocks,
            jax.ShapeDtypeStruct((D, 2 * FF), BF16),
            jax.ShapeDtypeStruct((FF, D), BF16),
        ),
        in_specs=[anywhere] * 4,
        out_specs=(anywhere, anywhere, inside, inside),
        scratch_shapes=[
            vmem((ROWS, D), BF16),
            vmem((ROWS, D), BF16),
            vmem((D, 2 * FF), BF16),
            vmem((FF, D), BF16),
            vmem((ROWS, FF), BF16),
            vmem((ROWS, 2 * FF), BF16),
            vmem((ROWS, D), BF16),
            vmem((ROWS, D), BF16),
            dma((EXPERTS,)),
            dma((EXPERTS,)),
            dma((EXPERTS,)),
            dma((EXPERTS,)),
            dma((EXPERTS,)),
            dma((2,)),
            dma((EXPERTS,)),
            dma((2,)),
        ],
        compiler_params=pltpu.CompilerParams(
            collective_id=2, has_side_effects=True, vmem_limit_bytes=58 * 1024 * 1024
        ),
        cost_estimate=pl.CostEstimate(
            flops=33_000_000_000, bytes_accessed=60_000_000, transcendentals=1_200_000
        ),
    )(sent, grads_in, gate_up, down)


def rms_scale(values, gain_vec):
    return (
        values * lax.rsqrt(jnp.mean(values * values, axis=-1, keepdims=True) + norm_eps) * gain_vec
    )


def rope_tables(position, half_dim):
    frequency = rope_base ** (-jnp.arange(half_dim, dtype=jnp.float32) / half_dim)
    angles = position.astype(jnp.float32)[:, None] * frequency[None, :]
    return (jnp.cos(angles)[:, None, :], jnp.sin(angles)[:, None, :])


def rotate(values, cosine, sine_tab):
    half_dim = values.shape[-1] // 2
    lower_half = values[..., :half_dim]
    upper_half = values[..., half_dim:]
    return jnp.concatenate(
        [lower_half * cosine - upper_half * sine_tab, lower_half * sine_tab + upper_half * cosine],
        axis=-1,
    )


def unrotate(grads_in, cosine, sine_tab):
    half_dim = grads_in.shape[-1] // 2
    lower_half = grads_in[..., :half_dim]
    upper_half = grads_in[..., half_dim:]
    return jnp.concatenate(
        [lower_half * cosine + upper_half * sine_tab, upper_half * cosine - lower_half * sine_tab],
        axis=-1,
    )


def seq_layout(seq_lens, row_ids):
    seq_ends = jnp.cumsum(seq_lens)
    segment = jnp.sum((row_ids[:, None] >= seq_ends[None, :]).astype(jnp.int32), axis=1)
    seq_start = jnp.sum(
        jnp.where(seq_ends[None, :] <= row_ids[:, None], seq_lens[None, :], 0), axis=1
    )
    return (segment, row_ids - seq_start)


def exchange(rows):
    return lax.all_to_all(
        rows.reshape(EXPERTS, CAP, D), "expert", split_axis=0, concat_axis=0, tiled=True
    ).reshape(EXPERTS * CAP, D)


def body(
    tokens, lengths, top_experts, w_qkv, w_out, gain_attn, gain_ffn, router, gate_up, down_proj, cotangent,
):
    count = tokens.shape[0]
    scale = HEAD_DIM ** (-0.5)
    pack = jnp.concatenate(
        [
            w_qkv,
            w_out.T,
            router,
            gain_attn[:, None],
            gain_ffn[:, None],
            jnp.zeros((PIECE, SMALL - EXPERTS - 2), BF16),
        ],
        axis=1,
    )
    pack = jnp.pad(pack, ((0, PADDED - PIECE), (0, 0)))
    full_a, full_b = gather_weights(pack)
    full_qkv = full_a.reshape(D, WA)
    full_b = full_b.reshape(D, WB)
    out_t = full_b[:, :D]
    full_router = full_b[:, D : D + EXPERTS]
    gains = full_b[:, D + EXPERTS : D + EXPERTS + 2].astype(F32).T
    attn_g, ffn_g = gains[0], gains[1]

    named = jnp.sum(
        (top_experts[:, :, None] == jnp.arange(EXPERTS, dtype=jnp.int32)).astype(F32), axis=1
    )
    row_ids = jnp.arange(count, dtype=jnp.int32)
    earlier = (row_ids[None, :] < row_ids[:, None]).astype(BF16)
    slot_of = jnp.dot(earlier, named.astype(BF16), preferred_element_type=F32)
    slot_of = jnp.where(named > 0, slot_of, -1.0)
    hits = slot_of[:, :, None] == jnp.arange(CAP, dtype=F32)
    any_slot = hits.reshape(count, EXPERTS * CAP).astype(BF16)
    logits = jnp.dot(tokens, full_router, preferred_element_type=F32)
    masked_logits = jnp.where(named > 0, logits, -jnp.inf)
    gates = jax.nn.softmax(masked_logits, axis=-1)
    slot_gates = jnp.sum(jnp.where(hits, gates[:, :, None], 0.0), axis=0).reshape(-1)
    row_grads = (
        jnp.dot(any_slot.T, cotangent, preferred_element_type=F32) * slot_gates[:, None]
    ).astype(BF16)
    arrived_grads = exchange(row_grads)

    tok_f = tokens.astype(F32)
    normed = rms_scale(tok_f, attn_g).astype(BF16)
    projected = jnp.dot(normed, full_qkv, preferred_element_type=F32)
    shard_pos = lax.axis_index("shard")
    group_rows = lax.axis_size("shard") * count
    all_ids = jnp.arange(group_rows, dtype=jnp.int32)
    key_segment, key_position = seq_layout(lengths[0], all_ids)
    own_ids = shard_pos * count + row_ids
    own_segment = lax.dynamic_slice_in_dim(key_segment, shard_pos * count, count)
    own_position = lax.dynamic_slice_in_dim(key_position, shard_pos * count, count)
    cosine, sine_tab = rope_tables(own_position, HEAD_DIM // 2)
    queries = rotate(
        projected[:, :WIDTH_Q].reshape(count, HEADS_Q, HEAD_DIM), cosine, sine_tab
    ).astype(BF16)
    keys_rot = rotate(
        projected[:, WIDTH_Q : WIDTH_Q + WIDTH_KV].reshape(count, HEADS_KV, HEAD_DIM),
        cosine,
        sine_tab,
    ).astype(BF16)
    values = projected[:, WIDTH_Q + WIDTH_KV :].astype(BF16)
    local_kv = jnp.concatenate([keys_rot.reshape(count, WIDTH_KV), values], axis=1)
    group_kv = lax.all_gather(local_kv, "shard", axis=0, tiled=True)
    keys_all = group_kv[:, :WIDTH_KV].reshape(group_rows, HEADS_KV, HEAD_DIM)
    values_all = group_kv[:, WIDTH_KV:].reshape(group_rows, HEADS_KV, HEAD_DIM)
    grouped = queries.reshape(count, HEADS_KV, REPEAT, HEAD_DIM)
    allowed = (own_segment[:, None] == key_segment[None, :]) & (
        all_ids[None, :] <= own_ids[:, None]
    )

    def attn_scores():
        raw_scores = (
            jnp.einsum("tgrd,kgd->grtk", grouped, keys_all, preferred_element_type=F32) * scale
        )
        return jnp.where(allowed, raw_scores, -1e30)

    masked = attn_scores()
    top_score = jnp.max(masked, axis=-1, keepdims=True)
    expo_vals = jnp.exp(masked - top_score)
    total_weight = jnp.sum(expo_vals, axis=-1, keepdims=True)
    probs_low = (expo_vals / total_weight).astype(BF16)
    attended = (
        jnp.einsum("grtk,kgd->tgrd", probs_low, values_all, preferred_element_type=F32)
        .reshape(count, WIDTH_Q)
        .astype(BF16)
    )
    branch = lax.dot_general(
        attended, out_t, (((1,), (1,)), ((), ())), preferred_element_type=F32
    )
    middle = tok_f + branch
    normed_ffn = rms_scale(middle, ffn_g).astype(BF16)
    dispatch = jnp.dot(any_slot.T, normed_ffn, preferred_element_type=F32).astype(BF16)
    back_rows, expert_out, grad_up_local, grad_down_local = run_experts(
        dispatch.reshape(EXPERTS, CAP, D),
        arrived_grads.reshape(EXPERTS, CAP, D),
        gate_up,
        down_proj,
    )
    back_rows = back_rows.reshape(ROWS, D)
    returned = exchange(expert_out)

    upstream = cotangent.astype(F32)
    grad_normed_ffn = jnp.dot(any_slot, back_rows, preferred_element_type=F32)
    ffn_value, ffn_pull = jax.vjp(rms_scale, middle, ffn_g)
    grad_mid_norm, grad_ffn_gain = ffn_pull(grad_normed_ffn)
    grad_middle = upstream + grad_mid_norm
    grad_branch = grad_middle.astype(BF16)
    grad_out_t = jnp.dot(grad_branch.T, attended, preferred_element_type=F32).astype(BF16)
    grad_attended = (
        jnp.dot(grad_branch, out_t, preferred_element_type=F32)
        .astype(BF16)
        .reshape(count, HEADS_KV, REPEAT, HEAD_DIM)
    )
    probs_again = jnp.exp(attn_scores() - top_score) / total_weight
    grad_probs = jnp.einsum(
        "tgrd,kgd->grtk", grad_attended, values_all, preferred_element_type=F32
    )
    grad_scores = (
        probs_again * (grad_probs - jnp.sum(probs_again * grad_probs, axis=-1, keepdims=True))
    ).astype(BF16)
    grad_queries = (
        jnp.einsum("grtk,kgd->tgrd", grad_scores, keys_all, preferred_element_type=F32) * scale
    )
    grad_keys = (
        jnp.einsum("grtk,tgrd->kgd", grad_scores, grouped, preferred_element_type=F32) * scale
    )
    grad_values = jnp.einsum(
        "grtk,tgrd->kgd", probs_low, grad_attended, preferred_element_type=F32
    )
    group_grads = jnp.concatenate(
        [grad_keys.reshape(group_rows, WIDTH_KV), grad_values.reshape(group_rows, WIDTH_KV)], axis=1
    )
    own_kv_grads = lax.psum_scatter(
        group_grads.astype(BF16), "shard", scatter_dimension=0, tiled=True
    ).astype(F32)
    grad_projected = jnp.concatenate(
        [
            unrotate(grad_queries.reshape(count, HEADS_Q, HEAD_DIM), cosine, sine_tab).reshape(
                count, WIDTH_Q
            ),
            unrotate(
                own_kv_grads[:, :WIDTH_KV].reshape(count, HEADS_KV, HEAD_DIM), cosine, sine_tab
            ).reshape(count, WIDTH_KV),
            own_kv_grads[:, WIDTH_KV:],
        ],
        axis=1,
    ).astype(BF16)
    grad_qkv_local = jnp.dot(normed.T, grad_projected, preferred_element_type=F32).astype(BF16)
    grad_normed = lax.dot_general(
        grad_projected, full_qkv, (((1,), (1,)), ((), ())), preferred_element_type=F32
    )
    attn_value, attn_pull = jax.vjp(rms_scale, tok_f, attn_g)
    grad_tok_norm, grad_attn_gain = attn_pull(grad_normed)

    mix = jnp.where(hits, gates[:, :, None], 0.0).reshape(count, EXPERTS * CAP)
    mix_high = mix.astype(BF16)
    mix_low = (mix - mix_high.astype(F32)).astype(BF16)
    combined = jnp.dot(mix_high, returned, preferred_element_type=F32) + jnp.dot(
        mix_low, returned, preferred_element_type=F32
    )
    output = (middle + combined).astype(BF16)
    products = lax.dot_general(
        cotangent, returned, (((1,), (1,)), ((), ())), preferred_element_type=F32
    ).reshape(count, EXPERTS, CAP)
    gate_grad = jnp.sum(jnp.where(hits, products, 0.0), axis=-1)
    logit_grad = gates * (gate_grad - jnp.sum(gates * gate_grad, axis=-1, keepdims=True))
    router_f = full_router.astype(F32)
    grad_router_local = jnp.dot(tok_f.T, logit_grad, precision=precise)
    grad_from_router = jnp.dot(logit_grad, router_f.T, precision=precise)
    grad_tokens = (grad_middle + grad_tok_norm + grad_from_router).astype(BF16)

    grad_small = jnp.concatenate(
        [
            grad_router_local,
            grad_attn_gain[:, None],
            grad_ffn_gain[:, None],
            jnp.zeros((D, SMALL - EXPERTS - 2), F32),
        ],
        axis=1,
    ).astype(BF16)
    sum_a, sum_b = scatter_sums(
        grad_qkv_local.reshape(4, 4, 2, BLOCK, WA),
        grad_out_t.reshape(4, 4, 2, BLOCK, D),
        grad_small.reshape(4, 4, 2, BLOCK, SMALL),
    )
    sum_b = sum_b[:PIECE]
    up_sum = lax.psum_scatter(
        grad_up_local[None], "shard", scatter_dimension=1, tiled=True
    ).astype(F32)
    down_sum = lax.psum_scatter(
        grad_down_local[None], "shard", scatter_dimension=2, tiled=True
    ).astype(F32)
    return (
        output,
        grad_tokens,
        sum_a[:PIECE],
        sum_b[:, :D].T,
        sum_b[:, D + EXPERTS],
        sum_b[:, D + EXPERTS + 1],
        sum_b[:, D : D + EXPERTS],
        up_sum,
        down_sum,
    )


def solution(mesh):
    return jax.shard_map(
        body,
        mesh=mesh,
        in_specs=(
            P(("expert", "shard"), None),
            P("expert", None),
            P(("expert", "shard"), None),
            P(("expert", "shard"), None),
            P(None, ("expert", "shard")),
            P(("expert", "shard")),
            P(("expert", "shard")),
            P(("expert", "shard"), None),
            P("expert", None, None),
            P("expert", None, None),
            P(("expert", "shard"), None),
        ),
        out_specs=(
            P(("expert", "shard"), None),
            P(("expert", "shard"), None),
            P(("expert", "shard"), None),
            P(None, ("expert", "shard")),
            P(("expert", "shard")),
            P(("expert", "shard")),
            P(("expert", "shard"), None),
            P("expert", "shard", None),
            P("expert", None, "shard"),
        ),
        check_vma=False,
    )
```

```python
import functools

import jax
import jax.numpy as jnp
from jax import lax
from jax.experimental import pallas as pl
from jax.experimental.pallas import tpu as pltpu
from jax.sharding import PartitionSpec as P

D = 1536
HEADS_Q = 12
HEADS_KV = 2
HEAD_DIM = 128
FF = 768
TOP = 4
EXPERTS = 32
CAP = 48
WIDTH_Q = HEADS_Q * HEAD_DIM
WIDTH_KV = HEADS_KV * HEAD_DIM
REPEAT = HEADS_Q // HEADS_KV

norm_eps = 1e-06
rope_base = 1000000.0
precise = lax.Precision.HIGHEST
MESH = pl.DeviceIdType.MESH
F32 = jnp.float32
BF16 = jnp.bfloat16

PIECE = 12
PADDED = 16
BLOCK = 48
WA = 2048
WB = 1664
SMALL = WB - D


def place():
    e = lax.axis_index("expert")
    return e // 8, (e // 2) % 4, e % 2, lax.axis_index("shard")


def device(y, z, c, x):
    return ((y * 4 + z) * 2 + c, x)


def greet(devices):
    barrier = pltpu.get_barrier_semaphore()
    for d in devices:
        pl.semaphore_signal(barrier, inc=1, device_id=d, device_id_type=MESH)
    pl.semaphore_wait(barrier, len(devices))


class Links:
    def __init__(self, send, recv):
        self.send, self.recv, self.made = send, recv, []

    def push(self, src, dst, where):
        i = len(self.made)
        copy = pltpu.make_async_remote_copy(
            src_ref=src,
            dst_ref=dst,
            send_sem=self.send.at[i],
            recv_sem=self.recv.at[i],
            device_id=where,
            device_id_type=MESH,
        )
        copy.start()
        self.made.append(copy)
        return copy

    def drain(self):
        for copy in self.made:
            copy.wait_send()


def neighbours(y, z, c, x):
    other = 1 - c
    return dict(
        x=[device(y, z, c, (x + d) % 4) for d in (1, 2, 3)],
        y=(device((y + 1) % 4, z, c, x), device((y + 3) % 4, z, c, x)),
        z=(device(y, (z + 1) % 4, c, x), device(y, (z + 3) % 4, c, x)),
        core=device(y, z, other, x),
    )


def everyone_near(near):
    return list(near["x"]) + list(near["y"]) + list(near["z"]) + [near["core"]]


def pick_rows(rows, columns, row_block, column_block):
    r = lax.broadcasted_iota(jnp.int32, (rows, columns), 0)
    q = lax.broadcasted_iota(jnp.int32, (rows, columns), 1)
    same = (r // row_block == q // column_block) & (r % row_block == q % column_block)
    return jnp.where(same, 1.0, 0.0).astype(BF16)


def route(top_experts, named, any_slot):
    lanes = iota((COUNT, 128), 1)
    for k in range(TOP):
        hit = jnp.where(top_experts[:, k : k + 1] == lanes, 1.0, 0.0)
        named[...] = hit if k == 0 else named[...] + hit
    earlier = hot(iota((COUNT, COUNT), 1) < iota((COUNT, COUNT), 0))
    slot_of = mul(earlier, named[...].astype(BF16))
    slot_of = jnp.where(named[...] > 0, slot_of, -1.0).astype(BF16)
    expand = hot(iota((128, ROWS), 0) == iota((128, ROWS), 1) // CAP)
    place_of = (iota((1, ROWS), 1) % CAP).astype(F32)
    any_slot[...] = hot(mul(slot_of, expand) == place_of)


def gather_kernel(
    pack, top_experts, cotangent, full_a, full_b, named, any_slot, dy_rows,
    xbuf, own_a, own_b, send, recv, local,
):
    y, z, c, x = place()
    near = neighbours(y, z, c, x)
    greet(everyone_near(near))
    link = Links(send, recv)
    first = [link.push(pack, xbuf.at[x], near["x"][d]) for d in range(3)]
    xbuf[pl.ds(x, 1)] = pack[...][None]
    for copy in first:
        copy.wait_recv()
    select = pick_rows(BLOCK, 4 * PADDED, PIECE, PADDED)
    pieces = xbuf[...].reshape(4 * PADDED, WA + WB)
    own_a[...] = jnp.dot(select, pieces[:, :WA], preferred_element_type=F32).astype(BF16)
    own_b[...] = jnp.dot(select, pieces[:, WA:], preferred_element_type=F32).astype(BF16)

    def at_a(far, close, columns=None):
        view = full_a.at[far, close, c]
        return view if columns is None else view.at[:, columns]

    def at_b(far, close, columns=None):
        view = full_b.at[close, far, c]
        return view if columns is None else view.at[:, columns]

    def line_a(far, part=slice(None)):
        return full_a.at[far, part, c]

    def line_b(far, part=slice(None)):
        return full_b.at[part, far, c]

    jobs = [
        dict(own=own_a, at=at_a, line=line_a, close="z", far="y", p=z, q=y, half=1024, i=0),
        dict(own=own_b, at=at_b, line=line_b, close="y", far="z", p=y, q=z, half=896, i=1),
    ]
    for j in jobs:
        here = j["at"](j["q"], j["p"])
        plus, minus = near[j["close"]]
        j["up"] = link.push(j["own"], here, plus)
        j["down"] = link.push(j["own"], here, minus)
        j["core"] = [link.push(j["own"], here, near["core"])]
        j["local"] = pltpu.make_async_copy(j["own"], here, local.at[j["i"]])
        j["local"].start()
    route(top_experts, named, any_slot)
    for j in jobs:
        plus, minus = near[j["close"]]
        left, right = (j["p"] + 3) % 4, (j["p"] + 1) % 4
        j["up"].wait_recv()
        part = j["at"](j["q"], left, pl.ds(0, j["half"]))
        j["up2"] = link.push(part, part, plus)
        j["down"].wait_recv()
        part = j["at"](j["q"], right, pl.ds(j["half"], j["own"].shape[1] - j["half"]))
        j["down2"] = link.push(part, part, minus)
        for side in (left, right):
            block = j["at"](j["q"], side)
            j["core"].append(link.push(block, block, near["core"]))
    for j in jobs:
        j["up2"].wait_recv()
        j["down2"].wait_recv()
        block = j["at"](j["q"], (j["p"] + 2) % 4)
        j["local"].wait()
        plus, minus = near[j["far"]]
        line = j["line"](j["q"])
        j["up"] = link.push(line, line, plus)
        j["down"] = link.push(line, line, minus)
        j["core"].append(link.push(block, block, near["core"]))

    def dy_tile(j, carry):
        lanes = pl.ds(pl.multiple_of(j * TILE, TILE), TILE)
        dy_rows[lanes, :] = mul(any_slot[:, lanes], cotangent[...], TN).astype(BF16)
        return carry

    lax.fori_loop(0, ROWS // TILE, dy_tile, 0)
    for j in jobs:
        plus, minus = near[j["far"]]
        left, right = (j["q"] + 3) % 4, (j["q"] + 1) % 4
        j["up"].wait_recv()
        part = j["line"](left, pl.ds(0, 2))
        j["up2"] = link.push(part, part, plus)
        j["down"].wait_recv()
        part = j["line"](right, pl.ds(2, 2))
        j["down2"] = link.push(part, part, minus)
        for side in (left, right):
            block = j["line"](side)
            j["core"].append(link.push(block, block, near["core"]))
    for j in jobs:
        opposite = (j["q"] + 2) % 4
        j["up2"].wait_recv()
        part = j["line"](opposite, pl.ds(0, 2))
        j["core"].append(link.push(part, part, near["core"]))
        j["down2"].wait_recv()
        part = j["line"](opposite, pl.ds(2, 2))
        j["core"].append(link.push(part, part, near["core"]))
    for j in jobs:
        for copy in j["core"]:
            copy.wait_recv()
    link.drain()


def gather_weights(pack, top_experts, cotangent):
    inside = pl.BlockSpec(memory_space=pltpu.VMEM)
    anywhere = pl.BlockSpec(memory_space=pl.ANY)
    copies = 3 + 2 * 16
    return pl.pallas_call(
        gather_kernel,
        name="gather_weights",
        out_shape=(
            jax.ShapeDtypeStruct((4, 4, 2, BLOCK, WA), BF16),
            jax.ShapeDtypeStruct((4, 4, 2, BLOCK, WB), BF16),
            jax.ShapeDtypeStruct((COUNT, 128), F32),
            jax.ShapeDtypeStruct((COUNT, ROWS), BF16),
            jax.ShapeDtypeStruct((ROWS, D), BF16),
        ),
        in_specs=[inside] * 3,
        out_specs=(anywhere, anywhere, inside, inside, inside),
        scratch_shapes=[
            pltpu.VMEM((4, PADDED, WA + WB), BF16),
            pltpu.VMEM((BLOCK, WA), BF16),
            pltpu.VMEM((BLOCK, WB), BF16),
            pltpu.SemaphoreType.DMA((copies,)),
            pltpu.SemaphoreType.DMA((copies,)),
            pltpu.SemaphoreType.DMA((2,)),
        ],
        compiler_params=pltpu.CompilerParams(
            collective_id=0, has_side_effects=True, vmem_limit_bytes=24 * 1024 * 1024
        ),
        cost_estimate=pl.CostEstimate(flops=0, bytes_accessed=24_000_000, transcendentals=0),
    )(pack, top_experts, cotangent)


def add_blocks(dst, far, start, count, sources):
    def step(i, carry):
        total = dst[far, start + i].astype(F32)
        for source in sources:
            total = total + source(i).astype(F32)
        dst[far, start + i] = total.astype(BF16)
        return carry

    lax.fori_loop(0, count, step, 0)


def scatter_kernel(
    ga, gb, gs, up_in, down_in, up_far, down_far, out_a, out_b, up_out, down_out,
    core_a, core_b, mine_a, mine_b, one_a, one_b, two_a, two_b,
    half_a0, half_a1, half_b0, half_b1, last_a, last_b, xout, xin,
    ups, downs, up_got, down_got, up_land, down_land,
    send, recv, local,
):
    y, z, c, x = place()
    near = neighbours(y, z, c, x)
    greet(everyone_near(near))
    link = Links(send, recv)
    other = 1 - c
    jobs = [
        dict(src=[(lambda f, s: ga.at[f, :, s], 0, WA)], core=core_a, mine=mine_a, one=one_a, two=two_a,
             halves=(half_a0, half_a1), last=last_a, far="y", close="z", q=y, p=z,
             width=WA, half=1024, lane=0, i=0),
        dict(src=[(lambda f, s: gb.at[:, f, s], 0, D), (lambda f, s: gs.at[:, f, s], D, SMALL)],
             core=core_b, mine=mine_b, one=one_b, two=two_b,
             halves=(half_b0, half_b1), last=last_b, far="z", close="y", q=z, p=y,
             width=WB, half=896, lane=WA, i=1),
    ]
    slots = 0
    for step in (2, 3, 1, 0):
        for j in jobs:
            f = (j["q"] + step) % 4
            j[step] = []
            for source, lane, width in j["src"]:
                lanes = pl.ds(lane, width)
                pushed = link.push(
                    source(f, other), j["core"].at[f, :, :, lanes], near["core"]
                )
                kept = pltpu.make_async_copy(
                    source(f, c), j["mine"].at[f, :, :, lanes], local.at[slots]
                )
                slots += 1
                kept.start()
                j[step].append((pushed, kept))

    fetches = []
    for i, d in enumerate((3, 1, 0)):
        part = (x + d) % 4
        up_rows = pl.ds(pl.multiple_of(part * UP_PART, UP_PART), UP_PART)
        lanes = pl.ds(pl.multiple_of(part * DOWN_PART, 128), DOWN_PART)
        fetches.append(pltpu.make_async_copy(up_in.at[up_rows], ups.at[i], local.at[slots]))
        fetches.append(
            pltpu.make_async_copy(down_in.at[:, lanes], downs.at[i], local.at[slots + 1])
        )
        slots += 2
    fetches.append(pltpu.make_async_copy(up_far, up_got, local.at[slots]))
    fetches.append(pltpu.make_async_copy(down_far, down_got, local.at[slots + 1]))
    for fetch in fetches:
        fetch.start()
    for fetch in fetches:
        fetch.wait()
    sides = []
    for i, peer in enumerate((near["x"][2], near["x"][0])):
        up_rows = slice(i * UP_HALF, (i + 1) * UP_HALF)
        down_rows = slice(i * DOWN_HALF, (i + 1) * DOWN_HALF)
        ups[i, up_rows, :] = (ups[i, up_rows, :].astype(F32) + up_got[i].astype(F32)).astype(BF16)
        downs[i, down_rows, :] = (
            downs[i, down_rows, :].astype(F32) + down_got[i].astype(F32)
        ).astype(BF16)
        sides.append(link.push(ups.at[i], up_land.at[i], peer))
        sides.append(link.push(downs.at[i], down_land.at[i], peer))

    def ready(j, step):
        for pushed, kept in j[step]:
            pushed.wait_recv()
            kept.wait()

    for j in jobs:
        f = (j["q"] + 2) % 4
        ready(j, 2)
        mine = j["mine"]
        add_blocks(j["core"], f, 0, 4, [lambda i, f=f, m=mine: m[f, i]])
        plus, minus = near[j["far"]]
        j["down"] = link.push(j["core"].at[f, pl.ds(0, 2)], j["one"].at[0], minus)
        j["up"] = link.push(j["core"].at[f, pl.ds(2, 2)], j["one"].at[1], plus)
    for j in jobs:
        plus, minus = near[j["far"]]
        mine, one = j["mine"], j["one"]
        f = (j["q"] + 3) % 4
        ready(j, 3)
        add_blocks(j["core"], f, 2, 2, [lambda i, f=f, m=mine: m[f, i + 2]])
        j["down"].wait_recv()
        add_blocks(
            j["core"], f, 0, 2, [lambda i, f=f, m=mine: m[f, i], lambda i, o=one: o[0, i]]
        )
        j["down2"] = link.push(j["core"].at[f], j["two"].at[0], minus)
        f = (j["q"] + 1) % 4
        ready(j, 1)
        add_blocks(j["core"], f, 0, 2, [lambda i, f=f, m=mine: m[f, i]])
        j["up"].wait_recv()
        add_blocks(
            j["core"], f, 2, 2, [lambda i, f=f, m=mine: m[f, i + 2], lambda i, o=one: o[1, i]]
        )
        j["up2"] = link.push(j["core"].at[f], j["two"].at[1], plus)
    for j in jobs:
        mine, two = j["mine"], j["two"]
        f = j["q"]
        ready(j, 0)
        j["down2"].wait_recv()
        j["up2"].wait_recv()
        add_blocks(
            j["core"], f, 0, 4,
            [lambda i, f=f, m=mine: m[f, i], lambda i, t=two: t[0, i], lambda i, t=two: t[1, i]],
        )
        plus, minus = near[j["close"]]
        g = (j["p"] + 2) % 4
        h, w = j["half"], j["width"]
        j["down"] = link.push(j["core"].at[f, g, :, pl.ds(0, h)], j["halves"][0], minus)
        j["up"] = link.push(j["core"].at[f, g, :, pl.ds(h, w - h)], j["halves"][1], plus)
    for j in jobs:
        plus, minus = near[j["close"]]
        f, h, w, core = j["q"], j["half"], j["width"], j["core"]
        g = (j["p"] + 3) % 4
        j["down"].wait_recv()
        core[f, g, :, 0:h] = (
            core[f, g, :, 0:h].astype(F32) + j["halves"][0][...].astype(F32)
        ).astype(BF16)
        j["down2"] = link.push(core.at[f, g], j["last"].at[0], minus)
        g = (j["p"] + 1) % 4
        j["up"].wait_recv()
        core[f, g, :, h:w] = (
            core[f, g, :, h:w].astype(F32) + j["halves"][1][...].astype(F32)
        ).astype(BF16)
        j["up2"] = link.push(core.at[f, g], j["last"].at[1], plus)
    select = pick_rows(4 * PADDED, BLOCK, PADDED, PIECE)
    for j in jobs:
        f, g = j["q"], j["p"]
        j["down2"].wait_recv()
        j["up2"].wait_recv()
        total = (
            j["core"][f, g].astype(F32)
            + j["last"][0].astype(F32)
            + j["last"][1].astype(F32)
        ).astype(BF16)
        spread = jnp.dot(select, total, preferred_element_type=F32).astype(BF16)
        xout[:, :, j["lane"] : j["lane"] + j["width"]] = spread.reshape(4, PADDED, j["width"])
    final = [
        link.push(xout.at[(x + d) % 4], xin.at[d - 1], near["x"][d - 1]) for d in (1, 2, 3)
    ]
    for copy in final:
        copy.wait_recv()
    mine = xout[x].astype(F32)
    for d in range(3):
        mine = mine + xin[d].astype(F32)
    out_a[...] = mine[:, :WA]
    out_b[...] = mine[:, WA:]
    for push in sides:
        push.wait_recv()
    up_out[...] = ups[2].astype(F32) + up_land[0].astype(F32) + up_land[1].astype(F32)
    down_out[...] = downs[2].astype(F32) + down_land[0].astype(F32) + down_land[1].astype(F32)
    link.drain()


def scatter_sums(*operands):
    copies = 2 * (4 + 4 + 4) + 4 + 3 + 4
    vmem = pltpu.VMEM
    scratch = []
    for shape in ((4, 4), (4, 4), (2, 2), (2, 4)):
        scratch += [vmem((*shape, BLOCK, WA), BF16), vmem((*shape, BLOCK, WB), BF16)]
    scratch += [
        vmem((BLOCK, 1024), BF16),
        vmem((BLOCK, 1024), BF16),
        vmem((BLOCK, 896), BF16),
        vmem((BLOCK, WB - 896), BF16),
        vmem((2, BLOCK, WA), BF16),
        vmem((2, BLOCK, WB), BF16),
        vmem((4, PADDED, WA + WB), BF16),
        vmem((3, PADDED, WA + WB), BF16),
        vmem((3, UP_PART, 2 * FF), BF16),
        vmem((3, FF, DOWN_PART), BF16),
        vmem((2, UP_HALF, 2 * FF), BF16),
        vmem((2, DOWN_HALF, DOWN_PART), BF16),
        vmem((2, UP_PART, 2 * FF), BF16),
        vmem((2, FF, DOWN_PART), BF16),
        pltpu.SemaphoreType.DMA((copies,)),
        pltpu.SemaphoreType.DMA((copies,)),
        pltpu.SemaphoreType.DMA((20,)),
    ]
    return pl.pallas_call(
        scatter_kernel,
        name="scatter_sums",
        out_shape=(
            jax.ShapeDtypeStruct((PADDED, WA), F32),
            jax.ShapeDtypeStruct((PADDED, WB), F32),
            jax.ShapeDtypeStruct((UP_PART, 2 * FF), F32),
            jax.ShapeDtypeStruct((FF, DOWN_PART), F32),
        ),
        in_specs=[pl.BlockSpec(memory_space=pl.ANY)] * 7,
        out_specs=(pl.BlockSpec(memory_space=pltpu.VMEM),) * 4,
        scratch_shapes=scratch,
        compiler_params=pltpu.CompilerParams(
            collective_id=1, has_side_effects=True, vmem_limit_bytes=40 * 1024 * 1024
        ),
        cost_estimate=pl.CostEstimate(flops=0, bytes_accessed=24_000_000, transcendentals=0),
    )(*operands)


NEAREST = (
    (0, 0), (0, 1), (1, 0), (0, 3),
    (3, 0), (1, 1), (3, 3), (1, 3),
    (3, 1), (0, 2), (2, 0), (1, 2),
    (2, 1), (3, 2), (2, 3), (2, 2),
)
ROWS = EXPERTS * CAP
CHUNKS = 4
CHUNK = ROWS // CHUNKS
TILE = 256


def gelu_parts(g):
    inner = 0.7978845608 * (g + 0.044715 * g * g * g)
    th = jnp.tanh(inner)
    half = 0.5 * (1.0 + th)
    slope = half + 0.5 * g * (1.0 - th * th) * (0.7978845608 * (1.0 + 0.134145 * g * g))
    return g * half, slope


def experts_kernel(
    sent, gates_in, dy_in, gate_up, down, back, gate_back, outs, up_grad, down_grad,
    rows, gates, dys, grads, gu, dn, mixed, ghid, grow, eout, dots,
    send, recv, tsend, trecv, bsend, brecv, dsend, drecv, gsem, wsem, osem, own,
):
    y, z, c, x = place()
    me = (y * 4 + z) * 2 + c
    weights = [
        pltpu.make_async_copy(gate_up.at[0], gu, wsem.at[0]),
        pltpu.make_async_copy(down.at[0], dn, wsem.at[1]),
    ]
    slots = []
    for s, (dy, dz) in enumerate(NEAREST):
        for b in (0, 1):
            core = c if b == 0 else 1 - c
            source = device((y + dy) % 4, (z + dz) % 4, core, x)
            target = device((y + 4 - dy) % 4, (z + 4 - dz) % 4, core, x)
            slots.append((2 * s + b, source, target))
    greet([source for _, source, _ in slots[1:]])
    links, tile_links, back_links, dot_links = [], [], [], []

    def move(src, dst, where, i, sends, recvs, k):
        if i == 0:
            copy = pltpu.make_async_copy(src, dst, own.at[k])
        else:
            copy = pltpu.make_async_remote_copy(
                src_ref=src, dst_ref=dst, send_sem=sends.at[i],
                recv_sem=recvs.at[i], device_id=where, device_id_type=MESH,
            )
        copy.start()
        return copy

    for i, source, target in slots:
        tile_links.append(
            move(gates_in.at[target[0]], gates.at[i], target, i, tsend, trecv, 0)
        )
        links.append(
            move(sent.at[target[0]], rows.at[pl.ds(i * CAP, CAP)], target, i, send, recv, 1)
        )
    incoming = []
    for copy in weights:
        copy.start()
    for i, source, target in slots:
        copy = pltpu.make_async_copy(
            dy_in.at[source[0]], dys.at[pl.ds(i * CAP, CAP)], gsem.at[i]
        )
        copy.start()
        incoming.append(copy)
    for copy in weights:
        copy.wait()
    leaving = []
    per = len(slots) // CHUNKS
    diagonal = lax.broadcasted_iota(jnp.int32, (CAP, 128), 0) == lax.broadcasted_iota(
        jnp.int32, (CAP, 128), 1
    )
    for k in range(CHUNKS):
        part = slots[k * per : (k + 1) * per]
        for i, source, target in part:
            incoming[i].wait()
            if i == 0:
                tile_links[0].wait()
                links[0].wait()
            else:
                tile_links[i].wait_recv()
                links[i].wait_recv()
        base = k * CHUNK
        block = pl.ds(base, CHUNK)

        def scale_block(i, carry):
            at = pl.ds(pl.multiple_of(i * CAP, CAP), CAP)
            column = jnp.sum(jnp.where(diagonal, gates[i, 0:1, :], 0.0), axis=1, keepdims=True)
            grads[at, :] = (dys[at, :].astype(F32) * column).astype(BF16)
            return carry

        lax.fori_loop(k * per, (k + 1) * per, scale_block, 0)

        def hidden_tile(j, carry, block=block):
            lanes = pl.ds(pl.multiple_of(j * TILE, TILE), TILE)
            upper = pl.ds(pl.multiple_of(FF + j * TILE, TILE), TILE)
            g = jnp.dot(rows[block, :], gu[:, lanes], preferred_element_type=F32)
            act, slope = gelu_parts(g)
            u = jnp.dot(rows[block, :], gu[:, upper], preferred_element_type=F32)
            mixed[block, lanes] = (act * u).astype(BF16)
            m = lax.dot_general(
                grads[block, :], dn[lanes, :], (((1,), (1,)), ((), ())),
                preferred_element_type=F32,
            )
            ghid[block, lanes] = (m * u * slope).astype(BF16)
            ghid[block, upper] = (m * act).astype(BF16)
            return carry

        lax.fori_loop(0, FF // TILE, hidden_tile, 0)

        def rows_tile(j, carry, block=block):
            lanes = pl.ds(pl.multiple_of(j * TILE, TILE), TILE)
            grow[block, lanes] = lax.dot_general(
                ghid[block, :], gu[lanes, :], (((1,), (1,)), ((), ())),
                preferred_element_type=F32,
            ).astype(BF16)
            return carry

        lax.fori_loop(0, D // TILE, rows_tile, 0)
        for i, source, target in part:
            back_links.append(
                move(grow.at[pl.ds(i * CAP, CAP)], back.at[me], source, i, bsend, brecv, 2)
            )

        def out_tile(j, carry, block=block):
            lanes = pl.ds(pl.multiple_of(j * TILE, TILE), TILE)
            eout[block, lanes] = jnp.dot(
                mixed[block, :], dn[:, lanes], preferred_element_type=F32
            ).astype(BF16)
            return carry

        lax.fori_loop(0, D // TILE, out_tile, 0)
        for i, source, target in part:
            copy = pltpu.make_async_copy(
                eout.at[pl.ds(i * CAP, CAP)], outs.at[source[0]], osem.at[i]
            )
            copy.start()
            leaving.append(copy)

        def dot_block(i, carry):
            at = pl.ds(pl.multiple_of(i * CAP, CAP), CAP)
            column = jnp.sum(
                eout[at, :].astype(F32) * dys[at, :].astype(F32), axis=1, keepdims=True
            )
            row = jnp.sum(jnp.where(diagonal, column, 0.0), axis=0, keepdims=True)
            dots[i] = jnp.broadcast_to(row, (8, 128))
            return carry

        lax.fori_loop(k * per, (k + 1) * per, dot_block, 0)
        for i, source, target in part:
            dot_links.append(
                move(dots.at[i], gate_back.at[me], source, i, dsend, drecv, 3)
            )

    def up_tile(j, carry):
        lanes = pl.ds(pl.multiple_of(j * TILE, TILE), TILE)
        up_grad[lanes, :] = lax.dot_general(
            rows[:, lanes], ghid[...], (((0,), (0,)), ((), ())), preferred_element_type=F32
        ).astype(BF16)
        return carry

    lax.fori_loop(0, D // TILE, up_tile, 0)

    def down_tile(j, carry):
        lanes = pl.ds(pl.multiple_of(j * TILE, TILE), TILE)
        down_grad[lanes, :] = lax.dot_general(
            mixed[:, lanes], grads[...], (((0,), (0,)), ((), ())), preferred_element_type=F32
        ).astype(BF16)
        return carry

    lax.fori_loop(0, FF // TILE, down_tile, 0)
    for copy in leaving:
        copy.wait()
    back_links[0].wait()
    dot_links[0].wait()
    for copy in back_links[1:] + dot_links[1:]:
        copy.wait_recv()
    for copy in tile_links[1:] + links[1:] + back_links[1:] + dot_links[1:]:
        copy.wait_send()


def run_experts(sent, gates_in, dy_in, gate_up, down):
    anywhere = pl.BlockSpec(memory_space=pl.ANY)
    inside = pl.BlockSpec(memory_space=pltpu.VMEM)
    blocks = jax.ShapeDtypeStruct((EXPERTS, CAP, D), BF16)
    vmem, dma = pltpu.VMEM, pltpu.SemaphoreType.DMA
    return pl.pallas_call(
        experts_kernel,
        name="experts",
        out_shape=(
            blocks,
            jax.ShapeDtypeStruct((EXPERTS, 8, 128), F32),
            blocks,
            jax.ShapeDtypeStruct((D, 2 * FF), BF16),
            jax.ShapeDtypeStruct((FF, D), BF16),
        ),
        in_specs=[anywhere] * 5,
        out_specs=(anywhere, anywhere, anywhere, inside, inside),
        scratch_shapes=[
            vmem((ROWS, D), BF16),
            vmem((EXPERTS, 8, 128), F32),
            vmem((ROWS, D), BF16),
            vmem((ROWS, D), BF16),
            vmem((D, 2 * FF), BF16),
            vmem((FF, D), BF16),
            vmem((ROWS, FF), BF16),
            vmem((ROWS, 2 * FF), BF16),
            vmem((ROWS, D), BF16),
            vmem((ROWS, D), BF16),
            vmem((EXPERTS, 8, 128), F32),
        ]
        + [dma((EXPERTS,))] * 8
        + [dma((EXPERTS,)), dma((2,)), dma((EXPERTS,)), dma((4,))],
        compiler_params=pltpu.CompilerParams(
            collective_id=2, has_side_effects=True, vmem_limit_bytes=58 * 1024 * 1024
        ),
        cost_estimate=pl.CostEstimate(
            flops=33_000_000_000, bytes_accessed=60_000_000, transcendentals=1_200_000
        ),
    )(sent, gates_in, dy_in, gate_up, down)


UP_PART = D // 4
UP_HALF = UP_PART // 2
DOWN_PART = D // 4
DOWN_HALF = FF // 2
SCALE = HEAD_DIM ** (-0.5)
GROUP_ROWS = 1024
COUNT = 256
NT = (((1,), (1,)), ((), ()))
TN = (((0,), (0,)), ((), ()))


def mul(a, b, dims=None):
    if dims is None:
        return jnp.dot(a, b, preferred_element_type=F32)
    return lax.dot_general(a, b, dims, preferred_element_type=F32)


def thirds(v):
    high = v.astype(BF16)
    rest = v - high.astype(F32)
    middle = rest.astype(BF16)
    return high, middle, (rest - middle.astype(F32)).astype(BF16)


def exact(v, one_hot, dims=None):
    return sum(mul(part, one_hot, dims) for part in thirds(v))


def iota(shape, axis):
    return lax.broadcasted_iota(jnp.int32, shape, axis)


def hot(same):
    return jnp.where(same, 1.0, 0.0).astype(BF16)


def read_gains(small):
    select = hot(iota((8, SMALL), 1) == iota((8, SMALL), 0) + EXPERTS)
    select = jnp.where(iota((8, SMALL), 0) < 2, select, jnp.zeros_like(select))
    return mul(select, small, NT), select


def fill_bias(lengths, bias, x):
    first = lengths[0, 0]
    second = first + lengths[0, 1]
    third = second + lengths[0, 2]
    own = x * COUNT + iota((1, COUNT), 1)
    own_seg = sum(jnp.where(own >= end, 1, 0) for end in (first, second, third))

    def step(i, carry):
        base = pl.multiple_of(i * COUNT, COUNT)
        key = base + iota((COUNT, 1), 0)
        key_seg = sum(jnp.where(key >= end, 1, 0) for end in (first, second, third))
        allowed = (key_seg == own_seg) & (key <= own)
        bias[pl.ds(base, COUNT), :] = jnp.where(allowed, 0.0, -1e30)
        return carry

    lax.fori_loop(0, GROUP_ROWS // COUNT, step, 0)


def turn(v, cosd, sind):
    return v * cosd + pltpu.roll(v, HEAD_DIM // 2, 1) * sind


def forward_kernel(
    lengths, tokens, wq_in, wb_in, any_slot, named, cosd, sind,
    q_out, kv_out, attended, middle, normed, tops, totals, gates_out, tiles, dispatch,
    wq, wb, kv, own_kv, bias, vt, nf, send, recv, local,
):
    y, z, c, x = place()
    peers = [device(y, z, c, (x + d) % 4) for d in (1, 2, 3)]
    loads = [
        pltpu.make_async_copy(wq_in.at[:, pl.ds(D, 512)], wq.at[:, pl.ds(D, 512)], local.at[0]),
        pltpu.make_async_copy(wq_in.at[:, pl.ds(0, D)], wq.at[:, pl.ds(0, D)], local.at[1]),
        pltpu.make_async_copy(wb_in, wb, local.at[2]),
    ]
    for load in loads:
        load.start()
    greet(peers)
    loads[2].wait()
    small = wb[:, D:]
    gains, _ = read_gains(small)
    xf = tokens[...].astype(F32)
    inverse = lax.rsqrt(jnp.mean(xf * xf, axis=1, keepdims=True) + norm_eps)
    normed[...] = (xf * inverse * gains[0:1, :]).astype(BF16)
    loads[0].wait()
    for j in range(2):
        part = mul(normed[...], wq[:, D + j * 256 : D + (j + 1) * 256])
        if j == 0:
            for h in range(2):
                lanes = slice(h * HEAD_DIM, (h + 1) * HEAD_DIM)
                own_kv[:, lanes] = turn(part[:, lanes], cosd[...], sind[...]).astype(BF16)
        else:
            own_kv[:, 256:512] = part.astype(BF16)
    rows = pl.ds(pl.multiple_of(x * COUNT, COUNT), COUNT)
    link = Links(send, recv)
    pushes = [link.push(own_kv, kv.at[rows], peer) for peer in peers]
    kv[rows, :] = own_kv[...]
    fill_bias(lengths, bias, x)
    loads[1].wait()

    def query_tile(j, carry):
        lanes = pl.ds(pl.multiple_of(j * 256, 256), 256)
        part = mul(normed[...], wq[:, lanes])
        q_out[:, lanes] = jnp.concatenate(
            [turn(part[:, h * 128 : (h + 1) * 128], cosd[...], sind[...]) for h in range(2)],
            axis=1,
        ).astype(BF16)
        return carry

    lax.fori_loop(0, D // 256, query_tile, 0)

    logits = jnp.where(named[...] > 0, mul(tokens[...], small), -jnp.inf)
    weight = jnp.exp(logits - jnp.max(logits, axis=1, keepdims=True))
    gates = weight / jnp.sum(weight, axis=1, keepdims=True)
    gates_out[...] = gates
    expand = hot(iota((128, ROWS), 0) == iota((128, ROWS), 1) // CAP)
    spread = exact(gates, expand)
    slot_gates = jnp.sum(any_slot[...].astype(F32) * spread, axis=0, keepdims=True)
    expert_of = iota((EXPERTS, ROWS), 1) // CAP == iota((EXPERTS, ROWS), 0)
    fold = hot(iota((128, ROWS), 1) % CAP == iota((128, ROWS), 0))
    tile = exact(jnp.where(expert_of, slot_gates, 0.0), fold, NT)
    tiles[...] = jnp.broadcast_to(tile[:, None, :], (EXPERTS, 8, 128))

    for push in pushes:
        push.wait_recv()
    kv_out[...] = kv[...]
    for g in range(HEADS_KV):
        vt[g] = kv[:, 256 + g * 128 : 384 + g * 128].T
    for g in range(HEADS_KV):

        def head(i, carry, g=g):
            h = g * REPEAT + i
            lanes = pl.ds(pl.multiple_of(h * HEAD_DIM, HEAD_DIM), HEAD_DIM)
            s = mul(kv[:, g * 128 : (g + 1) * 128], q_out[:, lanes], NT) * SCALE + bias[...]
            top = jnp.max(s, axis=0, keepdims=True)
            p = jnp.exp(s - top)
            total = jnp.sum(p, axis=0, keepdims=True)
            tops[pl.ds(h, 1), :] = top
            totals[pl.ds(h, 1), :] = total
            low = (p * (1.0 / total)).astype(BF16)
            attended[:, lanes] = mul(vt[g], low).T.astype(BF16)
            return carry

        lax.fori_loop(0, REPEAT, head, 0)

    def out_tile(j, carry):
        lanes = pl.ds(pl.multiple_of(j * 256, 256), 256)
        middle[:, lanes] = tokens[:, lanes].astype(F32) + mul(attended[...], wb[lanes, 0:D], NT)
        return carry

    lax.fori_loop(0, D // 256, out_tile, 0)
    m = middle[...]
    inverse = lax.rsqrt(jnp.mean(m * m, axis=1, keepdims=True) + norm_eps)
    nf[...] = (m * inverse * gains[1:2, :]).astype(BF16)

    def dispatch_tile(j, carry):
        lanes = pl.ds(pl.multiple_of(j * 256, 256), 256)
        dispatch[lanes, :] = mul(any_slot[:, lanes], nf[...], TN).astype(BF16)
        return carry

    lax.fori_loop(0, ROWS // 256, dispatch_tile, 0)
    link.drain()


def run_forward(lengths, tokens, wq, wb, any_slot, named, cosd, sind):
    anywhere = pl.BlockSpec(memory_space=pl.ANY)
    inside = pl.BlockSpec(memory_space=pltpu.VMEM)
    vmem, dma = pltpu.VMEM, pltpu.SemaphoreType.DMA
    shape = jax.ShapeDtypeStruct
    return pl.pallas_call(
        forward_kernel,
        name="forward",
        out_shape=(
            shape((COUNT, D), BF16),
            shape((GROUP_ROWS, 512), BF16),
            shape((COUNT, D), BF16),
            shape((COUNT, D), F32),
            shape((COUNT, D), BF16),
            shape((16, COUNT), F32),
            shape((16, COUNT), F32),
            shape((COUNT, 128), F32),
            shape((EXPERTS, 8, 128), F32),
            shape((ROWS, D), BF16),
        ),
        in_specs=[pl.BlockSpec(memory_space=pltpu.SMEM), inside, anywhere, anywhere] + [inside] * 4,
        out_specs=(inside,) * 10,
        scratch_shapes=[
            vmem((D, WA), BF16),
            vmem((D, WB), BF16),
            vmem((GROUP_ROWS, 512), BF16),
            vmem((COUNT, 512), BF16),
            vmem((GROUP_ROWS, COUNT), F32),
            vmem((HEADS_KV, HEAD_DIM, GROUP_ROWS), BF16),
            vmem((COUNT, D), BF16),
            dma((3,)),
            dma((3,)),
            dma((3,)),
        ],
        compiler_params=pltpu.CompilerParams(
            collective_id=3, has_side_effects=True, vmem_limit_bytes=48 * 1024 * 1024
        ),
        cost_estimate=pl.CostEstimate(
            flops=6_000_000_000, bytes_accessed=30_000_000, transcendentals=3_200_000
        ),
    )(lengths, tokens, wq, wb, any_slot, named, cosd, sind)


def norm_grad(values, gain, grad):
    inverse = lax.rsqrt(jnp.mean(values * values, axis=1, keepdims=True) + norm_eps)
    unit = values * inverse
    scaled = grad * gain
    drop = jnp.mean(scaled * unit, axis=1, keepdims=True)
    return inverse * (scaled - unit * drop), jnp.sum(grad * unit, axis=0, keepdims=True)


def backward_kernel(
    lengths, tokens, cotangent, any_slot, gates, gate_back, queries, kv_in, attended, middle,
    normed, tops, totals, cosd, sind, wq_in, wb_in, back_in, up_in, down_in,
    grad_tokens, grad_qkv, grad_out, grad_small, up_far, down_far,
    wq, wb, back, bias, kt, gn, gmid, gb, gatt, gp, dk, dv, leave, land, send, recv, local,
):
    y, z, c, x = place()
    peers = [device(y, z, c, (x + d) % 4) for d in (1, 2, 3)]
    loads = [
        pltpu.make_async_copy(back_in, back, local.at[0]),
        pltpu.make_async_copy(wb_in, wb, local.at[1]),
        pltpu.make_async_copy(wq_in, wq, local.at[2]),
    ]
    for load in loads:
        load.start()
    greet(peers)
    link = Links(send, recv)
    facing = (x + 2) % 4
    pushes = []
    for half, peer in ((0, peers[2]), (1, peers[0])):
        up_rows = pl.ds(pl.multiple_of(facing * UP_PART + half * UP_HALF, UP_HALF), UP_HALF)
        pushes.append(link.push(up_in.at[up_rows], up_far.at[half], peer))
        lanes = pl.ds(pl.multiple_of(facing * DOWN_PART, 128), DOWN_PART)
        down_rows = pl.ds(half * DOWN_HALF, DOWN_HALF)
        pushes.append(link.push(down_in.at[down_rows, lanes], down_far.at[half], peer))
    fill_bias(lengths, bias, x)
    for g in range(HEADS_KV):
        kt[g] = kv_in[:, g * 128 : (g + 1) * 128].T
    loads[0].wait()

    def ffn_tile(j, carry):
        lanes = pl.ds(pl.multiple_of(j * 256, 256), 256)
        gn[:, lanes] = mul(any_slot[...], back[:, lanes])
        return carry

    lax.fori_loop(0, D // 256, ffn_tile, 0)
    loads[1].wait()
    gains, select = read_gains(wb[:, D:])
    moved, ffn_gain = norm_grad(middle[...], gains[1:2, :], gn[...])
    gm = cotangent[...].astype(F32) + moved
    gmid[...] = gm
    gb[...] = gm.astype(BF16)

    def att_tile(j, carry):
        lanes = pl.ds(pl.multiple_of(j * 256, 256), 256)
        gatt[:, lanes] = mul(gb[...], wb[:, lanes]).astype(BF16)
        return carry

    lax.fori_loop(0, D // 256, att_tile, 0)
    kv_pushes = []
    for g in range(HEADS_KV):
        dk[...] = jnp.zeros_like(dk)
        dv[...] = jnp.zeros_like(dv)

        def head(i, carry, g=g):
            h = g * REPEAT + i
            lanes = pl.ds(pl.multiple_of(h * HEAD_DIM, HEAD_DIM), HEAD_DIM)
            s = mul(kv_in[:, g * 128 : (g + 1) * 128], queries[:, lanes], NT) * SCALE + bias[...]
            p = jnp.exp(s - tops[pl.ds(h, 1), :]) * (1.0 / totals[pl.ds(h, 1), :])
            dv[...] += mul(p.astype(BF16), gatt[:, lanes])
            t = p * mul(kv_in[:, 256 + g * 128 : 384 + g * 128], gatt[:, lanes], NT)
            ds = (t - p * jnp.sum(t, axis=0, keepdims=True)).astype(BF16)
            dk[...] += mul(ds, queries[:, lanes])
            dq = mul(kt[g], ds).T * SCALE
            gp[:, lanes] = turn(dq, cosd[...], -sind[...]).astype(BF16)
            return carry

        lax.fori_loop(0, REPEAT, head, 0)
        leave[g, :, 0:128] = (dk[...] * SCALE).astype(BF16)
        leave[g, :, 128:256] = dv[...].astype(BF16)
        for d in (1, 2, 3):
            away = pl.ds(pl.multiple_of(((x + d) % 4) * COUNT, COUNT), COUNT)
            kv_pushes.append(link.push(leave.at[g, away], land.at[g, d - 1], peers[d - 1]))

    def out_tile(j, carry):
        lanes = pl.ds(pl.multiple_of(j * 256, 256), 256)
        grad_out[lanes, :] = mul(gb[:, lanes], attended[...], TN).astype(BF16)
        return carry

    lax.fori_loop(0, D // 256, out_tile, 0)

    expert_of = iota((EXPERTS, ROWS), 1) // CAP == iota((EXPERTS, ROWS), 0)
    fold = hot(iota((128, ROWS), 1) % CAP == iota((128, ROWS), 0))
    wide = exact(gate_back[:, 0, :], fold)
    slot_grads = jnp.sum(jnp.where(expert_of, wide, 0.0), axis=0, keepdims=True)
    expand = hot(iota((128, ROWS), 0) == iota((128, ROWS), 1) // CAP)
    gate_grad = exact(any_slot[...].astype(F32) * slot_grads, expand, NT)
    weighted = gates[...] * gate_grad
    logit_grad = weighted - gates[...] * jnp.sum(weighted, axis=1, keepdims=True)
    parts = thirds(logit_grad)
    router_grad = sum(mul(tokens[...], part, TN) for part in parts)
    small = wb[:, D:]

    for push in kv_pushes:
        push.wait_recv()
    mine = pl.ds(pl.multiple_of(x * COUNT, COUNT), COUNT)
    for g in range(HEADS_KV):
        total = leave[g, mine, :].astype(F32)
        for d in range(3):
            total = total + land[g, d].astype(F32)
        gp[:, D + g * 128 : D + (g + 1) * 128] = turn(
            total[:, 0:128], cosd[...], -sind[...]
        ).astype(BF16)
        gp[:, D + 256 + g * 128 : D + 384 + g * 128] = total[:, 128:256].astype(BF16)
    loads[2].wait()

    def qkv_tile(j, carry):
        lanes = pl.ds(pl.multiple_of(j * 256, 256), 256)
        grad_qkv[lanes, :] = mul(normed[:, lanes], gp[...], TN).astype(BF16)
        gn[:, lanes] = mul(gp[...], wq[lanes, :], NT)
        return carry

    lax.fori_loop(0, D // 256, qkv_tile, 0)
    moved, attn_gain = norm_grad(tokens[...].astype(F32), gains[0:1, :], gn[...])
    from_router = sum(mul(part, small, NT) for part in parts)
    grad_tokens[...] = (gmid[...] + moved + from_router).astype(BF16)
    both = jnp.where(
        iota((8, D), 0) == 0, attn_gain, jnp.where(iota((8, D), 0) == 1, ffn_gain, 0.0)
    )
    gain_columns = sum(mul(part, select, TN) for part in thirds(both))
    grad_small[...] = (router_grad + gain_columns).astype(BF16)
    for push in pushes:
        push.wait_recv()
    link.drain()


def run_backward(*operands):
    anywhere = pl.BlockSpec(memory_space=pl.ANY)
    inside = pl.BlockSpec(memory_space=pltpu.VMEM)
    vmem, dma = pltpu.VMEM, pltpu.SemaphoreType.DMA
    shape = jax.ShapeDtypeStruct
    return pl.pallas_call(
        backward_kernel,
        name="backward",
        out_shape=(
            shape((COUNT, D), BF16),
            shape((D, WA), BF16),
            shape((D, D), BF16),
            shape((D, SMALL), BF16),
            shape((2, UP_HALF, 2 * FF), BF16),
            shape((2, DOWN_HALF, DOWN_PART), BF16),
        ),
        in_specs=[pl.BlockSpec(memory_space=pltpu.SMEM)] + [inside] * 14 + [anywhere] * 5,
        out_specs=(inside,) * 4 + (anywhere,) * 2,
        scratch_shapes=[
            vmem((D, WA), BF16),
            vmem((D, WB), BF16),
            vmem((ROWS, D), BF16),
            vmem((GROUP_ROWS, COUNT), F32),
            vmem((HEADS_KV, HEAD_DIM, GROUP_ROWS), BF16),
            vmem((COUNT, D), F32),
            vmem((COUNT, D), F32),
            vmem((COUNT, D), BF16),
            vmem((COUNT, D), BF16),
            vmem((COUNT, WA), BF16),
            vmem((GROUP_ROWS, HEAD_DIM), F32),
            vmem((GROUP_ROWS, HEAD_DIM), F32),
            vmem((HEADS_KV, GROUP_ROWS, 256), BF16),
            vmem((HEADS_KV, 3, COUNT, 256), BF16),
            dma((10,)),
            dma((10,)),
            dma((3,)),
        ],
        compiler_params=pltpu.CompilerParams(
            collective_id=4, has_side_effects=True, vmem_limit_bytes=58 * 1024 * 1024
        ),
        cost_estimate=pl.CostEstimate(
            flops=13_000_000_000, bytes_accessed=50_000_000, transcendentals=3_200_000
        ),
    )(*operands)


def rope_tables(position, half_dim):
    frequency = rope_base ** (-jnp.arange(half_dim, dtype=jnp.float32) / half_dim)
    angles = position.astype(jnp.float32)[:, None] * frequency[None, :]
    return jnp.cos(angles), jnp.sin(angles)


def seq_layout(seq_lens, row_ids):
    seq_ends = jnp.cumsum(seq_lens)
    segment = jnp.sum((row_ids[:, None] >= seq_ends[None, :]).astype(jnp.int32), axis=1)
    seq_start = jnp.sum(
        jnp.where(seq_ends[None, :] <= row_ids[:, None], seq_lens[None, :], 0), axis=1
    )
    return (segment, row_ids - seq_start)


def exchange(rows):
    return lax.all_to_all(
        rows.reshape(EXPERTS, CAP, D), "expert", split_axis=0, concat_axis=0, tiled=True
    ).reshape(EXPERTS * CAP, D)


def body(
    tokens, lengths, top_experts, w_qkv, w_out, gain_attn, gain_ffn, router, gate_up, down_proj, cotangent,
):
    pack = jnp.concatenate(
        [
            w_qkv,
            w_out.T,
            router,
            gain_attn[:, None],
            gain_ffn[:, None],
            jnp.zeros((PIECE, SMALL - EXPERTS - 2), BF16),
        ],
        axis=1,
    )
    pack = jnp.pad(pack, ((0, PADDED - PIECE), (0, 0)))

    row_ids = jnp.arange(COUNT, dtype=jnp.int32)
    own_ids = lax.axis_index("shard") * COUNT + row_ids
    _, own_position = seq_layout(lengths[0], own_ids)
    cosine, sine = rope_tables(own_position, HEAD_DIM // 2)
    cosd = jnp.concatenate([cosine, cosine], axis=1)
    sind = jnp.concatenate([-sine, sine], axis=1)

    full_a, full_b, named, any_slot, dy_rows = gather_weights(pack, top_experts, cotangent)
    dy_rows = exchange(dy_rows)
    wq = full_a.reshape(D, WA)
    wb = full_b.reshape(D, WB)
    queries, kv, attended, middle, normed, tops, totals, gates, tiles, dispatch = run_forward(
        lengths, tokens, wq, wb, any_slot, named, cosd, sind
    )
    back, gate_back, expert_out, up_local, down_local = run_experts(
        dispatch.reshape(EXPERTS, CAP, D),
        tiles,
        dy_rows.reshape(EXPERTS, CAP, D),
        gate_up,
        down_proj,
    )
    returned = exchange(expert_out)
    grad_tokens, grad_qkv, grad_out, grad_small, up_far, down_far = run_backward(
        lengths, tokens, cotangent, any_slot, gates, gate_back, queries, kv, attended, middle,
        normed, tops, totals, cosd, sind, wq, wb, back.reshape(ROWS, D), up_local, down_local,
    )
    sum_a, sum_b, up_sum, down_sum = scatter_sums(
        grad_qkv.reshape(4, 4, 2, BLOCK, WA),
        grad_out.reshape(4, 4, 2, BLOCK, D),
        grad_small.reshape(4, 4, 2, BLOCK, SMALL),
        up_local,
        down_local,
        up_far,
        down_far,
    )
    sum_b = sum_b[:PIECE]

    expand = jnp.arange(ROWS) // CAP == jnp.arange(128)[:, None]
    mix = jnp.dot(gates.astype(BF16), expand.astype(BF16), preferred_element_type=F32)
    mix = (mix * any_slot.astype(F32)).astype(BF16)
    combined = jnp.dot(mix, returned, preferred_element_type=F32)
    output = (middle + combined).astype(BF16)
    return (
        output,
        grad_tokens,
        sum_a[:PIECE],
        sum_b[:, :D].T,
        sum_b[:, D + EXPERTS],
        sum_b[:, D + EXPERTS + 1],
        sum_b[:, D : D + EXPERTS],
        up_sum[None],
        down_sum[None],
    )


def solution(mesh):
    return jax.shard_map(
        body,
        mesh=mesh,
        in_specs=(
            P(("expert", "shard"), None),
            P("expert", None),
            P(("expert", "shard"), None),
            P(("expert", "shard"), None),
            P(None, ("expert", "shard")),
            P(("expert", "shard")),
            P(("expert", "shard")),
            P(("expert", "shard"), None),
            P("expert", None, None),
            P("expert", None, None),
            P(("expert", "shard"), None),
        ),
        out_specs=(
            P(("expert", "shard"), None),
            P(("expert", "shard"), None),
            P(("expert", "shard"), None),
            P(None, ("expert", "shard")),
            P(("expert", "shard")),
            P(("expert", "shard")),
            P(("expert", "shard"), None),
            P("expert", "shard", None),
            P("expert", None, "shard"),
        ),
        check_vma=False,
    )
```

```python
import functools

import jax
import jax.numpy as jnp
from jax import lax
from jax.experimental import pallas as pl
from jax.experimental.pallas import tpu as pltpu
from jax.sharding import PartitionSpec as P

D = 1536
HEADS_Q = 12
HEADS_KV = 2
HEAD_DIM = 128
FF = 768
TOP = 4
EXPERTS = 32
CAP = 48
WIDTH_Q = HEADS_Q * HEAD_DIM
WIDTH_KV = HEADS_KV * HEAD_DIM
REPEAT = HEADS_Q // HEADS_KV

norm_eps = 1e-06
rope_base = 1000000.0
precise = lax.Precision.HIGHEST
MESH = pl.DeviceIdType.MESH
F32 = jnp.float32
BF16 = jnp.bfloat16

PIECE = 12
PADDED = 16
BLOCK = 48
WA = 2048
WB = 1664
SMALL = WB - D


def place():
    e = lax.axis_index("expert")
    return e // 8, (e // 2) % 4, e % 2, lax.axis_index("shard")


def device(y, z, c, x):
    return ((y * 4 + z) * 2 + c, x)


def greet(devices):
    barrier = pltpu.get_barrier_semaphore()
    for d in devices:
        pl.semaphore_signal(barrier, inc=1, device_id=d, device_id_type=MESH)
    pl.semaphore_wait(barrier, len(devices))


class Links:
    def __init__(self, send, recv):
        self.send, self.recv, self.made = send, recv, []

    def push(self, src, dst, where):
        i = len(self.made)
        copy = pltpu.make_async_remote_copy(
            src_ref=src,
            dst_ref=dst,
            send_sem=self.send.at[i],
            recv_sem=self.recv.at[i],
            device_id=where,
            device_id_type=MESH,
        )
        copy.start()
        self.made.append(copy)
        return copy

    def drain(self, skip=()):
        for copy in self.made:
            if not any(copy is done for done in skip):
                copy.wait_send()


def neighbours(y, z, c, x):
    other = 1 - c
    return dict(
        x=[device(y, z, c, (x + d) % 4) for d in (1, 2, 3)],
        y=(device((y + 1) % 4, z, c, x), device((y + 3) % 4, z, c, x)),
        z=(device(y, (z + 1) % 4, c, x), device(y, (z + 3) % 4, c, x)),
        core=device(y, z, other, x),
    )


def everyone_near(near):
    return list(near["x"]) + list(near["y"]) + list(near["z"]) + [near["core"]]


def pick_rows(rows, columns, row_block, column_block):
    r = lax.broadcasted_iota(jnp.int32, (rows, columns), 0)
    q = lax.broadcasted_iota(jnp.int32, (rows, columns), 1)
    same = (r // row_block == q // column_block) & (r % row_block == q % column_block)
    return jnp.where(same, 1.0, 0.0).astype(BF16)


def faces(y, z, c, x):
    along_z, along_y = [], []
    for d in range(4):
        for k in range(2):
            core = c if k == 0 else 1 - c
            along_z.append((device(y, (z + d) % 4, core, x), (z + d) % 4, core))
            along_y.append((device((y + d) % 4, z, core, x), (y + d) % 4, core))
    return along_z, along_y


def cross(y, z, c, x):
    along_z, along_y = faces(y, z, c, x)
    return [f[0] for f in along_z[1:] + along_y[2:]]


def lines(y, z, c, x):
    return (
        [device((y + d) % 4, z, c, x) for d in (1, 2, 3)],
        [device(y, (z + d) % 4, c, x) for d in (1, 2, 3)],
    )


def route(top_experts, named, own_slot):
    lanes = iota((COUNT, 128), 1)
    for k in range(TOP):
        hit = jnp.where(top_experts[:, k : k + 1] == lanes, 1.0, 0.0)
        named[...] = hit if k == 0 else named[...] + hit
    earlier = hot(iota((COUNT, COUNT), 1) < iota((COUNT, COUNT), 0))
    slot_of = mul(earlier, named[...].astype(BF16))
    own_slot[...] = jnp.where(named[...] > 0, slot_of, -1.0).astype(BF16)


def slot_hits(slot_of, hits, experts):
    p = iota((1, SLOTS), 1)
    q = p - 8 * FIRST
    wanted = jnp.where(p < 8 * FIRST, p % FIRST, FIRST + q % SECOND).astype(F32)
    local = jnp.where(p < 8 * FIRST, p // FIRST, q // SECOND)
    expand = hot(iota((128, SLOTS), 0) == experts(local))

    def step(s, carry):
        hits[s] = hot(mul(slot_of[s], expand) == wanted)
        return carry

    lax.fori_loop(0, 4, step, 0)


def gather_kernel(
    pack, top_experts, cotangent, full_a, full_b, named, hot_a, hot_b, dy_a, dy_b,
    xbuf, own_a, own_b, own_slot, slot_y, slot_z, send, recv, local,
):
    y, z, c, x = place()
    near = neighbours(y, z, c, x)
    line_y, line_z = lines(y, z, c, x)
    greet(everyone_near(near) + [line_y[1], line_z[1]])
    link = Links(send, recv)
    first = [link.push(pack, xbuf.at[x], near["x"][d]) for d in range(3)]
    xbuf[pl.ds(x, 1)] = pack[...][None]
    for copy in first:
        copy.wait_recv()
    select = pick_rows(BLOCK, 4 * PADDED, PIECE, PADDED)
    pieces = xbuf[...].reshape(4 * PADDED, WA + WB)
    own_a[...] = jnp.dot(select, pieces[:, :WA], preferred_element_type=F32).astype(BF16)
    own_b[...] = jnp.dot(select, pieces[:, WA:], preferred_element_type=F32).astype(BF16)

    def at_a(far, close, columns=None):
        view = full_a.at[far, close, c]
        return view if columns is None else view.at[:, columns]

    def at_b(far, close, columns=None):
        view = full_b.at[close, far, c]
        return view if columns is None else view.at[:, columns]

    def line_a(far, part=slice(None)):
        return full_a.at[far, part, c]

    def line_b(far, part=slice(None)):
        return full_b.at[part, far, c]

    jobs = [
        dict(own=own_a, at=at_a, line=line_a, close="z", far="y", p=z, q=y, half=1024, i=0),
        dict(own=own_b, at=at_b, line=line_b, close="y", far="z", p=y, q=z, half=896, i=1),
    ]
    for j in jobs:
        here = j["at"](j["q"], j["p"])
        plus, minus = near[j["close"]]
        j["up"] = link.push(j["own"], here, plus)
        j["down"] = link.push(j["own"], here, minus)
        j["core"] = [link.push(j["own"], here, near["core"])]
        j["local"] = pltpu.make_async_copy(j["own"], here, local.at[j["i"]])
        j["local"].start()
    route(top_experts, named, own_slot)
    slot_y[pl.ds(y, 1)] = own_slot[...][None]
    slot_z[pl.ds(z, 1)] = own_slot[...][None]
    slots = [link.push(own_slot, slot_y.at[y], peer) for peer in line_y]
    slots += [link.push(own_slot, slot_z.at[z], peer) for peer in line_z]
    for j in jobs:
        plus, minus = near[j["close"]]
        left, right = (j["p"] + 3) % 4, (j["p"] + 1) % 4
        j["up"].wait_recv()
        part = j["at"](j["q"], left, pl.ds(0, j["half"]))
        j["up2"] = link.push(part, part, plus)
        j["down"].wait_recv()
        part = j["at"](j["q"], right, pl.ds(j["half"], j["own"].shape[1] - j["half"]))
        j["down2"] = link.push(part, part, minus)
        for side in (left, right):
            block = j["at"](j["q"], side)
            j["core"].append(link.push(block, block, near["core"]))
    for j in jobs:
        j["up2"].wait_recv()
        j["down2"].wait_recv()
        block = j["at"](j["q"], (j["p"] + 2) % 4)
        j["local"].wait()
        plus, minus = near[j["far"]]
        line = j["line"](j["q"])
        j["up"] = link.push(line, line, plus)
        j["down"] = link.push(line, line, minus)
        j["core"].append(link.push(block, block, near["core"]))
    half_a, half_b = cotangent.at[:, pl.ds(0, HALF)], cotangent.at[:, pl.ds(HALF, HALF)]
    kept = [
        pltpu.make_async_copy(half_a, dy_a.at[y], local.at[2]),
        pltpu.make_async_copy(half_b, dy_b.at[z], local.at[3]),
    ]
    for copy in kept:
        copy.start()
    dys = [link.push(half_a, dy_a.at[y], peer) for peer in line_y]
    dys += [link.push(half_b, dy_b.at[z], peer) for peer in line_z]
    for copy in slots:
        copy.wait_recv()
    slot_hits(slot_y, hot_a, lambda e: y * 8 + e)
    slot_hits(slot_z, hot_b, lambda e: (e // 2) * 8 + z * 2 + e % 2)
    for j in jobs:
        plus, minus = near[j["far"]]
        left, right = (j["q"] + 3) % 4, (j["q"] + 1) % 4
        j["up"].wait_recv()
        part = j["line"](left, pl.ds(0, 2))
        j["up2"] = link.push(part, part, plus)
        j["down"].wait_recv()
        part = j["line"](right, pl.ds(2, 2))
        j["down2"] = link.push(part, part, minus)
        for side in (left, right):
            block = j["line"](side)
            j["core"].append(link.push(block, block, near["core"]))
    for j in jobs:
        opposite = (j["q"] + 2) % 4
        j["up2"].wait_recv()
        part = j["line"](opposite, pl.ds(0, 2))
        j["core"].append(link.push(part, part, near["core"]))
        j["down2"].wait_recv()
        part = j["line"](opposite, pl.ds(2, 2))
        j["core"].append(link.push(part, part, near["core"]))
    for j in jobs:
        for copy in j["core"]:
            copy.wait_recv()
    for copy in dys:
        copy.wait_recv()
    for copy in kept:
        copy.wait()
    link.drain()


def gather_weights(pack, top_experts, cotangent):
    inside = pl.BlockSpec(memory_space=pltpu.VMEM)
    anywhere = pl.BlockSpec(memory_space=pl.ANY)
    copies = 3 + 2 * 16 + 12
    return pl.pallas_call(
        gather_kernel,
        name="gather_weights",
        out_shape=(
            jax.ShapeDtypeStruct((4, 4, 2, BLOCK, WA), BF16),
            jax.ShapeDtypeStruct((4, 4, 2, BLOCK, WB), BF16),
            jax.ShapeDtypeStruct((COUNT, 128), F32),
            jax.ShapeDtypeStruct((4, COUNT, SLOTS), BF16),
            jax.ShapeDtypeStruct((4, COUNT, SLOTS), BF16),
            jax.ShapeDtypeStruct((4, COUNT, HALF), BF16),
            jax.ShapeDtypeStruct((4, COUNT, HALF), BF16),
        ),
        in_specs=[inside, inside, anywhere],
        out_specs=(anywhere, anywhere, inside, inside, inside, anywhere, anywhere),
        scratch_shapes=[
            pltpu.VMEM((4, PADDED, WA + WB), BF16),
            pltpu.VMEM((BLOCK, WA), BF16),
            pltpu.VMEM((BLOCK, WB), BF16),
            pltpu.VMEM((COUNT, 128), BF16),
            pltpu.VMEM((4, COUNT, 128), BF16),
            pltpu.VMEM((4, COUNT, 128), BF16),
            pltpu.SemaphoreType.DMA((copies,)),
            pltpu.SemaphoreType.DMA((copies,)),
            pltpu.SemaphoreType.DMA((4,)),
        ],
        compiler_params=pltpu.CompilerParams(
            collective_id=0, has_side_effects=True, vmem_limit_bytes=24 * 1024 * 1024
        ),
        cost_estimate=pl.CostEstimate(flops=0, bytes_accessed=24_000_000, transcendentals=0),
    )(pack, top_experts, cotangent)


def add_blocks(dst, far, start, count, sources):
    def step(i, carry):
        total = dst[far, start + i].astype(F32)
        for source in sources:
            total = total + source(i).astype(F32)
        dst[far, start + i] = total.astype(BF16)
        return carry

    lax.fori_loop(0, count, step, 0)


def scatter_kernel(
    ga, gb, gs, up_in, down_in, up_far, down_far, out_a, out_b, up_out, down_out,
    core_a, core_b, mine_a, mine_b, one_a, one_b, two_a, two_b,
    half_a0, half_a1, half_b0, half_b1, last_a, last_b, xout, xin,
    ups, downs, up_got, down_got, up_land, down_land,
    send, recv, local,
):
    y, z, c, x = place()
    near = neighbours(y, z, c, x)
    greet(everyone_near(near))
    link = Links(send, recv)
    other = 1 - c
    jobs = [
        dict(src=[(lambda f, s: ga.at[f, :, s], 0, WA)], core=core_a, mine=mine_a, one=one_a, two=two_a,
             halves=(half_a0, half_a1), last=last_a, far="y", close="z", q=y, p=z,
             width=WA, half=1024, lane=0, i=0),
        dict(src=[(lambda f, s: gb.at[:, f, s], 0, D), (lambda f, s: gs.at[:, f, s], D, SMALL)],
             core=core_b, mine=mine_b, one=one_b, two=two_b,
             halves=(half_b0, half_b1), last=last_b, far="z", close="y", q=z, p=y,
             width=WB, half=896, lane=WA, i=1),
    ]
    slots = 0
    for step in (2, 3, 1, 0):
        for j in jobs:
            f = (j["q"] + step) % 4
            j[step] = []
            for source, lane, width in j["src"]:
                lanes = pl.ds(lane, width)
                pushed = link.push(
                    source(f, other), j["core"].at[f, :, :, lanes], near["core"]
                )
                kept = pltpu.make_async_copy(
                    source(f, c), j["mine"].at[f, :, :, lanes], local.at[slots]
                )
                slots += 1
                kept.start()
                j[step].append((pushed, kept))

    fetches = []
    for i, d in enumerate((3, 1, 0)):
        part = (x + d) % 4
        up_rows = pl.ds(pl.multiple_of(part * UP_PART, UP_PART), UP_PART)
        lanes = pl.ds(pl.multiple_of(part * DOWN_PART, 128), DOWN_PART)
        fetches.append(pltpu.make_async_copy(up_in.at[up_rows], ups.at[i], local.at[slots]))
        fetches.append(
            pltpu.make_async_copy(down_in.at[:, lanes], downs.at[i], local.at[slots + 1])
        )
        slots += 2
    fetches.append(pltpu.make_async_copy(up_far, up_got, local.at[slots]))
    fetches.append(pltpu.make_async_copy(down_far, down_got, local.at[slots + 1]))
    for fetch in fetches:
        fetch.start()
    for fetch in fetches:
        fetch.wait()
    sides = []
    for i, peer in enumerate((near["x"][2], near["x"][0])):
        up_rows = slice(i * UP_HALF, (i + 1) * UP_HALF)
        down_rows = slice(i * DOWN_HALF, (i + 1) * DOWN_HALF)
        ups[i, up_rows, :] = (ups[i, up_rows, :].astype(F32) + up_got[i].astype(F32)).astype(BF16)
        downs[i, down_rows, :] = (
            downs[i, down_rows, :].astype(F32) + down_got[i].astype(F32)
        ).astype(BF16)
        sides.append(link.push(ups.at[i], up_land.at[i], peer))
        sides.append(link.push(downs.at[i], down_land.at[i], peer))

    def ready(j, step):
        for pushed, kept in j[step]:
            pushed.wait_recv()
            kept.wait()

    for j in jobs:
        f = (j["q"] + 2) % 4
        ready(j, 2)
        mine = j["mine"]
        add_blocks(j["core"], f, 0, 4, [lambda i, f=f, m=mine: m[f, i]])
        plus, minus = near[j["far"]]
        j["down"] = link.push(j["core"].at[f, pl.ds(0, 2)], j["one"].at[0], minus)
        j["up"] = link.push(j["core"].at[f, pl.ds(2, 2)], j["one"].at[1], plus)
    for j in jobs:
        plus, minus = near[j["far"]]
        mine, one = j["mine"], j["one"]
        f = (j["q"] + 3) % 4
        ready(j, 3)
        add_blocks(j["core"], f, 2, 2, [lambda i, f=f, m=mine: m[f, i + 2]])
        j["down"].wait_recv()
        add_blocks(
            j["core"], f, 0, 2, [lambda i, f=f, m=mine: m[f, i], lambda i, o=one: o[0, i]]
        )
        j["down2"] = link.push(j["core"].at[f], j["two"].at[0], minus)
        f = (j["q"] + 1) % 4
        ready(j, 1)
        add_blocks(j["core"], f, 0, 2, [lambda i, f=f, m=mine: m[f, i]])
        j["up"].wait_recv()
        add_blocks(
            j["core"], f, 2, 2, [lambda i, f=f, m=mine: m[f, i + 2], lambda i, o=one: o[1, i]]
        )
        j["up2"] = link.push(j["core"].at[f], j["two"].at[1], plus)
    for j in jobs:
        mine, two = j["mine"], j["two"]
        f = j["q"]
        ready(j, 0)
        j["down2"].wait_recv()
        j["up2"].wait_recv()
        add_blocks(
            j["core"], f, 0, 4,
            [lambda i, f=f, m=mine: m[f, i], lambda i, t=two: t[0, i], lambda i, t=two: t[1, i]],
        )
        plus, minus = near[j["close"]]
        g = (j["p"] + 2) % 4
        h, w = j["half"], j["width"]
        j["down"] = link.push(j["core"].at[f, g, :, pl.ds(0, h)], j["halves"][0], minus)
        j["up"] = link.push(j["core"].at[f, g, :, pl.ds(h, w - h)], j["halves"][1], plus)
    for j in jobs:
        plus, minus = near[j["close"]]
        f, h, w, core = j["q"], j["half"], j["width"], j["core"]
        g = (j["p"] + 3) % 4
        j["down"].wait_recv()
        core[f, g, :, 0:h] = (
            core[f, g, :, 0:h].astype(F32) + j["halves"][0][...].astype(F32)
        ).astype(BF16)
        j["down2"] = link.push(core.at[f, g], j["last"].at[0], minus)
        g = (j["p"] + 1) % 4
        j["up"].wait_recv()
        core[f, g, :, h:w] = (
            core[f, g, :, h:w].astype(F32) + j["halves"][1][...].astype(F32)
        ).astype(BF16)
        j["up2"] = link.push(core.at[f, g], j["last"].at[1], plus)
    select = pick_rows(4 * PADDED, BLOCK, PADDED, PIECE)
    for j in jobs:
        f, g = j["q"], j["p"]
        j["down2"].wait_recv()
        j["up2"].wait_recv()
        total = (
            j["core"][f, g].astype(F32)
            + j["last"][0].astype(F32)
            + j["last"][1].astype(F32)
        ).astype(BF16)
        spread = jnp.dot(select, total, preferred_element_type=F32).astype(BF16)
        xout[:, :, j["lane"] : j["lane"] + j["width"]] = spread.reshape(4, PADDED, j["width"])
    final = [
        link.push(xout.at[(x + d) % 4], xin.at[d - 1], near["x"][d - 1]) for d in (1, 2, 3)
    ]
    for copy in final:
        copy.wait_recv()
    mine = xout[x].astype(F32)
    for d in range(3):
        mine = mine + xin[d].astype(F32)
    out_a[...] = mine[:, :WA]
    out_b[...] = mine[:, WA:]
    for push in sides:
        push.wait_recv()
    up_out[...] = ups[2].astype(F32) + up_land[0].astype(F32) + up_land[1].astype(F32)
    down_out[...] = downs[2].astype(F32) + down_land[0].astype(F32) + down_land[1].astype(F32)
    link.drain()


def scatter_sums(*operands):
    copies = 2 * (4 + 4 + 4) + 4 + 3 + 4
    vmem = pltpu.VMEM
    scratch = []
    for shape in ((4, 4), (4, 4), (2, 2), (2, 4)):
        scratch += [vmem((*shape, BLOCK, WA), BF16), vmem((*shape, BLOCK, WB), BF16)]
    scratch += [
        vmem((BLOCK, 1024), BF16),
        vmem((BLOCK, 1024), BF16),
        vmem((BLOCK, 896), BF16),
        vmem((BLOCK, WB - 896), BF16),
        vmem((2, BLOCK, WA), BF16),
        vmem((2, BLOCK, WB), BF16),
        vmem((4, PADDED, WA + WB), BF16),
        vmem((3, PADDED, WA + WB), BF16),
        vmem((3, UP_PART, 2 * FF), BF16),
        vmem((3, FF, DOWN_PART), BF16),
        vmem((2, UP_HALF, 2 * FF), BF16),
        vmem((2, DOWN_HALF, DOWN_PART), BF16),
        vmem((2, UP_PART, 2 * FF), BF16),
        vmem((2, FF, DOWN_PART), BF16),
        pltpu.SemaphoreType.DMA((copies,)),
        pltpu.SemaphoreType.DMA((copies,)),
        pltpu.SemaphoreType.DMA((20,)),
    ]
    return pl.pallas_call(
        scatter_kernel,
        name="scatter_sums",
        out_shape=(
            jax.ShapeDtypeStruct((PADDED, WA), F32),
            jax.ShapeDtypeStruct((PADDED, WB), F32),
            jax.ShapeDtypeStruct((UP_PART, 2 * FF), F32),
            jax.ShapeDtypeStruct((FF, DOWN_PART), F32),
        ),
        in_specs=[pl.BlockSpec(memory_space=pl.ANY)] * 7,
        out_specs=(pl.BlockSpec(memory_space=pltpu.VMEM),) * 4,
        scratch_shapes=scratch,
        compiler_params=pltpu.CompilerParams(
            collective_id=1, has_side_effects=True, vmem_limit_bytes=40 * 1024 * 1024
        ),
        cost_estimate=pl.CostEstimate(flops=0, bytes_accessed=24_000_000, transcendentals=0),
    )(*operands)


ROWS = EXPERTS * CAP
TILE = 256
FIRST = 32
SECOND = 16
PIECES = (FIRST, SECOND)
SLOTS = 8 * CAP
HALF = D // 2
LANES = 128
WIDE = D + LANES
WIDE_A = HALF
WIDE_B = WIDE - HALF
SCALE = HEAD_DIM ** (-0.5)
GROUP_ROWS = 1024
COUNT = 256
NT = (((1,), (1,)), ((), ()))
TN = (((0,), (0,)), ((), ()))


def mul(a, b, dims=None):
    if dims is None:
        return jnp.dot(a, b, preferred_element_type=F32)
    return lax.dot_general(a, b, dims, preferred_element_type=F32)


def thirds(v):
    high = v.astype(BF16)
    rest = v - high.astype(F32)
    middle = rest.astype(BF16)
    return high, middle, (rest - middle.astype(F32)).astype(BF16)


def iota(shape, axis):
    return lax.broadcasted_iota(jnp.int32, shape, axis)


def hot(same):
    return jnp.where(same, 1.0, 0.0).astype(BF16)


class Moves(Links):
    def __init__(self, send, recv, local):
        super().__init__(send, recv)
        self.local, self.kept = local, 0

    def keep(self, src, dst):
        copy = pltpu.make_async_copy(src, dst, self.local.at[self.kept])
        self.kept += 1
        copy.start()
        return copy

    def send_or_keep(self, i, src, dst, where):
        if i == 0:
            return self.keep(src, dst).wait
        return self.push(src, dst, where).wait_recv


def to_slots(hits, rows, stage, piece):
    n = PIECES[piece]
    columns = slice(0, 8 * FIRST) if piece == 0 else slice(8 * FIRST, SLOTS)
    for s in range(4):
        taken = mul(hits[s, :, columns], rows[s], TN).astype(BF16)
        stage[:, s] = taken.reshape(8, n, taken.shape[1])


def deliver(moves, at, stage_a, stage_b, rows, split):
    y, z, c, x = at
    along_z, along_y = faces(y, z, c, x)
    width = rows.shape[3]
    waits = []
    for i, (where, zt, ct) in enumerate(along_z):
        dst = rows.at[z, pl.ds(c * 4, 4), :, pl.ds(0, split)]
        waits.append(moves.send_or_keep(i, stage_a.at[zt * 2 + ct], dst, where))
    for i, (where, yt, ct) in enumerate(along_y):
        dst = rows.at[:, c * 4 + y, :, pl.ds(split, width - split)]
        waits.append(moves.send_or_keep(i, stage_b.at[yt * 2 + ct], dst, where))
    return waits


def give_back_a(moves, at, rows, back_a, split):
    y, z, c, x = at
    along_z, _ = faces(y, z, c, x)
    return [
        moves.send_or_keep(
            i, rows.at[zt, pl.ds(ct * 4, 4), :, pl.ds(0, split)], back_a.at[z * 2 + c], where
        )
        for i, (where, zt, ct) in enumerate(along_z)
    ]


def give_back_b(moves, at, rows, back_b, split):
    y, z, c, x = at
    _, along_y = faces(y, z, c, x)
    width = rows.shape[3]
    return [
        moves.send_or_keep(
            i, rows.at[:, ct * 4 + yt, :, pl.ds(split, width - split)], back_b.at[y * 2 + c], where
        )
        for i, (where, yt, ct) in enumerate(along_y)
    ]


def add_up(hits, back_1, back_2, parts, land, me, line, moves):
    waits = []
    for d in (1, 2, 3, 0):
        s = (me + d) % 4
        first, second = back_1[:, s], back_2[:, s]
        width = first.shape[2]
        total = mul(hits[s, :, : 8 * FIRST], first.reshape(8 * FIRST, width))
        total = total + mul(hits[s, :, 8 * FIRST :], second.reshape(8 * SECOND, width))
        if d == 0:
            land[pl.ds(s, 1)] = total.astype(BF16)[None]
        else:
            parts[d - 1] = total.astype(BF16)
            waits.append(moves.push(parts.at[d - 1], land.at[me], line[d - 1]).wait_recv)
    return waits


def gelu_parts(g):
    inner = 0.7978845608 * (g + 0.044715 * g * g * g)
    th = jnp.tanh(inner)
    half = 0.5 * (1.0 + th)
    slope = half + 0.5 * g * (1.0 - th * th) * (0.7978845608 * (1.0 + 0.134145 * g * g))
    return g * half, slope


def experts_kernel(
    hot_a_in, hot_b_in, nf_a_in, nf_b_in, dy1_in, dy2_in, gate_up, down,
    back_a1, back_a2, back_b1, back_b2, out1, out2, up_out, down_out,
    hot_a, hot_b, nf_a, nf_b, sa1, sa2, sb1, sb2, rows1, rows2, dy1, dy2,
    gu, dn, grads, mixed, ghid, grow1, grow2, eo1, eo2, up_grad, down_grad,
    send, recv, local, load_sem,
):
    at = place()
    y, z, c, x = at
    me = (y * 4 + z) * 2 + c
    loads = [
        pltpu.make_async_copy(src, dst, load_sem.at[i])
        for i, (src, dst) in enumerate(
            (
                (hot_a_in, hot_a), (nf_a_in, nf_a), (hot_b_in, hot_b), (nf_b_in, nf_b),
                (gate_up.at[0], gu), (dy1_in, dy1), (down.at[0], dn), (dy2_in, dy2),
            )
        )
    ]
    for load in loads:
        load.start()
    greet(cross(*at))
    moves = Moves(send, recv, local)
    for load in loads[:4]:
        load.wait()
    to_slots(hot_a, nf_a, sa1, 0)
    to_slots(hot_b, nf_b, sb1, 0)
    waits1 = deliver(moves, at, sa1, sb1, rows1, WIDE_A)
    to_slots(hot_a, nf_a, sa2, 1)
    to_slots(hot_b, nf_b, sb2, 1)
    waits2 = deliver(moves, at, sa2, sb2, rows2, WIDE_A)
    for load in loads[4:]:
        load.wait()
    back_waits = []

    def work(rows, dy, grow, eo, n, start, blocks):
        small = 512 // n

        def at_small(i):
            return i // 8, i % 8

        def gate_of(zz, q):
            lanes = iota((n, LANES), 1)
            mine = (lanes == me) | (lanes == me + EXPERTS) | (lanes == me + 2 * EXPERTS)
            held = rows[zz, q, :, 0:LANES].astype(F32)
            return jnp.sum(jnp.where(mine, held, 0.0), axis=1, keepdims=True)

        def scale_step(i, carry):
            zz, q = at_small(i)
            base = pl.multiple_of(start + i * n, n)
            grads[pl.ds(base, n), :] = (dy[zz, q].astype(F32) * gate_of(zz, q)).astype(BF16)
            return carry

        lax.fori_loop(0, blocks * small, scale_step, 0)
        per = 4 // blocks
        for b in range(blocks):
            zs = slice(b * per, (b + 1) * per)
            block = slice(start + b * 512, start + (b + 1) * 512)

            def hidden_tile(j, carry, zs=zs, block=block):
                lanes = pl.ds(pl.multiple_of(j * TILE, TILE), TILE)
                upper = pl.ds(pl.multiple_of(FF + j * TILE, TILE), TILE)
                g = mul(rows[zs, :, :, LANES:].reshape(512, D), gu[:, lanes])
                act, slope = gelu_parts(g)
                u = mul(rows[zs, :, :, LANES:].reshape(512, D), gu[:, upper])
                mixed[block, lanes] = (act * u).astype(BF16)
                m = mul(grads[block, :], dn[lanes, :], NT)
                ghid[block, lanes] = (m * u * slope).astype(BF16)
                ghid[block, upper] = (m * act).astype(BF16)
                return carry

            lax.fori_loop(0, FF // TILE, hidden_tile, 0)

            def rows_tile(j, carry, zs=zs, block=block):
                lanes = pl.ds(pl.multiple_of(j * TILE, TILE), TILE)
                into = pl.ds(pl.multiple_of(LANES + j * TILE, LANES), TILE)
                part = mul(ghid[block, :], gu[lanes, :], NT).astype(BF16)
                grow[zs, :, :, into] = part.reshape(per, 8, n, TILE)
                return carry

            lax.fori_loop(0, D // TILE, rows_tile, 0)
        back_b = back_b1 if n == FIRST else back_b2
        back_waits.extend(give_back_b(moves, at, grow, back_b, WIDE_A))
        for b in range(blocks):
            zs = slice(b * per, (b + 1) * per)
            block = slice(start + b * 512, start + (b + 1) * 512)

            def out_tile(j, carry, zs=zs, block=block):
                lanes = pl.ds(pl.multiple_of(j * TILE, TILE), TILE)
                part = mul(mixed[block, :], dn[:, lanes]).astype(BF16)
                eo[zs, :, :, lanes] = part.reshape(per, 8, n, TILE)
                return carry

            lax.fori_loop(0, D // TILE, out_tile, 0)

        def gate_step(i, carry):
            zz, q = at_small(i)
            out = eo[zz, q].astype(F32)
            slope = jnp.sum(out * dy[zz, q].astype(F32), axis=1, keepdims=True)
            lanes = iota((n, LANES), 1)
            held = jnp.zeros((n, LANES), F32)
            for k, third in enumerate(thirds(slope)):
                held = jnp.where(lanes == me + k * EXPERTS, third.astype(F32), held)
            grow[zz, q, :, 0:LANES] = held.astype(BF16)
            eo[zz, q] = (out * gate_of(zz, q)).astype(BF16)
            return carry

        lax.fori_loop(0, blocks * small, gate_step, 0)
        back_a = back_a1 if n == FIRST else back_a2
        back_waits.extend(give_back_a(moves, at, grow, back_a, WIDE_A))

    for wait in waits1:
        wait()
    work(rows1, dy1, grow1, eo1, FIRST, 0, 2)
    back_waits.append(moves.keep(eo1, out1).wait)
    for wait in waits2:
        wait()
    work(rows2, dy2, grow2, eo2, SECOND, 1024, 1)
    back_waits.append(moves.keep(eo2, out2).wait)

    def up_tile(j, carry):
        lanes = pl.ds(pl.multiple_of(j * TILE, TILE), TILE)
        held = pl.ds(pl.multiple_of(LANES + j * TILE, LANES), TILE)
        part = mul(rows1[:, :, :, held].reshape(1024, TILE), ghid[0:1024, :], TN)
        part = part + mul(rows2[:, :, :, held].reshape(512, TILE), ghid[1024:, :], TN)
        up_grad[lanes, :] = part.astype(BF16)
        return carry

    lax.fori_loop(0, D // TILE, up_tile, 0)
    back_waits.append(moves.keep(up_grad, up_out).wait)

    def down_tile(j, carry):
        lanes = pl.ds(pl.multiple_of(j * TILE, TILE), TILE)
        down_grad[lanes, :] = mul(mixed[:, lanes], grads[...], TN).astype(BF16)
        return carry

    lax.fori_loop(0, FF // TILE, down_tile, 0)
    back_waits.append(moves.keep(down_grad, down_out).wait)
    for wait in back_waits:
        wait()
    moves.drain()


def pieces(*lead, width):
    return [(*lead, n, width) for n in PIECES]


def run_experts(*operands):
    anywhere = pl.BlockSpec(memory_space=pl.ANY)
    vmem, dma = pltpu.VMEM, pltpu.SemaphoreType.DMA
    outs = (
        pieces(8, 4, width=WIDE_A)
        + pieces(8, 4, width=WIDE_B)
        + pieces(4, 8, width=D)
        + [(D, 2 * FF), (FF, D)]
    )
    held = (
        [(4, COUNT, SLOTS)] * 2
        + [(4, COUNT, WIDE_A), (4, COUNT, WIDE_B)]
        + pieces(8, 4, width=WIDE_A)
        + pieces(8, 4, width=WIDE_B)
        + pieces(4, 8, width=WIDE)
        + pieces(4, 8, width=D)
        + [(D, 2 * FF), (FF, D), (ROWS, D), (ROWS, FF), (ROWS, 2 * FF)]
        + pieces(4, 8, width=WIDE)
        + pieces(4, 8, width=D)
        + [(D, 2 * FF), (FF, D)]
    )
    return pl.pallas_call(
        experts_kernel,
        name="experts",
        out_shape=tuple(jax.ShapeDtypeStruct(shape, BF16) for shape in outs),
        in_specs=[anywhere] * 8,
        out_specs=(anywhere,) * 8,
        scratch_shapes=[vmem(shape, BF16) for shape in held]
        + [dma((56,)), dma((56,)), dma((12,)), dma((8,))],
        compiler_params=pltpu.CompilerParams(
            collective_id=2, has_side_effects=True, vmem_limit_bytes=60 * 1024 * 1024
        ),
        cost_estimate=pl.CostEstimate(
            flops=33_000_000_000, bytes_accessed=60_000_000, transcendentals=1_200_000
        ),
    )(*operands)


UP_PART = D // 4
UP_HALF = UP_PART // 2
DOWN_PART = D // 4
DOWN_HALF = FF // 2


def read_gains(small):
    select = hot(iota((8, SMALL), 1) == iota((8, SMALL), 0) + EXPERTS)
    select = jnp.where(iota((8, SMALL), 0) < 2, select, jnp.zeros_like(select))
    return mul(select, small, NT), select


def fill_bias(lengths, bias, x):
    first = lengths[0, 0]
    second = first + lengths[0, 1]
    third = second + lengths[0, 2]
    own = x * COUNT + iota((1, COUNT), 1)
    own_seg = sum(jnp.where(own >= end, 1, 0) for end in (first, second, third))

    def step(i, carry):
        base = pl.multiple_of(i * COUNT, COUNT)
        key = base + iota((COUNT, 1), 0)
        key_seg = sum(jnp.where(key >= end, 1, 0) for end in (first, second, third))
        allowed = (key_seg == own_seg) & (key <= own)
        bias[pl.ds(base, COUNT), :] = jnp.where(allowed, 0.0, -1e30)
        return carry

    lax.fori_loop(0, GROUP_ROWS // COUNT, step, 0)


def turn(v, cosd, sind):
    return v * cosd + pltpu.roll(v, HEAD_DIM // 2, 1) * sind


def forward_kernel(
    lengths, tokens, wq_in, wb_in, named, cosd, sind, hot_a_in, hot_b_in, dy_a_in, dy_b_in,
    q_out, kv_out, attended_out, middle_out, normed_out, tops, totals, gates_out,
    nf_a, nf_b, dy1, dy2,
    wq, wb, kv, own_kv, bias, vt, q, attended, middle, normed, nf,
    hot_a, hot_b, dy_a, dy_b, sa1, sa2, sb1, sb2, send, recv, local, load_sem,
):
    at = place()
    y, z, c, x = at
    line_y, line_z = lines(y, z, c, x)
    peers = [device(y, z, c, (x + d) % 4) for d in (1, 2, 3)]
    loads = [
        pltpu.make_async_copy(wq_in.at[:, pl.ds(D, 512)], wq.at[:, pl.ds(D, 512)], load_sem.at[0]),
        pltpu.make_async_copy(wq_in.at[:, pl.ds(0, D)], wq.at[:, pl.ds(0, D)], load_sem.at[1]),
        pltpu.make_async_copy(wb_in, wb, load_sem.at[2]),
    ]
    pairs = ((hot_a_in, hot_a), (dy_a_in, dy_a), (hot_b_in, hot_b), (dy_b_in, dy_b))
    loads += [
        pltpu.make_async_copy(src, dst, load_sem.at[3 + i]) for i, (src, dst) in enumerate(pairs)
    ]
    for load in loads:
        load.start()
    greet(cross(*at) + peers)
    moves = Moves(send, recv, local)
    loads[2].wait()
    small = wb[:, D:]
    gains, _ = read_gains(small)
    xf = tokens[...].astype(F32)
    inverse = lax.rsqrt(jnp.mean(xf * xf, axis=1, keepdims=True) + norm_eps)
    normed[...] = (xf * inverse * gains[0:1, :]).astype(BF16)
    loads[0].wait()
    for j in range(2):
        part = mul(normed[...], wq[:, D + j * 256 : D + (j + 1) * 256])
        if j == 0:
            for h in range(2):
                lanes = slice(h * HEAD_DIM, (h + 1) * HEAD_DIM)
                own_kv[:, lanes] = turn(part[:, lanes], cosd[...], sind[...]).astype(BF16)
        else:
            own_kv[:, 256:512] = part.astype(BF16)
    rows = pl.ds(pl.multiple_of(x * COUNT, COUNT), COUNT)
    pushes = [moves.push(own_kv, kv.at[rows], peer) for peer in peers]
    kv[rows, :] = own_kv[...]
    for load in loads[3:]:
        load.wait()
    to_slots(hot_a, dy_a, sa1, 0)
    to_slots(hot_b, dy_b, sb1, 0)
    to_slots(hot_a, dy_a, sa2, 1)
    to_slots(hot_b, dy_b, sb2, 1)
    dy_waits = deliver(moves, at, sa1, sb1, dy1, HALF)
    dy_waits += deliver(moves, at, sa2, sb2, dy2, HALF)
    fill_bias(lengths, bias, x)
    loads[1].wait()

    def query_tile(j, carry):
        lanes = pl.ds(pl.multiple_of(j * 256, 256), 256)
        part = mul(normed[...], wq[:, lanes])
        q[:, lanes] = jnp.concatenate(
            [turn(part[:, h * 128 : (h + 1) * 128], cosd[...], sind[...]) for h in range(2)],
            axis=1,
        ).astype(BF16)
        return carry

    lax.fori_loop(0, D // 256, query_tile, 0)

    logits = jnp.where(named[...] > 0, mul(tokens[...], small), -jnp.inf)
    weight = jnp.exp(logits - jnp.max(logits, axis=1, keepdims=True))
    gates = weight / jnp.sum(weight, axis=1, keepdims=True)
    gates_out[...] = gates
    for push in pushes:
        push.wait_recv()
    stays = [moves.keep(q, q_out), moves.keep(normed, normed_out), moves.keep(kv, kv_out)]
    for g in range(HEADS_KV):
        vt[g] = kv[:, 256 + g * 128 : 384 + g * 128].T
    for g in range(HEADS_KV):

        def head(i, carry, g=g):
            h = g * REPEAT + i
            lanes = pl.ds(pl.multiple_of(h * HEAD_DIM, HEAD_DIM), HEAD_DIM)
            s = mul(kv[:, g * 128 : (g + 1) * 128], q[:, lanes], NT) * SCALE + bias[...]
            top = jnp.max(s, axis=0, keepdims=True)
            p = jnp.exp(s - top)
            total = jnp.sum(p, axis=0, keepdims=True)
            tops[pl.ds(h, 1), :] = top
            totals[pl.ds(h, 1), :] = total
            low = (p * (1.0 / total)).astype(BF16)
            attended[:, lanes] = mul(vt[g], low).T.astype(BF16)
            return carry

        lax.fori_loop(0, REPEAT, head, 0)

    def out_tile(j, carry):
        lanes = pl.ds(pl.multiple_of(j * 256, 256), 256)
        middle[:, lanes] = tokens[:, lanes].astype(F32) + mul(attended[...], wb[lanes, 0:D], NT)
        return carry

    lax.fori_loop(0, D // 256, out_tile, 0)
    m = middle[...]
    inverse = lax.rsqrt(jnp.mean(m * m, axis=1, keepdims=True) + norm_eps)
    stays += [moves.keep(attended, attended_out), moves.keep(middle, middle_out)]
    high, mid, low = (third.astype(F32) for third in thirds(gates))
    held = high + pltpu.roll(mid, EXPERTS, 1) + pltpu.roll(low, 2 * EXPERTS, 1)
    nf[:, 0:LANES] = held.astype(BF16)
    nf[:, LANES:] = (m * inverse * gains[1:2, :]).astype(BF16)
    half_a, half_b = nf.at[:, pl.ds(0, WIDE_A)], nf.at[:, pl.ds(WIDE_A, WIDE_B)]
    last = [moves.push(half_a, nf_a.at[y], peer) for peer in line_y]
    last += [moves.push(half_b, nf_b.at[z], peer) for peer in line_z]
    stays += [moves.keep(half_a, nf_a.at[y]), moves.keep(half_b, nf_b.at[z])]
    for push in last:
        push.wait_recv()
    for stay in stays:
        stay.wait()
    for wait in dy_waits:
        wait()
    moves.drain()


def run_forward(*operands):
    anywhere = pl.BlockSpec(memory_space=pl.ANY)
    inside = pl.BlockSpec(memory_space=pltpu.VMEM)
    vmem, dma = pltpu.VMEM, pltpu.SemaphoreType.DMA
    shape = jax.ShapeDtypeStruct
    return pl.pallas_call(
        forward_kernel,
        name="forward",
        out_shape=(
            shape((COUNT, D), BF16),
            shape((GROUP_ROWS, 512), BF16),
            shape((COUNT, D), BF16),
            shape((COUNT, D), F32),
            shape((COUNT, D), BF16),
            shape((16, COUNT), F32),
            shape((16, COUNT), F32),
            shape((COUNT, 128), F32),
            shape((4, COUNT, WIDE_A), BF16),
            shape((4, COUNT, WIDE_B), BF16),
            *(shape(piece, BF16) for piece in pieces(4, 8, width=D)),
        ),
        in_specs=[pl.BlockSpec(memory_space=pltpu.SMEM), inside, anywhere, anywhere]
        + [inside] * 3
        + [anywhere] * 4,
        out_specs=(anywhere,) * 5 + (inside,) * 3 + (anywhere,) * 4,
        scratch_shapes=[
            vmem((D, WA), BF16),
            vmem((D, WB), BF16),
            vmem((GROUP_ROWS, 512), BF16),
            vmem((COUNT, 512), BF16),
            vmem((GROUP_ROWS, COUNT), F32),
            vmem((HEADS_KV, HEAD_DIM, GROUP_ROWS), BF16),
            vmem((COUNT, D), BF16),
            vmem((COUNT, D), BF16),
            vmem((COUNT, D), F32),
            vmem((COUNT, D), BF16),
            vmem((COUNT, WIDE), BF16),
            vmem((4, COUNT, SLOTS), BF16),
            vmem((4, COUNT, SLOTS), BF16),
            vmem((4, COUNT, HALF), BF16),
            vmem((4, COUNT, HALF), BF16),
            *(vmem(piece, BF16) for piece in pieces(8, 4, width=HALF) * 2),
            dma((3 + 28 + 6,)),
            dma((3 + 28 + 6,)),
            dma((4 + 7,)),
            dma((7,)),
        ],
        compiler_params=pltpu.CompilerParams(
            collective_id=3, has_side_effects=True, vmem_limit_bytes=48 * 1024 * 1024
        ),
        cost_estimate=pl.CostEstimate(
            flops=6_000_000_000, bytes_accessed=30_000_000, transcendentals=3_200_000
        ),
    )(*operands)


def norm_grad(values, gain, grad):
    inverse = lax.rsqrt(jnp.mean(values * values, axis=1, keepdims=True) + norm_eps)
    unit = values * inverse
    scaled = grad * gain
    drop = jnp.mean(scaled * unit, axis=1, keepdims=True)
    return inverse * (scaled - unit * drop), jnp.sum(grad * unit, axis=0, keepdims=True)


def backward_kernel(
    lengths, tokens_in, cotangent_in, gates, queries_in, kv_src, attended_in, middle_in, normed_in,
    tops, totals, cosd, sind, wq_in, wb_in, hot_a_in, hot_b_in,
    back_a1_in, back_a2_in, back_b1_in, back_b2_in, out1, out2, up_in, down_in,
    output, grad_tokens, grad_qkv_out, grad_out_out, grad_small, up_far, down_far,
    far_a1, far_a2, far_b1, far_b2,
    tokens, cotangent, queries, kv_in, attended, middle, normed,
    wq, wb, hot_a, hot_b, back_a1, back_a2, back_b1, back_b2,
    part_a, part_b, land_a, land_b, late_a, late_b,
    bias, kt, gn, gmid, gb, gatt, gp, dk, dv, leave, land, grad_qkv,
    send, recv, local, load_sem,
):
    at = place()
    y, z, c, x = at
    line_y, line_z = lines(y, z, c, x)
    peers = [device(y, z, c, (x + d) % 4) for d in (1, 2, 3)]
    pairs = (
        (back_a1_in, back_a1), (back_a2_in, back_a2), (hot_a_in, hot_a),
        (back_b1_in, back_b1), (back_b2_in, back_b2), (hot_b_in, hot_b),
        (kv_src, kv_in), (wb_in, wb), (middle_in, middle), (cotangent_in, cotangent),
        (queries_in, queries), (attended_in, attended), (tokens_in, tokens),
        (normed_in, normed), (wq_in, wq),
    )
    loads = [
        pltpu.make_async_copy(src, dst, load_sem.at[i]) for i, (src, dst) in enumerate(pairs)
    ]
    for load in loads:
        load.start()
    greet(cross(*at) + peers)
    link = Moves(send, recv, local)
    for load in loads[:6]:
        load.wait()
    part_waits = add_up(hot_a, back_a1, back_a2, part_a, land_a, y, line_y, link)
    part_waits += add_up(hot_b, back_b1, back_b2, part_b, land_b, z, line_z, link)
    part_drain = list(link.made)
    facing = (x + 2) % 4
    pushes = []
    for half, peer in ((0, peers[2]), (1, peers[0])):
        up_rows = pl.ds(pl.multiple_of(facing * UP_PART + half * UP_HALF, UP_HALF), UP_HALF)
        pushes.append(link.push(up_in.at[up_rows], up_far.at[half], peer))
        lanes = pl.ds(pl.multiple_of(facing * DOWN_PART, 128), DOWN_PART)
        down_rows = pl.ds(half * DOWN_HALF, DOWN_HALF)
        pushes.append(link.push(down_in.at[down_rows, lanes], down_far.at[half], peer))
    fill_bias(lengths, bias, x)
    for load in loads[6:]:
        load.wait()
    for g in range(HEADS_KV):
        kt[g] = kv_in[:, g * 128 : (g + 1) * 128].T
    for wait in part_waits:
        wait()
    out_waits = give_back_a(link, at, out1, far_a1, HALF)
    out_waits += give_back_b(link, at, out1, far_b1, HALF)
    out_waits += give_back_a(link, at, out2, far_a2, HALF)
    out_waits += give_back_b(link, at, out2, far_b2, HALF)
    total = land_a[0].astype(F32)
    for s in range(1, 4):
        total = total + land_a[s].astype(F32)
    slopes = total[:, 0:LANES]
    gn[:, 0 : WIDE_A - LANES] = total[:, LANES:]
    total = land_b[0].astype(F32)
    for s in range(1, 4):
        total = total + land_b[s].astype(F32)
    gn[:, WIDE_A - LANES :] = total
    gains, select = read_gains(wb[:, D:])
    moved, ffn_gain = norm_grad(middle[...], gains[1:2, :], gn[...])
    gm = cotangent[...].astype(F32) + moved
    gmid[...] = gm
    gb[...] = gm.astype(BF16)

    def att_tile(j, carry):
        lanes = pl.ds(pl.multiple_of(j * 256, 256), 256)
        gatt[:, lanes] = mul(gb[...], wb[:, lanes]).astype(BF16)
        return carry

    lax.fori_loop(0, D // 256, att_tile, 0)
    kv_pushes = []
    for g in range(HEADS_KV):
        dk[...] = jnp.zeros_like(dk)
        dv[...] = jnp.zeros_like(dv)

        def head(i, carry, g=g):
            h = g * REPEAT + i
            lanes = pl.ds(pl.multiple_of(h * HEAD_DIM, HEAD_DIM), HEAD_DIM)
            s = mul(kv_in[:, g * 128 : (g + 1) * 128], queries[:, lanes], NT) * SCALE + bias[...]
            p = jnp.exp(s - tops[pl.ds(h, 1), :]) * (1.0 / totals[pl.ds(h, 1), :])
            dv[...] += mul(p.astype(BF16), gatt[:, lanes])
            t = p * mul(kv_in[:, 256 + g * 128 : 384 + g * 128], gatt[:, lanes], NT)
            ds = (t - p * jnp.sum(t, axis=0, keepdims=True)).astype(BF16)
            dk[...] += mul(ds, queries[:, lanes])
            dq = mul(kt[g], ds).T * SCALE
            gp[:, lanes] = turn(dq, cosd[...], -sind[...]).astype(BF16)
            return carry

        lax.fori_loop(0, REPEAT, head, 0)
        leave[g, :, 0:128] = (dk[...] * SCALE).astype(BF16)
        leave[g, :, 128:256] = dv[...].astype(BF16)
        for d in (1, 2, 3):
            away = pl.ds(pl.multiple_of(((x + d) % 4) * COUNT, COUNT), COUNT)
            kv_pushes.append(link.push(leave.at[g, away], land.at[g, d - 1], peers[d - 1]))

    def out_tile(j, carry):
        lanes = pl.ds(pl.multiple_of(j * 256, 256), 256)
        grad_qkv[lanes, 0:D] = mul(gb[:, lanes], attended[...], TN).astype(BF16)
        return carry

    lax.fori_loop(0, D // 256, out_tile, 0)

    out_kept = link.keep(grad_qkv.at[:, pl.ds(0, D)], grad_out_out)

    gate_grad = slopes + pltpu.roll(slopes, 128 - EXPERTS, 1) + pltpu.roll(
        slopes, 128 - 2 * EXPERTS, 1
    )
    weighted = gates[...] * gate_grad
    logit_grad = weighted - gates[...] * jnp.sum(weighted, axis=1, keepdims=True)
    parts = thirds(logit_grad)
    router_grad = sum(mul(tokens[...], part, TN) for part in parts)
    small = wb[:, D:]

    for wait in out_waits:
        wait()
    pairs = ((far_a1, back_a1), (far_a2, back_a2), (far_b1, back_b1), (far_b2, back_b2))
    again = [
        link.keep(src, dst.at[:, :, :, pl.ds(0, HALF)] if dst.shape[3] > HALF else dst)
        for src, dst in pairs
    ]
    for copy in again:
        copy.wait()
    for copy in part_drain:
        copy.wait_send()
    width = pl.ds(0, HALF)
    late = add_up(
        hot_a, back_a1, back_a2, part_a, late_a, y, line_y, link
    ) + add_up(
        hot_b, back_b1.at[:, :, :, width], back_b2.at[:, :, :, width],
        part_b.at[:, :, width], late_b, z, line_z, link,
    )
    for push in kv_pushes:
        push.wait_recv()
    mine = pl.ds(pl.multiple_of(x * COUNT, COUNT), COUNT)
    for g in range(HEADS_KV):
        total = leave[g, mine, :].astype(F32)
        for d in range(3):
            total = total + land[g, d].astype(F32)
        gp[:, D + g * 128 : D + (g + 1) * 128] = turn(
            total[:, 0:128], cosd[...], -sind[...]
        ).astype(BF16)
        gp[:, D + 256 + g * 128 : D + 384 + g * 128] = total[:, 128:256].astype(BF16)
    out_kept.wait()

    def qkv_tile(j, carry):
        lanes = pl.ds(pl.multiple_of(j * 256, 256), 256)
        grad_qkv[lanes, :] = mul(normed[:, lanes], gp[...], TN).astype(BF16)
        gn[:, lanes] = mul(gp[...], wq[lanes, :], NT)
        return carry

    lax.fori_loop(0, D // 256, qkv_tile, 0)
    stays = [link.keep(grad_qkv, grad_qkv_out)]
    moved, attn_gain = norm_grad(tokens[...].astype(F32), gains[0:1, :], gn[...])
    from_router = sum(mul(part, small, NT) for part in parts)
    grad_tokens[...] = (gmid[...] + moved + from_router).astype(BF16)
    both = jnp.where(
        iota((8, D), 0) == 0, attn_gain, jnp.where(iota((8, D), 0) == 1, ffn_gain, 0.0)
    )
    gain_columns = sum(mul(part, select, TN) for part in thirds(both))
    grad_small[...] = (router_grad + gain_columns).astype(BF16)
    for wait in late:
        wait()
    for half, landed in enumerate((late_a, late_b)):
        lanes = slice(half * HALF, (half + 1) * HALF)
        total = middle[:, lanes]
        for s in range(4):
            total = total + landed[s].astype(F32)
        output[:, lanes] = total.astype(BF16)
    for push in pushes:
        push.wait_recv()
    for stay in stays:
        stay.wait()
    link.drain(skip=part_drain)


def run_backward(*operands):
    anywhere = pl.BlockSpec(memory_space=pl.ANY)
    inside = pl.BlockSpec(memory_space=pltpu.VMEM)
    vmem, dma = pltpu.VMEM, pltpu.SemaphoreType.DMA
    shape = jax.ShapeDtypeStruct
    return pl.pallas_call(
        backward_kernel,
        name="backward",
        out_shape=(
            shape((COUNT, D), BF16),
            shape((COUNT, D), BF16),
            shape((D, WA), BF16),
            shape((D, D), BF16),
            shape((D, SMALL), BF16),
            shape((2, UP_HALF, 2 * FF), BF16),
            shape((2, DOWN_HALF, DOWN_PART), BF16),
            *(shape(piece, BF16) for piece in pieces(8, 4, width=HALF) * 2),
        ),
        in_specs=[pl.BlockSpec(memory_space=pltpu.SMEM)]
        + [anywhere] * 2
        + [inside]
        + [anywhere] * 5
        + [inside] * 4
        + [anywhere] * 12,
        out_specs=(inside, inside, anywhere, anywhere, inside) + (anywhere,) * 6,
        scratch_shapes=[
            vmem((COUNT, D), BF16),
            vmem((COUNT, D), BF16),
            vmem((COUNT, D), BF16),
            vmem((GROUP_ROWS, 512), BF16),
            vmem((COUNT, D), BF16),
            vmem((COUNT, D), F32),
            vmem((COUNT, D), BF16),
            vmem((D, WA), BF16),
            vmem((D, WB), BF16),
            vmem((4, COUNT, SLOTS), BF16),
            vmem((4, COUNT, SLOTS), BF16),
            *(vmem(piece, BF16) for piece in pieces(8, 4, width=WIDE_A)),
            *(vmem(piece, BF16) for piece in pieces(8, 4, width=WIDE_B)),
            vmem((3, COUNT, WIDE_A), BF16),
            vmem((3, COUNT, WIDE_B), BF16),
            vmem((4, COUNT, WIDE_A), BF16),
            vmem((4, COUNT, WIDE_B), BF16),
            vmem((4, COUNT, HALF), BF16),
            vmem((4, COUNT, HALF), BF16),
            vmem((GROUP_ROWS, COUNT), F32),
            vmem((HEADS_KV, HEAD_DIM, GROUP_ROWS), BF16),
            vmem((COUNT, D), F32),
            vmem((COUNT, D), F32),
            vmem((COUNT, D), BF16),
            vmem((COUNT, D), BF16),
            vmem((COUNT, WA), BF16),
            vmem((GROUP_ROWS, HEAD_DIM), F32),
            vmem((GROUP_ROWS, HEAD_DIM), F32),
            vmem((HEADS_KV, GROUP_ROWS, 256), BF16),
            vmem((HEADS_KV, 3, COUNT, 256), BF16),
            vmem((D, WA), BF16),
            dma((6 + 4 + 28 + 6 + 6,)),
            dma((6 + 4 + 28 + 6 + 6,)),
            dma((4 + 4 + 2,)),
            dma((15,)),
        ],
        compiler_params=pltpu.CompilerParams(
            collective_id=4, has_side_effects=True, vmem_limit_bytes=60 * 1024 * 1024
        ),
        cost_estimate=pl.CostEstimate(
            flops=13_000_000_000, bytes_accessed=50_000_000, transcendentals=3_200_000
        ),
    )(*operands)


def rope_tables(position, half_dim):
    frequency = rope_base ** (-jnp.arange(half_dim, dtype=jnp.float32) / half_dim)
    angles = position.astype(jnp.float32)[:, None] * frequency[None, :]
    return jnp.cos(angles), jnp.sin(angles)


def seq_layout(seq_lens, row_ids):
    seq_ends = jnp.cumsum(seq_lens)
    segment = jnp.sum((row_ids[:, None] >= seq_ends[None, :]).astype(jnp.int32), axis=1)
    seq_start = jnp.sum(
        jnp.where(seq_ends[None, :] <= row_ids[:, None], seq_lens[None, :], 0), axis=1
    )
    return (segment, row_ids - seq_start)


def body(
    tokens, lengths, top_experts, w_qkv, w_out, gain_attn, gain_ffn, router, gate_up, down_proj, cotangent,
):
    pack = jnp.concatenate(
        [
            w_qkv,
            w_out.T,
            router,
            gain_attn[:, None],
            gain_ffn[:, None],
            jnp.zeros((PIECE, SMALL - EXPERTS - 2), BF16),
        ],
        axis=1,
    )
    pack = jnp.pad(pack, ((0, PADDED - PIECE), (0, 0)))

    row_ids = jnp.arange(COUNT, dtype=jnp.int32)
    own_ids = lax.axis_index("shard") * COUNT + row_ids
    _, own_position = seq_layout(lengths[0], own_ids)
    cosine, sine = rope_tables(own_position, HEAD_DIM // 2)
    cosd = jnp.concatenate([cosine, cosine], axis=1)
    sind = jnp.concatenate([-sine, sine], axis=1)

    full_a, full_b, named, hot_a, hot_b, dy_a, dy_b = gather_weights(
        pack, top_experts, cotangent
    )
    wq = full_a.reshape(D, WA)
    wb = full_b.reshape(D, WB)
    (
        queries, kv, attended, middle, normed, tops, totals, gates, nf_a, nf_b, dy1, dy2,
    ) = run_forward(
        lengths, tokens, wq, wb, named, cosd, sind, hot_a, hot_b, dy_a, dy_b
    )
    back_a1, back_a2, back_b1, back_b2, out1, out2, up_local, down_local = run_experts(
        hot_a, hot_b, nf_a, nf_b, dy1, dy2, gate_up, down_proj
    )
    output, grad_tokens, grad_qkv, grad_out, grad_small, up_far, down_far, *_ = run_backward(
        lengths, tokens, cotangent, gates, queries, kv, attended, middle, normed, tops, totals,
        cosd, sind, wq, wb, hot_a, hot_b, back_a1, back_a2, back_b1, back_b2, out1, out2,
        up_local, down_local,
    )
    sum_a, sum_b, up_sum, down_sum = scatter_sums(
        grad_qkv.reshape(4, 4, 2, BLOCK, WA),
        grad_out.reshape(4, 4, 2, BLOCK, D),
        grad_small.reshape(4, 4, 2, BLOCK, SMALL),
        up_local,
        down_local,
        up_far,
        down_far,
    )
    sum_b = sum_b[:PIECE]

    return (
        output,
        grad_tokens,
        sum_a[:PIECE],
        sum_b[:, :D].T,
        sum_b[:, D + EXPERTS],
        sum_b[:, D + EXPERTS + 1],
        sum_b[:, D : D + EXPERTS],
        up_sum[None],
        down_sum[None],
    )


def solution(mesh):
    return jax.shard_map(
        body,
        mesh=mesh,
        in_specs=(
            P(("expert", "shard"), None),
            P("expert", None),
            P(("expert", "shard"), None),
            P(("expert", "shard"), None),
            P(None, ("expert", "shard")),
            P(("expert", "shard")),
            P(("expert", "shard")),
            P(("expert", "shard"), None),
            P("expert", None, None),
            P("expert", None, None),
            P(("expert", "shard"), None),
        ),
        out_specs=(
            P(("expert", "shard"), None),
            P(("expert", "shard"), None),
            P(("expert", "shard"), None),
            P(None, ("expert", "shard")),
            P(("expert", "shard")),
            P(("expert", "shard")),
            P(("expert", "shard"), None),
            P("expert", "shard", None),
            P("expert", None, "shard"),
        ),
        check_vma=False,
    )
```

```python
import functools

import jax
import jax.numpy as jnp
from jax import lax
from jax.experimental import pallas as pl
from jax.experimental.pallas import tpu as pltpu
from jax.sharding import PartitionSpec as P

D = 1536
HEADS_Q = 12
HEADS_KV = 2
HEAD_DIM = 128
FF = 768
TOP = 4
EXPERTS = 32
CAP = 48
WIDTH_Q = HEADS_Q * HEAD_DIM
WIDTH_KV = HEADS_KV * HEAD_DIM
REPEAT = HEADS_Q // HEADS_KV

norm_eps = 1e-06
rope_base = 1000000.0
precise = lax.Precision.HIGHEST
MESH = pl.DeviceIdType.MESH
F32 = jnp.float32
BF16 = jnp.bfloat16

PIECE = 12
PADDED = 16
BLOCK = 48
WA = 2048
WB = 1664
SMALL = WB - D


def place():
    e = lax.axis_index("expert")
    return e // 8, (e // 2) % 4, e % 2, lax.axis_index("shard")


def device(y, z, c, x):
    return ((y * 4 + z) * 2 + c, x)


def greet(devices):
    barrier = pltpu.get_barrier_semaphore()
    for d in devices:
        pl.semaphore_signal(barrier, inc=1, device_id=d, device_id_type=MESH)
    pl.semaphore_wait(barrier, len(devices))


class Links:
    def __init__(self, send, recv):
        self.send, self.recv, self.made = send, recv, []

    def push(self, src, dst, where):
        i = len(self.made)
        copy = pltpu.make_async_remote_copy(
            src_ref=src,
            dst_ref=dst,
            send_sem=self.send.at[i],
            recv_sem=self.recv.at[i],
            device_id=where,
            device_id_type=MESH,
        )
        copy.start()
        self.made.append(copy)
        return copy

    def drain(self):
        for copy in self.made:
            copy.wait_send()


def neighbours(y, z, c, x):
    other = 1 - c
    return dict(
        x=[device(y, z, c, (x + d) % 4) for d in (1, 2, 3)],
        y=(device((y + 1) % 4, z, c, x), device((y + 3) % 4, z, c, x)),
        z=(device(y, (z + 1) % 4, c, x), device(y, (z + 3) % 4, c, x)),
        core=device(y, z, other, x),
    )


def everyone_near(near):
    return list(near["x"]) + list(near["y"]) + list(near["z"]) + [near["core"]]


def pick_rows(rows, columns, row_block, column_block):
    r = lax.broadcasted_iota(jnp.int32, (rows, columns), 0)
    q = lax.broadcasted_iota(jnp.int32, (rows, columns), 1)
    same = (r // row_block == q // column_block) & (r % row_block == q % column_block)
    return jnp.where(same, 1.0, 0.0).astype(BF16)


def faces(y, z, c, x):
    along_z, along_y = [], []
    for d in range(4):
        for k in range(2):
            core = c if k == 0 else 1 - c
            along_z.append((device(y, (z + d) % 4, core, x), (z + d) % 4, core))
            along_y.append((device((y + d) % 4, z, core, x), (y + d) % 4, core))
    return along_z, along_y


def cross(y, z, c, x):
    along_z, along_y = faces(y, z, c, x)
    return [f[0] for f in along_z[1:] + along_y[2:]]


def lines(y, z, c, x):
    return (
        [device((y + d) % 4, z, c, x) for d in (1, 2, 3)],
        [device(y, (z + d) % 4, c, x) for d in (1, 2, 3)],
    )


def route(top_experts, named, own_slot):
    lanes = iota((COUNT, 128), 1)
    for k in range(TOP):
        hit = jnp.where(top_experts[:, k : k + 1] == lanes, 1.0, 0.0)
        named[...] = hit if k == 0 else named[...] + hit
    earlier = hot(iota((COUNT, COUNT), 1) < iota((COUNT, COUNT), 0))
    slot_of = mul(earlier, named[...].astype(BF16))
    own_slot[...] = jnp.where(named[...] > 0, slot_of, -1.0).astype(BF16)


def slot_hits(slot_of, hits, experts):
    p = iota((1, SLOTS), 1)
    q = p % PIECE_SLOTS
    wanted = ((p // PIECE_SLOTS) * PART + q % PART).astype(F32)
    local = q // PART
    expand = hot(iota((128, SLOTS), 0) == experts(local))

    def step(s, carry):
        hits[s] = hot(mul(slot_of[s], expand) == wanted)
        return carry

    lax.fori_loop(0, 4, step, 0)


def gather_kernel(
    pack, top_experts, cotangent, full_a, full_b, named, hot_a, hot_b, dy_a, dy_b,
    xbuf, own_a, own_b, own_slot, slot_y, slot_z, send, recv, local,
):
    y, z, c, x = place()
    near = neighbours(y, z, c, x)
    line_y, line_z = lines(y, z, c, x)
    greet(everyone_near(near) + [line_y[1], line_z[1]])
    link = Links(send, recv)
    first = [link.push(pack, xbuf.at[x], near["x"][d]) for d in range(3)]
    xbuf[pl.ds(x, 1)] = pack[...][None]
    half_a, half_b = cotangent.at[:, pl.ds(0, HALF)], cotangent.at[:, pl.ds(HALF, HALF)]
    kept = [
        pltpu.make_async_copy(half_a, dy_a.at[y], local.at[2]),
        pltpu.make_async_copy(half_b, dy_b.at[z], local.at[3]),
    ]
    for copy in kept:
        copy.start()
    dys = [
        around(link, half_a, dy_a, y, *near["y"]),
        around(link, half_b, dy_b, z, *near["z"]),
    ]
    for copy in first:
        copy.wait_recv()
    select = pick_rows(BLOCK, 4 * PADDED, PIECE, PADDED)
    pieces = xbuf[...].reshape(4 * PADDED, WA + WB)
    own_a[...] = jnp.dot(select, pieces[:, :WA], preferred_element_type=F32).astype(BF16)
    own_b[...] = jnp.dot(select, pieces[:, WA:], preferred_element_type=F32).astype(BF16)

    def at_a(far, close, columns=None):
        view = full_a.at[far, close, c]
        return view if columns is None else view.at[:, columns]

    def at_b(far, close, columns=None):
        view = full_b.at[close, far, c]
        return view if columns is None else view.at[:, columns]

    def line_a(far, part=slice(None)):
        return full_a.at[far, part, c]

    def line_b(far, part=slice(None)):
        return full_b.at[part, far, c]

    jobs = [
        dict(own=own_a, at=at_a, line=line_a, close="z", far="y", p=z, q=y, half=1024, i=0),
        dict(own=own_b, at=at_b, line=line_b, close="y", far="z", p=y, q=z, half=896, i=1),
    ]
    for j in jobs:
        here = j["at"](j["q"], j["p"])
        plus, minus = near[j["close"]]
        j["up"] = link.push(j["own"], here, plus)
        j["down"] = link.push(j["own"], here, minus)
        j["core"] = [link.push(j["own"], here, near["core"])]
        j["local"] = pltpu.make_async_copy(j["own"], here, local.at[j["i"]])
        j["local"].start()
    route(top_experts, named, own_slot)
    slot_y[pl.ds(y, 1)] = own_slot[...][None]
    slot_z[pl.ds(z, 1)] = own_slot[...][None]
    slots = [link.push(own_slot, slot_y.at[y], peer) for peer in line_y]
    slots += [link.push(own_slot, slot_z.at[z], peer) for peer in line_z]
    for j in jobs:
        plus, minus = near[j["close"]]
        left, right = (j["p"] + 3) % 4, (j["p"] + 1) % 4
        j["up"].wait_recv()
        part = j["at"](j["q"], left, pl.ds(0, j["half"]))
        j["up2"] = link.push(part, part, plus)
        j["down"].wait_recv()
        part = j["at"](j["q"], right, pl.ds(j["half"], j["own"].shape[1] - j["half"]))
        j["down2"] = link.push(part, part, minus)
        for side in (left, right):
            block = j["at"](j["q"], side)
            j["core"].append(link.push(block, block, near["core"]))
    for j in jobs:
        j["up2"].wait_recv()
        j["down2"].wait_recv()
        block = j["at"](j["q"], (j["p"] + 2) % 4)
        j["local"].wait()
        plus, minus = near[j["far"]]
        line = j["line"](j["q"])
        j["up"] = link.push(line, line, plus)
        j["down"] = link.push(line, line, minus)
        j["core"].append(link.push(block, block, near["core"]))
    dys = dys[0]() + dys[1]()
    for copy in slots:
        copy.wait_recv()
    slot_hits(slot_y, hot_a, lambda e: y * 8 + e)
    slot_hits(slot_z, hot_b, lambda e: (e // 2) * 8 + z * 2 + e % 2)
    for j in jobs:
        plus, minus = near[j["far"]]
        left, right = (j["q"] + 3) % 4, (j["q"] + 1) % 4
        j["up"].wait_recv()
        part = j["line"](left, pl.ds(0, 2))
        j["up2"] = link.push(part, part, plus)
        j["down"].wait_recv()
        part = j["line"](right, pl.ds(2, 2))
        j["down2"] = link.push(part, part, minus)
        for side in (left, right):
            block = j["line"](side)
            j["core"].append(link.push(block, block, near["core"]))
    for j in jobs:
        opposite = (j["q"] + 2) % 4
        j["up2"].wait_recv()
        part = j["line"](opposite, pl.ds(0, 2))
        j["core"].append(link.push(part, part, near["core"]))
        j["down2"].wait_recv()
        part = j["line"](opposite, pl.ds(2, 2))
        j["core"].append(link.push(part, part, near["core"]))
    for j in jobs:
        for copy in j["core"]:
            copy.wait_recv()
    for wait in dys:
        wait()
    for copy in kept:
        copy.wait()
    link.drain()


def gather_weights(pack, top_experts, cotangent):
    inside = pl.BlockSpec(memory_space=pltpu.VMEM)
    anywhere = pl.BlockSpec(memory_space=pltpu.HBM)
    copies = 3 + 2 * 16 + 6 + 8
    return pl.pallas_call(
        gather_kernel,
        name="gather_weights",
        out_shape=(
            jax.ShapeDtypeStruct((4, 4, 2, BLOCK, WA), BF16),
            jax.ShapeDtypeStruct((4, 4, 2, BLOCK, WB), BF16),
            jax.ShapeDtypeStruct((COUNT, 128), F32),
            jax.ShapeDtypeStruct((4, COUNT, SLOTS), BF16),
            jax.ShapeDtypeStruct((4, COUNT, SLOTS), BF16),
            jax.ShapeDtypeStruct((4, COUNT, HALF), BF16),
            jax.ShapeDtypeStruct((4, COUNT, HALF), BF16),
        ),
        in_specs=[inside, inside, inside],
        out_specs=(anywhere, anywhere, inside, inside, inside, anywhere, anywhere),
        scratch_shapes=[
            pltpu.VMEM((4, PADDED, WA + WB), BF16),
            pltpu.VMEM((BLOCK, WA), BF16),
            pltpu.VMEM((BLOCK, WB), BF16),
            pltpu.VMEM((COUNT, 128), BF16),
            pltpu.VMEM((4, COUNT, 128), BF16),
            pltpu.VMEM((4, COUNT, 128), BF16),
            pltpu.SemaphoreType.DMA((copies,)),
            pltpu.SemaphoreType.DMA((copies,)),
            pltpu.SemaphoreType.DMA((4,)),
        ],
        compiler_params=pltpu.CompilerParams(
            collective_id=0, has_side_effects=True, vmem_limit_bytes=60 * 1024 * 1024
        ),
        cost_estimate=pl.CostEstimate(flops=0, bytes_accessed=24_000_000, transcendentals=0),
    )(pack, top_experts, cotangent)


def add_blocks(dst, far, start, count, sources):
    def step(i, carry):
        total = dst[far, start + i].astype(F32)
        for source in sources:
            total = total + source(i).astype(F32)
        dst[far, start + i] = total.astype(BF16)
        return carry

    lax.fori_loop(0, count, step, 0)


def scatter_kernel(
    ga, gb, gs, up_in, down_in, up_far, down_far, late_a, late_b, came_a, came_b, middle,
    out_a, out_b, up_out, down_out, output,
    core_a, core_b, mine_a, mine_b, one_a, one_b, two_a, two_b,
    half_a0, half_a1, half_b0, half_b1, last_a, last_b, xout, xin,
    ups, downs, up_got, down_got, up_land, down_land, mid, land_a, land_b,
    send, recv, local,
):
    y, z, c, x = place()
    near = neighbours(y, z, c, x)
    line_y, line_z = lines(y, z, c, x)
    greet(everyone_near(near) + [line_y[1], line_z[1]])
    link = Links(send, recv)
    other = 1 - c
    jobs = [
        dict(src=[(lambda f, s: ga.at[f, :, s], 0, WA)], core=core_a, mine=mine_a, one=one_a, two=two_a,
             halves=(half_a0, half_a1), last=last_a, far="y", close="z", q=y, p=z,
             width=WA, half=1024, lane=0, i=0),
        dict(src=[(lambda f, s: gb.at[:, f, s], 0, D), (lambda f, s: gs.at[:, f, s], D, SMALL)],
             core=core_b, mine=mine_b, one=one_b, two=two_b,
             halves=(half_b0, half_b1), last=last_b, far="z", close="y", q=z, p=y,
             width=WB, half=896, lane=WA, i=1),
    ]
    slots = 0
    for step in (2, 3, 1, 0):
        for j in jobs:
            f = (j["q"] + step) % 4
            j[step] = []
            for source, lane, width in j["src"]:
                lanes = pl.ds(lane, width)
                pushed = link.push(
                    source(f, other), j["core"].at[f, :, :, lanes], near["core"]
                )
                kept = pltpu.make_async_copy(
                    source(f, c), j["mine"].at[f, :, :, lanes], local.at[slots]
                )
                slots += 1
                kept.start()
                j[step].append((pushed, kept))

    late = []
    first, second = pl.ds(0, COUNT // 2), pl.ds(COUNT // 2, COUNT // 2)
    for src, dst, me, line in ((late_a, land_a, y, line_y), (late_b, land_b, z, line_z)):
        for d in (1, 2, 3):
            late.append(link.push(src.at[(me + d) % 4], dst.at[me, second], line[d - 1]))
    fetches = []
    for i, d in enumerate((3, 1, 0)):
        part = (x + d) % 4
        up_rows = pl.ds(pl.multiple_of(part * UP_PART, UP_PART), UP_PART)
        lanes = pl.ds(pl.multiple_of(part * DOWN_PART, 128), DOWN_PART)
        fetches.append((up_in.at[up_rows], ups.at[i]))
        fetches.append((down_in.at[:, lanes], downs.at[i]))
    fetches += [
        (up_far, up_got),
        (down_far, down_got),
        (middle, mid),
        (came_a, land_a.at[:, first]),
        (came_b, land_b.at[:, first]),
        (late_a.at[y], land_a.at[y, second]),
        (late_b.at[z], land_b.at[z, second]),
    ]
    fetches = [
        pltpu.make_async_copy(src, dst, local.at[slots + i]) for i, (src, dst) in enumerate(fetches)
    ]
    for fetch in fetches:
        fetch.start()
    for fetch in fetches:
        fetch.wait()
    sides = []
    for i, peer in enumerate((near["x"][2], near["x"][0])):
        up_rows = slice(i * UP_HALF, (i + 1) * UP_HALF)
        down_rows = slice(i * DOWN_HALF, (i + 1) * DOWN_HALF)
        ups[i, up_rows, :] = (ups[i, up_rows, :].astype(F32) + up_got[i].astype(F32)).astype(BF16)
        downs[i, down_rows, :] = (
            downs[i, down_rows, :].astype(F32) + down_got[i].astype(F32)
        ).astype(BF16)
        sides.append(link.push(ups.at[i], up_land.at[i], peer))
        sides.append(link.push(downs.at[i], down_land.at[i], peer))

    def ready(j, step):
        for pushed, kept in j[step]:
            pushed.wait_recv()
            kept.wait()

    for j in jobs:
        f = (j["q"] + 2) % 4
        ready(j, 2)
        mine = j["mine"]
        add_blocks(j["core"], f, 0, 4, [lambda i, f=f, m=mine: m[f, i]])
        plus, minus = near[j["far"]]
        j["down"] = link.push(j["core"].at[f, pl.ds(0, 2)], j["one"].at[0], minus)
        j["up"] = link.push(j["core"].at[f, pl.ds(2, 2)], j["one"].at[1], plus)
    for j in jobs:
        plus, minus = near[j["far"]]
        mine, one = j["mine"], j["one"]
        f = (j["q"] + 3) % 4
        ready(j, 3)
        add_blocks(j["core"], f, 2, 2, [lambda i, f=f, m=mine: m[f, i + 2]])
        j["down"].wait_recv()
        add_blocks(
            j["core"], f, 0, 2, [lambda i, f=f, m=mine: m[f, i], lambda i, o=one: o[0, i]]
        )
        j["down2"] = link.push(j["core"].at[f], j["two"].at[0], minus)
        f = (j["q"] + 1) % 4
        ready(j, 1)
        add_blocks(j["core"], f, 0, 2, [lambda i, f=f, m=mine: m[f, i]])
        j["up"].wait_recv()
        add_blocks(
            j["core"], f, 2, 2, [lambda i, f=f, m=mine: m[f, i + 2], lambda i, o=one: o[1, i]]
        )
        j["up2"] = link.push(j["core"].at[f], j["two"].at[1], plus)
    for j in jobs:
        mine, two = j["mine"], j["two"]
        f = j["q"]
        ready(j, 0)
        j["down2"].wait_recv()
        j["up2"].wait_recv()
        add_blocks(
            j["core"], f, 0, 4,
            [lambda i, f=f, m=mine: m[f, i], lambda i, t=two: t[0, i], lambda i, t=two: t[1, i]],
        )
        plus, minus = near[j["close"]]
        g = (j["p"] + 2) % 4
        h, w = j["half"], j["width"]
        j["down"] = link.push(j["core"].at[f, g, :, pl.ds(0, h)], j["halves"][0], minus)
        j["up"] = link.push(j["core"].at[f, g, :, pl.ds(h, w - h)], j["halves"][1], plus)
    for j in jobs:
        plus, minus = near[j["close"]]
        f, h, w, core = j["q"], j["half"], j["width"], j["core"]
        g = (j["p"] + 3) % 4
        j["down"].wait_recv()
        core[f, g, :, 0:h] = (
            core[f, g, :, 0:h].astype(F32) + j["halves"][0][...].astype(F32)
        ).astype(BF16)
        j["down2"] = link.push(core.at[f, g], j["last"].at[0], minus)
        g = (j["p"] + 1) % 4
        j["up"].wait_recv()
        core[f, g, :, h:w] = (
            core[f, g, :, h:w].astype(F32) + j["halves"][1][...].astype(F32)
        ).astype(BF16)
        j["up2"] = link.push(core.at[f, g], j["last"].at[1], plus)
    select = pick_rows(4 * PADDED, BLOCK, PADDED, PIECE)
    for j in jobs:
        f, g = j["q"], j["p"]
        j["down2"].wait_recv()
        j["up2"].wait_recv()
        total = (
            j["core"][f, g].astype(F32)
            + j["last"][0].astype(F32)
            + j["last"][1].astype(F32)
        ).astype(BF16)
        spread = jnp.dot(select, total, preferred_element_type=F32).astype(BF16)
        xout[:, :, j["lane"] : j["lane"] + j["width"]] = spread.reshape(4, PADDED, j["width"])
    final = [
        link.push(xout.at[(x + d) % 4], xin.at[d - 1], near["x"][d - 1]) for d in (1, 2, 3)
    ]
    for copy in final:
        copy.wait_recv()
    mine = xout[x].astype(F32)
    for d in range(3):
        mine = mine + xin[d].astype(F32)
    out_a[...] = mine[:, :WA]
    out_b[...] = mine[:, WA:]
    for push in sides:
        push.wait_recv()
    up_out[...] = ups[2].astype(F32) + up_land[0].astype(F32) + up_land[1].astype(F32)
    down_out[...] = downs[2].astype(F32) + down_land[0].astype(F32) + down_land[1].astype(F32)
    for push in late:
        push.wait_recv()
    for half, landed in enumerate((land_a, land_b)):
        lanes = slice(half * HALF, (half + 1) * HALF)
        total = mid[:, lanes]
        for s in range(4):
            total = total + landed[s].astype(F32)
        output[:, lanes] = total.astype(BF16)
    link.drain()


def scatter_sums(*operands):
    copies = 2 * (4 + 4 + 4) + 4 + 3 + 6 + 4
    vmem = pltpu.VMEM
    scratch = []
    for shape in ((4, 4), (4, 4), (2, 2), (2, 4)):
        scratch += [vmem((*shape, BLOCK, WA), BF16), vmem((*shape, BLOCK, WB), BF16)]
    scratch += [
        vmem((BLOCK, 1024), BF16),
        vmem((BLOCK, 1024), BF16),
        vmem((BLOCK, 896), BF16),
        vmem((BLOCK, WB - 896), BF16),
        vmem((2, BLOCK, WA), BF16),
        vmem((2, BLOCK, WB), BF16),
        vmem((4, PADDED, WA + WB), BF16),
        vmem((3, PADDED, WA + WB), BF16),
        vmem((3, UP_PART, 2 * FF), BF16),
        vmem((3, FF, DOWN_PART), BF16),
        vmem((2, UP_HALF, 2 * FF), BF16),
        vmem((2, DOWN_HALF, DOWN_PART), BF16),
        vmem((2, UP_PART, 2 * FF), BF16),
        vmem((2, FF, DOWN_PART), BF16),
        vmem((COUNT, D), F32),
        vmem((4, COUNT, HALF), BF16),
        vmem((4, COUNT, HALF), BF16),
        pltpu.SemaphoreType.DMA((copies,)),
        pltpu.SemaphoreType.DMA((copies,)),
        pltpu.SemaphoreType.DMA((12 + 13,)),
    ]
    return pl.pallas_call(
        scatter_kernel,
        name="scatter_sums",
        out_shape=(
            jax.ShapeDtypeStruct((PADDED, WA), F32),
            jax.ShapeDtypeStruct((PADDED, WB), F32),
            jax.ShapeDtypeStruct((UP_PART, 2 * FF), F32),
            jax.ShapeDtypeStruct((FF, DOWN_PART), F32),
            jax.ShapeDtypeStruct((COUNT, D), BF16),
        ),
        in_specs=[pl.BlockSpec(memory_space=pltpu.HBM)] * 12,
        out_specs=(pl.BlockSpec(memory_space=pltpu.VMEM),) * 5,
        scratch_shapes=scratch,
        compiler_params=pltpu.CompilerParams(
            collective_id=1, has_side_effects=True, vmem_limit_bytes=60 * 1024 * 1024
        ),
        cost_estimate=pl.CostEstimate(flops=0, bytes_accessed=24_000_000, transcendentals=0),
    )(*operands)


ROWS = EXPERTS * CAP
TILE = 256
PARTS = 3
PART = CAP // PARTS
SLOTS = 8 * CAP
PIECE_SLOTS = 8 * PART
PIECE_ROWS = EXPERTS * PART
HALF = D // 2
LANES = 128
WIDE = D + LANES
WIDE_A = HALF
WIDE_B = WIDE - HALF
SCALE = HEAD_DIM ** (-0.5)
GROUP_ROWS = 1024
COUNT = 256
NT = (((1,), (1,)), ((), ()))
TN = (((0,), (0,)), ((), ()))


def mul(a, b, dims=None):
    if dims is None:
        return jnp.dot(a, b, preferred_element_type=F32)
    return lax.dot_general(a, b, dims, preferred_element_type=F32)


def thirds(v):
    high = v.astype(BF16)
    rest = v - high.astype(F32)
    middle = rest.astype(BF16)
    return high, middle, (rest - middle.astype(F32)).astype(BF16)


def iota(shape, axis):
    return lax.broadcasted_iota(jnp.int32, shape, axis)


def hot(same):
    return jnp.where(same, 1.0, 0.0).astype(BF16)


class Moves(Links):
    def __init__(self, send, recv, local):
        super().__init__(send, recv)
        self.local, self.kept = local, 0

    def keep(self, src, dst):
        copy = pltpu.make_async_copy(src, dst, self.local.at[self.kept])
        self.kept += 1
        copy.start()
        return copy

    def send_or_keep(self, i, src, dst, where):
        if i == 0:
            return self.keep(src, dst).wait
        return self.push(src, dst, where).wait_recv


def to_slots(hits, rows, stage, piece):
    columns = slice(piece * PIECE_SLOTS, (piece + 1) * PIECE_SLOTS)
    for s in range(4):
        taken = mul(hits[s, :, columns], rows[s], TN).astype(BF16)
        stage[piece, :, s] = taken.reshape(8, PART, taken.shape[1])


def deliver(moves, at, stage_a, stage_b, rows, split, piece):
    y, z, c, x = at
    along_z, along_y = faces(y, z, c, x)
    width = rows.shape[4]
    waits = []
    for i, (where, zt, ct) in enumerate(along_z):
        dst = rows.at[piece, z, pl.ds(c * 4, 4), :, pl.ds(0, split)]
        waits.append(moves.send_or_keep(i, stage_a.at[piece, zt * 2 + ct], dst, where))
    for i, (where, yt, ct) in enumerate(along_y):
        dst = rows.at[piece, :, c * 4 + y, :, pl.ds(split, width - split)]
        waits.append(moves.send_or_keep(i, stage_b.at[piece, yt * 2 + ct], dst, where))
    return waits


def give_back(moves, at, rows, back_a, back_b, split, piece):
    y, z, c, x = at
    along_z, along_y = faces(y, z, c, x)
    width = rows.shape[4]
    waits = []
    for i, (where, zt, ct) in enumerate(along_z):
        src = rows.at[piece, zt, pl.ds(ct * 4, 4), :, pl.ds(0, split)]
        dst = back_a.at[piece, z * 2 + c, :, :, pl.ds(0, split)]
        waits.append(moves.send_or_keep(i, src, dst, where))
    for i, (where, yt, ct) in enumerate(along_y):
        src = rows.at[piece, :, ct * 4 + yt, :, pl.ds(split, width - split)]
        dst = back_b.at[piece, y * 2 + c, :, :, pl.ds(0, width - split)]
        waits.append(moves.send_or_keep(i, src, dst, where))
    return waits


def add_up(hits, back, s, width):
    rows = back[:, :, s, :, 0:width].reshape(SLOTS, width)
    return mul(hits[s], rows).astype(BF16)


def around(link, own, land, me, plus, minus):
    up = link.push(own, land.at[me], plus)
    down = link.push(own, land.at[me], minus)

    def forward():
        half = COUNT // 2
        up.wait_recv()
        block = land.at[(me + 3) % 4, pl.ds(0, half)]
        waits = [link.push(block, block, plus).wait_recv]
        down.wait_recv()
        block = land.at[(me + 1) % 4, pl.ds(half, half)]
        return waits + [link.push(block, block, minus).wait_recv]

    return forward


def gelu_parts(g):
    inner = 0.7978845608 * (g + 0.044715 * g * g * g)
    th = jnp.tanh(inner)
    half = 0.5 * (1.0 + th)
    slope = half + 0.5 * g * (1.0 - th * th) * (0.7978845608 * (1.0 + 0.134145 * g * g))
    return g * half, slope


def experts_kernel(
    hot_a_in, hot_b_in, nf_a_in, nf_b_in, dy_in, gate_up, down,
    back_a, back_b, out, up_out, down_out,
    hot_a, hot_b, nf_a, nf_b, stage_a, stage_b, rows, dy,
    gu, dn, raw, mixed, ghid, grow, eo, up_grad, down_grad,
    send, recv, local, load_sem,
):
    at = place()
    y, z, c, x = at
    me = (y * 4 + z) * 2 + c
    loads = [
        pltpu.make_async_copy(src, dst, load_sem.at[i])
        for i, (src, dst) in enumerate(
            (
                (hot_a_in, hot_a), (nf_a_in, nf_a), (hot_b_in, hot_b), (nf_b_in, nf_b),
                (dy_in, dy), (down.at[0], dn), (gate_up.at[0], gu),
            )
        )
    ]
    for load in loads:
        load.start()
    greet(cross(*at))
    moves = Moves(send, recv, local)
    for load in loads[:4]:
        load.wait()
    waits = []
    for piece in range(PARTS):
        to_slots(hot_a, nf_a, stage_a, piece)
        to_slots(hot_b, nf_b, stage_b, piece)
        waits.append(deliver(moves, at, stage_a, stage_b, rows, WIDE_A, piece))
    for load in loads[4:]:
        load.wait()

    def raw_tile(j, carry):
        lanes = pl.ds(pl.multiple_of(j * TILE, TILE), TILE)
        raw[:, lanes] = mul(dy[...].reshape(ROWS, D), dn[lanes, :], NT)
        return carry

    lax.fori_loop(0, FF // TILE, raw_tile, 0)
    back_waits = []
    for piece in range(PARTS):
        for wait in waits[piece]:
            wait()
        block = slice(piece * PIECE_ROWS, (piece + 1) * PIECE_ROWS)
        gate_lanes = iota((PIECE_ROWS, LANES), 1)
        mine = (
            (gate_lanes == me)
            | (gate_lanes == me + EXPERTS)
            | (gate_lanes == me + 2 * EXPERTS)
        )
        held = rows[piece, :, :, :, 0:LANES].reshape(PIECE_ROWS, LANES).astype(F32)
        gate = jnp.sum(jnp.where(mine, held, 0.0), axis=1, keepdims=True)

        def hidden_tile(j, slope_sum, piece=piece, block=block, gate=gate):
            lanes = pl.ds(pl.multiple_of(j * TILE, TILE), TILE)
            upper = pl.ds(pl.multiple_of(FF + j * TILE, TILE), TILE)
            g = mul(rows[piece, :, :, :, LANES:].reshape(PIECE_ROWS, D), gu[:, lanes])
            act, slope = gelu_parts(g)
            u = mul(rows[piece, :, :, :, LANES:].reshape(PIECE_ROWS, D), gu[:, upper])
            m = raw[block, lanes]
            both = act * u
            mixed[block, lanes] = (both * gate).astype(BF16)
            slope_sum = slope_sum + jnp.sum(both * m, axis=1, keepdims=True)
            m = m * gate
            ghid[block, lanes] = (m * u * slope).astype(BF16)
            ghid[block, upper] = (m * act).astype(BF16)
            return slope_sum

        slopes = lax.fori_loop(0, FF // TILE, hidden_tile, jnp.zeros((PIECE_ROWS, 1), F32))
        held = jnp.zeros((PIECE_ROWS, LANES), F32)
        for k, third in enumerate(thirds(slopes)):
            held = jnp.where(gate_lanes == me + k * EXPERTS, third.astype(F32), held)
        grow[piece, :, :, :, 0:LANES] = held.astype(BF16).reshape(4, 8, PART, LANES)

        def rows_tile(j, carry, piece=piece, block=block):
            lanes = pl.ds(pl.multiple_of(j * TILE, TILE), TILE)
            into = pl.ds(pl.multiple_of(LANES + j * TILE, LANES), TILE)
            part = mul(ghid[block, :], gu[lanes, :], NT).astype(BF16)
            grow[piece, :, :, :, into] = part.reshape(4, 8, PART, TILE)
            return carry

        lax.fori_loop(0, D // TILE, rows_tile, 0)
        back_waits += give_back(moves, at, grow, back_a, back_b, WIDE_A, piece)

    def out_tile(j, carry):
        lanes = pl.ds(pl.multiple_of(j * TILE, TILE), TILE)
        part = mul(mixed[...], dn[:, lanes]).astype(BF16)
        eo[:, :, :, :, lanes] = part.reshape(PARTS, 4, 8, PART, TILE)
        return carry

    lax.fori_loop(0, D // TILE, out_tile, 0)
    back_waits.append(moves.keep(eo, out).wait)

    def up_tile(j, carry):
        lanes = pl.ds(pl.multiple_of(j * TILE, TILE), TILE)
        held = pl.ds(pl.multiple_of(LANES + j * TILE, LANES), TILE)
        part = mul(rows[:, :, :, :, held].reshape(ROWS, TILE), ghid[...], TN)
        up_grad[lanes, :] = part.astype(BF16)
        return carry

    lax.fori_loop(0, D // TILE, up_tile, 0)
    back_waits.append(moves.keep(up_grad, up_out).wait)

    def down_tile(j, carry):
        lanes = pl.ds(pl.multiple_of(j * TILE, TILE), TILE)
        part = mul(mixed[:, lanes], dy[...].reshape(ROWS, D), TN)
        down_grad[lanes, :] = part.astype(BF16)
        return carry

    lax.fori_loop(0, FF // TILE, down_tile, 0)
    back_waits.append(moves.keep(down_grad, down_out).wait)
    for wait in back_waits:
        wait()
    moves.drain()


def run_experts(*operands):
    anywhere = pl.BlockSpec(memory_space=pltpu.HBM)
    vmem, dma = pltpu.VMEM, pltpu.SemaphoreType.DMA
    outs = (
        (PARTS, 8, 4, PART, WIDE_A),
        (PARTS, 8, 4, PART, WIDE_B),
        (PARTS, 4, 8, PART, D),
        (D, 2 * FF),
        (FF, D),
    )
    held = (
        (4, COUNT, SLOTS),
        (4, COUNT, SLOTS),
        (4, COUNT, WIDE_A),
        (4, COUNT, WIDE_B),
        (PARTS, 8, 4, PART, WIDE_A),
        (PARTS, 8, 4, PART, WIDE_B),
        (PARTS, 4, 8, PART, WIDE),
        (PARTS, 4, 8, PART, D),
        (D, 2 * FF),
        (FF, D),
        None,
        (ROWS, FF),
        (ROWS, 2 * FF),
        (PARTS, 4, 8, PART, WIDE),
        (PARTS, 4, 8, PART, D),
        (D, 2 * FF),
        (FF, D),
    )
    return pl.pallas_call(
        experts_kernel,
        name="experts",
        out_shape=tuple(jax.ShapeDtypeStruct(shape, BF16) for shape in outs),
        in_specs=[anywhere] * 7,
        out_specs=(anywhere,) * 5,
        scratch_shapes=[vmem(shape, BF16) if shape else vmem((ROWS, FF), F32) for shape in held]
        + [dma((84,)), dma((84,)), dma((15,)), dma((7,))],
        compiler_params=pltpu.CompilerParams(
            collective_id=2, has_side_effects=True, vmem_limit_bytes=60 * 1024 * 1024
        ),
        cost_estimate=pl.CostEstimate(
            flops=33_000_000_000, bytes_accessed=60_000_000, transcendentals=1_200_000
        ),
    )(*operands)


UP_PART = D // 4
UP_HALF = UP_PART // 2
DOWN_PART = D // 4
DOWN_HALF = FF // 2


def read_gains(small):
    select = hot(iota((8, SMALL), 1) == iota((8, SMALL), 0) + EXPERTS)
    select = jnp.where(iota((8, SMALL), 0) < 2, select, jnp.zeros_like(select))
    return mul(select, small, NT), select


def fill_bias(lengths, bias, x):
    first = lengths[0, 0]
    second = first + lengths[0, 1]
    third = second + lengths[0, 2]
    own = x * COUNT + iota((1, COUNT), 1)
    own_seg = sum(jnp.where(own >= end, 1, 0) for end in (first, second, third))

    def step(i, carry):
        base = pl.multiple_of(i * COUNT, COUNT)
        key = base + iota((COUNT, 1), 0)
        key_seg = sum(jnp.where(key >= end, 1, 0) for end in (first, second, third))
        allowed = (key_seg == own_seg) & (key <= own)
        bias[pl.ds(base, COUNT), :] = jnp.where(allowed, 0.0, -1e30)
        return carry

    lax.fori_loop(0, GROUP_ROWS // COUNT, step, 0)


def turn(v, cosd, sind):
    return v * cosd + pltpu.roll(v, HEAD_DIM // 2, 1) * sind


def forward_kernel(
    lengths, tokens, wq_in, wb_in, named, cosd, sind, hot_a_in, hot_b_in, dy_a_in, dy_b_in,
    q_out, kv_out, attended_out, middle_out, normed_out, tops, totals, gates_out,
    nf_a, nf_b, dy_rows,
    wq, wb, kv, own_kv, bias, vt, q, attended, middle, normed, nf,
    hot_a, hot_b, dy_a, dy_b, stage_a, stage_b, send, recv, local, load_sem,
):
    at = place()
    y, z, c, x = at
    line_y, line_z = lines(y, z, c, x)
    peers = [device(y, z, c, (x + d) % 4) for d in (1, 2, 3)]
    loads = [
        pltpu.make_async_copy(wq_in.at[:, pl.ds(D, 512)], wq.at[:, pl.ds(D, 512)], load_sem.at[0]),
        pltpu.make_async_copy(wq_in.at[:, pl.ds(0, D)], wq.at[:, pl.ds(0, D)], load_sem.at[1]),
        pltpu.make_async_copy(wb_in, wb, load_sem.at[2]),
    ]
    pairs = ((hot_a_in, hot_a), (dy_a_in, dy_a), (hot_b_in, hot_b), (dy_b_in, dy_b))
    loads += [
        pltpu.make_async_copy(src, dst, load_sem.at[3 + i]) for i, (src, dst) in enumerate(pairs)
    ]
    for load in loads:
        load.start()
    greet(cross(*at) + peers)
    moves = Moves(send, recv, local)
    loads[2].wait()
    small = wb[:, D:]
    gains, _ = read_gains(small)
    xf = tokens[...].astype(F32)
    inverse = lax.rsqrt(jnp.mean(xf * xf, axis=1, keepdims=True) + norm_eps)
    normed[...] = (xf * inverse * gains[0:1, :]).astype(BF16)
    loads[0].wait()
    for j in range(2):
        part = mul(normed[...], wq[:, D + j * 256 : D + (j + 1) * 256])
        if j == 0:
            for h in range(2):
                lanes = slice(h * HEAD_DIM, (h + 1) * HEAD_DIM)
                own_kv[:, lanes] = turn(part[:, lanes], cosd[...], sind[...]).astype(BF16)
        else:
            own_kv[:, 256:512] = part.astype(BF16)
    rows = pl.ds(pl.multiple_of(x * COUNT, COUNT), COUNT)
    pushes = [moves.push(own_kv, kv.at[rows], peer) for peer in peers]
    kv[rows, :] = own_kv[...]
    for load in loads[3:]:
        load.wait()
    for piece in range(PARTS):
        to_slots(hot_a, dy_a, stage_a, piece)
        to_slots(hot_b, dy_b, stage_b, piece)
    dy_waits = deliver(moves, at, stage_a, stage_b, dy_rows, HALF, slice(None))
    fill_bias(lengths, bias, x)
    loads[1].wait()

    def query_tile(j, carry):
        lanes = pl.ds(pl.multiple_of(j * 256, 256), 256)
        part = mul(normed[...], wq[:, lanes])
        q[:, lanes] = jnp.concatenate(
            [turn(part[:, h * 128 : (h + 1) * 128], cosd[...], sind[...]) for h in range(2)],
            axis=1,
        ).astype(BF16)
        return carry

    lax.fori_loop(0, D // 256, query_tile, 0)

    logits = jnp.where(named[...] > 0, mul(tokens[...], small), -jnp.inf)
    weight = jnp.exp(logits - jnp.max(logits, axis=1, keepdims=True))
    gates = weight / jnp.sum(weight, axis=1, keepdims=True)
    gates_out[...] = gates
    for push in pushes:
        push.wait_recv()
    stays = [moves.keep(q, q_out), moves.keep(normed, normed_out), moves.keep(kv, kv_out)]
    for g in range(HEADS_KV):
        vt[g] = kv[:, 256 + g * 128 : 384 + g * 128].T
    for g in range(HEADS_KV):

        def head(i, carry, g=g):
            h = g * REPEAT + i
            lanes = pl.ds(pl.multiple_of(h * HEAD_DIM, HEAD_DIM), HEAD_DIM)
            s = mul(kv[:, g * 128 : (g + 1) * 128], q[:, lanes], NT) * SCALE + bias[...]
            top = jnp.max(s, axis=0, keepdims=True)
            p = jnp.exp(s - top)
            total = jnp.sum(p, axis=0, keepdims=True)
            tops[pl.ds(h, 1), :] = top
            totals[pl.ds(h, 1), :] = total
            low = (p * (1.0 / total)).astype(BF16)
            attended[:, lanes] = mul(vt[g], low).T.astype(BF16)
            return carry

        lax.fori_loop(0, REPEAT, head, 0)

    def out_tile(j, carry):
        lanes = pl.ds(pl.multiple_of(j * 256, 256), 256)
        middle[:, lanes] = tokens[:, lanes].astype(F32) + mul(attended[...], wb[lanes, 0:D], NT)
        return carry

    lax.fori_loop(0, D // 256, out_tile, 0)
    m = middle[...]
    inverse = lax.rsqrt(jnp.mean(m * m, axis=1, keepdims=True) + norm_eps)
    stays += [moves.keep(attended, attended_out), moves.keep(middle, middle_out)]
    high, mid, low = (third.astype(F32) for third in thirds(gates))
    held = high + pltpu.roll(mid, EXPERTS, 1) + pltpu.roll(low, 2 * EXPERTS, 1)
    nf[:, 0:LANES] = held.astype(BF16)
    nf[:, LANES:] = (m * inverse * gains[1:2, :]).astype(BF16)
    half_a, half_b = nf.at[:, pl.ds(0, WIDE_A)], nf.at[:, pl.ds(WIDE_A, WIDE_B)]
    last = [
        around(moves, half_a, nf_a, y, line_y[0], line_y[2]),
        around(moves, half_b, nf_b, z, line_z[0], line_z[2]),
    ]
    stays += [moves.keep(half_a, nf_a.at[y]), moves.keep(half_b, nf_b.at[z])]
    for wait in last[0]() + last[1]():
        wait()
    for stay in stays:
        stay.wait()
    for wait in dy_waits:
        wait()
    moves.drain()


def run_forward(*operands):
    anywhere = pl.BlockSpec(memory_space=pltpu.HBM)
    inside = pl.BlockSpec(memory_space=pltpu.VMEM)
    vmem, dma = pltpu.VMEM, pltpu.SemaphoreType.DMA
    shape = jax.ShapeDtypeStruct
    return pl.pallas_call(
        forward_kernel,
        name="forward",
        out_shape=(
            shape((COUNT, D), BF16),
            shape((GROUP_ROWS, 512), BF16),
            shape((COUNT, D), BF16),
            shape((COUNT, D), F32),
            shape((COUNT, D), BF16),
            shape((16, COUNT), F32),
            shape((16, COUNT), F32),
            shape((COUNT, 128), F32),
            shape((4, COUNT, WIDE_A), BF16),
            shape((4, COUNT, WIDE_B), BF16),
            shape((PARTS, 4, 8, PART, D), BF16),
        ),
        in_specs=[pl.BlockSpec(memory_space=pltpu.SMEM), inside, anywhere, anywhere]
        + [inside] * 3
        + [anywhere] * 4,
        out_specs=(anywhere,) * 5 + (inside,) * 3 + (anywhere,) * 3,
        scratch_shapes=[
            vmem((D, WA), BF16),
            vmem((D, WB), BF16),
            vmem((GROUP_ROWS, 512), BF16),
            vmem((COUNT, 512), BF16),
            vmem((GROUP_ROWS, COUNT), F32),
            vmem((HEADS_KV, HEAD_DIM, GROUP_ROWS), BF16),
            vmem((COUNT, D), BF16),
            vmem((COUNT, D), BF16),
            vmem((COUNT, D), F32),
            vmem((COUNT, D), BF16),
            vmem((COUNT, WIDE), BF16),
            vmem((4, COUNT, SLOTS), BF16),
            vmem((4, COUNT, SLOTS), BF16),
            vmem((4, COUNT, HALF), BF16),
            vmem((4, COUNT, HALF), BF16),
            *(vmem((PARTS, 8, 4, PART, HALF), BF16),) * 2,
            dma((3 + 14 + 8,)),
            dma((3 + 14 + 8,)),
            dma((2 + 7,)),
            dma((7,)),
        ],
        compiler_params=pltpu.CompilerParams(
            collective_id=3, has_side_effects=True, vmem_limit_bytes=60 * 1024 * 1024
        ),
        cost_estimate=pl.CostEstimate(
            flops=6_000_000_000, bytes_accessed=30_000_000, transcendentals=3_200_000
        ),
    )(*operands)


def norm_grad(values, gain, grad):
    inverse = lax.rsqrt(jnp.mean(values * values, axis=1, keepdims=True) + norm_eps)
    unit = values * inverse
    scaled = grad * gain
    drop = jnp.mean(scaled * unit, axis=1, keepdims=True)
    return inverse * (scaled - unit * drop), jnp.sum(grad * unit, axis=0, keepdims=True)


def backward_kernel(
    lengths, tokens_in, cotangent_in, gates, queries_in, kv_src, attended_in, middle_in, normed_in,
    tops, totals, cosd, sind, wq_in, wb_in, hot_a_in, hot_b_in,
    back_a_in, back_b_in, out_in, up_in, down_in,
    grad_tokens, grad_qkv_out, grad_out_out, grad_small, up_far, down_far,
    late_a, late_b, came_a, came_b,
    tokens, cotangent, queries, kv_in, attended, middle, normed,
    wq, wb, hot_a, hot_b, back_a, back_b,
    part_a, part_b, land_a, land_b,
    bias, kt, gn, gmid, gb, gatt, gp, dk, dv, leave, land, grad_qkv,
    send, recv, local, load_sem, empty,
):
    at = place()
    y, z, c, x = at
    line_y, line_z = lines(y, z, c, x)
    peers = [device(y, z, c, (x + d) % 4) for d in (1, 2, 3)]
    pairs = (
        (back_a_in, back_a), (hot_a_in, hot_a), (back_b_in, back_b), (hot_b_in, hot_b),
        (kv_src, kv_in), (wb_in, wb), (middle_in, middle), (cotangent_in, cotangent),
        (queries_in, queries), (attended_in, attended), (tokens_in, tokens),
        (normed_in, normed), (wq_in, wq),
    )
    loads = [
        pltpu.make_async_copy(src, dst, load_sem.at[i]) for i, (src, dst) in enumerate(pairs)
    ]
    for load in loads:
        load.start()
    greet(cross(*at) + peers)
    link = Moves(send, recv, local)
    for load in loads[:4]:
        load.wait()
    part_waits = []
    for hits, back, parts, land_here, me, line, width in (
        (hot_a, back_a, part_a, land_a, y, line_y, WIDE_A),
        (hot_b, back_b, part_b, land_b, z, line_z, WIDE_B),
    ):
        for d in (1, 2, 3):
            parts[d - 1] = add_up(hits, back, (me + d) % 4, width)
            push = link.push(parts.at[d - 1], land_here.at[me], line[d - 1])
            part_waits.append(push.wait_recv)
        land_here[pl.ds(me, 1)] = add_up(hits, back, me, width)[None]
    for peer in cross(*at):
        pl.semaphore_signal(empty, inc=1, device_id=peer, device_id_type=MESH)
    facing = (x + 2) % 4
    pushes = []
    for half, peer in ((0, peers[2]), (1, peers[0])):
        up_rows = pl.ds(pl.multiple_of(facing * UP_PART + half * UP_HALF, UP_HALF), UP_HALF)
        pushes.append(link.push(up_in.at[up_rows], up_far.at[half], peer))
        lanes = pl.ds(pl.multiple_of(facing * DOWN_PART, 128), DOWN_PART)
        down_rows = pl.ds(half * DOWN_HALF, DOWN_HALF)
        pushes.append(link.push(down_in.at[down_rows, lanes], down_far.at[half], peer))
    fill_bias(lengths, bias, x)
    for load in loads[4:]:
        load.wait()
    for g in range(HEADS_KV):
        kt[g] = kv_in[:, g * 128 : (g + 1) * 128].T
    for wait in part_waits:
        wait()
    pl.semaphore_wait(empty, 13)
    out_waits = give_back(link, at, out_in, back_a, back_b, HALF, slice(None))
    total = land_a[0].astype(F32)
    for s in range(1, 4):
        total = total + land_a[s].astype(F32)
    slopes = total[:, 0:LANES]
    gn[:, 0 : WIDE_A - LANES] = total[:, LANES:]
    total = land_b[0].astype(F32)
    for s in range(1, 4):
        total = total + land_b[s].astype(F32)
    gn[:, WIDE_A - LANES :] = total
    gains, select = read_gains(wb[:, D:])
    moved, ffn_gain = norm_grad(middle[...], gains[1:2, :], gn[...])
    gm = cotangent[...].astype(F32) + moved
    gmid[...] = gm
    gb[...] = gm.astype(BF16)

    def att_tile(j, carry):
        lanes = pl.ds(pl.multiple_of(j * 256, 256), 256)
        gatt[:, lanes] = mul(gb[...], wb[:, lanes]).astype(BF16)
        return carry

    lax.fori_loop(0, D // 256, att_tile, 0)
    kv_pushes = []
    for g in range(HEADS_KV):
        dk[...] = jnp.zeros_like(dk)
        dv[...] = jnp.zeros_like(dv)

        def head(i, carry, g=g):
            h = g * REPEAT + i
            lanes = pl.ds(pl.multiple_of(h * HEAD_DIM, HEAD_DIM), HEAD_DIM)
            s = mul(kv_in[:, g * 128 : (g + 1) * 128], queries[:, lanes], NT) * SCALE + bias[...]
            p = jnp.exp(s - tops[pl.ds(h, 1), :]) * (1.0 / totals[pl.ds(h, 1), :])
            dv[...] += mul(p.astype(BF16), gatt[:, lanes])
            t = p * mul(kv_in[:, 256 + g * 128 : 384 + g * 128], gatt[:, lanes], NT)
            ds = (t - p * jnp.sum(t, axis=0, keepdims=True)).astype(BF16)
            dk[...] += mul(ds, queries[:, lanes])
            dq = mul(kt[g], ds).T * SCALE
            gp[:, lanes] = turn(dq, cosd[...], -sind[...]).astype(BF16)
            return carry

        lax.fori_loop(0, REPEAT, head, 0)
        leave[g, :, 0:128] = (dk[...] * SCALE).astype(BF16)
        leave[g, :, 128:256] = dv[...].astype(BF16)
        for d in (1, 2, 3):
            away = pl.ds(pl.multiple_of(((x + d) % 4) * COUNT, COUNT), COUNT)
            kv_pushes.append(link.push(leave.at[g, away], land.at[g, d - 1], peers[d - 1]))

    for wait in out_waits:
        wait()
    for s in range(4):
        land_a[s, :, 0:HALF] = add_up(hot_a, back_a, s, HALF)
        land_b[s, :, 0:HALF] = add_up(hot_b, back_b, s, HALF)
    first, second, lanes = pl.ds(0, COUNT // 2), pl.ds(COUNT // 2, COUNT // 2), pl.ds(0, HALF)
    late, stays = [], []
    for parts, came, left, me, line in (
        (land_a, came_a, late_a, y, line_y),
        (land_b, came_b, late_b, z, line_z),
    ):
        for d in (1, 2, 3):
            push = link.push(parts.at[(me + d) % 4, first, lanes], came.at[me], line[d - 1])
            late.append(push.wait_recv)
        stays.append(link.keep(parts.at[me, first, lanes], came.at[me]))
        stays.append(link.keep(parts.at[:, second, lanes], left))

    def out_tile(j, carry):
        lanes = pl.ds(pl.multiple_of(j * 256, 256), 256)
        grad_qkv[lanes, 0:D] = mul(gb[:, lanes], attended[...], TN).astype(BF16)
        return carry

    lax.fori_loop(0, D // 256, out_tile, 0)

    out_kept = link.keep(grad_qkv.at[:, pl.ds(0, D)], grad_out_out)

    gate_grad = slopes + pltpu.roll(slopes, 128 - EXPERTS, 1) + pltpu.roll(
        slopes, 128 - 2 * EXPERTS, 1
    )
    weighted = gates[...] * gate_grad
    logit_grad = weighted - gates[...] * jnp.sum(weighted, axis=1, keepdims=True)
    parts = thirds(logit_grad)
    router_grad = sum(mul(tokens[...], part, TN) for part in parts)
    small = wb[:, D:]

    for push in kv_pushes:
        push.wait_recv()
    mine = pl.ds(pl.multiple_of(x * COUNT, COUNT), COUNT)
    for g in range(HEADS_KV):
        total = leave[g, mine, :].astype(F32)
        for d in range(3):
            total = total + land[g, d].astype(F32)
        gp[:, D + g * 128 : D + (g + 1) * 128] = turn(
            total[:, 0:128], cosd[...], -sind[...]
        ).astype(BF16)
        gp[:, D + 256 + g * 128 : D + 384 + g * 128] = total[:, 128:256].astype(BF16)
    out_kept.wait()

    def qkv_tile(j, carry):
        lanes = pl.ds(pl.multiple_of(j * 256, 256), 256)
        grad_qkv[lanes, :] = mul(normed[:, lanes], gp[...], TN).astype(BF16)
        gn[:, lanes] = mul(gp[...], wq[lanes, :], NT)
        return carry

    lax.fori_loop(0, D // 256, qkv_tile, 0)
    stays.append(link.keep(grad_qkv, grad_qkv_out))
    moved, attn_gain = norm_grad(tokens[...].astype(F32), gains[0:1, :], gn[...])
    from_router = sum(mul(part, small, NT) for part in parts)
    grad_tokens[...] = (gmid[...] + moved + from_router).astype(BF16)
    both = jnp.where(
        iota((8, D), 0) == 0, attn_gain, jnp.where(iota((8, D), 0) == 1, ffn_gain, 0.0)
    )
    gain_columns = sum(mul(part, select, TN) for part in thirds(both))
    grad_small[...] = (router_grad + gain_columns).astype(BF16)
    for push in pushes:
        push.wait_recv()
    for wait in late:
        wait()
    for stay in stays:
        stay.wait()
    link.drain()


def run_backward(*operands):
    anywhere = pl.BlockSpec(memory_space=pltpu.HBM)
    inside = pl.BlockSpec(memory_space=pltpu.VMEM)
    vmem, dma = pltpu.VMEM, pltpu.SemaphoreType.DMA
    shape = jax.ShapeDtypeStruct
    return pl.pallas_call(
        backward_kernel,
        name="backward",
        out_shape=(
            shape((COUNT, D), BF16),
            shape((D, WA), BF16),
            shape((D, D), BF16),
            shape((D, SMALL), BF16),
            shape((2, UP_HALF, 2 * FF), BF16),
            shape((2, DOWN_HALF, DOWN_PART), BF16),
            *(shape((4, COUNT // 2, HALF), BF16),) * 4,
        ),
        in_specs=[pl.BlockSpec(memory_space=pltpu.SMEM)]
        + [anywhere] * 2
        + [inside]
        + [anywhere] * 5
        + [inside] * 4
        + [anywhere] * 9,
        out_specs=(inside, anywhere, anywhere, inside) + (anywhere,) * 6,
        scratch_shapes=[
            vmem((COUNT, D), BF16),
            vmem((COUNT, D), BF16),
            vmem((COUNT, D), BF16),
            vmem((GROUP_ROWS, 512), BF16),
            vmem((COUNT, D), BF16),
            vmem((COUNT, D), F32),
            vmem((COUNT, D), BF16),
            vmem((D, WA), BF16),
            vmem((D, WB), BF16),
            vmem((4, COUNT, SLOTS), BF16),
            vmem((4, COUNT, SLOTS), BF16),
            vmem((PARTS, 8, 4, PART, WIDE_A), BF16),
            vmem((PARTS, 8, 4, PART, WIDE_B), BF16),
            vmem((3, COUNT, WIDE_A), BF16),
            vmem((3, COUNT, WIDE_B), BF16),
            vmem((4, COUNT, WIDE_A), BF16),
            vmem((4, COUNT, WIDE_B), BF16),
            vmem((GROUP_ROWS, COUNT), F32),
            vmem((HEADS_KV, HEAD_DIM, GROUP_ROWS), BF16),
            vmem((COUNT, D), F32),
            vmem((COUNT, D), F32),
            vmem((COUNT, D), BF16),
            vmem((COUNT, D), BF16),
            vmem((COUNT, WA), BF16),
            vmem((GROUP_ROWS, HEAD_DIM), F32),
            vmem((GROUP_ROWS, HEAD_DIM), F32),
            vmem((HEADS_KV, GROUP_ROWS, 256), BF16),
            vmem((HEADS_KV, 3, COUNT, 256), BF16),
            vmem((D, WA), BF16),
            dma((6 + 4 + 14 + 6 + 6,)),
            dma((6 + 4 + 14 + 6 + 6,)),
            dma((2 + 4 + 2,)),
            dma((13,)),
            pltpu.SemaphoreType.REGULAR,
        ],
        compiler_params=pltpu.CompilerParams(
            collective_id=4, has_side_effects=True, vmem_limit_bytes=60 * 1024 * 1024
        ),
        cost_estimate=pl.CostEstimate(
            flops=13_000_000_000, bytes_accessed=50_000_000, transcendentals=3_200_000
        ),
    )(*operands)


def rope_tables(position, half_dim):
    frequency = rope_base ** (-jnp.arange(half_dim, dtype=jnp.float32) / half_dim)
    angles = position.astype(jnp.float32)[:, None] * frequency[None, :]
    return jnp.cos(angles), jnp.sin(angles)


def seq_layout(seq_lens, row_ids):
    seq_ends = jnp.cumsum(seq_lens)
    segment = jnp.sum((row_ids[:, None] >= seq_ends[None, :]).astype(jnp.int32), axis=1)
    seq_start = jnp.sum(
        jnp.where(seq_ends[None, :] <= row_ids[:, None], seq_lens[None, :], 0), axis=1
    )
    return (segment, row_ids - seq_start)


def body(
    tokens, lengths, top_experts, w_qkv, w_out, gain_attn, gain_ffn, router, gate_up, down_proj, cotangent,
):
    pack = jnp.concatenate(
        [
            w_qkv,
            w_out.T,
            router,
            gain_attn[:, None],
            gain_ffn[:, None],
            jnp.zeros((PIECE, SMALL - EXPERTS - 2), BF16),
        ],
        axis=1,
    )
    pack = jnp.pad(pack, ((0, PADDED - PIECE), (0, 0)))

    row_ids = jnp.arange(COUNT, dtype=jnp.int32)
    own_ids = lax.axis_index("shard") * COUNT + row_ids
    _, own_position = seq_layout(lengths[0], own_ids)
    cosine, sine = rope_tables(own_position, HEAD_DIM // 2)
    cosd = jnp.concatenate([cosine, cosine], axis=1)
    sind = jnp.concatenate([-sine, sine], axis=1)

    full_a, full_b, named, hot_a, hot_b, dy_a, dy_b = gather_weights(
        pack, top_experts, cotangent
    )
    wq = full_a.reshape(D, WA)
    wb = full_b.reshape(D, WB)
    (
        queries, kv, attended, middle, normed, tops, totals, gates, nf_a, nf_b, dy_rows,
    ) = run_forward(
        lengths, tokens, wq, wb, named, cosd, sind, hot_a, hot_b, dy_a, dy_b
    )
    back_a, back_b, expert_out, up_local, down_local = run_experts(
        hot_a, hot_b, nf_a, nf_b, dy_rows, gate_up, down_proj
    )
    grad_tokens, grad_qkv, grad_out, grad_small, *passed_on = run_backward(
        lengths, tokens, cotangent, gates, queries, kv, attended, middle, normed, tops, totals,
        cosd, sind, wq, wb, hot_a, hot_b, back_a, back_b, expert_out, up_local, down_local,
    )
    sum_a, sum_b, up_sum, down_sum, output = scatter_sums(
        grad_qkv.reshape(4, 4, 2, BLOCK, WA),
        grad_out.reshape(4, 4, 2, BLOCK, D),
        grad_small.reshape(4, 4, 2, BLOCK, SMALL),
        up_local,
        down_local,
        *passed_on,
        middle,
    )
    sum_b = sum_b[:PIECE]

    return (
        output,
        grad_tokens,
        sum_a[:PIECE],
        sum_b[:, :D].T,
        sum_b[:, D + EXPERTS],
        sum_b[:, D + EXPERTS + 1],
        sum_b[:, D : D + EXPERTS],
        up_sum[None],
        down_sum[None],
    )


def solution(mesh):
    return jax.shard_map(
        body,
        mesh=mesh,
        in_specs=(
            P(("expert", "shard"), None),
            P("expert", None),
            P(("expert", "shard"), None),
            P(("expert", "shard"), None),
            P(None, ("expert", "shard")),
            P(("expert", "shard")),
            P(("expert", "shard")),
            P(("expert", "shard"), None),
            P("expert", None, None),
            P("expert", None, None),
            P(("expert", "shard"), None),
        ),
        out_specs=(
            P(("expert", "shard"), None),
            P(("expert", "shard"), None),
            P(("expert", "shard"), None),
            P(None, ("expert", "shard")),
            P(("expert", "shard")),
            P(("expert", "shard")),
            P(("expert", "shard"), None),
            P("expert", "shard", None),
            P("expert", None, "shard"),
        ),
        check_vma=False,
    )
```

```python
import jax
import jax.numpy as jnp
import numpy as np
from jax import lax
from jax.experimental import pallas as pl
from jax.experimental.pallas import tpu as pltpu
from jax.sharding import PartitionSpec as P

D = 1536
HEADS_Q = 12
HEADS_KV = 2
HEAD_DIM = 128
FF = 768
TOP = 4
EXPERTS = 32
CAP = 48
WIDTH_Q = HEADS_Q * HEAD_DIM
WIDTH_KV = HEADS_KV * HEAD_DIM
REPEAT = HEADS_Q // HEADS_KV

norm_eps = 1e-06
rope_base = 1000000.0
MESH = pl.DeviceIdType.MESH
F32 = jnp.float32
BF16 = jnp.bfloat16

PIECE = 12
PADDED = 16
BLOCK = 48
WA = 2048
WB = 1664
SMALL = WB - D


def place():
    e = lax.axis_index("expert")
    return e // 8, (e // 2) % 4, e % 2, lax.axis_index("shard")


def device(y, z, c, x):
    return ((y * 4 + z) * 2 + c, x)


def greet(devices):
    barrier = pltpu.get_barrier_semaphore()
    for d in devices:
        pl.semaphore_signal(barrier, inc=1, device_id=d, device_id_type=MESH)
    pl.semaphore_wait(barrier, len(devices))


class Links:
    def __init__(self, send, recv):
        self.send, self.recv, self.made = send, recv, []

    def push(self, src, dst, where):
        i = len(self.made)
        copy = pltpu.make_async_remote_copy(
            src_ref=src,
            dst_ref=dst,
            send_sem=self.send.at[i],
            recv_sem=self.recv.at[i],
            device_id=where,
            device_id_type=MESH,
        )
        copy.start()
        self.made.append(copy)
        return copy

    def drain(self):
        for copy in self.made:
            copy.wait_send()


def neighbours(y, z, c, x):
    other = 1 - c
    return dict(
        x=[device(y, z, c, (x + d) % 4) for d in (1, 2, 3)],
        y=(device((y + 1) % 4, z, c, x), device((y + 3) % 4, z, c, x)),
        z=(device(y, (z + 1) % 4, c, x), device(y, (z + 3) % 4, c, x)),
        core=device(y, z, other, x),
    )


def everyone_near(near):
    return list(near["x"]) + list(near["y"]) + list(near["z"]) + [near["core"]]


def pick_rows(rows, columns, row_block, column_block):
    r = lax.broadcasted_iota(jnp.int32, (rows, columns), 0)
    q = lax.broadcasted_iota(jnp.int32, (rows, columns), 1)
    same = (r // row_block == q // column_block) & (r % row_block == q % column_block)
    return jnp.where(same, 1.0, 0.0).astype(BF16)


def faces(y, z, c, x):
    along_z, along_y = [], []
    for d in range(4):
        for k in range(2):
            core = c if k == 0 else 1 - c
            along_z.append((device(y, (z + d) % 4, core, x), (z + d) % 4, core))
            along_y.append((device((y + d) % 4, z, core, x), (y + d) % 4, core))
    return along_z, along_y


def cross(y, z, c, x):
    along_z, along_y = faces(y, z, c, x)
    return [f[0] for f in along_z[1:] + along_y[2:]]


def lines(y, z, c, x):
    return (
        [device((y + d) % 4, z, c, x) for d in (1, 2, 3)],
        [device(y, (z + d) % 4, c, x) for d in (1, 2, 3)],
    )


def route(top_experts, named, own_slot):
    experts = iota((EXPERTS, COUNT), 0)
    names = sum(jnp.where(top_experts[k : k + 1, :] == experts, 1.0, 0.0) for k in range(TOP))
    low = names.astype(BF16)
    earlier = hot(iota((COUNT, COUNT), 0) < iota((COUNT, COUNT), 1))
    own_slot[...] = jnp.where(names > 0, mul(low, earlier), -1.0).astype(BF16)
    named[...] = mul(low, hot(iota((EXPERTS, 128), 0) == iota((EXPERTS, 128), 1)), TN)


def rope(lengths, rates, cosd, sind, x):
    own = x * COUNT + iota((COUNT, 1), 0)
    first = lengths[0, 0]
    second = first + lengths[0, 1]
    third = second + lengths[0, 2]
    start = jnp.zeros((COUNT, 1), jnp.int32)
    for end in (first, second, third):
        start = jnp.where(own >= end, end, start)
    angles = (own - start).astype(F32) * rates[...]
    cosd[...] = jnp.cos(angles)
    sine = jnp.sin(angles)
    sind[...] = jnp.where(iota((COUNT, HEAD_DIM), 1) < HEAD_DIM // 2, -sine, sine)


def fill_pack(pack, w_qkv, w_out_t, router, gain_attn, gain_ffn):
    pack[...] = jnp.zeros_like(pack)
    pack[0:PIECE, 0:WA] = w_qkv[...]
    pack[0:PIECE, WA : WA + D] = w_out_t[...]
    small = mul(router[...], hot(iota((EXPERTS, SMALL), 0) == iota((EXPERTS, SMALL), 1)))
    diagonal = iota((PIECE, PIECE), 0) == iota((PIECE, PIECE), 1)
    for k, gain in enumerate((gain_attn, gain_ffn)):
        column = jnp.sum(jnp.where(diagonal, gain[...].astype(F32), 0.0), axis=1, keepdims=True)
        small = jnp.where(iota((PIECE, SMALL), 1) == EXPERTS + k, column, small)
    pack[0:PIECE, WA + D :] = small.astype(BF16)


def slot_hits(slot_of, hits, experts):
    p = iota((1, SLOTS), 1)
    q = p % PIECE_SLOTS
    wanted = ((p // PIECE_SLOTS) * PART + q % PART).astype(F32)
    local = q // PART
    expand = hot(iota((EXPERTS, SLOTS), 0) == experts(local))

    def step(s, carry):
        hits[s] = hot(mul(slot_of[s], expand, TN) == wanted)
        return carry

    lax.fori_loop(0, 4, step, 0)


def gather_kernel(
    lengths, rates, w_qkv, w_out_t, router, gain_attn, gain_ffn, top_experts, cotangent,
    full_a, full_b, named, hot_a, hot_b, dy_a, dy_b, cosd, sind,
    pack, xbuf, own_a, own_b, own_slot, slot_y, slot_z, send, recv, local,
):
    y, z, c, x = place()
    near = neighbours(y, z, c, x)
    line_y, line_z = lines(y, z, c, x)
    fill_pack(pack, w_qkv, w_out_t, router, gain_attn, gain_ffn)
    greet(everyone_near(near) + [line_y[1], line_z[1]])
    link = Links(send, recv)
    first = [link.push(pack, xbuf.at[x], near["x"][d]) for d in range(3)]
    xbuf[pl.ds(x, 1)] = pack[...][None]
    half_a, half_b = cotangent.at[:, pl.ds(0, HALF)], cotangent.at[:, pl.ds(HALF, HALF)]
    kept = [
        pltpu.make_async_copy(half_a, dy_a.at[y], local.at[2]),
        pltpu.make_async_copy(half_b, dy_b.at[z], local.at[3]),
    ]
    for copy in kept:
        copy.start()
    dys = [
        around(link, half_a, dy_a, y, *near["y"]),
        around(link, half_b, dy_b, z, *near["z"]),
    ]
    for copy in first:
        copy.wait_recv()
    select = pick_rows(BLOCK, 4 * PADDED, PIECE, PADDED)
    pieces = xbuf[...].reshape(4 * PADDED, WA + WB)
    own_a[...] = jnp.dot(select, pieces[:, :WA], preferred_element_type=F32).astype(BF16)
    own_b[...] = jnp.dot(select, pieces[:, WA:], preferred_element_type=F32).astype(BF16)

    def at_a(far, close, columns=None):
        view = full_a.at[far, close, c]
        return view if columns is None else view.at[:, columns]

    def at_b(far, close, columns=None):
        view = full_b.at[close, far, c]
        return view if columns is None else view.at[:, columns]

    def line_a(far, part=slice(None)):
        return full_a.at[far, part, c]

    def line_b(far, part=slice(None)):
        return full_b.at[part, far, c]

    jobs = [
        dict(own=own_a, at=at_a, line=line_a, close="z", far="y", p=z, q=y, half=1024, i=0),
        dict(own=own_b, at=at_b, line=line_b, close="y", far="z", p=y, q=z, half=896, i=1),
    ]
    for j in jobs:
        here = j["at"](j["q"], j["p"])
        plus, minus = near[j["close"]]
        j["up"] = link.push(j["own"], here, plus)
        j["down"] = link.push(j["own"], here, minus)
        j["core"] = [link.push(j["own"], here, near["core"])]
        j["local"] = pltpu.make_async_copy(j["own"], here, local.at[j["i"]])
        j["local"].start()
    route(top_experts, named, own_slot)
    slot_y[pl.ds(y, 1)] = own_slot[...][None]
    slot_z[pl.ds(z, 1)] = own_slot[...][None]
    slots = [link.push(own_slot, slot_y.at[y], peer) for peer in line_y]
    slots += [link.push(own_slot, slot_z.at[z], peer) for peer in line_z]
    for j in jobs:
        plus, minus = near[j["close"]]
        left, right = (j["p"] + 3) % 4, (j["p"] + 1) % 4
        j["up"].wait_recv()
        part = j["at"](j["q"], left, pl.ds(0, j["half"]))
        j["up2"] = link.push(part, part, plus)
        j["down"].wait_recv()
        part = j["at"](j["q"], right, pl.ds(j["half"], j["own"].shape[1] - j["half"]))
        j["down2"] = link.push(part, part, minus)
        for side in (left, right):
            block = j["at"](j["q"], side)
            j["core"].append(link.push(block, block, near["core"]))
    for j in jobs:
        j["up2"].wait_recv()
        j["down2"].wait_recv()
        block = j["at"](j["q"], (j["p"] + 2) % 4)
        j["local"].wait()
        plus, minus = near[j["far"]]
        line = j["line"](j["q"])
        j["up"] = link.push(line, line, plus)
        j["down"] = link.push(line, line, minus)
        j["core"].append(link.push(block, block, near["core"]))
    dys = dys[0]() + dys[1]()
    for copy in slots:
        copy.wait_recv()
    slot_hits(slot_y, hot_a, lambda e: y * 8 + e)
    slot_hits(slot_z, hot_b, lambda e: (e // 2) * 8 + z * 2 + e % 2)
    rope(lengths, rates, cosd, sind, x)
    for j in jobs:
        plus, minus = near[j["far"]]
        left, right = (j["q"] + 3) % 4, (j["q"] + 1) % 4
        j["up"].wait_recv()
        part = j["line"](left, pl.ds(0, 2))
        j["up2"] = link.push(part, part, plus)
        j["down"].wait_recv()
        part = j["line"](right, pl.ds(2, 2))
        j["down2"] = link.push(part, part, minus)
        for side in (left, right):
            block = j["line"](side)
            j["core"].append(link.push(block, block, near["core"]))
    for j in jobs:
        opposite = (j["q"] + 2) % 4
        j["up2"].wait_recv()
        part = j["line"](opposite, pl.ds(0, 2))
        j["core"].append(link.push(part, part, near["core"]))
        j["down2"].wait_recv()
        part = j["line"](opposite, pl.ds(2, 2))
        j["core"].append(link.push(part, part, near["core"]))
    for j in jobs:
        for copy in j["core"]:
            copy.wait_recv()
    for wait in dys:
        wait()
    for copy in kept:
        copy.wait()
    link.drain()


def gather_weights(*operands):
    inside = pl.BlockSpec(memory_space=pltpu.VMEM)
    anywhere = pl.BlockSpec(memory_space=pltpu.HBM)
    copies = 3 + 2 * 16 + 6 + 8
    return pl.pallas_call(
        gather_kernel,
        name="gather_weights",
        out_shape=(
            jax.ShapeDtypeStruct((4, 4, 2, BLOCK, WA), BF16),
            jax.ShapeDtypeStruct((4, 4, 2, BLOCK, WB), BF16),
            jax.ShapeDtypeStruct((COUNT, 128), F32),
            jax.ShapeDtypeStruct((4, COUNT, SLOTS), BF16),
            jax.ShapeDtypeStruct((4, COUNT, SLOTS), BF16),
            jax.ShapeDtypeStruct((4, COUNT, HALF), BF16),
            jax.ShapeDtypeStruct((4, COUNT, HALF), BF16),
            jax.ShapeDtypeStruct((COUNT, HEAD_DIM), F32),
            jax.ShapeDtypeStruct((COUNT, HEAD_DIM), F32),
        ),
        in_specs=[pl.BlockSpec(memory_space=pltpu.SMEM)] + [inside] * 8,
        out_specs=(anywhere,) * 2 + (inside,) * 3 + (anywhere,) * 2 + (inside,) * 2,
        scratch_shapes=[
            pltpu.VMEM((PADDED, WA + WB), BF16),
            pltpu.VMEM((4, PADDED, WA + WB), BF16),
            pltpu.VMEM((BLOCK, WA), BF16),
            pltpu.VMEM((BLOCK, WB), BF16),
            pltpu.VMEM((EXPERTS, COUNT), BF16),
            pltpu.VMEM((4, EXPERTS, COUNT), BF16),
            pltpu.VMEM((4, EXPERTS, COUNT), BF16),
            pltpu.SemaphoreType.DMA((copies,)),
            pltpu.SemaphoreType.DMA((copies,)),
            pltpu.SemaphoreType.DMA((4,)),
        ],
        compiler_params=pltpu.CompilerParams(
            collective_id=0, has_side_effects=True, vmem_limit_bytes=60 * 1024 * 1024
        ),
        cost_estimate=pl.CostEstimate(flops=0, bytes_accessed=24_000_000, transcendentals=0),
    )(*operands)


def add_blocks(dst, far, start, count, sources):
    def step(i, carry):
        total = dst[far, start + i].astype(F32)
        for source in sources:
            total = total + source(i).astype(F32)
        dst[far, start + i] = total.astype(BF16)
        return carry

    lax.fori_loop(0, count, step, 0)


def scatter_kernel(
    ga, gb, gs, up_in, down_in, up_far, down_far, late_a, late_b, came_a, came_b, middle,
    out_a, out_b, up_out, down_out, output,
    core_a, core_b, mine_a, mine_b, one_a, one_b, two_a, two_b,
    half_a0, half_a1, half_b0, half_b1, last_a, last_b, xout, xin,
    ups, downs, up_got, up_land, mid, land_a, land_b,
    send, recv, local,
):
    y, z, c, x = place()
    near = neighbours(y, z, c, x)
    line_y, line_z = lines(y, z, c, x)
    greet(everyone_near(near) + [line_y[1], line_z[1]])
    link = Links(send, recv)
    other = 1 - c
    jobs = [
        dict(src=[(lambda f, s: ga.at[f, :, s], 0, WA)], core=core_a, mine=mine_a, one=one_a, two=two_a,
             halves=(half_a0, half_a1), last=last_a, far="y", close="z", q=y, p=z,
             width=WA, half=1024, lane=0, i=0),
        dict(src=[(lambda f, s: gb.at[:, f, s], 0, D), (lambda f, s: gs.at[:, f, s], D, SMALL)],
             core=core_b, mine=mine_b, one=one_b, two=two_b,
             halves=(half_b0, half_b1), last=last_b, far="z", close="y", q=z, p=y,
             width=WB, half=896, lane=WA, i=1),
    ]
    slots = 0
    for step in (2, 3, 1, 0):
        for j in jobs:
            f = (j["q"] + step) % 4
            j[step] = []
            for source, lane, width in j["src"]:
                lanes = pl.ds(lane, width)
                pushed = link.push(
                    source(f, other), j["core"].at[f, :, :, lanes], near["core"]
                )
                kept = pltpu.make_async_copy(
                    source(f, c), j["mine"].at[f, :, :, lanes], local.at[slots]
                )
                slots += 1
                kept.start()
                j[step].append((pushed, kept))

    late = []
    first, second = pl.ds(0, COUNT // 2), pl.ds(COUNT // 2, COUNT // 2)
    for src, dst, me, line in ((late_a, land_a, y, line_y), (late_b, land_b, z, line_z)):
        for d in (1, 2, 3):
            late.append(link.push(src.at[(me + d) % 4], dst.at[me, second], line[d - 1]))
    fetches = [(up_far, up_got)]
    for i, d in enumerate((3, 1, 0)):
        up_rows = pl.ds(pl.multiple_of(((x + d) % 4) * UP_PART, UP_PART), UP_PART)
        fetches.append((up_in.at[up_rows], ups.at[i]))
    lanes = pl.ds(pl.multiple_of(x * DOWN_PART, 128), DOWN_PART)
    fetches += [
        (down_in.at[:, lanes], downs.at[0]),
        (down_far, downs.at[pl.ds(1, 2)]),
        (middle, mid),
        (came_a, land_a.at[:, first]),
        (came_b, land_b.at[:, first]),
        (late_a.at[y], land_a.at[y, second]),
        (late_b.at[z], land_b.at[z, second]),
    ]
    fetches = [
        pltpu.make_async_copy(src, dst, local.at[slots + i]) for i, (src, dst) in enumerate(fetches)
    ]
    for fetch in fetches:
        fetch.start()
    for fetch in fetches[:4]:
        fetch.wait()
    sides = []
    for i, peer in enumerate((near["x"][2], near["x"][0])):
        up_rows = slice(i * UP_HALF, (i + 1) * UP_HALF)
        ups[i, up_rows, :] = (ups[i, up_rows, :].astype(F32) + up_got[i].astype(F32)).astype(BF16)
        sides.append(link.push(ups.at[i], up_land.at[i], peer))

    def ready(j, step):
        for pushed, kept in j[step]:
            pushed.wait_recv()
            kept.wait()

    for j in jobs:
        f = (j["q"] + 2) % 4
        ready(j, 2)
        mine = j["mine"]
        add_blocks(j["core"], f, 0, 4, [lambda i, f=f, m=mine: m[f, i]])
        plus, minus = near[j["far"]]
        j["down"] = link.push(j["core"].at[f, pl.ds(0, 2)], j["one"].at[0], minus)
        j["up"] = link.push(j["core"].at[f, pl.ds(2, 2)], j["one"].at[1], plus)
    for j in jobs:
        plus, minus = near[j["far"]]
        mine, one = j["mine"], j["one"]
        f = (j["q"] + 3) % 4
        ready(j, 3)
        add_blocks(j["core"], f, 2, 2, [lambda i, f=f, m=mine: m[f, i + 2]])
        j["down"].wait_recv()
        add_blocks(
            j["core"], f, 0, 2, [lambda i, f=f, m=mine: m[f, i], lambda i, o=one: o[0, i]]
        )
        j["down2"] = link.push(j["core"].at[f], j["two"].at[0], minus)
        f = (j["q"] + 1) % 4
        ready(j, 1)
        add_blocks(j["core"], f, 0, 2, [lambda i, f=f, m=mine: m[f, i]])
        j["up"].wait_recv()
        add_blocks(
            j["core"], f, 2, 2, [lambda i, f=f, m=mine: m[f, i + 2], lambda i, o=one: o[1, i]]
        )
        j["up2"] = link.push(j["core"].at[f], j["two"].at[1], plus)
    for j in jobs:
        mine, two = j["mine"], j["two"]
        f = j["q"]
        ready(j, 0)
        j["down2"].wait_recv()
        j["up2"].wait_recv()
        add_blocks(
            j["core"], f, 0, 4,
            [lambda i, f=f, m=mine: m[f, i], lambda i, t=two: t[0, i], lambda i, t=two: t[1, i]],
        )
        plus, minus = near[j["close"]]
        g = (j["p"] + 2) % 4
        h, w = j["half"], j["width"]
        j["down"] = link.push(j["core"].at[f, g, :, pl.ds(0, h)], j["halves"][0], minus)
        j["up"] = link.push(j["core"].at[f, g, :, pl.ds(h, w - h)], j["halves"][1], plus)
    for j in jobs:
        plus, minus = near[j["close"]]
        f, h, w, core = j["q"], j["half"], j["width"], j["core"]
        g = (j["p"] + 3) % 4
        j["down"].wait_recv()
        core[f, g, :, 0:h] = (
            core[f, g, :, 0:h].astype(F32) + j["halves"][0][...].astype(F32)
        ).astype(BF16)
        j["down2"] = link.push(core.at[f, g], j["last"].at[0], minus)
        g = (j["p"] + 1) % 4
        j["up"].wait_recv()
        core[f, g, :, h:w] = (
            core[f, g, :, h:w].astype(F32) + j["halves"][1][...].astype(F32)
        ).astype(BF16)
        j["up2"] = link.push(core.at[f, g], j["last"].at[1], plus)
    select = pick_rows(4 * PADDED, BLOCK, PADDED, PIECE)
    for j in jobs:
        f, g = j["q"], j["p"]
        j["down2"].wait_recv()
        j["up2"].wait_recv()
        total = (
            j["core"][f, g].astype(F32)
            + j["last"][0].astype(F32)
            + j["last"][1].astype(F32)
        ).astype(BF16)
        spread = jnp.dot(select, total, preferred_element_type=F32).astype(BF16)
        xout[:, :, j["lane"] : j["lane"] + j["width"]] = spread.reshape(4, PADDED, j["width"])
    final = [
        link.push(xout.at[(x + d) % 4], xin.at[d - 1], near["x"][d - 1]) for d in (1, 2, 3)
    ]
    for copy in final:
        copy.wait_recv()
    mine = xout[x].astype(F32)
    for d in range(3):
        mine = mine + xin[d].astype(F32)
    out_a[...] = mine[:, :WA]
    out_b[...] = mine[:, WA:]
    for push in sides:
        push.wait_recv()
    up_out[...] = ups[2].astype(F32) + up_land[0].astype(F32) + up_land[1].astype(F32)
    for fetch in fetches[4:]:
        fetch.wait()
    down_out[...] = downs[0].astype(F32) + downs[1].astype(F32) + downs[2].astype(F32)
    for push in late:
        push.wait_recv()
    for half, landed in enumerate((land_a, land_b)):
        lanes = slice(half * HALF, (half + 1) * HALF)
        total = mid[:, lanes]
        for s in range(4):
            total = total + landed[s].astype(F32)
        output[:, lanes] = total.astype(BF16)
    link.drain()


def scatter_sums(*operands):
    copies = 2 * (4 + 4 + 4) + 4 + 3 + 6 + 2
    vmem = pltpu.VMEM
    scratch = []
    for shape in ((4, 4), (4, 4), (2, 2), (2, 4)):
        scratch += [vmem((*shape, BLOCK, WA), BF16), vmem((*shape, BLOCK, WB), BF16)]
    scratch += [
        vmem((BLOCK, 1024), BF16),
        vmem((BLOCK, 1024), BF16),
        vmem((BLOCK, 896), BF16),
        vmem((BLOCK, WB - 896), BF16),
        vmem((2, BLOCK, WA), BF16),
        vmem((2, BLOCK, WB), BF16),
        vmem((4, PADDED, WA + WB), BF16),
        vmem((3, PADDED, WA + WB), BF16),
        vmem((3, UP_PART, 2 * FF), BF16),
        vmem((3, FF, DOWN_PART), BF16),
        vmem((2, UP_HALF, 2 * FF), BF16),
        vmem((2, UP_PART, 2 * FF), BF16),
        vmem((COUNT, D), F32),
        vmem((4, COUNT, HALF), BF16),
        vmem((4, COUNT, HALF), BF16),
        pltpu.SemaphoreType.DMA((copies,)),
        pltpu.SemaphoreType.DMA((copies,)),
        pltpu.SemaphoreType.DMA((12 + 11,)),
    ]
    return pl.pallas_call(
        scatter_kernel,
        name="scatter_sums",
        out_shape=(
            jax.ShapeDtypeStruct((PADDED, WA), F32),
            jax.ShapeDtypeStruct((PADDED, WB), F32),
            jax.ShapeDtypeStruct((UP_PART, 2 * FF), F32),
            jax.ShapeDtypeStruct((FF, DOWN_PART), F32),
            jax.ShapeDtypeStruct((COUNT, D), BF16),
        ),
        in_specs=[pl.BlockSpec(memory_space=pltpu.HBM)] * 12,
        out_specs=(pl.BlockSpec(memory_space=pltpu.VMEM),) * 5,
        scratch_shapes=scratch,
        compiler_params=pltpu.CompilerParams(
            collective_id=1, has_side_effects=True, vmem_limit_bytes=60 * 1024 * 1024
        ),
        cost_estimate=pl.CostEstimate(flops=0, bytes_accessed=24_000_000, transcendentals=0),
    )(*operands)


ROWS = EXPERTS * CAP
TILE = 256
PARTS = 3
PART = CAP // PARTS
SLOTS = 8 * CAP
PIECE_SLOTS = 8 * PART
PIECE_ROWS = EXPERTS * PART
HALF = D // 2
LANES = 128
WIDE = D + LANES
WIDE_A = HALF
WIDE_B = WIDE - HALF
SCALE = HEAD_DIM ** (-0.5)
GROUP_ROWS = 1024
COUNT = 256
NT = (((1,), (1,)), ((), ()))
TN = (((0,), (0,)), ((), ()))


def mul(a, b, dims=None):
    if dims is None:
        return jnp.dot(a, b, preferred_element_type=F32)
    return lax.dot_general(a, b, dims, preferred_element_type=F32)


def thirds(v):
    high = v.astype(BF16)
    rest = v - high.astype(F32)
    middle = rest.astype(BF16)
    return high, middle, (rest - middle.astype(F32)).astype(BF16)


def iota(shape, axis):
    return lax.broadcasted_iota(jnp.int32, shape, axis)


def hot(same):
    return jnp.where(same, 1.0, 0.0).astype(BF16)


class Moves(Links):
    def __init__(self, send, recv, local):
        super().__init__(send, recv)
        self.local, self.kept = local, 0

    def keep(self, src, dst):
        copy = pltpu.make_async_copy(src, dst, self.local.at[self.kept])
        self.kept += 1
        copy.start()
        return copy

    def send_or_keep(self, i, src, dst, where):
        if i == 0:
            return self.keep(src, dst).wait
        return self.push(src, dst, where).wait_recv


def to_slots(hits, rows, stage, piece):
    columns = slice(piece * PIECE_SLOTS, (piece + 1) * PIECE_SLOTS)
    for s in range(4):
        taken = mul(hits[s, :, columns], rows[s], TN).astype(BF16)
        stage[piece, :, s] = taken.reshape(8, PART, taken.shape[1])


def deliver(moves, at, stage_a, stage_b, rows, split, piece):
    y, z, c, x = at
    along_z, along_y = faces(y, z, c, x)
    width = rows.shape[4]
    waits = []
    for i, (where, zt, ct) in enumerate(along_z):
        dst = rows.at[piece, z, pl.ds(c * 4, 4), :, pl.ds(0, split)]
        waits.append(moves.send_or_keep(i, stage_a.at[piece, zt * 2 + ct], dst, where))
    for i, (where, yt, ct) in enumerate(along_y):
        dst = rows.at[piece, :, c * 4 + y, :, pl.ds(split, width - split)]
        waits.append(moves.send_or_keep(i, stage_b.at[piece, yt * 2 + ct], dst, where))
    return waits


def give_back(moves, at, rows, back_a, back_b, split, piece):
    y, z, c, x = at
    along_z, along_y = faces(y, z, c, x)
    width = rows.shape[4]
    waits = []
    for i, (where, zt, ct) in enumerate(along_z):
        src = rows.at[piece, zt, pl.ds(ct * 4, 4), :, pl.ds(0, split)]
        dst = back_a.at[piece, z * 2 + c, :, :, pl.ds(0, split)]
        waits.append(moves.send_or_keep(i, src, dst, where))
    for i, (where, yt, ct) in enumerate(along_y):
        src = rows.at[piece, :, ct * 4 + yt, :, pl.ds(split, width - split)]
        dst = back_b.at[piece, y * 2 + c, :, :, pl.ds(0, width - split)]
        waits.append(moves.send_or_keep(i, src, dst, where))
    return waits


def add_up(hits, back, s, width):
    rows = back[:, :, s, :, 0:width].reshape(SLOTS, width)
    return mul(hits[s], rows).astype(BF16)


def around(link, own, land, me, plus, minus):
    up = link.push(own, land.at[me], plus)
    down = link.push(own, land.at[me], minus)

    def forward():
        half = COUNT // 2
        up.wait_recv()
        block = land.at[(me + 3) % 4, pl.ds(0, half)]
        waits = [link.push(block, block, plus).wait_recv]
        down.wait_recv()
        block = land.at[(me + 1) % 4, pl.ds(half, half)]
        return waits + [link.push(block, block, minus).wait_recv]

    return forward


def gelu_parts(g):
    inner = 0.7978845608 * (g + 0.044715 * g * g * g)
    th = jnp.tanh(inner)
    half = 0.5 * (1.0 + th)
    slope = half + 0.5 * g * (1.0 - th * th) * (0.7978845608 * (1.0 + 0.134145 * g * g))
    return g * half, slope


def experts_kernel(
    hot_a_in, hot_b_in, nf_a_in, nf_b_in, dy_in, gate_up, down,
    back_a, back_b, out, up_out, down_out,
    hot_a, hot_b, nf_a, nf_b, stage_a, stage_b, rows, dy,
    gu, dn, raw, mixed, ghid, grow, eo, up_grad, down_grad,
    send, recv, local, load_sem,
):
    at = place()
    y, z, c, x = at
    me = (y * 4 + z) * 2 + c
    loads = [
        pltpu.make_async_copy(src, dst, load_sem.at[i])
        for i, (src, dst) in enumerate(
            (
                (hot_a_in, hot_a), (nf_a_in, nf_a), (hot_b_in, hot_b), (nf_b_in, nf_b),
                (dy_in, dy), (down.at[0], dn), (gate_up.at[0], gu),
            )
        )
    ]
    for load in loads:
        load.start()
    greet(cross(*at))
    moves = Moves(send, recv, local)
    for load in loads[:4]:
        load.wait()
    waits = []
    for piece in range(PARTS):
        to_slots(hot_a, nf_a, stage_a, piece)
        to_slots(hot_b, nf_b, stage_b, piece)
        waits.append(deliver(moves, at, stage_a, stage_b, rows, WIDE_A, piece))
    for load in loads[4:]:
        load.wait()

    def raw_tile(j, carry):
        lanes = pl.ds(pl.multiple_of(j * TILE, TILE), TILE)
        raw[:, lanes] = mul(dy[...].reshape(ROWS, D), dn[lanes, :], NT)
        return carry

    lax.fori_loop(0, FF // TILE, raw_tile, 0, unroll=True)
    back_waits = []
    for piece in range(PARTS):
        for wait in waits[piece]:
            wait()
        block = slice(piece * PIECE_ROWS, (piece + 1) * PIECE_ROWS)
        gate_lanes = iota((PIECE_ROWS, LANES), 1)
        mine = (
            (gate_lanes == me)
            | (gate_lanes == me + EXPERTS)
            | (gate_lanes == me + 2 * EXPERTS)
        )
        held = rows[piece, :, :, :, 0:LANES].reshape(PIECE_ROWS, LANES).astype(F32)
        gate = jnp.sum(jnp.where(mine, held, 0.0), axis=1, keepdims=True)

        def hidden_tile(j, slope_sum, piece=piece, block=block, gate=gate):
            lanes = pl.ds(pl.multiple_of(j * TILE, TILE), TILE)
            upper = pl.ds(pl.multiple_of(FF + j * TILE, TILE), TILE)
            g = mul(rows[piece, :, :, :, LANES:].reshape(PIECE_ROWS, D), gu[:, lanes])
            act, slope = gelu_parts(g)
            u = mul(rows[piece, :, :, :, LANES:].reshape(PIECE_ROWS, D), gu[:, upper])
            m = raw[block, lanes]
            both = act * u
            mixed[block, lanes] = (both * gate).astype(BF16)
            slope_sum = slope_sum + jnp.sum(both * m, axis=1, keepdims=True)
            m = m * gate
            ghid[block, lanes] = (m * u * slope).astype(BF16)
            ghid[block, upper] = (m * act).astype(BF16)
            return slope_sum

        slopes = lax.fori_loop(
            0, FF // TILE, hidden_tile, jnp.zeros((PIECE_ROWS, 1), F32), unroll=True
        )
        held = jnp.zeros((PIECE_ROWS, LANES), F32)
        for k, third in enumerate(thirds(slopes)):
            held = jnp.where(gate_lanes == me + k * EXPERTS, third.astype(F32), held)
        grow[piece, :, :, :, 0:LANES] = held.astype(BF16).reshape(4, 8, PART, LANES)

        def rows_tile(j, carry, piece=piece, block=block):
            lanes = pl.ds(pl.multiple_of(j * TILE, TILE), TILE)
            into = pl.ds(pl.multiple_of(LANES + j * TILE, LANES), TILE)
            part = mul(ghid[block, :], gu[lanes, :], NT).astype(BF16)
            grow[piece, :, :, :, into] = part.reshape(4, 8, PART, TILE)
            return carry

        lax.fori_loop(0, D // TILE, rows_tile, 0, unroll=True)
        back_waits += give_back(moves, at, grow, back_a, back_b, WIDE_A, piece)

    def out_tile(j, carry):
        lanes = pl.ds(pl.multiple_of(j * TILE, TILE), TILE)
        part = mul(mixed[...], dn[:, lanes]).astype(BF16)
        eo[:, :, :, :, lanes] = part.reshape(PARTS, 4, 8, PART, TILE)
        return carry

    lax.fori_loop(0, D // TILE, out_tile, 0, unroll=2)
    back_waits.append(moves.keep(eo, out).wait)

    def up_tile(j, carry):
        lanes = pl.ds(pl.multiple_of(j * TILE, TILE), TILE)
        held = pl.ds(pl.multiple_of(LANES + j * TILE, LANES), TILE)
        part = mul(rows[:, :, :, :, held].reshape(ROWS, TILE), ghid[...], TN)
        up_grad[lanes, :] = part.astype(BF16)
        return carry

    lax.fori_loop(0, D // TILE, up_tile, 0, unroll=2)
    back_waits.append(moves.keep(up_grad, up_out).wait)

    def down_tile(j, carry):
        lanes = pl.ds(pl.multiple_of(j * TILE, TILE), TILE)
        part = mul(mixed[:, lanes], dy[...].reshape(ROWS, D), TN)
        down_grad[lanes, :] = part.astype(BF16)
        return carry

    lax.fori_loop(0, FF // TILE, down_tile, 0, unroll=True)
    back_waits.append(moves.keep(down_grad, down_out).wait)
    for wait in back_waits:
        wait()
    moves.drain()


def run_experts(*operands):
    anywhere = pl.BlockSpec(memory_space=pltpu.HBM)
    vmem, dma = pltpu.VMEM, pltpu.SemaphoreType.DMA
    outs = (
        (PARTS, 8, 4, PART, WIDE_A),
        (PARTS, 8, 4, PART, WIDE_B),
        (PARTS, 4, 8, PART, D),
        (D, 2 * FF),
        (FF, D),
    )
    held = (
        (4, COUNT, SLOTS),
        (4, COUNT, SLOTS),
        (4, COUNT, WIDE_A),
        (4, COUNT, WIDE_B),
        (PARTS, 8, 4, PART, WIDE_A),
        (PARTS, 8, 4, PART, WIDE_B),
        (PARTS, 4, 8, PART, WIDE),
        (PARTS, 4, 8, PART, D),
        (D, 2 * FF),
        (FF, D),
        None,
        (ROWS, FF),
        (ROWS, 2 * FF),
        (PARTS, 4, 8, PART, WIDE),
        (PARTS, 4, 8, PART, D),
        (D, 2 * FF),
        (FF, D),
    )
    return pl.pallas_call(
        experts_kernel,
        name="experts",
        out_shape=tuple(jax.ShapeDtypeStruct(shape, BF16) for shape in outs),
        in_specs=[anywhere] * 7,
        out_specs=(anywhere,) * 5,
        scratch_shapes=[vmem(shape, BF16) if shape else vmem((ROWS, FF), F32) for shape in held]
        + [dma((84,)), dma((84,)), dma((15,)), dma((7,))],
        compiler_params=pltpu.CompilerParams(
            collective_id=2, has_side_effects=True, vmem_limit_bytes=60 * 1024 * 1024
        ),
        cost_estimate=pl.CostEstimate(
            flops=33_000_000_000, bytes_accessed=60_000_000, transcendentals=1_200_000
        ),
    )(*operands)


UP_PART = D // 4
UP_HALF = UP_PART // 2
DOWN_PART = D // 4
DOWN_HALF = FF // 2


def read_gains(small):
    select = hot(iota((8, SMALL), 1) == iota((8, SMALL), 0) + EXPERTS)
    select = jnp.where(iota((8, SMALL), 0) < 2, select, jnp.zeros_like(select))
    return mul(select, small, NT), select


def fill_bias(lengths, bias, x):
    first = lengths[0, 0]
    second = first + lengths[0, 1]
    third = second + lengths[0, 2]
    own = x * COUNT + iota((1, COUNT), 1)
    own_seg = sum(jnp.where(own >= end, 1, 0) for end in (first, second, third))

    def step(i, carry):
        base = pl.multiple_of(i * COUNT, COUNT)
        key = base + iota((COUNT, 1), 0)
        key_seg = sum(jnp.where(key >= end, 1, 0) for end in (first, second, third))
        allowed = (key_seg == own_seg) & (key <= own)
        bias[pl.ds(base, COUNT), :] = jnp.where(allowed, 0.0, -1e30)
        return carry

    lax.fori_loop(0, GROUP_ROWS // COUNT, step, 0)


def turn(v, cosd, sind):
    return v * cosd + pltpu.roll(v, HEAD_DIM // 2, 1) * sind


def forward_kernel(
    lengths, tokens, wq_in, wb_in, named, cosd, sind, hot_a_in, hot_b_in, dy_a_in, dy_b_in,
    q_out, kv_out, attended_out, middle_out, normed_out, tops, totals, gates_out,
    nf_a, nf_b, dy_rows,
    wq, wb, kv, own_kv, bias, vt, q, attended, middle, normed, nf,
    hot_a, hot_b, dy_a, dy_b, stage_a, stage_b, send, recv, local, load_sem,
):
    at = place()
    y, z, c, x = at
    line_y, line_z = lines(y, z, c, x)
    peers = [device(y, z, c, (x + d) % 4) for d in (1, 2, 3)]
    pairs = (
        (wb_in.at[:, pl.ds(D, SMALL)], wb.at[:, pl.ds(D, SMALL)]),
        (wq_in.at[:, pl.ds(D, 512)], wq.at[:, pl.ds(D, 512)]),
        (hot_a_in, hot_a), (dy_a_in, dy_a), (hot_b_in, hot_b), (dy_b_in, dy_b),
        (wq_in.at[:, pl.ds(0, D)], wq.at[:, pl.ds(0, D)]),
        (wb_in.at[:, pl.ds(0, D)], wb.at[:, pl.ds(0, D)]),
    )
    loads = [
        pltpu.make_async_copy(src, dst, load_sem.at[i]) for i, (src, dst) in enumerate(pairs)
    ]
    for load in loads:
        load.start()
    greet(cross(*at) + peers)
    moves = Moves(send, recv, local)
    loads[0].wait()
    small = wb[:, D:]
    gains, _ = read_gains(small)
    xf = tokens[...].astype(F32)
    inverse = lax.rsqrt(jnp.mean(xf * xf, axis=1, keepdims=True) + norm_eps)
    normed[...] = (xf * inverse * gains[0:1, :]).astype(BF16)
    loads[1].wait()
    for j in range(2):
        part = mul(normed[...], wq[:, D + j * 256 : D + (j + 1) * 256])
        if j == 0:
            for h in range(2):
                lanes = slice(h * HEAD_DIM, (h + 1) * HEAD_DIM)
                own_kv[:, lanes] = turn(part[:, lanes], cosd[...], sind[...]).astype(BF16)
        else:
            own_kv[:, 256:512] = part.astype(BF16)
    rows = pl.ds(pl.multiple_of(x * COUNT, COUNT), COUNT)
    pushes = [moves.push(own_kv, kv.at[rows], peer) for peer in peers]
    kv[rows, :] = own_kv[...]
    for load in loads[2:6]:
        load.wait()
    for piece in range(PARTS):
        to_slots(hot_a, dy_a, stage_a, piece)
        to_slots(hot_b, dy_b, stage_b, piece)
    dy_waits = deliver(moves, at, stage_a, stage_b, dy_rows, HALF, slice(None))
    fill_bias(lengths, bias, x)
    loads[6].wait()

    def query_tile(j, carry):
        lanes = pl.ds(pl.multiple_of(j * 256, 256), 256)
        part = mul(normed[...], wq[:, lanes])
        q[:, lanes] = jnp.concatenate(
            [turn(part[:, h * 128 : (h + 1) * 128], cosd[...], sind[...]) for h in range(2)],
            axis=1,
        ).astype(BF16)
        return carry

    lax.fori_loop(0, D // 256, query_tile, 0, unroll=True)

    logits = jnp.where(named[...] > 0, mul(tokens[...], small), -jnp.inf)
    weight = jnp.exp(logits - jnp.max(logits, axis=1, keepdims=True))
    gates = weight / jnp.sum(weight, axis=1, keepdims=True)
    gates_out[...] = gates
    for push in pushes:
        push.wait_recv()
    stays = [moves.keep(q, q_out), moves.keep(normed, normed_out), moves.keep(kv, kv_out)]
    for g in range(HEADS_KV):
        vt[g] = kv[:, 256 + g * 128 : 384 + g * 128].T
    for g in range(HEADS_KV):

        def head(i, carry, g=g):
            h = g * REPEAT + i
            lanes = pl.ds(pl.multiple_of(h * HEAD_DIM, HEAD_DIM), HEAD_DIM)
            s = mul(kv[:, g * 128 : (g + 1) * 128], q[:, lanes], NT) * SCALE + bias[...]
            top = jnp.max(s, axis=0, keepdims=True)
            p = jnp.exp(s - top)
            total = jnp.sum(p, axis=0, keepdims=True)
            tops[pl.ds(h, 1), :] = top
            totals[pl.ds(h, 1), :] = total
            low = (p * (1.0 / total)).astype(BF16)
            attended[:, lanes] = mul(vt[g], low).T.astype(BF16)
            return carry

        lax.fori_loop(0, REPEAT, head, 0, unroll=3)

    loads[7].wait()

    def out_tile(j, carry):
        lanes = pl.ds(pl.multiple_of(j * 256, 256), 256)
        middle[:, lanes] = tokens[:, lanes].astype(F32) + mul(attended[...], wb[lanes, 0:D], NT)
        return carry

    lax.fori_loop(0, D // 256, out_tile, 0, unroll=True)
    m = middle[...]
    inverse = lax.rsqrt(jnp.mean(m * m, axis=1, keepdims=True) + norm_eps)
    stays += [moves.keep(attended, attended_out), moves.keep(middle, middle_out)]
    high, mid, low = (third.astype(F32) for third in thirds(gates))
    held = high + pltpu.roll(mid, EXPERTS, 1) + pltpu.roll(low, 2 * EXPERTS, 1)
    nf[:, 0:LANES] = held.astype(BF16)
    nf[:, LANES:] = (m * inverse * gains[1:2, :]).astype(BF16)
    half_a, half_b = nf.at[:, pl.ds(0, WIDE_A)], nf.at[:, pl.ds(WIDE_A, WIDE_B)]
    last = [
        around(moves, half_a, nf_a, y, line_y[0], line_y[2]),
        around(moves, half_b, nf_b, z, line_z[0], line_z[2]),
    ]
    stays += [moves.keep(half_a, nf_a.at[y]), moves.keep(half_b, nf_b.at[z])]
    for wait in last[0]() + last[1]():
        wait()
    for stay in stays:
        stay.wait()
    for wait in dy_waits:
        wait()
    moves.drain()


def run_forward(*operands):
    anywhere = pl.BlockSpec(memory_space=pltpu.HBM)
    inside = pl.BlockSpec(memory_space=pltpu.VMEM)
    vmem, dma = pltpu.VMEM, pltpu.SemaphoreType.DMA
    shape = jax.ShapeDtypeStruct
    return pl.pallas_call(
        forward_kernel,
        name="forward",
        out_shape=(
            shape((COUNT, D), BF16),
            shape((GROUP_ROWS, 512), BF16),
            shape((COUNT, D), BF16),
            shape((COUNT, D), F32),
            shape((COUNT, D), BF16),
            shape((16, COUNT), F32),
            shape((16, COUNT), F32),
            shape((COUNT, 128), F32),
            shape((4, COUNT, WIDE_A), BF16),
            shape((4, COUNT, WIDE_B), BF16),
            shape((PARTS, 4, 8, PART, D), BF16),
        ),
        in_specs=[pl.BlockSpec(memory_space=pltpu.SMEM), inside, anywhere, anywhere]
        + [inside] * 3
        + [anywhere] * 4,
        out_specs=(anywhere,) * 5 + (inside,) * 3 + (anywhere,) * 3,
        scratch_shapes=[
            vmem((D, WA), BF16),
            vmem((D, WB), BF16),
            vmem((GROUP_ROWS, 512), BF16),
            vmem((COUNT, 512), BF16),
            vmem((GROUP_ROWS, COUNT), F32),
            vmem((HEADS_KV, HEAD_DIM, GROUP_ROWS), BF16),
            vmem((COUNT, D), BF16),
            vmem((COUNT, D), BF16),
            vmem((COUNT, D), F32),
            vmem((COUNT, D), BF16),
            vmem((COUNT, WIDE), BF16),
            vmem((4, COUNT, SLOTS), BF16),
            vmem((4, COUNT, SLOTS), BF16),
            vmem((4, COUNT, HALF), BF16),
            vmem((4, COUNT, HALF), BF16),
            *(vmem((PARTS, 8, 4, PART, HALF), BF16),) * 2,
            dma((3 + 14 + 8,)),
            dma((3 + 14 + 8,)),
            dma((2 + 7,)),
            dma((8,)),
        ],
        compiler_params=pltpu.CompilerParams(
            collective_id=3, has_side_effects=True, vmem_limit_bytes=60 * 1024 * 1024
        ),
        cost_estimate=pl.CostEstimate(
            flops=6_000_000_000, bytes_accessed=30_000_000, transcendentals=3_200_000
        ),
    )(*operands)


def norm_grad(values, gain, grad):
    inverse = lax.rsqrt(jnp.mean(values * values, axis=1, keepdims=True) + norm_eps)
    unit = values * inverse
    scaled = grad * gain
    drop = jnp.mean(scaled * unit, axis=1, keepdims=True)
    return inverse * (scaled - unit * drop), jnp.sum(grad * unit, axis=0, keepdims=True)


def backward_kernel(
    lengths, tokens_in, cotangent_in, gates, queries_in, kv_src, attended_in, middle_in, normed_in,
    tops, totals, cosd, sind, wq_in, wb_in, hot_a_in, hot_b_in,
    back_a_in, back_b_in, out_in, up_in, down_in,
    grad_tokens, grad_qkv_out, grad_out_out, grad_small, up_far, down_far,
    late_a, late_b, came_a, came_b,
    tokens, cotangent, queries, kv_in, attended, middle, normed,
    wq, wb, hot_a, hot_b, back_a, back_b,
    part_a, part_b, land_a, land_b, down_own, down_got,
    bias, kt, gn, gmid, gb, gatt, gp, dk, dv, leave, land, grad_qkv,
    send, recv, local, load_sem, empty,
):
    at = place()
    y, z, c, x = at
    line_y, line_z = lines(y, z, c, x)
    peers = [device(y, z, c, (x + d) % 4) for d in (1, 2, 3)]
    pairs = (
        (back_a_in, back_a), (hot_a_in, hot_a), (back_b_in, back_b), (hot_b_in, hot_b),
        (kv_src, kv_in), (wb_in, wb), (middle_in, middle), (cotangent_in, cotangent),
        (queries_in, queries), (attended_in, attended), (tokens_in, tokens),
        (normed_in, normed), (wq_in, wq),
    )
    pairs += tuple(
        (
            down_in.at[
                pl.ds(half * DOWN_HALF, DOWN_HALF),
                pl.ds(pl.multiple_of(((x + d) % 4) * DOWN_PART, 128), DOWN_PART),
            ],
            down_own.at[half],
        )
        for half, d in ((0, 3), (1, 1))
    )
    loads = [
        pltpu.make_async_copy(src, dst, load_sem.at[i]) for i, (src, dst) in enumerate(pairs)
    ]
    for load in loads:
        load.start()
    greet(cross(*at) + peers)
    link = Moves(send, recv, local)
    for load in loads[:4]:
        load.wait()
    part_waits = []
    for hits, back, parts, land_here, me, line, width in (
        (hot_a, back_a, part_a, land_a, y, line_y, WIDE_A),
        (hot_b, back_b, part_b, land_b, z, line_z, WIDE_B),
    ):
        for d in (1, 2, 3):
            parts[d - 1] = add_up(hits, back, (me + d) % 4, width)
            push = link.push(parts.at[d - 1], land_here.at[me], line[d - 1])
            part_waits.append(push.wait_recv)
        land_here[pl.ds(me, 1)] = add_up(hits, back, me, width)[None]
    for peer in cross(*at):
        pl.semaphore_signal(empty, inc=1, device_id=peer, device_id_type=MESH)
    facing = (x + 2) % 4
    pushes, down_pushes = [], []
    for half, peer in ((0, peers[2]), (1, peers[0])):
        up_rows = pl.ds(pl.multiple_of(facing * UP_PART + half * UP_HALF, UP_HALF), UP_HALF)
        pushes.append(link.push(up_in.at[up_rows], up_far.at[half], peer))
        lanes = pl.ds(pl.multiple_of(facing * DOWN_PART, 128), DOWN_PART)
        down_rows = pl.ds(half * DOWN_HALF, DOWN_HALF)
        down_pushes.append(link.push(down_in.at[down_rows, lanes], down_got.at[half], peer))
    fill_bias(lengths, bias, x)
    for load in loads[4:]:
        load.wait()
    for g in range(HEADS_KV):
        kt[g] = kv_in[:, g * 128 : (g + 1) * 128].T
    for wait in part_waits:
        wait()
    pl.semaphore_wait(empty, 13)
    out_waits = give_back(link, at, out_in, back_a, back_b, HALF, slice(None))
    total = land_a[0].astype(F32)
    for s in range(1, 4):
        total = total + land_a[s].astype(F32)
    slopes = total[:, 0:LANES]
    gn[:, 0 : WIDE_A - LANES] = total[:, LANES:]
    total = land_b[0].astype(F32)
    for s in range(1, 4):
        total = total + land_b[s].astype(F32)
    gn[:, WIDE_A - LANES :] = total
    gains, select = read_gains(wb[:, D:])
    moved, ffn_gain = norm_grad(middle[...], gains[1:2, :], gn[...])
    gm = cotangent[...].astype(F32) + moved
    gmid[...] = gm
    gb[...] = gm.astype(BF16)

    def att_tile(j, carry):
        lanes = pl.ds(pl.multiple_of(j * 256, 256), 256)
        gatt[:, lanes] = mul(gb[...], wb[:, lanes]).astype(BF16)
        return carry

    lax.fori_loop(0, D // 256, att_tile, 0, unroll=True)
    kv_pushes = []
    for g in range(HEADS_KV):
        dk[...] = jnp.zeros_like(dk)
        dv[...] = jnp.zeros_like(dv)

        def head(i, carry, g=g):
            h = g * REPEAT + i
            lanes = pl.ds(pl.multiple_of(h * HEAD_DIM, HEAD_DIM), HEAD_DIM)
            s = mul(kv_in[:, g * 128 : (g + 1) * 128], queries[:, lanes], NT) * SCALE + bias[...]
            p = jnp.exp(s - tops[pl.ds(h, 1), :]) * (1.0 / totals[pl.ds(h, 1), :])
            dv[...] += mul(p.astype(BF16), gatt[:, lanes])
            t = p * mul(kv_in[:, 256 + g * 128 : 384 + g * 128], gatt[:, lanes], NT)
            ds = (t - p * jnp.sum(t, axis=0, keepdims=True)).astype(BF16)
            dk[...] += mul(ds, queries[:, lanes])
            dq = mul(kt[g], ds).T * SCALE
            gp[:, lanes] = turn(dq, cosd[...], -sind[...]).astype(BF16)
            return carry

        lax.fori_loop(0, REPEAT, head, 0, unroll=3)
        leave[g, :, 0:128] = (dk[...] * SCALE).astype(BF16)
        leave[g, :, 128:256] = dv[...].astype(BF16)
        for d in (1, 2, 3):
            away = pl.ds(pl.multiple_of(((x + d) % 4) * COUNT, COUNT), COUNT)
            kv_pushes.append(link.push(leave.at[g, away], land.at[g, d - 1], peers[d - 1]))

    def out_tile(j, carry):
        lanes = pl.ds(pl.multiple_of(j * 256, 256), 256)
        grad_qkv[lanes, 0:D] = mul(gb[:, lanes], attended[...], TN).astype(BF16)
        return carry

    lax.fori_loop(0, D // 256, out_tile, 0, unroll=True)

    out_kept = link.keep(grad_qkv.at[:, pl.ds(0, D)], grad_out_out)

    for push in down_pushes:
        push.wait_recv()
    for half, (peer, part) in enumerate(((peers[2], (x + 3) % 4), (peers[0], (x + 1) % 4))):
        down_own[half] = (down_own[half].astype(F32) + down_got[half].astype(F32)).astype(BF16)
        lanes = pl.ds(pl.multiple_of(part * DOWN_PART, 128), DOWN_PART)
        here, rest = (pl.ds(k * DOWN_HALF, DOWN_HALF) for k in (half, 1 - half))
        pushes.append(link.push(down_own.at[half], down_far.at[half, here], peer))
        pushes.append(link.push(down_in.at[rest, lanes], down_far.at[half, rest], peer))

    gate_grad = slopes + pltpu.roll(slopes, 128 - EXPERTS, 1) + pltpu.roll(
        slopes, 128 - 2 * EXPERTS, 1
    )
    weighted = gates[...] * gate_grad
    logit_grad = weighted - gates[...] * jnp.sum(weighted, axis=1, keepdims=True)
    parts = thirds(logit_grad)
    router_grad = sum(mul(tokens[...], part, TN) for part in parts)
    small = wb[:, D:]

    for wait in out_waits:
        wait()
    for s in range(4):
        land_a[s, :, 0:HALF] = add_up(hot_a, back_a, s, HALF)
        land_b[s, :, 0:HALF] = add_up(hot_b, back_b, s, HALF)
    first, second, lanes = pl.ds(0, COUNT // 2), pl.ds(COUNT // 2, COUNT // 2), pl.ds(0, HALF)
    late, stays = [], []
    for summed, came, left, me, line in (
        (land_a, came_a, late_a, y, line_y),
        (land_b, came_b, late_b, z, line_z),
    ):
        for d in (1, 2, 3):
            push = link.push(summed.at[(me + d) % 4, first, lanes], came.at[me], line[d - 1])
            late.append(push.wait_recv)
        stays.append(link.keep(summed.at[me, first, lanes], came.at[me]))
        stays.append(link.keep(summed.at[:, second, lanes], left))

    for push in kv_pushes:
        push.wait_recv()
    mine = pl.ds(pl.multiple_of(x * COUNT, COUNT), COUNT)
    for g in range(HEADS_KV):
        total = leave[g, mine, :].astype(F32)
        for d in range(3):
            total = total + land[g, d].astype(F32)
        gp[:, D + g * 128 : D + (g + 1) * 128] = turn(
            total[:, 0:128], cosd[...], -sind[...]
        ).astype(BF16)
        gp[:, D + 256 + g * 128 : D + 384 + g * 128] = total[:, 128:256].astype(BF16)
    out_kept.wait()

    def qkv_tile(j, carry):
        lanes = pl.ds(pl.multiple_of(j * 256, 256), 256)
        grad_qkv[lanes, :] = mul(normed[:, lanes], gp[...], TN).astype(BF16)
        gn[:, lanes] = mul(gp[...], wq[lanes, :], NT)
        return carry

    lax.fori_loop(0, D // 256, qkv_tile, 0, unroll=True)
    stays.append(link.keep(grad_qkv, grad_qkv_out))
    moved, attn_gain = norm_grad(tokens[...].astype(F32), gains[0:1, :], gn[...])
    from_router = sum(mul(part, small, NT) for part in parts)
    grad_tokens[...] = (gmid[...] + moved + from_router).astype(BF16)
    both = jnp.where(
        iota((8, D), 0) == 0, attn_gain, jnp.where(iota((8, D), 0) == 1, ffn_gain, 0.0)
    )
    gain_columns = sum(mul(part, select, TN) for part in thirds(both))
    grad_small[...] = (router_grad + gain_columns).astype(BF16)
    for push in pushes:
        push.wait_recv()
    for wait in late:
        wait()
    for stay in stays:
        stay.wait()
    link.drain()


def run_backward(*operands):
    anywhere = pl.BlockSpec(memory_space=pltpu.HBM)
    inside = pl.BlockSpec(memory_space=pltpu.VMEM)
    vmem, dma = pltpu.VMEM, pltpu.SemaphoreType.DMA
    shape = jax.ShapeDtypeStruct
    return pl.pallas_call(
        backward_kernel,
        name="backward",
        out_shape=(
            shape((COUNT, D), BF16),
            shape((D, WA), BF16),
            shape((D, D), BF16),
            shape((D, SMALL), BF16),
            shape((2, UP_HALF, 2 * FF), BF16),
            shape((2, FF, DOWN_PART), BF16),
            *(shape((4, COUNT // 2, HALF), BF16),) * 4,
        ),
        in_specs=[pl.BlockSpec(memory_space=pltpu.SMEM)]
        + [anywhere] * 2
        + [inside]
        + [anywhere] * 5
        + [inside] * 4
        + [anywhere] * 9,
        out_specs=(inside, anywhere, anywhere, inside) + (anywhere,) * 6,
        scratch_shapes=[
            vmem((COUNT, D), BF16),
            vmem((COUNT, D), BF16),
            vmem((COUNT, D), BF16),
            vmem((GROUP_ROWS, 512), BF16),
            vmem((COUNT, D), BF16),
            vmem((COUNT, D), F32),
            vmem((COUNT, D), BF16),
            vmem((D, WA), BF16),
            vmem((D, WB), BF16),
            vmem((4, COUNT, SLOTS), BF16),
            vmem((4, COUNT, SLOTS), BF16),
            vmem((PARTS, 8, 4, PART, WIDE_A), BF16),
            vmem((PARTS, 8, 4, PART, WIDE_B), BF16),
            vmem((3, COUNT, WIDE_A), BF16),
            vmem((3, COUNT, WIDE_B), BF16),
            vmem((4, COUNT, WIDE_A), BF16),
            vmem((4, COUNT, WIDE_B), BF16),
            vmem((2, DOWN_HALF, DOWN_PART), BF16),
            vmem((2, DOWN_HALF, DOWN_PART), BF16),
            vmem((GROUP_ROWS, COUNT), F32),
            vmem((HEADS_KV, HEAD_DIM, GROUP_ROWS), BF16),
            vmem((COUNT, D), F32),
            vmem((COUNT, D), F32),
            vmem((COUNT, D), BF16),
            vmem((COUNT, D), BF16),
            vmem((COUNT, WA), BF16),
            vmem((GROUP_ROWS, HEAD_DIM), F32),
            vmem((GROUP_ROWS, HEAD_DIM), F32),
            vmem((HEADS_KV, GROUP_ROWS, 256), BF16),
            vmem((HEADS_KV, 3, COUNT, 256), BF16),
            vmem((D, WA), BF16),
            dma((6 + 4 + 14 + 6 + 6 + 4,)),
            dma((6 + 4 + 14 + 6 + 6 + 4,)),
            dma((2 + 4 + 2,)),
            dma((15,)),
            pltpu.SemaphoreType.REGULAR,
        ],
        compiler_params=pltpu.CompilerParams(
            collective_id=4, has_side_effects=True, vmem_limit_bytes=60 * 1024 * 1024
        ),
        cost_estimate=pl.CostEstimate(
            flops=13_000_000_000, bytes_accessed=50_000_000, transcendentals=3_200_000
        ),
    )(*operands)


def finish_kernel(
    sum_a, sum_b, up, down, out, tokens,
    output, grad_tokens, grad_qkv, grad_out_t, grad_attn, grad_ffn, grad_router, grad_up, grad_down,
):
    output[...] = out[...]
    grad_tokens[...] = tokens[...]
    grad_qkv[...] = sum_a[0:PIECE, :]
    grad_out_t[...] = sum_b[0:PIECE, 0:D]
    small = sum_b[0:PIECE, D:]
    grad_router[...] = small[:, 0:EXPERTS]
    diagonal = iota((PIECE, SMALL), 0) == iota((PIECE, SMALL), 1)
    for k, gain in enumerate((grad_attn, grad_ffn)):
        lanes = iota((PIECE, SMALL), 1) == EXPERTS + k
        column = jnp.sum(jnp.where(lanes, small, 0.0), axis=1, keepdims=True)
        row = jnp.sum(jnp.where(diagonal, column, 0.0), axis=0, keepdims=True)
        gain[...] = row[:, 0:PIECE]
    grad_up[...] = up[...]
    grad_down[...] = down[...]


def finish(*operands):
    inside = pl.BlockSpec(memory_space=pltpu.VMEM)
    shape = jax.ShapeDtypeStruct
    return pl.pallas_call(
        finish_kernel,
        name="finish",
        out_shape=(
            shape((COUNT, D), BF16),
            shape((COUNT, D), BF16),
            shape((PIECE, WA), F32),
            shape((PIECE, D), F32),
            shape((1, PIECE), F32),
            shape((1, PIECE), F32),
            shape((PIECE, EXPERTS), F32),
            shape((UP_PART, 2 * FF), F32),
            shape((FF, DOWN_PART), F32),
        ),
        in_specs=[inside] * 6,
        out_specs=(inside,) * 9,
        compiler_params=pltpu.CompilerParams(vmem_limit_bytes=32 * 1024 * 1024),
    )(*operands)


def body(
    tokens, lengths, top_experts, w_qkv, w_out, gain_attn, gain_ffn, router, gate_up, down_proj, cotangent,
):
    half = HEAD_DIM // 2
    rates = rope_base ** (-(np.arange(HEAD_DIM, dtype=np.float32) % half) / half)
    full_a, full_b, named, hot_a, hot_b, dy_a, dy_b, cosd, sind = gather_weights(
        lengths, jnp.asarray(rates.astype(np.float32))[None], w_qkv, w_out.T, router,
        gain_attn[None], gain_ffn[None], top_experts.T, cotangent,
    )
    wq = full_a.reshape(D, WA)
    wb = full_b.reshape(D, WB)
    (
        queries, kv, attended, middle, normed, tops, totals, gates, nf_a, nf_b, dy_rows,
    ) = run_forward(
        lengths, tokens, wq, wb, named, cosd, sind, hot_a, hot_b, dy_a, dy_b
    )
    back_a, back_b, expert_out, up_local, down_local = run_experts(
        hot_a, hot_b, nf_a, nf_b, dy_rows, gate_up, down_proj
    )
    grad_tokens, grad_qkv, grad_out, grad_small, *passed_on = run_backward(
        lengths, tokens, cotangent, gates, queries, kv, attended, middle, normed, tops, totals,
        cosd, sind, wq, wb, hot_a, hot_b, back_a, back_b, expert_out, up_local, down_local,
    )
    sum_a, sum_b, up_sum, down_sum, output = scatter_sums(
        grad_qkv.reshape(4, 4, 2, BLOCK, WA),
        grad_out.reshape(4, 4, 2, BLOCK, D),
        grad_small.reshape(4, 4, 2, BLOCK, SMALL),
        up_local,
        down_local,
        *passed_on,
        middle,
    )
    (
        output, grad_tokens, grad_qkv, grad_out_t, grad_attn, grad_ffn, grad_router, up_sum, down_sum,
    ) = finish(sum_a, sum_b, up_sum, down_sum, output, grad_tokens)
    return (
        output,
        grad_tokens,
        grad_qkv,
        grad_out_t.T,
        grad_attn[0],
        grad_ffn[0],
        grad_router,
        up_sum[None],
        down_sum[None],
    )


def solution(mesh):
    return jax.shard_map(
        body,
        mesh=mesh,
        in_specs=(
            P(("expert", "shard"), None),
            P("expert", None),
            P(("expert", "shard"), None),
            P(("expert", "shard"), None),
            P(None, ("expert", "shard")),
            P(("expert", "shard")),
            P(("expert", "shard")),
            P(("expert", "shard"), None),
            P("expert", None, None),
            P("expert", None, None),
            P(("expert", "shard"), None),
        ),
        out_specs=(
            P(("expert", "shard"), None),
            P(("expert", "shard"), None),
            P(("expert", "shard"), None),
            P(None, ("expert", "shard")),
            P(("expert", "shard")),
            P(("expert", "shard")),
            P(("expert", "shard"), None),
            P("expert", "shard", None),
            P("expert", None, "shard"),
        ),
        check_vma=False,
    )
```

```python
import jax
import jax.numpy as jnp
import numpy as np
from jax import lax
from jax.experimental import pallas as pl
from jax.experimental.pallas import tpu as pltpu
from jax.sharding import PartitionSpec as P

D = 1536
HEADS_Q = 12
HEADS_KV = 2
HEAD_DIM = 128
FF = 768
TOP = 4
EXPERTS = 32
CAP = 48
WIDTH_Q = HEADS_Q * HEAD_DIM
WIDTH_KV = HEADS_KV * HEAD_DIM
REPEAT = HEADS_Q // HEADS_KV

norm_eps = 1e-06
rope_base = 1000000.0
MESH = pl.DeviceIdType.MESH
F32 = jnp.float32
BF16 = jnp.bfloat16

PIECE = 12
PADDED = 16
BLOCK = 48
WA = 2048
WB = 1664
SMALL = WB - D
QUARTER = WA // 4


def place():
    e = lax.axis_index("expert")
    return e // 8, (e // 2) % 4, e % 2, lax.axis_index("shard")


def device(y, z, c, x):
    return ((y * 4 + z) * 2 + c, x)


def greet(devices):
    barrier = pltpu.get_barrier_semaphore()
    for d in devices:
        pl.semaphore_signal(barrier, inc=1, device_id=d, device_id_type=MESH)
    pl.semaphore_wait(barrier, len(devices))


class Links:
    def __init__(self, send, recv):
        self.send, self.recv, self.made = send, recv, []

    def push(self, src, dst, where):
        i = len(self.made)
        copy = pltpu.make_async_remote_copy(
            src_ref=src,
            dst_ref=dst,
            send_sem=self.send.at[i],
            recv_sem=self.recv.at[i],
            device_id=where,
            device_id_type=MESH,
        )
        copy.start()
        self.made.append(copy)
        return copy

    def drain(self):
        for copy in self.made:
            copy.wait_send()


def neighbours(y, z, c, x):
    other = 1 - c
    return dict(
        x=[device(y, z, c, (x + d) % 4) for d in (1, 2, 3)],
        y=(device((y + 1) % 4, z, c, x), device((y + 3) % 4, z, c, x)),
        z=(device(y, (z + 1) % 4, c, x), device(y, (z + 3) % 4, c, x)),
        core=device(y, z, other, x),
    )


def everyone_near(near):
    return list(near["x"]) + list(near["y"]) + list(near["z"]) + [near["core"]]


def pick_rows(rows, columns, row_block, column_block):
    r = lax.broadcasted_iota(jnp.int32, (rows, columns), 0)
    q = lax.broadcasted_iota(jnp.int32, (rows, columns), 1)
    same = (r // row_block == q // column_block) & (r % row_block == q % column_block)
    return jnp.where(same, 1.0, 0.0).astype(BF16)


def faces(y, z, c, x):
    along_z, along_y = [], []
    for d in range(4):
        for k in range(2):
            core = c if k == 0 else 1 - c
            along_z.append((device(y, (z + d) % 4, core, x), (z + d) % 4, core))
            along_y.append((device((y + d) % 4, z, core, x), (y + d) % 4, core))
    return along_z, along_y


def cross(y, z, c, x):
    along_z, along_y = faces(y, z, c, x)
    return [f[0] for f in along_z[1:] + along_y[2:]]


def lines(y, z, c, x):
    return (
        [device((y + d) % 4, z, c, x) for d in (1, 2, 3)],
        [device(y, (z + d) % 4, c, x) for d in (1, 2, 3)],
    )


def route(top_experts, named, own_slot):
    experts = iota((EXPERTS, COUNT), 0)
    names = sum(jnp.where(top_experts[k : k + 1, :] == experts, 1.0, 0.0) for k in range(TOP))
    low = names.astype(BF16)
    earlier = hot(iota((COUNT, COUNT), 0) < iota((COUNT, COUNT), 1))
    own_slot[...] = jnp.where(names > 0, mul(low, earlier), -1.0).astype(BF16)
    named[...] = mul(low, hot(iota((EXPERTS, 128), 0) == iota((EXPERTS, 128), 1)), TN)


def rope(lengths, rates, cosd, sind, x):
    own = x * COUNT + iota((COUNT, 1), 0)
    first = lengths[0, 0]
    second = first + lengths[0, 1]
    third = second + lengths[0, 2]
    start = jnp.zeros((COUNT, 1), jnp.int32)
    for end in (first, second, third):
        start = jnp.where(own >= end, end, start)
    angles = (own - start).astype(F32) * rates[...]
    cosd[...] = jnp.cos(angles)
    sine = jnp.sin(angles)
    sind[...] = jnp.where(iota((COUNT, HEAD_DIM), 1) < HEAD_DIM // 2, -sine, sine)


def fill_pack(pack, w_qkv, w_out_t, router, gain_attn, gain_ffn):
    pack[...] = jnp.zeros_like(pack)
    pack[0:PIECE, 0:WA] = w_qkv[...]
    pack[0:PIECE, WA : WA + D] = w_out_t[...]
    small = mul(router[...], hot(iota((EXPERTS, SMALL), 0) == iota((EXPERTS, SMALL), 1)))
    diagonal = iota((PIECE, PIECE), 0) == iota((PIECE, PIECE), 1)
    for k, gain in enumerate((gain_attn, gain_ffn)):
        column = jnp.sum(jnp.where(diagonal, gain[...].astype(F32), 0.0), axis=1, keepdims=True)
        small = jnp.where(iota((PIECE, SMALL), 1) == EXPERTS + k, column, small)
    pack[0:PIECE, WA + D :] = small.astype(BF16)


def slot_hits(slot_of, hits, experts):
    p = iota((1, SLOTS), 1)
    q = p % PIECE_SLOTS
    wanted = ((p // PIECE_SLOTS) * PART + q % PART).astype(F32)
    local = q // PART
    expand = hot(iota((EXPERTS, SLOTS), 0) == experts(local))

    def step(s, carry):
        hits[s] = hot(mul(slot_of[s], expand, TN) == wanted)
        return carry

    lax.fori_loop(0, 4, step, 0)


def gather_kernel(
    lengths, rates, w_qkv, w_out_t, router, gain_attn, gain_ffn, top_experts, cotangent,
    full_a, full_b, named, hot_a, hot_b, dy_a, dy_b, cosd, sind,
    pack, xbuf, own_0, own_1, own_2, own_slot, slot_y, slot_z, send, recv, local,
):
    y, z, c, x = place()
    near = neighbours(y, z, c, x)
    line_y, line_z = lines(y, z, c, x)
    fill_pack(pack, w_qkv, w_out_t, router, gain_attn, gain_ffn)
    greet(everyone_near(near) + [line_y[1], line_z[1]])
    link = Links(send, recv)
    first = [link.push(pack, xbuf.at[x], near["x"][d]) for d in range(3)]
    xbuf[pl.ds(x, 1)] = pack[...][None]
    half_a, half_b = cotangent.at[:, pl.ds(0, HALF)], cotangent.at[:, pl.ds(HALF, HALF)]
    kept = [
        pltpu.make_async_copy(half_a, dy_a.at[y], local.at[2]),
        pltpu.make_async_copy(half_b, dy_b.at[z], local.at[3]),
    ]
    for copy in kept:
        copy.start()
    dys = [
        around(link, half_a, dy_a, y, *near["y"]),
        around(link, half_b, dy_b, z, *near["z"]),
    ]
    for copy in first:
        copy.wait_recv()
    select = pick_rows(BLOCK, 4 * PADDED, PIECE, PADDED)
    pieces = xbuf[...].reshape(4 * PADDED, WA + WB)
    quarter = pl.multiple_of(x * QUARTER, QUARTER)
    mine = xbuf[:, :, pl.ds(quarter, QUARTER)].reshape(4 * PADDED, QUARTER)
    own_0[...] = mul(select, mine).astype(BF16)
    own_1[...] = mul(select, pieces[:, WA : WA + HALF]).astype(BF16)
    own_2[...] = mul(select, pieces[:, WA + HALF :]).astype(BF16)
    spot = dict(y=y, z=z)
    jobs = [
        dict(own=own_0, full=full_a, off=quarter, half=QUARTER // 2, close="y", far="z", i=0),
        dict(own=own_1, full=full_b, off=0, half=HALF // 2, close="y", far="z", i=1),
        dict(own=own_2, full=full_b, off=HALF, half=512, close="z", far="y", i=4),
    ]

    def block_at(j, far, close, first=0, count=None):
        yy, zz = (far, close) if j["far"] == "y" else (close, far)
        count = j["own"].shape[1] if count is None else count
        lanes = j["off"] + first
        lanes = lanes if isinstance(lanes, int) else pl.multiple_of(lanes, 128)
        return j["full"].at[yy, zz, c, :, pl.ds(lanes, count)]

    def line_at(j, far, start=0, count=4):
        return block_at(j, far, pl.ds(start, count))

    for j in jobs:
        j["p"], j["q"] = spot[j["close"]], spot[j["far"]]
        here = block_at(j, j["q"], j["p"])
        plus, minus = near[j["close"]]
        j["up"] = link.push(j["own"], here, plus)
        j["down"] = link.push(j["own"], here, minus)
        j["core"] = []
        if j["full"] is full_b:
            j["core"].append(link.push(j["own"], here, near["core"]))
        j["local"] = pltpu.make_async_copy(j["own"], here, local.at[j["i"]])
        j["local"].start()
    route(top_experts, named, own_slot)
    slot_y[pl.ds(y, 1)] = own_slot[...][None]
    slot_z[pl.ds(z, 1)] = own_slot[...][None]
    slots = [link.push(own_slot, slot_y.at[y], peer) for peer in line_y]
    slots += [link.push(own_slot, slot_z.at[z], peer) for peer in line_z]
    for j in jobs:
        plus, minus = near[j["close"]]
        left, right = (j["p"] + 3) % 4, (j["p"] + 1) % 4
        j["up"].wait_recv()
        part = block_at(j, j["q"], left, 0, j["half"])
        j["up2"] = link.push(part, part, plus)
        j["down"].wait_recv()
        part = block_at(j, j["q"], right, j["half"], j["own"].shape[1] - j["half"])
        j["down2"] = link.push(part, part, minus)
        if j["full"] is full_b:
            for side in (left, right):
                block = block_at(j, j["q"], side)
                j["core"].append(link.push(block, block, near["core"]))

    around_x = {}

    def quarter_at(far, which, start=0, count=4):
        lanes = pl.ds(pl.multiple_of(which * QUARTER, QUARTER), QUARTER)
        return full_a.at[pl.ds(start, count), far, c, :, lanes]

    def x_start(name, far):
        block = quarter_at(far, x)
        around_x[name] = [
            far, link.push(block, block, near["x"][0]), link.push(block, block, near["x"][2])
        ]

    def x_forward(name):
        far, up, down = around_x[name]
        up.wait_recv()
        part = quarter_at(far, (x + 3) % 4, 0, 2)
        up = link.push(part, part, near["x"][0])
        down.wait_recv()
        part = quarter_at(far, (x + 1) % 4, 2, 2)
        around_x[name] = [far, up, link.push(part, part, near["x"][2])]

    def x_done(name):
        far, up, down = around_x[name]
        up.wait_recv()
        down.wait_recv()
        line = full_a.at[:, far, c]
        jobs[0]["core"].append(link.push(line, line, near["core"]))

    def far_start(j):
        j["up2"].wait_recv()
        j["down2"].wait_recv()
        block = block_at(j, j["q"], (j["p"] + 2) % 4)
        j["local"].wait()
        plus, minus = near[j["far"]]
        line = line_at(j, j["q"])
        j["up"] = link.push(line, line, plus)
        j["down"] = link.push(line, line, minus)
        if j["full"] is full_b:
            j["core"].append(link.push(block, block, near["core"]))
        else:
            x_start("own", j["q"])

    far_start(jobs[0])
    far_start(jobs[2])
    dys = dys[0]() + dys[1]()
    for copy in slots:
        copy.wait_recv()
    def far_next(j):
        plus, minus = near[j["far"]]
        left, right = (j["q"] + 3) % 4, (j["q"] + 1) % 4
        j["up"].wait_recv()
        part = line_at(j, left, 0, 2)
        j["up2"] = link.push(part, part, plus)
        j["down"].wait_recv()
        part = line_at(j, right, 2, 2)
        j["down2"] = link.push(part, part, minus)
        if j["full"] is full_b:
            for side in (left, right):
                block = line_at(j, side)
                j["core"].append(link.push(block, block, near["core"]))
        else:
            x_start("left", left)
            x_start("right", right)

    def far_end(j):
        opposite = (j["q"] + 2) % 4
        j["up2"].wait_recv()
        j["down2"].wait_recv()
        if j["full"] is full_b:
            block = line_at(j, opposite)
            j["core"].append(link.push(block, block, near["core"]))
        else:
            x_start("opposite", opposite)

    far_next(jobs[0])
    far_start(jobs[1])
    x_forward("own")
    far_end(jobs[0])
    far_next(jobs[2])
    x_done("own")
    x_forward("left")
    x_forward("right")
    slot_hits(slot_y, hot_a, lambda e: y * 8 + e)
    far_next(jobs[1])
    slot_hits(slot_z, hot_b, lambda e: (e // 2) * 8 + z * 2 + e % 2)
    far_end(jobs[2])
    x_done("left")
    x_done("right")
    x_forward("opposite")
    far_end(jobs[1])
    rope(lengths, rates, cosd, sind, x)
    x_done("opposite")
    for j in jobs:
        for copy in j["core"]:
            copy.wait_recv()
    for wait in dys:
        wait()
    for copy in kept:
        copy.wait()
    link.drain()


def gather_weights(*operands):
    inside = pl.BlockSpec(memory_space=pltpu.VMEM)
    anywhere = pl.BlockSpec(memory_space=pltpu.HBM)
    copies = 3 + 2 * 15 + 8 + 16 + 4 + 6 + 8
    return pl.pallas_call(
        gather_kernel,
        name="gather_weights",
        out_shape=(
            jax.ShapeDtypeStruct((4, 4, 2, BLOCK, WA), BF16),
            jax.ShapeDtypeStruct((4, 4, 2, BLOCK, WB), BF16),
            jax.ShapeDtypeStruct((COUNT, 128), F32),
            jax.ShapeDtypeStruct((4, COUNT, SLOTS), BF16),
            jax.ShapeDtypeStruct((4, COUNT, SLOTS), BF16),
            jax.ShapeDtypeStruct((4, COUNT, HALF), BF16),
            jax.ShapeDtypeStruct((4, COUNT, HALF), BF16),
            jax.ShapeDtypeStruct((COUNT, HEAD_DIM), F32),
            jax.ShapeDtypeStruct((COUNT, HEAD_DIM), F32),
        ),
        in_specs=[pl.BlockSpec(memory_space=pltpu.SMEM)] + [inside] * 8,
        out_specs=(anywhere,) * 2 + (inside,) * 3 + (anywhere,) * 2 + (inside,) * 2,
        scratch_shapes=[
            pltpu.VMEM((PADDED, WA + WB), BF16),
            pltpu.VMEM((4, PADDED, WA + WB), BF16),
            pltpu.VMEM((BLOCK, QUARTER), BF16),
            pltpu.VMEM((BLOCK, HALF), BF16),
            pltpu.VMEM((BLOCK, WB - HALF), BF16),
            pltpu.VMEM((EXPERTS, COUNT), BF16),
            pltpu.VMEM((4, EXPERTS, COUNT), BF16),
            pltpu.VMEM((4, EXPERTS, COUNT), BF16),
            pltpu.SemaphoreType.DMA((copies,)),
            pltpu.SemaphoreType.DMA((copies,)),
            pltpu.SemaphoreType.DMA((5,)),
        ],
        compiler_params=pltpu.CompilerParams(
            collective_id=0, has_side_effects=True, vmem_limit_bytes=60 * 1024 * 1024
        ),
        cost_estimate=pl.CostEstimate(flops=0, bytes_accessed=24_000_000, transcendentals=0),
    )(*operands)


def add_blocks(dst, far, start, count, sources):
    def step(i, carry):
        total = dst[far, start + i].astype(F32)
        for source in sources:
            total = total + source(i).astype(F32)
        dst[far, start + i] = total.astype(BF16)
        return carry

    lax.fori_loop(0, count, step, 0)


def scatter_kernel(
    ga, gb, gs, up_in, down_in, up_far, down_far, late_a, late_b, came_a, came_b, middle,
    out_a, out_b, up_out, down_out, output,
    core_a, core_b, mine_a, mine_b, one_a, one_b, two_a, two_b,
    half_a0, half_a1, half_b0, half_b1, last_a, last_b, xout, xin,
    ups, downs, up_got, up_land, mid, land_a, land_b,
    send, recv, local,
):
    y, z, c, x = place()
    near = neighbours(y, z, c, x)
    line_y, line_z = lines(y, z, c, x)
    greet(everyone_near(near) + [line_y[1], line_z[1]])
    link = Links(send, recv)
    other = 1 - c
    jobs = [
        dict(src=[(lambda f, s: ga.at[f, :, s], 0, WA)], core=core_a, mine=mine_a, one=one_a, two=two_a,
             halves=(half_a0, half_a1), last=last_a, far="y", close="z", q=y, p=z,
             width=WA, half=1024, lane=0, i=0),
        dict(src=[(lambda f, s: gb.at[:, f, s], 0, D), (lambda f, s: gs.at[:, f, s], D, SMALL)],
             core=core_b, mine=mine_b, one=one_b, two=two_b,
             halves=(half_b0, half_b1), last=last_b, far="z", close="y", q=z, p=y,
             width=WB, half=896, lane=WA, i=1),
    ]
    slots = 0
    for step in (2, 3, 1, 0):
        for j in jobs:
            f = (j["q"] + step) % 4
            j[step] = []
            for source, lane, width in j["src"]:
                lanes = pl.ds(lane, width)
                pushed = link.push(
                    source(f, other), j["core"].at[f, :, :, lanes], near["core"]
                )
                kept = pltpu.make_async_copy(
                    source(f, c), j["mine"].at[f, :, :, lanes], local.at[slots]
                )
                slots += 1
                kept.start()
                j[step].append((pushed, kept))

    first, second = pl.ds(0, COUNT // 2), pl.ds(COUNT // 2, COUNT // 2)
    fetches = [(up_far, up_got)]
    for i, d in enumerate((3, 1, 0)):
        up_rows = pl.ds(pl.multiple_of(((x + d) % 4) * UP_PART, UP_PART), UP_PART)
        fetches.append((up_in.at[up_rows], ups.at[i]))
    lanes = pl.ds(pl.multiple_of(x * DOWN_PART, 128), DOWN_PART)
    fetches += [
        (down_in.at[:, lanes], downs.at[0]),
        (down_far, downs.at[pl.ds(1, 2)]),
        (middle, mid),
        (came_a, land_a.at[:, first]),
        (came_b, land_b.at[:, first]),
        (late_a.at[y], land_a.at[y, second]),
        (late_b.at[z], land_b.at[z, second]),
    ]
    fetches = [
        pltpu.make_async_copy(src, dst, local.at[slots + i]) for i, (src, dst) in enumerate(fetches)
    ]
    for fetch in fetches:
        fetch.start()
    for fetch in fetches[:4]:
        fetch.wait()
    sides = []
    for i, peer in enumerate((near["x"][2], near["x"][0])):
        up_rows = slice(i * UP_HALF, (i + 1) * UP_HALF)
        ups[i, up_rows, :] = (ups[i, up_rows, :].astype(F32) + up_got[i].astype(F32)).astype(BF16)
        sides.append(link.push(ups.at[i], up_land.at[i], peer))

    def ready(j, step):
        for pushed, kept in j[step]:
            pushed.wait_recv()
            kept.wait()

    for j in jobs:
        f = (j["q"] + 2) % 4
        ready(j, 2)
        mine = j["mine"]
        add_blocks(j["core"], f, 0, 4, [lambda i, f=f, m=mine: m[f, i]])
        plus, minus = near[j["far"]]
        j["down"] = link.push(j["core"].at[f, pl.ds(0, 2)], j["one"].at[0], minus)
        j["up"] = link.push(j["core"].at[f, pl.ds(2, 2)], j["one"].at[1], plus)
    for j in jobs:
        plus, minus = near[j["far"]]
        mine, one = j["mine"], j["one"]
        f = (j["q"] + 3) % 4
        ready(j, 3)
        add_blocks(j["core"], f, 2, 2, [lambda i, f=f, m=mine: m[f, i + 2]])
        j["down"].wait_recv()
        add_blocks(
            j["core"], f, 0, 2, [lambda i, f=f, m=mine: m[f, i], lambda i, o=one: o[0, i]]
        )
        j["down2"] = link.push(j["core"].at[f], j["two"].at[0], minus)
        f = (j["q"] + 1) % 4
        ready(j, 1)
        add_blocks(j["core"], f, 0, 2, [lambda i, f=f, m=mine: m[f, i]])
        j["up"].wait_recv()
        add_blocks(
            j["core"], f, 2, 2, [lambda i, f=f, m=mine: m[f, i + 2], lambda i, o=one: o[1, i]]
        )
        j["up2"] = link.push(j["core"].at[f], j["two"].at[1], plus)
    for j in jobs:
        mine, two = j["mine"], j["two"]
        f = j["q"]
        ready(j, 0)
        j["down2"].wait_recv()
        j["up2"].wait_recv()
        add_blocks(
            j["core"], f, 0, 4,
            [lambda i, f=f, m=mine: m[f, i], lambda i, t=two: t[0, i], lambda i, t=two: t[1, i]],
        )
        plus, minus = near[j["close"]]
        g = (j["p"] + 2) % 4
        h, w = j["half"], j["width"]
        j["down"] = link.push(j["core"].at[f, g, :, pl.ds(0, h)], j["halves"][0], minus)
        j["up"] = link.push(j["core"].at[f, g, :, pl.ds(h, w - h)], j["halves"][1], plus)
    for j in jobs:
        plus, minus = near[j["close"]]
        f, h, w, core = j["q"], j["half"], j["width"], j["core"]
        g = (j["p"] + 3) % 4
        j["down"].wait_recv()
        core[f, g, :, 0:h] = (
            core[f, g, :, 0:h].astype(F32) + j["halves"][0][...].astype(F32)
        ).astype(BF16)
        j["down2"] = link.push(core.at[f, g], j["last"].at[0], minus)
        g = (j["p"] + 1) % 4
        j["up"].wait_recv()
        core[f, g, :, h:w] = (
            core[f, g, :, h:w].astype(F32) + j["halves"][1][...].astype(F32)
        ).astype(BF16)
        j["up2"] = link.push(core.at[f, g], j["last"].at[1], plus)
    late = []
    for src, dst, me, line in ((late_a, land_a, y, line_y), (late_b, land_b, z, line_z)):
        for d in (1, 2, 3):
            late.append(link.push(src.at[(me + d) % 4], dst.at[me, second], line[d - 1]))
    select = pick_rows(4 * PADDED, BLOCK, PADDED, PIECE)
    for j in jobs:
        f, g = j["q"], j["p"]
        j["down2"].wait_recv()
        j["up2"].wait_recv()
        total = (
            j["core"][f, g].astype(F32)
            + j["last"][0].astype(F32)
            + j["last"][1].astype(F32)
        ).astype(BF16)
        spread = jnp.dot(select, total, preferred_element_type=F32).astype(BF16)
        xout[:, :, j["lane"] : j["lane"] + j["width"]] = spread.reshape(4, PADDED, j["width"])
    final = [
        link.push(xout.at[(x + d) % 4], xin.at[d - 1], near["x"][d - 1]) for d in (1, 2, 3)
    ]
    for copy in final:
        copy.wait_recv()
    mine = xout[x].astype(F32)
    for d in range(3):
        mine = mine + xin[d].astype(F32)
    out_a[...] = mine[:, :WA]
    out_b[...] = mine[:, WA:]
    for push in sides:
        push.wait_recv()
    up_out[...] = ups[2].astype(F32) + up_land[0].astype(F32) + up_land[1].astype(F32)
    for fetch in fetches[4:]:
        fetch.wait()
    down_out[...] = downs[0].astype(F32) + downs[1].astype(F32) + downs[2].astype(F32)
    for push in late:
        push.wait_recv()
    for half, landed in enumerate((land_a, land_b)):
        lanes = slice(half * HALF, (half + 1) * HALF)
        total = mid[:, lanes]
        for s in range(4):
            total = total + landed[s].astype(F32)
        output[:, lanes] = total.astype(BF16)
    link.drain()


def scatter_sums(*operands):
    copies = 2 * (4 + 4 + 4) + 4 + 3 + 6 + 2
    vmem = pltpu.VMEM
    scratch = []
    for shape in ((4, 4), (4, 4), (2, 2), (2, 4)):
        scratch += [vmem((*shape, BLOCK, WA), BF16), vmem((*shape, BLOCK, WB), BF16)]
    scratch += [
        vmem((BLOCK, 1024), BF16),
        vmem((BLOCK, 1024), BF16),
        vmem((BLOCK, 896), BF16),
        vmem((BLOCK, WB - 896), BF16),
        vmem((2, BLOCK, WA), BF16),
        vmem((2, BLOCK, WB), BF16),
        vmem((4, PADDED, WA + WB), BF16),
        vmem((3, PADDED, WA + WB), BF16),
        vmem((3, UP_PART, 2 * FF), BF16),
        vmem((3, FF, DOWN_PART), BF16),
        vmem((2, UP_HALF, 2 * FF), BF16),
        vmem((2, UP_PART, 2 * FF), BF16),
        vmem((COUNT, D), F32),
        vmem((4, COUNT, HALF), BF16),
        vmem((4, COUNT, HALF), BF16),
        pltpu.SemaphoreType.DMA((copies,)),
        pltpu.SemaphoreType.DMA((copies,)),
        pltpu.SemaphoreType.DMA((12 + 11,)),
    ]
    return pl.pallas_call(
        scatter_kernel,
        name="scatter_sums",
        out_shape=(
            jax.ShapeDtypeStruct((PADDED, WA), F32),
            jax.ShapeDtypeStruct((PADDED, WB), F32),
            jax.ShapeDtypeStruct((UP_PART, 2 * FF), F32),
            jax.ShapeDtypeStruct((FF, DOWN_PART), F32),
            jax.ShapeDtypeStruct((COUNT, D), BF16),
        ),
        in_specs=[pl.BlockSpec(memory_space=pltpu.HBM)] * 12,
        out_specs=(pl.BlockSpec(memory_space=pltpu.VMEM),) * 5,
        scratch_shapes=scratch,
        compiler_params=pltpu.CompilerParams(
            collective_id=1, has_side_effects=True, vmem_limit_bytes=60 * 1024 * 1024
        ),
        cost_estimate=pl.CostEstimate(flops=0, bytes_accessed=24_000_000, transcendentals=0),
    )(*operands)


ROWS = EXPERTS * CAP
TILE = 256
PARTS = 3
PART = CAP // PARTS
SLOTS = 8 * CAP
PIECE_SLOTS = 8 * PART
PIECE_ROWS = EXPERTS * PART
HALF = D // 2
LANES = 128
SCALE = HEAD_DIM ** (-0.5)
GROUP_ROWS = 1024
COUNT = 256
NT = (((1,), (1,)), ((), ()))
TN = (((0,), (0,)), ((), ()))


def mul(a, b, dims=None):
    if dims is None:
        return jnp.dot(a, b, preferred_element_type=F32)
    return lax.dot_general(a, b, dims, preferred_element_type=F32)


def thirds(v):
    high = v.astype(BF16)
    rest = v - high.astype(F32)
    middle = rest.astype(BF16)
    return high, middle, (rest - middle.astype(F32)).astype(BF16)


def exact(v, one_hot, dims=None):
    return sum(mul(part, one_hot, dims) for part in thirds(v))


def exact_right(one_hot, v):
    return sum(mul(one_hot, part, NT) for part in thirds(v))


def iota(shape, axis):
    return lax.broadcasted_iota(jnp.int32, shape, axis)


def hot(same):
    return jnp.where(same, 1.0, 0.0).astype(BF16)


class Moves(Links):
    def __init__(self, send, recv, local):
        super().__init__(send, recv)
        self.local, self.kept = local, 0

    def keep(self, src, dst):
        copy = pltpu.make_async_copy(src, dst, self.local.at[self.kept])
        self.kept += 1
        copy.start()
        return copy

    def send_or_keep(self, i, src, dst, where):
        if i == 0:
            return self.keep(src, dst).wait
        return self.push(src, dst, where).wait_recv


def to_slots(hits, rows, stage, piece):
    columns = slice(piece * PIECE_SLOTS, (piece + 1) * PIECE_SLOTS)
    for s in range(4):
        taken = mul(hits[s, :, columns], rows[s], TN).astype(BF16)
        stage[piece, :, s] = taken.reshape(8, PART, taken.shape[1])


def deliver(moves, at, stage_a, stage_b, rows, split, piece):
    y, z, c, x = at
    along_z, along_y = faces(y, z, c, x)
    width = rows.shape[4]
    waits = []
    for i, (where, zt, ct) in enumerate(along_z):
        dst = rows.at[piece, z, pl.ds(c * 4, 4), :, pl.ds(0, split)]
        waits.append(moves.send_or_keep(i, stage_a.at[piece, zt * 2 + ct], dst, where))
    for i, (where, yt, ct) in enumerate(along_y):
        dst = rows.at[piece, :, c * 4 + y, :, pl.ds(split, width - split)]
        waits.append(moves.send_or_keep(i, stage_b.at[piece, yt * 2 + ct], dst, where))
    return waits


def give_back(moves, at, rows, back_a, back_b, split, piece):
    y, z, c, x = at
    along_z, along_y = faces(y, z, c, x)
    width = rows.shape[4]
    waits = []
    for i, (where, zt, ct) in enumerate(along_z):
        src = rows.at[piece, zt, pl.ds(ct * 4, 4), :, pl.ds(0, split)]
        dst = back_a.at[piece, z * 2 + c, :, :, pl.ds(0, split)]
        waits.append(moves.send_or_keep(i, src, dst, where))
    for i, (where, yt, ct) in enumerate(along_y):
        src = rows.at[piece, :, ct * 4 + yt, :, pl.ds(split, width - split)]
        dst = back_b.at[piece, y * 2 + c, :, :, pl.ds(0, width - split)]
        waits.append(moves.send_or_keep(i, src, dst, where))
    return waits


def slot_fold():
    p = iota((LANES, SLOTS), 1)
    return hot((p // PIECE_SLOTS) * PART + p % PART == iota((LANES, SLOTS), 0))


def slot_owner():
    return (iota((8, SLOTS), 1) % PIECE_SLOTS) // PART == iota((8, SLOTS), 0)


def add_up(hits, back, s, width):
    rows = back[:, :, s, :, 0:width].reshape(SLOTS, width)
    return mul(hits[s], rows).astype(BF16)


def around(link, own, land, me, plus, minus):
    up = link.push(own, land.at[me], plus)
    down = link.push(own, land.at[me], minus)

    def forward():
        half = COUNT // 2
        up.wait_recv()
        block = land.at[(me + 3) % 4, pl.ds(0, half)]
        waits = [link.push(block, block, plus).wait_recv]
        down.wait_recv()
        block = land.at[(me + 1) % 4, pl.ds(half, half)]
        return waits + [link.push(block, block, minus).wait_recv]

    return forward


def gelu_parts(g):
    inner = 0.7978845608 * (g + 0.044715 * g * g * g)
    th = jnp.tanh(inner)
    half = 0.5 * (1.0 + th)
    slope = half + 0.5 * g * (1.0 - th * th) * (0.7978845608 * (1.0 + 0.134145 * g * g))
    return g * half, slope


def experts_kernel(
    hot_a_in, hot_b_in, nf_a_in, nf_b_in, dy_in, tiles_in, gate_up, down,
    back_a, back_b, out, up_out, down_out, tiles_back,
    hot_a, hot_b, nf_a, nf_b, stage_a, stage_b, rows, dy,
    gu, dn, raw, mixed, ghid, grow, eo, up_grad, down_grad, tiles, slope_tiles,
    send, recv, local, load_sem,
):
    at = place()
    y, z, c, x = at
    me = (y * 4 + z) * 2 + c
    loads = [
        pltpu.make_async_copy(src, dst, load_sem.at[i])
        for i, (src, dst) in enumerate(
            (
                (hot_a_in, hot_a), (nf_a_in, nf_a), (hot_b_in, hot_b), (nf_b_in, nf_b),
                (dy_in, dy), (down.at[0], dn), (gate_up.at[0], gu), (tiles_in, tiles),
            )
        )
    ]
    for load in loads:
        load.start()
    greet(cross(*at))
    moves = Moves(send, recv, local)
    for load in loads[:4]:
        load.wait()
    waits = []
    for piece in range(PARTS):
        to_slots(hot_a, nf_a, stage_a, piece)
        to_slots(hot_b, nf_b, stage_b, piece)
        waits.append(deliver(moves, at, stage_a, stage_b, rows, HALF, piece))
    for load in loads[4:]:
        load.wait()

    def raw_tile(j, carry):
        lanes = pl.ds(pl.multiple_of(j * TILE, TILE), TILE)
        raw[:, lanes] = mul(dy[...].reshape(ROWS, D), dn[lanes, :], NT)
        return carry

    lax.fori_loop(0, FF // TILE, raw_tile, 0, unroll=True)
    back_waits = []
    slope_tiles[...] = jnp.zeros_like(slope_tiles)
    for piece in range(PARTS):
        for wait in waits[piece]:
            wait()
        block = slice(piece * PIECE_ROWS, (piece + 1) * PIECE_ROWS)
        slot = piece * PART + iota((PIECE_ROWS, LANES), 0) % PART
        held = iota((PIECE_ROWS, LANES), 1) == slot
        spread = jnp.broadcast_to(tiles[:, 0:4, :][:, :, None, :], (8, 4, PART, LANES))
        spread = spread.reshape(PIECE_ROWS, LANES)
        gate = jnp.sum(jnp.where(held, spread, 0.0), axis=1, keepdims=True)

        def hidden_tile(j, slope_sum, piece=piece, block=block, gate=gate):
            lanes = pl.ds(pl.multiple_of(j * TILE, TILE), TILE)
            upper = pl.ds(pl.multiple_of(FF + j * TILE, TILE), TILE)
            g = mul(rows[piece].reshape(PIECE_ROWS, D), gu[:, lanes])
            act, slope = gelu_parts(g)
            u = mul(rows[piece].reshape(PIECE_ROWS, D), gu[:, upper])
            m = raw[block, lanes]
            both = act * u
            mixed[block, lanes] = (both * gate).astype(BF16)
            slope_sum = slope_sum + jnp.sum(both * m, axis=1, keepdims=True)
            m = m * gate
            ghid[block, lanes] = (m * u * slope).astype(BF16)
            ghid[block, upper] = (m * act).astype(BF16)
            return slope_sum

        slopes = lax.fori_loop(
            0, FF // TILE, hidden_tile, jnp.zeros((PIECE_ROWS, 1), F32), unroll=True
        )
        slopes = jnp.where(held, slopes, 0.0).reshape(8, 4, PART, LANES)
        slope_tiles[:, 0:4, :] += jnp.sum(slopes, axis=2)

        def rows_tile(j, carry, piece=piece, block=block):
            lanes = pl.ds(pl.multiple_of(j * TILE, TILE), TILE)
            part = mul(ghid[block, :], gu[lanes, :], NT).astype(BF16)
            grow[piece, :, :, :, lanes] = part.reshape(4, 8, PART, TILE)
            return carry

        lax.fori_loop(0, D // TILE, rows_tile, 0, unroll=True)
        back_waits += give_back(moves, at, grow, back_a, back_b, HALF, piece)

    along_z, _ = faces(*at)
    back_waits += [
        moves.send_or_keep(i, slope_tiles.at[zt * 2 + ct], tiles_back.at[z * 2 + c], where)
        for i, (where, zt, ct) in enumerate(along_z)
    ]

    def out_tile(j, carry):
        lanes = pl.ds(pl.multiple_of(j * TILE, TILE), TILE)
        part = mul(mixed[...], dn[:, lanes]).astype(BF16)
        eo[:, :, :, :, lanes] = part.reshape(PARTS, 4, 8, PART, TILE)
        return carry

    lax.fori_loop(0, D // TILE, out_tile, 0, unroll=2)
    back_waits.append(moves.keep(eo, out).wait)

    def up_tile(j, carry):
        lanes = pl.ds(pl.multiple_of(j * TILE, TILE), TILE)
        part = mul(rows[:, :, :, :, lanes].reshape(ROWS, TILE), ghid[...], TN)
        up_grad[lanes, :] = part.astype(BF16)
        return carry

    lax.fori_loop(0, D // TILE, up_tile, 0, unroll=2)
    back_waits.append(moves.keep(up_grad, up_out).wait)

    def down_tile(j, carry):
        lanes = pl.ds(pl.multiple_of(j * TILE, TILE), TILE)
        part = mul(mixed[:, lanes], dy[...].reshape(ROWS, D), TN)
        down_grad[lanes, :] = part.astype(BF16)
        return carry

    lax.fori_loop(0, FF // TILE, down_tile, 0, unroll=True)
    back_waits.append(moves.keep(down_grad, down_out).wait)
    for wait in back_waits:
        wait()
    moves.drain()


def run_experts(*operands):
    anywhere = pl.BlockSpec(memory_space=pltpu.HBM)
    vmem, dma = pltpu.VMEM, pltpu.SemaphoreType.DMA
    outs = (
        (PARTS, 8, 4, PART, HALF),
        (PARTS, 8, 4, PART, HALF),
        (PARTS, 4, 8, PART, D),
        (D, 2 * FF),
        (FF, D),
    )
    held = (
        (4, COUNT, SLOTS),
        (4, COUNT, SLOTS),
        (4, COUNT, HALF),
        (4, COUNT, HALF),
        (PARTS, 8, 4, PART, HALF),
        (PARTS, 8, 4, PART, HALF),
        (PARTS, 4, 8, PART, D),
        (PARTS, 4, 8, PART, D),
        (D, 2 * FF),
        (FF, D),
        None,
        (ROWS, FF),
        (ROWS, 2 * FF),
        (PARTS, 4, 8, PART, D),
        (PARTS, 4, 8, PART, D),
        (D, 2 * FF),
        (FF, D),
    )
    return pl.pallas_call(
        experts_kernel,
        name="experts",
        out_shape=tuple(jax.ShapeDtypeStruct(shape, BF16) for shape in outs)
        + (jax.ShapeDtypeStruct((8, 8, LANES), F32),),
        in_specs=[anywhere] * 8,
        out_specs=(anywhere,) * 6,
        scratch_shapes=[vmem(shape, BF16) if shape else vmem((ROWS, FF), F32) for shape in held]
        + [vmem((8, 8, LANES), F32)] * 2
        + [dma((84 + 7,)), dma((84 + 7,)), dma((15 + 1,)), dma((8,))],
        compiler_params=pltpu.CompilerParams(
            collective_id=2, has_side_effects=True, vmem_limit_bytes=60 * 1024 * 1024
        ),
        cost_estimate=pl.CostEstimate(
            flops=33_000_000_000, bytes_accessed=60_000_000, transcendentals=1_200_000
        ),
    )(*operands)


UP_PART = D // 4
UP_HALF = UP_PART // 2
DOWN_PART = D // 4
DOWN_HALF = FF // 2


def read_gains(small):
    select = hot(iota((8, SMALL), 1) == iota((8, SMALL), 0) + EXPERTS)
    select = jnp.where(iota((8, SMALL), 0) < 2, select, jnp.zeros_like(select))
    return mul(select, small, NT), select


def fill_bias(lengths, bias, x):
    first = lengths[0, 0]
    second = first + lengths[0, 1]
    third = second + lengths[0, 2]
    own = x * COUNT + iota((1, COUNT), 1)
    own_seg = sum(jnp.where(own >= end, 1, 0) for end in (first, second, third))

    def step(i, carry):
        base = pl.multiple_of(i * COUNT, COUNT)
        key = base + iota((COUNT, 1), 0)
        key_seg = sum(jnp.where(key >= end, 1, 0) for end in (first, second, third))
        allowed = (key_seg == own_seg) & (key <= own)
        bias[pl.ds(base, COUNT), :] = jnp.where(allowed, 0.0, -1e30)
        return carry

    lax.fori_loop(0, GROUP_ROWS // COUNT, step, 0)


def turn(v, cosd, sind):
    return v * cosd + pltpu.roll(v, HEAD_DIM // 2, 1) * sind


def forward_kernel(
    lengths, tokens, wq_in, wb_in, named, cosd, sind, hot_a_in, hot_b_in, dy_a_in, dy_b_in,
    q_out, kv_out, attended_out, middle_out, normed_out, tops, totals, gates_out,
    nf_a, nf_b, dy_rows, tiles_out,
    wq, wb, kv, own_kv, bias, vt, q, attended, middle, normed, nf,
    hot_a, hot_b, dy_a, dy_b, stage_a, stage_b, own_gates, gates_y, tiles, send, recv, local, load_sem,
):
    at = place()
    y, z, c, x = at
    line_y, line_z = lines(y, z, c, x)
    peers = [device(y, z, c, (x + d) % 4) for d in (1, 2, 3)]
    pairs = (
        (hot_a_in, hot_a), (dy_a_in, dy_a), (hot_b_in, hot_b), (dy_b_in, dy_b),
        (wb_in.at[:, pl.ds(D, SMALL)], wb.at[:, pl.ds(D, SMALL)]),
        (wq_in.at[:, pl.ds(D, 512)], wq.at[:, pl.ds(D, 512)]),
        (wq_in.at[:, pl.ds(0, D)], wq.at[:, pl.ds(0, D)]),
        (wb_in.at[:, pl.ds(0, D)], wb.at[:, pl.ds(0, D)]),
    )
    loads = [
        pltpu.make_async_copy(src, dst, load_sem.at[i]) for i, (src, dst) in enumerate(pairs)
    ]
    for load in loads:
        load.start()
    greet(cross(*at) + peers)
    moves = Moves(send, recv, local)
    for load in loads[0:4]:
        load.wait()
    for piece in range(PARTS):
        to_slots(hot_a, dy_a, stage_a, piece)
        to_slots(hot_b, dy_b, stage_b, piece)
    dy_waits = deliver(moves, at, stage_a, stage_b, dy_rows, HALF, slice(None))
    loads[4].wait()
    small = wb[:, D:]
    gains, _ = read_gains(small)
    xf = tokens[...].astype(F32)
    inverse = lax.rsqrt(jnp.mean(xf * xf, axis=1, keepdims=True) + norm_eps)
    normed[...] = (xf * inverse * gains[0:1, :]).astype(BF16)
    loads[5].wait()
    part = mul(normed[...], wq[:, D : D + 512])
    for g in range(HEADS_KV):
        key = turn(part[:, g * 128 : (g + 1) * 128], cosd[...], sind[...])
        own_kv[:, g * 256 : g * 256 + 128] = key.astype(BF16)
        own_kv[:, g * 256 + 128 : (g + 1) * 256] = part[:, 256 + g * 128 : 384 + g * 128].astype(BF16)
    rows = pl.ds(pl.multiple_of(x * COUNT, COUNT), COUNT)
    pushes = []
    for g in range(HEADS_KV):
        lanes = pl.ds(g * 256, 256)
        pushes.append(
            [moves.push(own_kv.at[:, lanes], kv.at[rows, lanes], peer) for peer in peers]
        )
    kv[rows, :] = own_kv[...]
    fill_bias(lengths, bias, x)
    loads[6].wait()

    def query_tile(j, carry):
        lanes = pl.ds(pl.multiple_of(j * 256, 256), 256)
        part = mul(normed[...], wq[:, lanes])
        q[:, lanes] = jnp.concatenate(
            [turn(part[:, h * 128 : (h + 1) * 128], cosd[...], sind[...]) for h in range(2)],
            axis=1,
        ).astype(BF16)
        return carry

    lax.fori_loop(0, D // 256, query_tile, 0, unroll=True)

    logits = jnp.where(named[...] > 0, mul(tokens[...], small), -jnp.inf)
    weight = jnp.exp(logits - jnp.max(logits, axis=1, keepdims=True))
    gates = weight / jnp.sum(weight, axis=1, keepdims=True)
    gates_out[...] = gates
    flat = exact_right(hot(iota((EXPERTS, LANES), 0) == iota((EXPERTS, LANES), 1)), gates)
    own_gates[...] = flat.reshape(4, 8, COUNT)
    gates_y[pl.ds(y, 1)] = own_gates[pl.ds(y, 1)]
    gate_pushes = [
        moves.push(own_gates.at[(y + d) % 4], gates_y.at[y], line_y[d - 1]) for d in (1, 2, 3)
    ]

    stays = [moves.keep(q, q_out), moves.keep(normed, normed_out)]
    for g in range(HEADS_KV):
        for push in pushes[g]:
            push.wait_recv()
        vt[g] = kv[:, g * 256 + 128 : (g + 1) * 256].T

        def head(i, carry, g=g):
            h = g * REPEAT + i
            lanes = pl.ds(pl.multiple_of(h * HEAD_DIM, HEAD_DIM), HEAD_DIM)
            s = mul(kv[:, g * 256 : g * 256 + 128], q[:, lanes], NT) * SCALE + bias[...]
            top = jnp.max(s, axis=0, keepdims=True)
            p = jnp.exp(s - top)
            total = jnp.sum(p, axis=0, keepdims=True)
            tops[pl.ds(h, 1), :] = top
            totals[pl.ds(h, 1), :] = total
            low = (p * (1.0 / total)).astype(BF16)
            attended[:, lanes] = mul(vt[g], low).T.astype(BF16)
            return carry

        lax.fori_loop(0, REPEAT, head, 0, unroll=3)

    stays.append(moves.keep(kv, kv_out))
    loads[7].wait()

    def out_tile(j, carry):
        lanes = pl.ds(pl.multiple_of(j * 256, 256), 256)
        middle[:, lanes] = tokens[:, lanes].astype(F32) + mul(attended[...], wb[lanes, 0:D], NT)
        return carry

    lax.fori_loop(0, D // 256, out_tile, 0, unroll=True)
    m = middle[...]
    inverse = lax.rsqrt(jnp.mean(m * m, axis=1, keepdims=True) + norm_eps)
    stays += [moves.keep(attended, attended_out), moves.keep(middle, middle_out)]
    nf[...] = (m * inverse * gains[1:2, :]).astype(BF16)
    half_a, half_b = nf.at[:, pl.ds(0, HALF)], nf.at[:, pl.ds(HALF, HALF)]
    last = [
        around(moves, half_a, nf_a, y, line_y[0], line_y[2]),
        around(moves, half_b, nf_b, z, line_z[0], line_z[2]),
    ]
    stays += [moves.keep(half_a, nf_a.at[y]), moves.keep(half_b, nf_b.at[z])]
    for push in gate_pushes:
        push.wait_recv()
    tiles[...] = jnp.zeros_like(tiles)
    owner = hot(slot_owner())
    for s in range(4):
        spread = exact(gates_y[s], owner, TN) * hot_a[s].astype(F32)
        row = jnp.sum(spread, axis=0, keepdims=True)
        tile = exact(jnp.where(slot_owner(), row, 0.0), slot_fold(), NT)
        tiles[:, s : s + 1, :] = tile[:, None, :]
    along_z, _ = faces(*at)
    dy_waits += [
        moves.send_or_keep(i, tiles.at[zt * 2 + ct], tiles_out.at[z * 2 + c], where)
        for i, (where, zt, ct) in enumerate(along_z)
    ]
    for wait in last[0]() + last[1]():
        wait()
    for stay in stays:
        stay.wait()
    for wait in dy_waits:
        wait()
    moves.drain()


def run_forward(*operands):
    anywhere = pl.BlockSpec(memory_space=pltpu.HBM)
    inside = pl.BlockSpec(memory_space=pltpu.VMEM)
    vmem, dma = pltpu.VMEM, pltpu.SemaphoreType.DMA
    shape = jax.ShapeDtypeStruct
    return pl.pallas_call(
        forward_kernel,
        name="forward",
        out_shape=(
            shape((COUNT, D), BF16),
            shape((GROUP_ROWS, 512), BF16),
            shape((COUNT, D), BF16),
            shape((COUNT, D), F32),
            shape((COUNT, D), BF16),
            shape((16, COUNT), F32),
            shape((16, COUNT), F32),
            shape((COUNT, 128), F32),
            shape((4, COUNT, HALF), BF16),
            shape((4, COUNT, HALF), BF16),
            shape((PARTS, 4, 8, PART, D), BF16),
            shape((8, 8, LANES), F32),
        ),
        in_specs=[pl.BlockSpec(memory_space=pltpu.SMEM), inside, anywhere, anywhere]
        + [inside] * 3
        + [anywhere] * 4,
        out_specs=(anywhere,) * 5 + (inside,) * 3 + (anywhere,) * 4,
        scratch_shapes=[
            vmem((D, WA), BF16),
            vmem((D, WB), BF16),
            vmem((GROUP_ROWS, 512), BF16),
            vmem((COUNT, 512), BF16),
            vmem((GROUP_ROWS, COUNT), F32),
            vmem((HEADS_KV, HEAD_DIM, GROUP_ROWS), BF16),
            vmem((COUNT, D), BF16),
            vmem((COUNT, D), BF16),
            vmem((COUNT, D), F32),
            vmem((COUNT, D), BF16),
            vmem((COUNT, D), BF16),
            vmem((4, COUNT, SLOTS), BF16),
            vmem((4, COUNT, SLOTS), BF16),
            vmem((4, COUNT, HALF), BF16),
            vmem((4, COUNT, HALF), BF16),
            *(vmem((PARTS, 8, 4, PART, HALF), BF16),) * 2,
            vmem((4, 8, COUNT), F32),
            vmem((4, 8, COUNT), F32),
            vmem((8, 8, LANES), F32),
            dma((6 + 14 + 8 + 3 + 7,)),
            dma((6 + 14 + 8 + 3 + 7,)),
            dma((2 + 7 + 1,)),
            dma((8,)),
        ],
        compiler_params=pltpu.CompilerParams(
            collective_id=3, has_side_effects=True, vmem_limit_bytes=60 * 1024 * 1024
        ),
        cost_estimate=pl.CostEstimate(
            flops=6_000_000_000, bytes_accessed=30_000_000, transcendentals=3_200_000
        ),
    )(*operands)


def norm_grad(values, gain, grad):
    inverse = lax.rsqrt(jnp.mean(values * values, axis=1, keepdims=True) + norm_eps)
    unit = values * inverse
    scaled = grad * gain
    drop = jnp.mean(scaled * unit, axis=1, keepdims=True)
    return inverse * (scaled - unit * drop), jnp.sum(grad * unit, axis=0, keepdims=True)


def backward_kernel(
    lengths, tokens_in, cotangent_in, gates, queries_in, kv_src, attended_in, middle_in, normed_in,
    tops, totals, cosd, sind, wq_in, wb_in, hot_a_in, hot_b_in,
    back_a_in, back_b_in, out_in, up_in, down_in, tiles_in,
    grad_tokens, grad_qkv_out, grad_out_out, grad_small, up_far, down_far,
    late_a, late_b, came_a, came_b,
    tokens, cotangent, queries, kv_in, attended, middle, normed,
    wq, wb, hot_a, hot_b, back_a, back_b,
    part_a, part_b, land_a, land_b, down_own, down_got,
    tiles, slopes, slopes_y,
    bias, kt, gn, gmid, gb, gatt, gp, dk, dv, leave, land, grad_qkv,
    send, recv, local, load_sem, empty,
):
    at = place()
    y, z, c, x = at
    line_y, line_z = lines(y, z, c, x)
    peers = [device(y, z, c, (x + d) % 4) for d in (1, 2, 3)]
    pairs = (
        (back_a_in, back_a), (hot_a_in, hot_a), (back_b_in, back_b), (hot_b_in, hot_b),
        (tiles_in, tiles),
        (kv_src, kv_in), (wb_in, wb), (middle_in, middle), (cotangent_in, cotangent),
        (queries_in, queries), (attended_in, attended), (tokens_in, tokens),
        (normed_in, normed), (wq_in, wq),
    )
    pairs += tuple(
        (
            down_in.at[
                pl.ds(half * DOWN_HALF, DOWN_HALF),
                pl.ds(pl.multiple_of(((x + d) % 4) * DOWN_PART, 128), DOWN_PART),
            ],
            down_own.at[half],
        )
        for half, d in ((0, 3), (1, 1))
    )
    loads = [
        pltpu.make_async_copy(src, dst, load_sem.at[i]) for i, (src, dst) in enumerate(pairs)
    ]
    for load in loads:
        load.start()
    greet(cross(*at) + peers)
    link = Moves(send, recv, local)
    for load in loads[:5]:
        load.wait()
    part_waits = []
    for hits, back, parts, land_here, me, line, width in (
        (hot_a, back_a, part_a, land_a, y, line_y, HALF),
        (hot_b, back_b, part_b, land_b, z, line_z, HALF),
    ):
        for d in (1, 2, 3):
            parts[d - 1] = add_up(hits, back, (me + d) % 4, width)
            push = link.push(parts.at[d - 1], land_here.at[me], line[d - 1])
            part_waits.append(push.wait_recv)
        land_here[pl.ds(me, 1)] = add_up(hits, back, me, width)[None]
    for peer in cross(*at):
        pl.semaphore_signal(empty, inc=1, device_id=peer, device_id_type=MESH)
    facing = (x + 2) % 4
    pushes, down_pushes = [], []
    for half, peer in ((0, peers[2]), (1, peers[0])):
        up_rows = pl.ds(pl.multiple_of(facing * UP_PART + half * UP_HALF, UP_HALF), UP_HALF)
        pushes.append(link.push(up_in.at[up_rows], up_far.at[half], peer))
        lanes = pl.ds(pl.multiple_of(facing * DOWN_PART, 128), DOWN_PART)
        down_rows = pl.ds(half * DOWN_HALF, DOWN_HALF)
        down_pushes.append(link.push(down_in.at[down_rows, lanes], down_got.at[half], peer))
    slope_pushes = []
    for d in (1, 2, 3, 0):
        source = (y + d) % 4
        chosen = iota((8, 8, LANES), 1) == source
        tile = jnp.sum(jnp.where(chosen, tiles[...], 0.0), axis=1)
        spread = jnp.where(slot_owner(), exact(tile, slot_fold()), 0.0)
        slope = exact(spread, hot_a[source], NT)
        if d == 0:
            slopes_y[pl.ds(y, 1)] = slope[None]
        else:
            slopes[d - 1] = slope
            slope_pushes.append(link.push(slopes.at[d - 1], slopes_y.at[y], line_y[d - 1]))
    fill_bias(lengths, bias, x)
    for load in loads[5:]:
        load.wait()
    for g in range(HEADS_KV):
        kt[g] = kv_in[:, g * 256 : g * 256 + 128].T
    for wait in part_waits:
        wait()
    pl.semaphore_wait(empty, 13)
    out_waits = give_back(link, at, out_in, back_a, back_b, HALF, slice(None))
    total = land_a[0].astype(F32)
    for s in range(1, 4):
        total = total + land_a[s].astype(F32)
    gn[:, 0:HALF] = total
    total = land_b[0].astype(F32)
    for s in range(1, 4):
        total = total + land_b[s].astype(F32)
    gn[:, HALF:] = total
    gains, select = read_gains(wb[:, D:])
    moved, ffn_gain = norm_grad(middle[...], gains[1:2, :], gn[...])
    gm = cotangent[...].astype(F32) + moved
    gmid[...] = gm
    gb[...] = gm.astype(BF16)

    def att_tile(j, carry):
        lanes = pl.ds(pl.multiple_of(j * 256, 256), 256)
        gatt[:, lanes] = mul(gb[...], wb[:, lanes]).astype(BF16)
        return carry

    lax.fori_loop(0, D // 256, att_tile, 0, unroll=True)
    kv_pushes = []
    for g in range(HEADS_KV):
        dk[...] = jnp.zeros_like(dk)
        dv[...] = jnp.zeros_like(dv)

        def head(i, carry, g=g):
            h = g * REPEAT + i
            lanes = pl.ds(pl.multiple_of(h * HEAD_DIM, HEAD_DIM), HEAD_DIM)
            s = mul(kv_in[:, g * 256 : g * 256 + 128], queries[:, lanes], NT) * SCALE + bias[...]
            p = jnp.exp(s - tops[pl.ds(h, 1), :]) * (1.0 / totals[pl.ds(h, 1), :])
            dv[...] += mul(p.astype(BF16), gatt[:, lanes])
            t = p * mul(kv_in[:, g * 256 + 128 : (g + 1) * 256], gatt[:, lanes], NT)
            ds = (t - p * jnp.sum(t, axis=0, keepdims=True)).astype(BF16)
            dk[...] += mul(ds, queries[:, lanes])
            dq = mul(kt[g], ds).T * SCALE
            gp[:, lanes] = turn(dq, cosd[...], -sind[...]).astype(BF16)
            return carry

        lax.fori_loop(0, REPEAT, head, 0, unroll=3)
        leave[g, :, 0:128] = (dk[...] * SCALE).astype(BF16)
        leave[g, :, 128:256] = dv[...].astype(BF16)
        for d in (1, 2, 3):
            away = pl.ds(pl.multiple_of(((x + d) % 4) * COUNT, COUNT), COUNT)
            kv_pushes.append(link.push(leave.at[g, away], land.at[g, d - 1], peers[d - 1]))

    def out_tile(j, carry):
        lanes = pl.ds(pl.multiple_of(j * 256, 256), 256)
        grad_qkv[lanes, 0:D] = mul(gb[:, lanes], attended[...], TN).astype(BF16)
        return carry

    lax.fori_loop(0, D // 256, out_tile, 0, unroll=True)

    out_kept = link.keep(grad_qkv.at[:, pl.ds(0, D)], grad_out_out)

    for push in down_pushes:
        push.wait_recv()
    for half, (peer, part) in enumerate(((peers[2], (x + 3) % 4), (peers[0], (x + 1) % 4))):
        down_own[half] = (down_own[half].astype(F32) + down_got[half].astype(F32)).astype(BF16)
        lanes = pl.ds(pl.multiple_of(part * DOWN_PART, 128), DOWN_PART)
        here, rest = (pl.ds(k * DOWN_HALF, DOWN_HALF) for k in (half, 1 - half))
        pushes.append(link.push(down_own.at[half], down_far.at[half, here], peer))
        pushes.append(link.push(down_in.at[rest, lanes], down_far.at[half, rest], peer))

    for push in slope_pushes:
        push.wait_recv()
    same = hot(iota((EXPERTS, LANES), 0) == iota((EXPERTS, LANES), 1))
    gate_grad = exact(slopes_y[...].reshape(EXPERTS, COUNT), same, TN)
    weighted = gates[...] * gate_grad
    logit_grad = weighted - gates[...] * jnp.sum(weighted, axis=1, keepdims=True)
    parts = thirds(logit_grad)
    router_grad = sum(mul(tokens[...], part, TN) for part in parts)
    small = wb[:, D:]

    for wait in out_waits:
        wait()
    for s in range(4):
        land_a[s, :, 0:HALF] = add_up(hot_a, back_a, s, HALF)
        land_b[s, :, 0:HALF] = add_up(hot_b, back_b, s, HALF)
    first, second, lanes = pl.ds(0, COUNT // 2), pl.ds(COUNT // 2, COUNT // 2), pl.ds(0, HALF)
    late, stays = [], []
    for summed, came, left, me, line in (
        (land_a, came_a, late_a, y, line_y),
        (land_b, came_b, late_b, z, line_z),
    ):
        for d in (1, 2, 3):
            push = link.push(summed.at[(me + d) % 4, first, lanes], came.at[me], line[d - 1])
            late.append(push.wait_recv)
        stays.append(link.keep(summed.at[me, first, lanes], came.at[me]))
        stays.append(link.keep(summed.at[:, second, lanes], left))

    for push in kv_pushes:
        push.wait_recv()
    mine = pl.ds(pl.multiple_of(x * COUNT, COUNT), COUNT)
    for g in range(HEADS_KV):
        total = leave[g, mine, :].astype(F32)
        for d in range(3):
            total = total + land[g, d].astype(F32)
        gp[:, D + g * 128 : D + (g + 1) * 128] = turn(
            total[:, 0:128], cosd[...], -sind[...]
        ).astype(BF16)
        gp[:, D + 256 + g * 128 : D + 384 + g * 128] = total[:, 128:256].astype(BF16)
    out_kept.wait()

    def qkv_tile(j, carry):
        lanes = pl.ds(pl.multiple_of(j * 256, 256), 256)
        grad_qkv[lanes, :] = mul(normed[:, lanes], gp[...], TN).astype(BF16)
        gn[:, lanes] = mul(gp[...], wq[lanes, :], NT)
        return carry

    lax.fori_loop(0, D // 256, qkv_tile, 0, unroll=True)
    stays.append(link.keep(grad_qkv, grad_qkv_out))
    moved, attn_gain = norm_grad(tokens[...].astype(F32), gains[0:1, :], gn[...])
    from_router = sum(mul(part, small, NT) for part in parts)
    grad_tokens[...] = (gmid[...] + moved + from_router).astype(BF16)
    both = jnp.where(
        iota((8, D), 0) == 0, attn_gain, jnp.where(iota((8, D), 0) == 1, ffn_gain, 0.0)
    )
    gain_columns = sum(mul(part, select, TN) for part in thirds(both))
    grad_small[...] = (router_grad + gain_columns).astype(BF16)
    for push in pushes:
        push.wait_recv()
    for wait in late:
        wait()
    for stay in stays:
        stay.wait()
    link.drain()


def run_backward(*operands):
    anywhere = pl.BlockSpec(memory_space=pltpu.HBM)
    inside = pl.BlockSpec(memory_space=pltpu.VMEM)
    vmem, dma = pltpu.VMEM, pltpu.SemaphoreType.DMA
    shape = jax.ShapeDtypeStruct
    return pl.pallas_call(
        backward_kernel,
        name="backward",
        out_shape=(
            shape((COUNT, D), BF16),
            shape((D, WA), BF16),
            shape((D, D), BF16),
            shape((D, SMALL), BF16),
            shape((2, UP_HALF, 2 * FF), BF16),
            shape((2, FF, DOWN_PART), BF16),
            *(shape((4, COUNT // 2, HALF), BF16),) * 4,
        ),
        in_specs=[pl.BlockSpec(memory_space=pltpu.SMEM)]
        + [anywhere] * 2
        + [inside]
        + [anywhere] * 5
        + [inside] * 4
        + [anywhere] * 10,
        out_specs=(inside, anywhere, anywhere, inside) + (anywhere,) * 6,
        scratch_shapes=[
            vmem((COUNT, D), BF16),
            vmem((COUNT, D), BF16),
            vmem((COUNT, D), BF16),
            vmem((GROUP_ROWS, 512), BF16),
            vmem((COUNT, D), BF16),
            vmem((COUNT, D), F32),
            vmem((COUNT, D), BF16),
            vmem((D, WA), BF16),
            vmem((D, WB), BF16),
            vmem((4, COUNT, SLOTS), BF16),
            vmem((4, COUNT, SLOTS), BF16),
            vmem((PARTS, 8, 4, PART, HALF), BF16),
            vmem((PARTS, 8, 4, PART, HALF), BF16),
            vmem((3, COUNT, HALF), BF16),
            vmem((3, COUNT, HALF), BF16),
            vmem((4, COUNT, HALF), BF16),
            vmem((4, COUNT, HALF), BF16),
            vmem((2, DOWN_HALF, DOWN_PART), BF16),
            vmem((2, DOWN_HALF, DOWN_PART), BF16),
            vmem((8, 8, LANES), F32),
            vmem((3, 8, COUNT), F32),
            vmem((4, 8, COUNT), F32),
            vmem((GROUP_ROWS, COUNT), F32),
            vmem((HEADS_KV, HEAD_DIM, GROUP_ROWS), BF16),
            vmem((COUNT, D), F32),
            vmem((COUNT, D), F32),
            vmem((COUNT, D), BF16),
            vmem((COUNT, D), BF16),
            vmem((COUNT, WA), BF16),
            vmem((GROUP_ROWS, HEAD_DIM), F32),
            vmem((GROUP_ROWS, HEAD_DIM), F32),
            vmem((HEADS_KV, GROUP_ROWS, 256), BF16),
            vmem((HEADS_KV, 3, COUNT, 256), BF16),
            vmem((D, WA), BF16),
            dma((6 + 4 + 14 + 6 + 6 + 4 + 3,)),
            dma((6 + 4 + 14 + 6 + 6 + 4 + 3,)),
            dma((2 + 4 + 2,)),
            dma((16,)),
            pltpu.SemaphoreType.REGULAR,
        ],
        compiler_params=pltpu.CompilerParams(
            collective_id=4, has_side_effects=True, vmem_limit_bytes=60 * 1024 * 1024
        ),
        cost_estimate=pl.CostEstimate(
            flops=13_000_000_000, bytes_accessed=50_000_000, transcendentals=3_200_000
        ),
    )(*operands)


def finish_kernel(
    sum_a, sum_b, up, down, out, tokens,
    output, grad_tokens, grad_qkv, grad_out_t, grad_attn, grad_ffn, grad_router, grad_up, grad_down,
):
    output[...] = out[...]
    grad_tokens[...] = tokens[...]
    grad_qkv[...] = sum_a[0:PIECE, :]
    grad_out_t[...] = sum_b[0:PIECE, 0:D]
    small = sum_b[0:PIECE, D:]
    grad_router[...] = small[:, 0:EXPERTS]
    diagonal = iota((PIECE, SMALL), 0) == iota((PIECE, SMALL), 1)
    for k, gain in enumerate((grad_attn, grad_ffn)):
        lanes = iota((PIECE, SMALL), 1) == EXPERTS + k
        column = jnp.sum(jnp.where(lanes, small, 0.0), axis=1, keepdims=True)
        row = jnp.sum(jnp.where(diagonal, column, 0.0), axis=0, keepdims=True)
        gain[...] = row[:, 0:PIECE]
    grad_up[...] = up[...]
    grad_down[...] = down[...]


def finish(*operands):
    inside = pl.BlockSpec(memory_space=pltpu.VMEM)
    shape = jax.ShapeDtypeStruct
    return pl.pallas_call(
        finish_kernel,
        name="finish",
        out_shape=(
            shape((COUNT, D), BF16),
            shape((COUNT, D), BF16),
            shape((PIECE, WA), F32),
            shape((PIECE, D), F32),
            shape((1, PIECE), F32),
            shape((1, PIECE), F32),
            shape((PIECE, EXPERTS), F32),
            shape((UP_PART, 2 * FF), F32),
            shape((FF, DOWN_PART), F32),
        ),
        in_specs=[inside] * 6,
        out_specs=(inside,) * 9,
        compiler_params=pltpu.CompilerParams(vmem_limit_bytes=32 * 1024 * 1024),
    )(*operands)


def body(
    tokens, lengths, top_experts, w_qkv, w_out, gain_attn, gain_ffn, router, gate_up, down_proj, cotangent,
):
    half = HEAD_DIM // 2
    rates = rope_base ** (-(np.arange(HEAD_DIM, dtype=np.float32) % half) / half)
    full_a, full_b, named, hot_a, hot_b, dy_a, dy_b, cosd, sind = gather_weights(
        lengths, jnp.asarray(rates.astype(np.float32))[None], w_qkv, w_out.T, router,
        gain_attn[None], gain_ffn[None], top_experts.T, cotangent,
    )
    wq = full_a.reshape(D, WA)
    wb = full_b.reshape(D, WB)
    (
        queries, kv, attended, middle, normed, tops, totals, gates, nf_a, nf_b, dy_rows, tiles,
    ) = run_forward(
        lengths, tokens, wq, wb, named, cosd, sind, hot_a, hot_b, dy_a, dy_b
    )
    back_a, back_b, expert_out, up_local, down_local, tiles_back = run_experts(
        hot_a, hot_b, nf_a, nf_b, dy_rows, tiles, gate_up, down_proj
    )
    grad_tokens, grad_qkv, grad_out, grad_small, *passed_on = run_backward(
        lengths, tokens, cotangent, gates, queries, kv, attended, middle, normed, tops, totals,
        cosd, sind, wq, wb, hot_a, hot_b, back_a, back_b, expert_out, up_local, down_local,
        tiles_back,
    )
    sum_a, sum_b, up_sum, down_sum, output = scatter_sums(
        grad_qkv.reshape(4, 4, 2, BLOCK, WA),
        grad_out.reshape(4, 4, 2, BLOCK, D),
        grad_small.reshape(4, 4, 2, BLOCK, SMALL),
        up_local,
        down_local,
        *passed_on,
        middle,
    )
    (
        output, grad_tokens, grad_qkv, grad_out_t, grad_attn, grad_ffn, grad_router, up_sum, down_sum,
    ) = finish(sum_a, sum_b, up_sum, down_sum, output, grad_tokens)
    return (
        output,
        grad_tokens,
        grad_qkv,
        grad_out_t.T,
        grad_attn[0],
        grad_ffn[0],
        grad_router,
        up_sum[None],
        down_sum[None],
    )


def solution(mesh):
    return jax.shard_map(
        body,
        mesh=mesh,
        in_specs=(
            P(("expert", "shard"), None),
            P("expert", None),
            P(("expert", "shard"), None),
            P(("expert", "shard"), None),
            P(None, ("expert", "shard")),
            P(("expert", "shard")),
            P(("expert", "shard")),
            P(("expert", "shard"), None),
            P("expert", None, None),
            P("expert", None, None),
            P(("expert", "shard"), None),
        ),
        out_specs=(
            P(("expert", "shard"), None),
            P(("expert", "shard"), None),
            P(("expert", "shard"), None),
            P(None, ("expert", "shard")),
            P(("expert", "shard")),
            P(("expert", "shard")),
            P(("expert", "shard"), None),
            P("expert", "shard", None),
            P("expert", None, "shard"),
        ),
        check_vma=False,
    )
```

```python
import jax
import jax.numpy as jnp
import numpy as np
from jax import lax
from jax.experimental import pallas as pl
from jax.experimental.pallas import tpu as pltpu
from jax.sharding import PartitionSpec as P

D = 1536
HEADS_Q = 12
HEADS_KV = 2
HEAD_DIM = 128
FF = 768
TOP = 4
EXPERTS = 32
CAP = 48
WIDTH_Q = HEADS_Q * HEAD_DIM
WIDTH_KV = HEADS_KV * HEAD_DIM
REPEAT = HEADS_Q // HEADS_KV

norm_eps = 1e-06
rope_base = 1000000.0
MESH = pl.DeviceIdType.MESH
F32 = jnp.float32
BF16 = jnp.bfloat16

PIECE = 12
PADDED = 16
BLOCK = 48
WA = 2048
WB = 1664
SMALL = WB - D
JOB_A = 1920
JOB_B = WA + WB - JOB_A
QUARTER = WA // 4


def place():
    e = lax.axis_index("expert")
    return e // 8, (e // 2) % 4, e % 2, lax.axis_index("shard")


def device(y, z, c, x):
    return ((y * 4 + z) * 2 + c, x)


def greet(devices):
    barrier = pltpu.get_barrier_semaphore()
    for d in devices:
        pl.semaphore_signal(barrier, inc=1, device_id=d, device_id_type=MESH)
    pl.semaphore_wait(barrier, len(devices))


class Links:
    def __init__(self, send, recv):
        self.send, self.recv, self.made = send, recv, []

    def push(self, src, dst, where):
        i = len(self.made)
        copy = pltpu.make_async_remote_copy(
            src_ref=src,
            dst_ref=dst,
            send_sem=self.send.at[i],
            recv_sem=self.recv.at[i],
            device_id=where,
            device_id_type=MESH,
        )
        copy.start()
        self.made.append(copy)
        return copy

    def drain(self):
        for copy in self.made:
            copy.wait_send()


def neighbours(y, z, c, x):
    other = 1 - c
    return dict(
        x=[device(y, z, c, (x + d) % 4) for d in (1, 2, 3)],
        y=(device((y + 1) % 4, z, c, x), device((y + 3) % 4, z, c, x)),
        z=(device(y, (z + 1) % 4, c, x), device(y, (z + 3) % 4, c, x)),
        core=device(y, z, other, x),
    )


def everyone_near(near):
    return list(near["x"]) + list(near["y"]) + list(near["z"]) + [near["core"]]


def pick_rows(rows, columns, row_block, column_block):
    r = lax.broadcasted_iota(jnp.int32, (rows, columns), 0)
    q = lax.broadcasted_iota(jnp.int32, (rows, columns), 1)
    same = (r // row_block == q // column_block) & (r % row_block == q % column_block)
    return jnp.where(same, 1.0, 0.0).astype(BF16)


def faces(y, z, c, x):
    along_z, along_y = [], []
    for d in range(4):
        for k in range(2):
            core = c if k == 0 else 1 - c
            along_z.append((device(y, (z + d) % 4, core, x), (z + d) % 4, core))
            along_y.append((device((y + d) % 4, z, core, x), (y + d) % 4, core))
    return along_z, along_y


def cross(y, z, c, x):
    along_z, along_y = faces(y, z, c, x)
    return [f[0] for f in along_z[1:] + along_y[2:]]


def lines(y, z, c, x):
    return (
        [device((y + d) % 4, z, c, x) for d in (1, 2, 3)],
        [device(y, (z + d) % 4, c, x) for d in (1, 2, 3)],
    )


def route(top_experts, named, own_slot):
    experts = iota((EXPERTS, COUNT), 0)
    names = sum(jnp.where(top_experts[k : k + 1, :] == experts, 1.0, 0.0) for k in range(TOP))
    low = names.astype(BF16)
    earlier = hot(iota((COUNT, COUNT), 0) < iota((COUNT, COUNT), 1))
    own_slot[...] = jnp.where(names > 0, mul(low, earlier), -1.0).astype(BF16)
    named[...] = mul(low, hot(iota((EXPERTS, 128), 0) == iota((EXPERTS, 128), 1)), TN)


def rope(lengths, rates, cosd, sind, x):
    own = x * COUNT + iota((COUNT, 1), 0)
    first = lengths[0, 0]
    second = first + lengths[0, 1]
    third = second + lengths[0, 2]
    start = jnp.zeros((COUNT, 1), jnp.int32)
    for end in (first, second, third):
        start = jnp.where(own >= end, end, start)
    angles = (own - start).astype(F32) * rates[...]
    cosd[...] = jnp.cos(angles)
    sine = jnp.sin(angles)
    sind[...] = jnp.where(iota((COUNT, HEAD_DIM), 1) < HEAD_DIM // 2, -sine, sine)


def fill_pack(pack, w_qkv, w_out_t, router, gain_attn, gain_ffn):
    pack[...] = jnp.zeros_like(pack)
    pack[0:PIECE, 0:WA] = w_qkv[...]
    pack[0:PIECE, WA : WA + D] = w_out_t[...]
    small = mul(router[...], hot(iota((EXPERTS, SMALL), 0) == iota((EXPERTS, SMALL), 1)))
    diagonal = iota((PIECE, PIECE), 0) == iota((PIECE, PIECE), 1)
    for k, gain in enumerate((gain_attn, gain_ffn)):
        column = jnp.sum(jnp.where(diagonal, gain[...].astype(F32), 0.0), axis=1, keepdims=True)
        small = jnp.where(iota((PIECE, SMALL), 1) == EXPERTS + k, column, small)
    pack[0:PIECE, WA + D :] = small.astype(BF16)


def slot_hits(slot_of, hits, experts):
    p = iota((1, SLOTS), 1)
    q = p % PIECE_SLOTS
    wanted = ((p // PIECE_SLOTS) * PART + q % PART).astype(F32)
    local = q // PART
    expand = hot(iota((EXPERTS, SLOTS), 0) == experts(local))

    def step(s, carry):
        hits[s] = hot(mul(slot_of[s], expand, TN) == wanted)
        return carry

    lax.fori_loop(0, 4, step, 0)


def gather_kernel(
    lengths, rates, w_qkv, w_out_t, router, gain_attn, gain_ffn, top_experts, cotangent,
    full_a, full_b, named, hot_a, hot_b, dy_a, dy_b, cosd, sind,
    pack, xbuf, own_0, own_1, own_2, own_slot, slot_y, slot_z, send, recv, local,
):
    y, z, c, x = place()
    near = neighbours(y, z, c, x)
    line_y, line_z = lines(y, z, c, x)
    fill_pack(pack, w_qkv, w_out_t, router, gain_attn, gain_ffn)
    greet(everyone_near(near) + [line_y[1], line_z[1]])
    link = Links(send, recv)
    first = [link.push(pack, xbuf.at[x], near["x"][d]) for d in range(3)]
    xbuf[pl.ds(x, 1)] = pack[...][None]
    half_a, half_b = cotangent.at[:, pl.ds(0, HALF)], cotangent.at[:, pl.ds(HALF, HALF)]
    kept = [
        pltpu.make_async_copy(half_a, dy_a.at[y], local.at[2]),
        pltpu.make_async_copy(half_b, dy_b.at[z], local.at[3]),
    ]
    for copy in kept:
        copy.start()
    dys = [
        around(link, half_a, dy_a, y, *near["y"]),
        around(link, half_b, dy_b, z, *near["z"]),
    ]
    for copy in first:
        copy.wait_recv()
    select = pick_rows(BLOCK, 4 * PADDED, PIECE, PADDED)
    pieces = xbuf[...].reshape(4 * PADDED, WA + WB)
    quarter = pl.multiple_of(x * QUARTER, QUARTER)
    mine = xbuf[:, :, pl.ds(quarter, QUARTER)].reshape(4 * PADDED, QUARTER)
    own_0[...] = mul(select, mine).astype(BF16)
    own_1[...] = mul(select, pieces[:, WA : WA + HALF]).astype(BF16)
    own_2[...] = mul(select, pieces[:, WA + HALF :]).astype(BF16)
    spot = dict(y=y, z=z)
    jobs = [
        dict(own=own_0, full=full_a, off=quarter, half=QUARTER // 2, close="y", far="z", i=0),
        dict(own=own_1, full=full_b, off=0, half=HALF // 2, close="y", far="z", i=1),
        dict(own=own_2, full=full_b, off=HALF, half=512, close="z", far="y", i=4),
    ]

    def block_at(j, far, close, first=0, count=None):
        yy, zz = (far, close) if j["far"] == "y" else (close, far)
        count = j["own"].shape[1] if count is None else count
        lanes = j["off"] + first
        lanes = lanes if isinstance(lanes, int) else pl.multiple_of(lanes, 128)
        return j["full"].at[yy, zz, c, :, pl.ds(lanes, count)]

    def line_at(j, far, start=0, count=4):
        return block_at(j, far, pl.ds(start, count))

    for j in jobs:
        j["p"], j["q"] = spot[j["close"]], spot[j["far"]]
        here = block_at(j, j["q"], j["p"])
        plus, minus = near[j["close"]]
        j["up"] = link.push(j["own"], here, plus)
        j["down"] = link.push(j["own"], here, minus)
        j["core"] = []
        if j["full"] is full_b:
            j["core"].append(link.push(j["own"], here, near["core"]))
        j["local"] = pltpu.make_async_copy(j["own"], here, local.at[j["i"]])
        j["local"].start()
    route(top_experts, named, own_slot)
    slot_y[pl.ds(y, 1)] = own_slot[...][None]
    slot_z[pl.ds(z, 1)] = own_slot[...][None]
    slots = [link.push(own_slot, slot_y.at[y], peer) for peer in line_y]
    slots += [link.push(own_slot, slot_z.at[z], peer) for peer in line_z]
    for j in jobs:
        plus, minus = near[j["close"]]
        left, right = (j["p"] + 3) % 4, (j["p"] + 1) % 4
        j["up"].wait_recv()
        part = block_at(j, j["q"], left, 0, j["half"])
        j["up2"] = link.push(part, part, plus)
        j["down"].wait_recv()
        part = block_at(j, j["q"], right, j["half"], j["own"].shape[1] - j["half"])
        j["down2"] = link.push(part, part, minus)
        if j["full"] is full_b:
            for side in (left, right):
                block = block_at(j, j["q"], side)
                j["core"].append(link.push(block, block, near["core"]))

    around_x = {}

    def quarter_at(far, which, start=0, count=4):
        lanes = pl.ds(pl.multiple_of(which * QUARTER, QUARTER), QUARTER)
        return full_a.at[pl.ds(start, count), far, c, :, lanes]

    def x_start(name, far):
        block = quarter_at(far, x)
        around_x[name] = [
            far, link.push(block, block, near["x"][0]), link.push(block, block, near["x"][2])
        ]

    def x_forward(name):
        far, up, down = around_x[name]
        up.wait_recv()
        part = quarter_at(far, (x + 3) % 4, 0, 2)
        up = link.push(part, part, near["x"][0])
        down.wait_recv()
        part = quarter_at(far, (x + 1) % 4, 2, 2)
        around_x[name] = [far, up, link.push(part, part, near["x"][2])]

    def x_done(name):
        far, up, down = around_x[name]
        up.wait_recv()
        down.wait_recv()
        line = full_a.at[:, far, c]
        jobs[0]["core"].append(link.push(line, line, near["core"]))

    def far_start(j):
        j["up2"].wait_recv()
        j["down2"].wait_recv()
        block = block_at(j, j["q"], (j["p"] + 2) % 4)
        j["local"].wait()
        plus, minus = near[j["far"]]
        line = line_at(j, j["q"])
        j["up"] = link.push(line, line, plus)
        j["down"] = link.push(line, line, minus)
        if j["full"] is full_b:
            j["core"].append(link.push(block, block, near["core"]))
        else:
            x_start("own", j["q"])

    far_start(jobs[0])
    far_start(jobs[2])
    dys = dys[0]() + dys[1]()
    for copy in slots:
        copy.wait_recv()
    def far_next(j):
        plus, minus = near[j["far"]]
        left, right = (j["q"] + 3) % 4, (j["q"] + 1) % 4
        j["up"].wait_recv()
        part = line_at(j, left, 0, 2)
        j["up2"] = link.push(part, part, plus)
        j["down"].wait_recv()
        part = line_at(j, right, 2, 2)
        j["down2"] = link.push(part, part, minus)
        if j["full"] is full_b:
            for side in (left, right):
                block = line_at(j, side)
                j["core"].append(link.push(block, block, near["core"]))
        else:
            x_start("left", left)
            x_start("right", right)

    def far_end(j):
        opposite = (j["q"] + 2) % 4
        j["up2"].wait_recv()
        j["down2"].wait_recv()
        if j["full"] is full_b:
            block = line_at(j, opposite)
            j["core"].append(link.push(block, block, near["core"]))
        else:
            x_start("opposite", opposite)

    far_next(jobs[0])
    far_start(jobs[1])
    x_forward("own")
    far_end(jobs[0])
    far_next(jobs[2])
    x_done("own")
    x_forward("left")
    x_forward("right")
    slot_hits(slot_y, hot_a, lambda e: y * 8 + e)
    far_next(jobs[1])
    slot_hits(slot_z, hot_b, lambda e: (e // 2) * 8 + z * 2 + e % 2)
    far_end(jobs[2])
    x_done("left")
    x_done("right")
    x_forward("opposite")
    far_end(jobs[1])
    rope(lengths, rates, cosd, sind, x)
    x_done("opposite")
    for j in jobs:
        for copy in j["core"]:
            copy.wait_recv()
    for wait in dys:
        wait()
    for copy in kept:
        copy.wait()
    link.drain()


def gather_weights(*operands):
    inside = pl.BlockSpec(memory_space=pltpu.VMEM)
    anywhere = pl.BlockSpec(memory_space=pltpu.HBM)
    copies = 3 + 2 * 15 + 8 + 16 + 4 + 6 + 8
    return pl.pallas_call(
        gather_kernel,
        name="gather_weights",
        out_shape=(
            jax.ShapeDtypeStruct((4, 4, 2, BLOCK, WA), BF16),
            jax.ShapeDtypeStruct((4, 4, 2, BLOCK, WB), BF16),
            jax.ShapeDtypeStruct((COUNT, 128), F32),
            jax.ShapeDtypeStruct((4, COUNT, SLOTS), BF16),
            jax.ShapeDtypeStruct((4, COUNT, SLOTS), BF16),
            jax.ShapeDtypeStruct((4, COUNT, HALF), BF16),
            jax.ShapeDtypeStruct((4, COUNT, HALF), BF16),
            jax.ShapeDtypeStruct((COUNT, HEAD_DIM), F32),
            jax.ShapeDtypeStruct((COUNT, HEAD_DIM), F32),
        ),
        in_specs=[pl.BlockSpec(memory_space=pltpu.SMEM)] + [inside] * 8,
        out_specs=(anywhere,) * 2 + (inside,) * 3 + (anywhere,) * 2 + (inside,) * 2,
        scratch_shapes=[
            pltpu.VMEM((PADDED, WA + WB), BF16),
            pltpu.VMEM((4, PADDED, WA + WB), BF16),
            pltpu.VMEM((BLOCK, QUARTER), BF16),
            pltpu.VMEM((BLOCK, HALF), BF16),
            pltpu.VMEM((BLOCK, WB - HALF), BF16),
            pltpu.VMEM((EXPERTS, COUNT), BF16),
            pltpu.VMEM((4, EXPERTS, COUNT), BF16),
            pltpu.VMEM((4, EXPERTS, COUNT), BF16),
            pltpu.SemaphoreType.DMA((copies,)),
            pltpu.SemaphoreType.DMA((copies,)),
            pltpu.SemaphoreType.DMA((5,)),
        ],
        compiler_params=pltpu.CompilerParams(
            collective_id=0, has_side_effects=True, vmem_limit_bytes=60 * 1024 * 1024
        ),
        cost_estimate=pl.CostEstimate(flops=0, bytes_accessed=24_000_000, transcendentals=0),
    )(*operands)


def add_blocks(dst, far, start, count, sources):
    def step(i, carry):
        total = dst[far, start + i].astype(F32)
        for source in sources:
            total = total + source(i).astype(F32)
        dst[far, start + i] = total.astype(BF16)
        return carry

    lax.fori_loop(0, count, step, 0)


def scatter_kernel(
    ga, gb, gs, up_in, down_in, up_far, down_far, late_a, late_b, came_a, came_b, middle,
    out_a, out_b, up_out, down_out, output,
    core_a, core_b, mine_a, mine_b, one_a, one_b, two_a, two_b,
    half_a0, half_a1, half_b0, half_b1, last_a, last_b, xout, xin,
    ups, downs, up_got, up_land, mid, land_a, land_b,
    send, recv, local,
):
    y, z, c, x = place()
    near = neighbours(y, z, c, x)
    line_y, line_z = lines(y, z, c, x)
    greet(everyone_near(near) + [line_y[1], line_z[1]])
    link = Links(send, recv)
    other = 1 - c
    jobs = [
        dict(src=[(lambda f, s: ga.at[f, :, s, :, pl.ds(0, JOB_A)], 0, JOB_A)], core=core_a, mine=mine_a, one=one_a, two=two_a,
             halves=(half_a0, half_a1), last=last_a, far="y", close="z", q=y, p=z,
             width=JOB_A, half=1024, lane=0, i=0),
        dict(src=[
                 (lambda f, s: ga.at[:, f, s, :, pl.ds(JOB_A, WA - JOB_A)], 0, WA - JOB_A),
                 (lambda f, s: gb.at[:, f, s], WA - JOB_A, D),
                 (lambda f, s: gs.at[:, f, s], WA - JOB_A + D, SMALL),
             ],
             core=core_b, mine=mine_b, one=one_b, two=two_b,
             halves=(half_b0, half_b1), last=last_b, far="z", close="y", q=z, p=y,
             width=JOB_B, half=896, lane=JOB_A, i=1),
    ]
    slots = 0
    for step in (2, 3, 1, 0):
        for j in jobs:
            f = (j["q"] + step) % 4
            j[step] = []
            for source, lane, width in j["src"]:
                lanes = pl.ds(lane, width)
                pushed = link.push(
                    source(f, other), j["core"].at[f, :, :, lanes], near["core"]
                )
                kept = pltpu.make_async_copy(
                    source(f, c), j["mine"].at[f, :, :, lanes], local.at[slots]
                )
                slots += 1
                kept.start()
                j[step].append((pushed, kept))

    first, second = pl.ds(0, COUNT // 2), pl.ds(COUNT // 2, COUNT // 2)
    fetches = [(up_far, up_got)]
    for i, d in enumerate((3, 1, 0)):
        up_rows = pl.ds(pl.multiple_of(((x + d) % 4) * UP_PART, UP_PART), UP_PART)
        fetches.append((up_in.at[up_rows], ups.at[i]))
    lanes = pl.ds(pl.multiple_of(x * DOWN_PART, 128), DOWN_PART)
    fetches += [
        (down_in.at[:, lanes], downs.at[0]),
        (down_far, downs.at[pl.ds(1, 2)]),
        (middle, mid),
        (came_a, land_a.at[:, first]),
        (came_b, land_b.at[:, first]),
        (late_a.at[y], land_a.at[y, second]),
        (late_b.at[z], land_b.at[z, second]),
    ]
    fetches = [
        pltpu.make_async_copy(src, dst, local.at[slots + i]) for i, (src, dst) in enumerate(fetches)
    ]
    for fetch in fetches:
        fetch.start()
    for fetch in fetches[:4]:
        fetch.wait()
    sides = []
    for i, peer in enumerate((near["x"][2], near["x"][0])):
        up_rows = slice(i * UP_HALF, (i + 1) * UP_HALF)
        ups[i, up_rows, :] = (ups[i, up_rows, :].astype(F32) + up_got[i].astype(F32)).astype(BF16)
        sides.append(link.push(ups.at[i], up_land.at[i], peer))

    def ready(j, step):
        for pushed, kept in j[step]:
            pushed.wait_recv()
            kept.wait()

    for j in jobs:
        f = (j["q"] + 2) % 4
        ready(j, 2)
        mine = j["mine"]
        add_blocks(j["core"], f, 0, 4, [lambda i, f=f, m=mine: m[f, i]])
        plus, minus = near[j["far"]]
        j["down"] = link.push(j["core"].at[f, pl.ds(0, 2)], j["one"].at[0], minus)
        j["up"] = link.push(j["core"].at[f, pl.ds(2, 2)], j["one"].at[1], plus)
    for j in jobs:
        plus, minus = near[j["far"]]
        mine, one = j["mine"], j["one"]
        f = (j["q"] + 3) % 4
        ready(j, 3)
        add_blocks(j["core"], f, 2, 2, [lambda i, f=f, m=mine: m[f, i + 2]])
        j["down"].wait_recv()
        add_blocks(
            j["core"], f, 0, 2, [lambda i, f=f, m=mine: m[f, i], lambda i, o=one: o[0, i]]
        )
        j["down2"] = link.push(j["core"].at[f], j["two"].at[0], minus)
        f = (j["q"] + 1) % 4
        ready(j, 1)
        add_blocks(j["core"], f, 0, 2, [lambda i, f=f, m=mine: m[f, i]])
        j["up"].wait_recv()
        add_blocks(
            j["core"], f, 2, 2, [lambda i, f=f, m=mine: m[f, i + 2], lambda i, o=one: o[1, i]]
        )
        j["up2"] = link.push(j["core"].at[f], j["two"].at[1], plus)
    for j in jobs:
        mine, two = j["mine"], j["two"]
        f = j["q"]
        ready(j, 0)
        j["down2"].wait_recv()
        j["up2"].wait_recv()
        add_blocks(
            j["core"], f, 0, 4,
            [lambda i, f=f, m=mine: m[f, i], lambda i, t=two: t[0, i], lambda i, t=two: t[1, i]],
        )
        plus, minus = near[j["close"]]
        g = (j["p"] + 2) % 4
        h, w = j["half"], j["width"]
        j["down"] = link.push(j["core"].at[f, g, :, pl.ds(0, h)], j["halves"][0], minus)
        j["up"] = link.push(j["core"].at[f, g, :, pl.ds(h, w - h)], j["halves"][1], plus)
    for j in jobs:
        plus, minus = near[j["close"]]
        f, h, w, core = j["q"], j["half"], j["width"], j["core"]
        g = (j["p"] + 3) % 4
        j["down"].wait_recv()
        core[f, g, :, 0:h] = (
            core[f, g, :, 0:h].astype(F32) + j["halves"][0][...].astype(F32)
        ).astype(BF16)
        j["down2"] = link.push(core.at[f, g], j["last"].at[0], minus)
        g = (j["p"] + 1) % 4
        j["up"].wait_recv()
        core[f, g, :, h:w] = (
            core[f, g, :, h:w].astype(F32) + j["halves"][1][...].astype(F32)
        ).astype(BF16)
        j["up2"] = link.push(core.at[f, g], j["last"].at[1], plus)
    late = []
    for src, dst, me, line in ((late_a, land_a, y, line_y), (late_b, land_b, z, line_z)):
        for d in (1, 2, 3):
            late.append(link.push(src.at[(me + d) % 4], dst.at[me, second], line[d - 1]))
    select = pick_rows(4 * PADDED, BLOCK, PADDED, PIECE)
    for j in jobs:
        f, g = j["q"], j["p"]
        j["down2"].wait_recv()
        j["up2"].wait_recv()
        total = (
            j["core"][f, g].astype(F32)
            + j["last"][0].astype(F32)
            + j["last"][1].astype(F32)
        ).astype(BF16)
        spread = jnp.dot(select, total, preferred_element_type=F32).astype(BF16)
        xout[:, :, j["lane"] : j["lane"] + j["width"]] = spread.reshape(4, PADDED, j["width"])
    final = [
        link.push(xout.at[(x + d) % 4], xin.at[d - 1], near["x"][d - 1]) for d in (1, 2, 3)
    ]
    for copy in final:
        copy.wait_recv()
    mine = xout[x].astype(F32)
    for d in range(3):
        mine = mine + xin[d].astype(F32)
    out_a[...] = mine[:, :WA]
    out_b[...] = mine[:, WA:]
    for push in sides:
        push.wait_recv()
    up_out[...] = ups[2].astype(F32) + up_land[0].astype(F32) + up_land[1].astype(F32)
    for fetch in fetches[4:]:
        fetch.wait()
    down_out[...] = downs[0].astype(F32) + downs[1].astype(F32) + downs[2].astype(F32)
    for push in late:
        push.wait_recv()
    for half, landed in enumerate((land_a, land_b)):
        lanes = slice(half * HALF, (half + 1) * HALF)
        total = mid[:, lanes]
        for s in range(4):
            total = total + landed[s].astype(F32)
        output[:, lanes] = total.astype(BF16)
    link.drain()


def scatter_sums(*operands):
    copies = 2 * (4 + 4 + 4) + 8 + 3 + 6 + 2
    vmem = pltpu.VMEM
    scratch = []
    for shape in ((4, 4), (4, 4), (2, 2), (2, 4)):
        scratch += [vmem((*shape, BLOCK, JOB_A), BF16), vmem((*shape, BLOCK, JOB_B), BF16)]
    scratch += [
        vmem((BLOCK, 1024), BF16),
        vmem((BLOCK, JOB_A - 1024), BF16),
        vmem((BLOCK, 896), BF16),
        vmem((BLOCK, JOB_B - 896), BF16),
        vmem((2, BLOCK, JOB_A), BF16),
        vmem((2, BLOCK, JOB_B), BF16),
        vmem((4, PADDED, WA + WB), BF16),
        vmem((3, PADDED, WA + WB), BF16),
        vmem((3, UP_PART, 2 * FF), BF16),
        vmem((3, FF, DOWN_PART), BF16),
        vmem((2, UP_HALF, 2 * FF), BF16),
        vmem((2, UP_PART, 2 * FF), BF16),
        vmem((COUNT, D), F32),
        vmem((4, COUNT, HALF), BF16),
        vmem((4, COUNT, HALF), BF16),
        pltpu.SemaphoreType.DMA((copies,)),
        pltpu.SemaphoreType.DMA((copies,)),
        pltpu.SemaphoreType.DMA((16 + 11,)),
    ]
    return pl.pallas_call(
        scatter_kernel,
        name="scatter_sums",
        out_shape=(
            jax.ShapeDtypeStruct((PADDED, WA), F32),
            jax.ShapeDtypeStruct((PADDED, WB), F32),
            jax.ShapeDtypeStruct((UP_PART, 2 * FF), F32),
            jax.ShapeDtypeStruct((FF, DOWN_PART), F32),
            jax.ShapeDtypeStruct((COUNT, D), BF16),
        ),
        in_specs=[pl.BlockSpec(memory_space=pltpu.HBM)] * 12,
        out_specs=(pl.BlockSpec(memory_space=pltpu.VMEM),) * 5,
        scratch_shapes=scratch,
        compiler_params=pltpu.CompilerParams(
            collective_id=1, has_side_effects=True, vmem_limit_bytes=60 * 1024 * 1024
        ),
        cost_estimate=pl.CostEstimate(flops=0, bytes_accessed=24_000_000, transcendentals=0),
    )(*operands)


ROWS = EXPERTS * CAP
TILE = 256
PARTS = 3
PART = CAP // PARTS
SLOTS = 8 * CAP
PIECE_SLOTS = 8 * PART
PIECE_ROWS = EXPERTS * PART
HALF = D // 2
LANES = 128
SCALE = HEAD_DIM ** (-0.5)
GROUP_ROWS = 1024
COUNT = 256
NT = (((1,), (1,)), ((), ()))
TN = (((0,), (0,)), ((), ()))


def mul(a, b, dims=None):
    if dims is None:
        return jnp.dot(a, b, preferred_element_type=F32)
    return lax.dot_general(a, b, dims, preferred_element_type=F32)


def thirds(v):
    high = v.astype(BF16)
    rest = v - high.astype(F32)
    middle = rest.astype(BF16)
    return high, middle, (rest - middle.astype(F32)).astype(BF16)


def exact(v, one_hot, dims=None):
    return sum(mul(part, one_hot, dims) for part in thirds(v))


def exact_right(one_hot, v):
    return sum(mul(one_hot, part, NT) for part in thirds(v))


def iota(shape, axis):
    return lax.broadcasted_iota(jnp.int32, shape, axis)


def hot(same):
    return jnp.where(same, 1.0, 0.0).astype(BF16)


class Moves(Links):
    def __init__(self, send, recv, local):
        super().__init__(send, recv)
        self.local, self.kept = local, 0

    def keep(self, src, dst):
        copy = pltpu.make_async_copy(src, dst, self.local.at[self.kept])
        self.kept += 1
        copy.start()
        return copy

    def send_or_keep(self, i, src, dst, where):
        if i == 0:
            return self.keep(src, dst).wait
        return self.push(src, dst, where).wait_recv


def to_slots(hits, rows, stage, piece):
    columns = slice(piece * PIECE_SLOTS, (piece + 1) * PIECE_SLOTS)
    for s in range(4):
        taken = mul(hits[s, :, columns], rows[s], TN).astype(BF16)
        stage[piece, :, s] = taken.reshape(8, PART, taken.shape[1])


def deliver(moves, at, stage_a, stage_b, rows, split, piece):
    y, z, c, x = at
    along_z, along_y = faces(y, z, c, x)
    width = rows.shape[4]
    waits = []
    for i, (where, zt, ct) in enumerate(along_z):
        dst = rows.at[piece, z, pl.ds(c * 4, 4), :, pl.ds(0, split)]
        waits.append(moves.send_or_keep(i, stage_a.at[piece, zt * 2 + ct], dst, where))
    for i, (where, yt, ct) in enumerate(along_y):
        dst = rows.at[piece, :, c * 4 + y, :, pl.ds(split, width - split)]
        waits.append(moves.send_or_keep(i, stage_b.at[piece, yt * 2 + ct], dst, where))
    return waits


def give_back(moves, at, rows, back_a, back_b, split, piece):
    y, z, c, x = at
    along_z, along_y = faces(y, z, c, x)
    width = rows.shape[4]
    waits = []
    for i, (where, zt, ct) in enumerate(along_z):
        src = rows.at[piece, zt, pl.ds(ct * 4, 4), :, pl.ds(0, split)]
        dst = back_a.at[piece, z * 2 + c, :, :, pl.ds(0, split)]
        waits.append(moves.send_or_keep(i, src, dst, where))
    for i, (where, yt, ct) in enumerate(along_y):
        src = rows.at[piece, :, ct * 4 + yt, :, pl.ds(split, width - split)]
        dst = back_b.at[piece, y * 2 + c, :, :, pl.ds(0, width - split)]
        waits.append(moves.send_or_keep(i, src, dst, where))
    return waits


def slot_fold():
    p = iota((LANES, SLOTS), 1)
    return hot((p // PIECE_SLOTS) * PART + p % PART == iota((LANES, SLOTS), 0))


def slot_owner():
    return (iota((8, SLOTS), 1) % PIECE_SLOTS) // PART == iota((8, SLOTS), 0)


def add_up(hits, back, s, width):
    rows = back[:, :, s, :, 0:width].reshape(SLOTS, width)
    return mul(hits[s], rows).astype(BF16)


def around(link, own, land, me, plus, minus):
    up = link.push(own, land.at[me], plus)
    down = link.push(own, land.at[me], minus)

    def forward():
        half = COUNT // 2
        up.wait_recv()
        block = land.at[(me + 3) % 4, pl.ds(0, half)]
        waits = [link.push(block, block, plus).wait_recv]
        down.wait_recv()
        block = land.at[(me + 1) % 4, pl.ds(half, half)]
        return waits + [link.push(block, block, minus).wait_recv]

    return forward


def gelu_parts(g):
    inner = 0.7978845608 * (g + 0.044715 * g * g * g)
    th = jnp.tanh(inner)
    half = 0.5 * (1.0 + th)
    slope = half + 0.5 * g * (1.0 - th * th) * (0.7978845608 * (1.0 + 0.134145 * g * g))
    return g * half, slope


def experts_kernel(
    hot_a_in, hot_b_in, nf_a_in, nf_b_in, dy_in, tiles_in, gate_up, down,
    back_a, back_b, out, up_out, down_out, tiles_back,
    hot_a, hot_b, nf_a, nf_b, stage_a, stage_b, rows, dy,
    gu, dn, raw, mixed, ghid, grow, eo, up_grad, down_grad, tiles, slope_tiles,
    send, recv, local, load_sem,
):
    at = place()
    y, z, c, x = at
    me = (y * 4 + z) * 2 + c
    loads = [
        pltpu.make_async_copy(src, dst, load_sem.at[i])
        for i, (src, dst) in enumerate(
            (
                (hot_a_in, hot_a), (nf_a_in, nf_a), (hot_b_in, hot_b), (nf_b_in, nf_b),
                (dy_in, dy), (down.at[0], dn), (gate_up.at[0], gu), (tiles_in, tiles),
            )
        )
    ]
    for load in loads:
        load.start()
    greet(cross(*at))
    moves = Moves(send, recv, local)
    for load in loads[:4]:
        load.wait()
    waits = []
    for piece in range(PARTS):
        to_slots(hot_a, nf_a, stage_a, piece)
        to_slots(hot_b, nf_b, stage_b, piece)
        waits.append(deliver(moves, at, stage_a, stage_b, rows, HALF, piece))
    for load in loads[4:]:
        load.wait()

    def raw_tile(j, carry):
        lanes = pl.ds(pl.multiple_of(j * TILE, TILE), TILE)
        raw[:, lanes] = mul(dy[...].reshape(ROWS, D), dn[lanes, :], NT)
        return carry

    lax.fori_loop(0, FF // TILE, raw_tile, 0, unroll=True)
    back_waits = []
    slope_tiles[...] = jnp.zeros_like(slope_tiles)
    for piece in range(PARTS):
        for wait in waits[piece]:
            wait()
        block = slice(piece * PIECE_ROWS, (piece + 1) * PIECE_ROWS)
        slot = piece * PART + iota((PIECE_ROWS, LANES), 0) % PART
        held = iota((PIECE_ROWS, LANES), 1) == slot
        spread = jnp.broadcast_to(tiles[:, 0:4, :][:, :, None, :], (8, 4, PART, LANES))
        spread = spread.reshape(PIECE_ROWS, LANES)
        gate = jnp.sum(jnp.where(held, spread, 0.0), axis=1, keepdims=True)

        def hidden_tile(j, slope_sum, piece=piece, block=block, gate=gate):
            lanes = pl.ds(pl.multiple_of(j * TILE, TILE), TILE)
            upper = pl.ds(pl.multiple_of(FF + j * TILE, TILE), TILE)
            g = mul(rows[piece].reshape(PIECE_ROWS, D), gu[:, lanes])
            act, slope = gelu_parts(g)
            u = mul(rows[piece].reshape(PIECE_ROWS, D), gu[:, upper])
            m = raw[block, lanes]
            both = act * u
            mixed[block, lanes] = (both * gate).astype(BF16)
            slope_sum = slope_sum + jnp.sum(both * m, axis=1, keepdims=True)
            m = m * gate
            ghid[block, lanes] = (m * u * slope).astype(BF16)
            ghid[block, upper] = (m * act).astype(BF16)
            return slope_sum

        slopes = lax.fori_loop(
            0, FF // TILE, hidden_tile, jnp.zeros((PIECE_ROWS, 1), F32), unroll=True
        )
        slopes = jnp.where(held, slopes, 0.0).reshape(8, 4, PART, LANES)
        slope_tiles[:, 0:4, :] += jnp.sum(slopes, axis=2)

        def rows_tile(j, carry, piece=piece, block=block):
            lanes = pl.ds(pl.multiple_of(j * TILE, TILE), TILE)
            part = mul(ghid[block, :], gu[lanes, :], NT).astype(BF16)
            grow[piece, :, :, :, lanes] = part.reshape(4, 8, PART, TILE)
            return carry

        lax.fori_loop(0, D // TILE, rows_tile, 0, unroll=True)
        back_waits += give_back(moves, at, grow, back_a, back_b, HALF, piece)

    along_z, _ = faces(*at)
    back_waits += [
        moves.send_or_keep(i, slope_tiles.at[zt * 2 + ct], tiles_back.at[z * 2 + c], where)
        for i, (where, zt, ct) in enumerate(along_z)
    ]

    def out_tile(j, carry):
        lanes = pl.ds(pl.multiple_of(j * TILE, TILE), TILE)
        part = mul(mixed[...], dn[:, lanes]).astype(BF16)
        eo[:, :, :, :, lanes] = part.reshape(PARTS, 4, 8, PART, TILE)
        return carry

    lax.fori_loop(0, D // TILE, out_tile, 0, unroll=2)
    back_waits.append(moves.keep(eo, out).wait)

    def up_tile(j, carry):
        lanes = pl.ds(pl.multiple_of(j * TILE, TILE), TILE)
        part = mul(rows[:, :, :, :, lanes].reshape(ROWS, TILE), ghid[...], TN)
        up_grad[lanes, :] = part.astype(BF16)
        return carry

    lax.fori_loop(0, D // TILE, up_tile, 0, unroll=2)
    back_waits.append(moves.keep(up_grad, up_out).wait)

    def down_tile(j, carry):
        lanes = pl.ds(pl.multiple_of(j * TILE, TILE), TILE)
        part = mul(mixed[:, lanes], dy[...].reshape(ROWS, D), TN)
        down_grad[lanes, :] = part.astype(BF16)
        return carry

    lax.fori_loop(0, FF // TILE, down_tile, 0, unroll=True)
    back_waits.append(moves.keep(down_grad, down_out).wait)
    for wait in back_waits:
        wait()
    moves.drain()


def run_experts(*operands):
    anywhere = pl.BlockSpec(memory_space=pltpu.HBM)
    vmem, dma = pltpu.VMEM, pltpu.SemaphoreType.DMA
    outs = (
        (PARTS, 8, 4, PART, HALF),
        (PARTS, 8, 4, PART, HALF),
        (PARTS, 4, 8, PART, D),
        (D, 2 * FF),
        (FF, D),
    )
    held = (
        (4, COUNT, SLOTS),
        (4, COUNT, SLOTS),
        (4, COUNT, HALF),
        (4, COUNT, HALF),
        (PARTS, 8, 4, PART, HALF),
        (PARTS, 8, 4, PART, HALF),
        (PARTS, 4, 8, PART, D),
        (PARTS, 4, 8, PART, D),
        (D, 2 * FF),
        (FF, D),
        None,
        (ROWS, FF),
        (ROWS, 2 * FF),
        (PARTS, 4, 8, PART, D),
        (PARTS, 4, 8, PART, D),
        (D, 2 * FF),
        (FF, D),
    )
    return pl.pallas_call(
        experts_kernel,
        name="experts",
        out_shape=tuple(jax.ShapeDtypeStruct(shape, BF16) for shape in outs)
        + (jax.ShapeDtypeStruct((8, 8, LANES), F32),),
        in_specs=[anywhere] * 8,
        out_specs=(anywhere,) * 6,
        scratch_shapes=[vmem(shape, BF16) if shape else vmem((ROWS, FF), F32) for shape in held]
        + [vmem((8, 8, LANES), F32)] * 2
        + [dma((84 + 7,)), dma((84 + 7,)), dma((15 + 1,)), dma((8,))],
        compiler_params=pltpu.CompilerParams(
            collective_id=2, has_side_effects=True, vmem_limit_bytes=60 * 1024 * 1024
        ),
        cost_estimate=pl.CostEstimate(
            flops=33_000_000_000, bytes_accessed=60_000_000, transcendentals=1_200_000
        ),
    )(*operands)


UP_PART = D // 4
UP_HALF = UP_PART // 2
DOWN_PART = D // 4
DOWN_HALF = FF // 2


def read_gains(small):
    select = hot(iota((8, SMALL), 1) == iota((8, SMALL), 0) + EXPERTS)
    select = jnp.where(iota((8, SMALL), 0) < 2, select, jnp.zeros_like(select))
    return mul(select, small, NT), select


def fill_bias(lengths, bias, x):
    first = lengths[0, 0]
    second = first + lengths[0, 1]
    third = second + lengths[0, 2]
    own = x * COUNT + iota((1, COUNT), 1)
    own_seg = sum(jnp.where(own >= end, 1, 0) for end in (first, second, third))

    def step(i, carry):
        base = pl.multiple_of(i * COUNT, COUNT)
        key = base + iota((COUNT, 1), 0)
        key_seg = sum(jnp.where(key >= end, 1, 0) for end in (first, second, third))
        allowed = (key_seg == own_seg) & (key <= own)
        bias[pl.ds(base, COUNT), :] = jnp.where(allowed, 0.0, -1e30)
        return carry

    lax.fori_loop(0, GROUP_ROWS // COUNT, step, 0)


def turn(v, cosd, sind):
    return v * cosd + pltpu.roll(v, HEAD_DIM // 2, 1) * sind


def forward_kernel(
    lengths, tokens, wq_in, wb_in, named, cosd, sind, hot_a_in, hot_b_in, dy_a_in, dy_b_in,
    q_out, kv_out, attended_out, middle_out, normed_out, tops, totals, gates_out,
    nf_a, nf_b, dy_rows, tiles_out,
    wq, wb, kv, own_kv, bias, vt, q, attended, middle, normed, nf,
    hot_a, hot_b, dy_a, dy_b, stage_a, stage_b, own_gates, gates_y, tiles, send, recv, local, load_sem,
):
    at = place()
    y, z, c, x = at
    line_y, line_z = lines(y, z, c, x)
    peers = [device(y, z, c, (x + d) % 4) for d in (1, 2, 3)]
    pairs = (
        (hot_a_in, hot_a), (dy_a_in, dy_a), (hot_b_in, hot_b), (dy_b_in, dy_b),
        (wb_in.at[:, pl.ds(D, SMALL)], wb.at[:, pl.ds(D, SMALL)]),
        (wq_in.at[:, pl.ds(D, 512)], wq.at[:, pl.ds(D, 512)]),
        (wq_in.at[:, pl.ds(0, D)], wq.at[:, pl.ds(0, D)]),
        (wb_in.at[:, pl.ds(0, D)], wb.at[:, pl.ds(0, D)]),
    )
    loads = [
        pltpu.make_async_copy(src, dst, load_sem.at[i]) for i, (src, dst) in enumerate(pairs)
    ]
    for load in loads:
        load.start()
    greet(cross(*at) + peers)
    moves = Moves(send, recv, local)
    for load in loads[0:4]:
        load.wait()
    for piece in range(PARTS):
        to_slots(hot_a, dy_a, stage_a, piece)
        to_slots(hot_b, dy_b, stage_b, piece)
    dy_waits = deliver(moves, at, stage_a, stage_b, dy_rows, HALF, slice(None))
    loads[4].wait()
    small = wb[:, D:]
    gains, _ = read_gains(small)
    xf = tokens[...].astype(F32)
    inverse = lax.rsqrt(jnp.mean(xf * xf, axis=1, keepdims=True) + norm_eps)
    normed[...] = (xf * inverse * gains[0:1, :]).astype(BF16)
    loads[5].wait()
    part = mul(normed[...], wq[:, D : D + 512])
    for g in range(HEADS_KV):
        key = turn(part[:, g * 128 : (g + 1) * 128], cosd[...], sind[...])
        own_kv[:, g * 256 : g * 256 + 128] = key.astype(BF16)
        own_kv[:, g * 256 + 128 : (g + 1) * 256] = part[:, 256 + g * 128 : 384 + g * 128].astype(BF16)
    rows = pl.ds(pl.multiple_of(x * COUNT, COUNT), COUNT)
    pushes = []
    for g in range(HEADS_KV):
        lanes = pl.ds(g * 256, 256)
        pushes.append(
            [moves.push(own_kv.at[:, lanes], kv.at[rows, lanes], peer) for peer in peers]
        )
    kv[rows, :] = own_kv[...]
    fill_bias(lengths, bias, x)
    loads[6].wait()

    def query_tile(j, carry):
        lanes = pl.ds(pl.multiple_of(j * 256, 256), 256)
        part = mul(normed[...], wq[:, lanes])
        q[:, lanes] = jnp.concatenate(
            [turn(part[:, h * 128 : (h + 1) * 128], cosd[...], sind[...]) for h in range(2)],
            axis=1,
        ).astype(BF16)
        return carry

    lax.fori_loop(0, D // 256, query_tile, 0, unroll=True)

    logits = jnp.where(named[...] > 0, mul(tokens[...], small), -jnp.inf)
    weight = jnp.exp(logits - jnp.max(logits, axis=1, keepdims=True))
    gates = weight / jnp.sum(weight, axis=1, keepdims=True)
    gates_out[...] = gates
    flat = exact_right(hot(iota((EXPERTS, LANES), 0) == iota((EXPERTS, LANES), 1)), gates)
    own_gates[...] = flat.reshape(4, 8, COUNT)
    gates_y[pl.ds(y, 1)] = own_gates[pl.ds(y, 1)]
    gate_pushes = [
        moves.push(own_gates.at[(y + d) % 4], gates_y.at[y], line_y[d - 1]) for d in (1, 2, 3)
    ]

    stays = [moves.keep(q, q_out), moves.keep(normed, normed_out)]
    for g in range(HEADS_KV):
        for push in pushes[g]:
            push.wait_recv()
        vt[g] = kv[:, g * 256 + 128 : (g + 1) * 256].T

        def head(i, carry, g=g):
            h = g * REPEAT + i
            lanes = pl.ds(pl.multiple_of(h * HEAD_DIM, HEAD_DIM), HEAD_DIM)
            s = mul(kv[:, g * 256 : g * 256 + 128], q[:, lanes], NT) * SCALE + bias[...]
            top = jnp.max(s, axis=0, keepdims=True)
            p = jnp.exp(s - top)
            total = jnp.sum(p, axis=0, keepdims=True)
            tops[pl.ds(h, 1), :] = top
            totals[pl.ds(h, 1), :] = total
            low = (p * (1.0 / total)).astype(BF16)
            attended[:, lanes] = mul(vt[g], low).T.astype(BF16)
            return carry

        lax.fori_loop(0, REPEAT, head, 0, unroll=3)

    stays.append(moves.keep(kv, kv_out))
    loads[7].wait()

    def out_tile(j, carry):
        lanes = pl.ds(pl.multiple_of(j * 256, 256), 256)
        middle[:, lanes] = tokens[:, lanes].astype(F32) + mul(attended[...], wb[lanes, 0:D], NT)
        return carry

    lax.fori_loop(0, D // 256, out_tile, 0, unroll=True)
    m = middle[...]
    inverse = lax.rsqrt(jnp.mean(m * m, axis=1, keepdims=True) + norm_eps)
    stays += [moves.keep(attended, attended_out), moves.keep(middle, middle_out)]
    nf[...] = (m * inverse * gains[1:2, :]).astype(BF16)
    half_a, half_b = nf.at[:, pl.ds(0, HALF)], nf.at[:, pl.ds(HALF, HALF)]
    last = [
        around(moves, half_a, nf_a, y, line_y[0], line_y[2]),
        around(moves, half_b, nf_b, z, line_z[0], line_z[2]),
    ]
    stays += [moves.keep(half_a, nf_a.at[y]), moves.keep(half_b, nf_b.at[z])]
    for push in gate_pushes:
        push.wait_recv()
    tiles[...] = jnp.zeros_like(tiles)
    owner = hot(slot_owner())
    for s in range(4):
        spread = exact(gates_y[s], owner, TN) * hot_a[s].astype(F32)
        row = jnp.sum(spread, axis=0, keepdims=True)
        tile = exact(jnp.where(slot_owner(), row, 0.0), slot_fold(), NT)
        tiles[:, s : s + 1, :] = tile[:, None, :]
    along_z, _ = faces(*at)
    dy_waits += [
        moves.send_or_keep(i, tiles.at[zt * 2 + ct], tiles_out.at[z * 2 + c], where)
        for i, (where, zt, ct) in enumerate(along_z)
    ]
    for wait in last[0]() + last[1]():
        wait()
    for stay in stays:
        stay.wait()
    for wait in dy_waits:
        wait()
    moves.drain()


def run_forward(*operands):
    anywhere = pl.BlockSpec(memory_space=pltpu.HBM)
    inside = pl.BlockSpec(memory_space=pltpu.VMEM)
    vmem, dma = pltpu.VMEM, pltpu.SemaphoreType.DMA
    shape = jax.ShapeDtypeStruct
    return pl.pallas_call(
        forward_kernel,
        name="forward",
        out_shape=(
            shape((COUNT, D), BF16),
            shape((GROUP_ROWS, 512), BF16),
            shape((COUNT, D), BF16),
            shape((COUNT, D), F32),
            shape((COUNT, D), BF16),
            shape((16, COUNT), F32),
            shape((16, COUNT), F32),
            shape((COUNT, 128), F32),
            shape((4, COUNT, HALF), BF16),
            shape((4, COUNT, HALF), BF16),
            shape((PARTS, 4, 8, PART, D), BF16),
            shape((8, 8, LANES), F32),
        ),
        in_specs=[pl.BlockSpec(memory_space=pltpu.SMEM), inside, anywhere, anywhere]
        + [inside] * 3
        + [anywhere] * 4,
        out_specs=(anywhere,) * 5 + (inside,) * 3 + (anywhere,) * 4,
        scratch_shapes=[
            vmem((D, WA), BF16),
            vmem((D, WB), BF16),
            vmem((GROUP_ROWS, 512), BF16),
            vmem((COUNT, 512), BF16),
            vmem((GROUP_ROWS, COUNT), F32),
            vmem((HEADS_KV, HEAD_DIM, GROUP_ROWS), BF16),
            vmem((COUNT, D), BF16),
            vmem((COUNT, D), BF16),
            vmem((COUNT, D), F32),
            vmem((COUNT, D), BF16),
            vmem((COUNT, D), BF16),
            vmem((4, COUNT, SLOTS), BF16),
            vmem((4, COUNT, SLOTS), BF16),
            vmem((4, COUNT, HALF), BF16),
            vmem((4, COUNT, HALF), BF16),
            *(vmem((PARTS, 8, 4, PART, HALF), BF16),) * 2,
            vmem((4, 8, COUNT), F32),
            vmem((4, 8, COUNT), F32),
            vmem((8, 8, LANES), F32),
            dma((6 + 14 + 8 + 3 + 7,)),
            dma((6 + 14 + 8 + 3 + 7,)),
            dma((2 + 7 + 1,)),
            dma((8,)),
        ],
        compiler_params=pltpu.CompilerParams(
            collective_id=3, has_side_effects=True, vmem_limit_bytes=60 * 1024 * 1024
        ),
        cost_estimate=pl.CostEstimate(
            flops=6_000_000_000, bytes_accessed=30_000_000, transcendentals=3_200_000
        ),
    )(*operands)


def norm_grad(values, gain, grad):
    inverse = lax.rsqrt(jnp.mean(values * values, axis=1, keepdims=True) + norm_eps)
    unit = values * inverse
    scaled = grad * gain
    drop = jnp.mean(scaled * unit, axis=1, keepdims=True)
    return inverse * (scaled - unit * drop), jnp.sum(grad * unit, axis=0, keepdims=True)


def backward_kernel(
    lengths, tokens_in, cotangent_in, gates, queries_in, kv_src, attended_in, middle_in, normed_in,
    tops, totals, cosd, sind, wq_in, wb_in, hot_a_in, hot_b_in,
    back_a_in, back_b_in, out_in, up_in, down_in, tiles_in,
    grad_tokens, grad_qkv_out, grad_out_out, grad_small, up_far, down_far,
    late_a, late_b, came_a, came_b,
    tokens, cotangent, queries, kv_in, attended, middle, normed,
    wq, wb, hot_a, hot_b, back_a, back_b,
    part_a, part_b, land_a, land_b, down_own, down_got,
    tiles, slopes, slopes_y,
    bias, kt, gn, gmid, gb, gatt, gp, dk, dv, leave, land, grad_qkv,
    send, recv, local, load_sem, empty,
):
    at = place()
    y, z, c, x = at
    line_y, line_z = lines(y, z, c, x)
    peers = [device(y, z, c, (x + d) % 4) for d in (1, 2, 3)]
    pairs = (
        (back_a_in, back_a), (hot_a_in, hot_a), (back_b_in, back_b), (hot_b_in, hot_b),
        (tiles_in, tiles),
        (kv_src, kv_in), (wb_in, wb), (middle_in, middle), (cotangent_in, cotangent),
        (queries_in, queries), (attended_in, attended), (tokens_in, tokens),
        (normed_in, normed), (wq_in, wq),
    )
    pairs += tuple(
        (
            down_in.at[
                pl.ds(half * DOWN_HALF, DOWN_HALF),
                pl.ds(pl.multiple_of(((x + d) % 4) * DOWN_PART, 128), DOWN_PART),
            ],
            down_own.at[half],
        )
        for half, d in ((0, 3), (1, 1))
    )
    loads = [
        pltpu.make_async_copy(src, dst, load_sem.at[i]) for i, (src, dst) in enumerate(pairs)
    ]
    for load in loads:
        load.start()
    greet(cross(*at) + peers)
    link = Moves(send, recv, local)
    for load in loads[:5]:
        load.wait()
    part_waits = []
    for hits, back, parts, land_here, me, line, width in (
        (hot_a, back_a, part_a, land_a, y, line_y, HALF),
        (hot_b, back_b, part_b, land_b, z, line_z, HALF),
    ):
        for d in (1, 2, 3):
            parts[d - 1] = add_up(hits, back, (me + d) % 4, width)
            push = link.push(parts.at[d - 1], land_here.at[me], line[d - 1])
            part_waits.append(push.wait_recv)
        land_here[pl.ds(me, 1)] = add_up(hits, back, me, width)[None]
    for peer in cross(*at):
        pl.semaphore_signal(empty, inc=1, device_id=peer, device_id_type=MESH)
    facing = (x + 2) % 4
    pushes, down_pushes = [], []
    for half, peer in ((0, peers[2]), (1, peers[0])):
        up_rows = pl.ds(pl.multiple_of(facing * UP_PART + half * UP_HALF, UP_HALF), UP_HALF)
        pushes.append(link.push(up_in.at[up_rows], up_far.at[half], peer))
        lanes = pl.ds(pl.multiple_of(facing * DOWN_PART, 128), DOWN_PART)
        down_rows = pl.ds(half * DOWN_HALF, DOWN_HALF)
        down_pushes.append(link.push(down_in.at[down_rows, lanes], down_got.at[half], peer))
    slope_pushes = []
    for d in (1, 2, 3, 0):
        source = (y + d) % 4
        chosen = iota((8, 8, LANES), 1) == source
        tile = jnp.sum(jnp.where(chosen, tiles[...], 0.0), axis=1)
        spread = jnp.where(slot_owner(), exact(tile, slot_fold()), 0.0)
        slope = exact(spread, hot_a[source], NT)
        if d == 0:
            slopes_y[pl.ds(y, 1)] = slope[None]
        else:
            slopes[d - 1] = slope
            slope_pushes.append(link.push(slopes.at[d - 1], slopes_y.at[y], line_y[d - 1]))
    fill_bias(lengths, bias, x)
    for load in loads[5:]:
        load.wait()
    for g in range(HEADS_KV):
        kt[g] = kv_in[:, g * 256 : g * 256 + 128].T
    def softmax(h, g):
        lanes = pl.ds(pl.multiple_of(h * HEAD_DIM, HEAD_DIM), HEAD_DIM)
        s = mul(kv_in[:, g * 256 : g * 256 + 128], queries[:, lanes], NT) * SCALE + bias[...]
        p = jnp.exp(s - tops[pl.ds(h, 1), :]) * (1.0 / totals[pl.ds(h, 1), :])
        p = p.astype(BF16)
        for k in range(8):
            grad_qkv[lanes, k * 256 : (k + 1) * 256] = p[k * 128 : (k + 1) * 128, :]

    for g in range(HEADS_KV):

        def softmax_step(i, carry, g=g):
            softmax(g * REPEAT + i, g)
            return carry

        lax.fori_loop(0, REPEAT, softmax_step, 0, unroll=2)

    for push in slope_pushes:
        push.wait_recv()
    same = hot(iota((EXPERTS, LANES), 0) == iota((EXPERTS, LANES), 1))
    gate_grad = exact(slopes_y[...].reshape(EXPERTS, COUNT), same, TN)
    weighted = gates[...] * gate_grad
    logit_grad = weighted - gates[...] * jnp.sum(weighted, axis=1, keepdims=True)
    parts = thirds(logit_grad)
    router_grad = sum(mul(tokens[...], part, TN) for part in parts)
    for wait in part_waits:
        wait()
    pl.semaphore_wait(empty, 13)
    out_waits = give_back(link, at, out_in, back_a, back_b, HALF, slice(None))
    total = land_a[0].astype(F32)
    for s in range(1, 4):
        total = total + land_a[s].astype(F32)
    gn[:, 0:HALF] = total
    total = land_b[0].astype(F32)
    for s in range(1, 4):
        total = total + land_b[s].astype(F32)
    gn[:, HALF:] = total
    gains, select = read_gains(wb[:, D:])
    moved, ffn_gain = norm_grad(middle[...], gains[1:2, :], gn[...])
    gm = cotangent[...].astype(F32) + moved
    gmid[...] = gm
    gb[...] = gm.astype(BF16)

    def att_tile(j, carry):
        lanes = pl.ds(pl.multiple_of(j * 256, 256), 256)
        gatt[:, lanes] = mul(gb[...], wb[:, lanes]).astype(BF16)
        return carry

    lax.fori_loop(0, D // 256, att_tile, 0, unroll=True)
    kv_pushes = []
    for g in range(HEADS_KV):
        dk[...] = jnp.zeros_like(dk)
        dv[...] = jnp.zeros_like(dv)

        def head(i, carry, g=g):
            h = g * REPEAT + i
            lanes = pl.ds(pl.multiple_of(h * HEAD_DIM, HEAD_DIM), HEAD_DIM)
            low = jnp.concatenate(
                [grad_qkv[lanes, k * 256 : (k + 1) * 256] for k in range(8)], axis=0
            )
            p = low.astype(F32)
            dv[...] += mul(low, gatt[:, lanes])
            t = p * mul(kv_in[:, g * 256 + 128 : (g + 1) * 256], gatt[:, lanes], NT)
            ds = (t - p * jnp.sum(t, axis=0, keepdims=True)).astype(BF16)
            dk[...] += mul(ds, queries[:, lanes])
            dq = mul(kt[g], ds).T * SCALE
            gp[:, lanes] = turn(dq, cosd[...], -sind[...]).astype(BF16)
            return carry

        lax.fori_loop(0, REPEAT, head, 0, unroll=3)
        leave[g, :, 0:128] = (dk[...] * SCALE).astype(BF16)
        leave[g, :, 128:256] = dv[...].astype(BF16)
        for d in (1, 2, 3):
            away = pl.ds(pl.multiple_of(((x + d) % 4) * COUNT, COUNT), COUNT)
            kv_pushes.append(link.push(leave.at[g, away], land.at[g, d - 1], peers[d - 1]))

    def out_tile(j, carry):
        lanes = pl.ds(pl.multiple_of(j * 256, 256), 256)
        grad_qkv[lanes, 0:D] = mul(gb[:, lanes], attended[...], TN).astype(BF16)
        return carry

    lax.fori_loop(0, D // 256, out_tile, 0, unroll=True)

    out_kept = link.keep(grad_qkv.at[:, pl.ds(0, D)], grad_out_out)

    for push in down_pushes:
        push.wait_recv()
    for half, (peer, part) in enumerate(((peers[2], (x + 3) % 4), (peers[0], (x + 1) % 4))):
        down_own[half] = (down_own[half].astype(F32) + down_got[half].astype(F32)).astype(BF16)
        lanes = pl.ds(pl.multiple_of(part * DOWN_PART, 128), DOWN_PART)
        here, rest = (pl.ds(k * DOWN_HALF, DOWN_HALF) for k in (half, 1 - half))
        pushes.append(link.push(down_own.at[half], down_far.at[half, here], peer))
        pushes.append(link.push(down_in.at[rest, lanes], down_far.at[half, rest], peer))

    small = wb[:, D:]

    for wait in out_waits:
        wait()
    first, second, lanes = pl.ds(0, COUNT // 2), pl.ds(COUNT // 2, COUNT // 2), pl.ds(0, HALF)
    late, stays = [], []
    ends = (
        (hot_a, back_a, land_a, came_a, late_a, y, line_y),
        (hot_b, back_b, land_b, came_b, late_b, z, line_z),
    )
    for d in (2, 1, 3, 0):
        for hits, back, summed, came, left, me, line in ends:
            s = (me + d) % 4
            summed[pl.ds(s, 1), :, 0:HALF] = add_up(hits, back, s, HALF)[None]
            if d == 0:
                stays.append(link.keep(summed.at[me, first, lanes], came.at[me]))
                stays.append(link.keep(summed.at[:, second, lanes], left))
            else:
                push = link.push(summed.at[s, first, lanes], came.at[me], line[d - 1])
                late.append(push.wait_recv)
    for push in kv_pushes:
        push.wait_recv()
    mine = pl.ds(pl.multiple_of(x * COUNT, COUNT), COUNT)
    for g in range(HEADS_KV):
        total = leave[g, mine, :].astype(F32)
        for d in range(3):
            total = total + land[g, d].astype(F32)
        gp[:, D + g * 128 : D + (g + 1) * 128] = turn(
            total[:, 0:128], cosd[...], -sind[...]
        ).astype(BF16)
        gp[:, D + 256 + g * 128 : D + 384 + g * 128] = total[:, 128:256].astype(BF16)
    out_kept.wait()

    def qkv_tile(j, carry):
        lanes = pl.ds(pl.multiple_of(j * 256, 256), 256)
        grad_qkv[lanes, :] = mul(normed[:, lanes], gp[...], TN).astype(BF16)
        gn[:, lanes] = mul(gp[...], wq[lanes, :], NT)
        return carry

    lax.fori_loop(0, D // 256, qkv_tile, 0, unroll=True)
    stays.append(link.keep(grad_qkv, grad_qkv_out))
    moved, attn_gain = norm_grad(tokens[...].astype(F32), gains[0:1, :], gn[...])
    from_router = sum(mul(part, small, NT) for part in parts)
    grad_tokens[...] = (gmid[...] + moved + from_router).astype(BF16)
    both = jnp.where(
        iota((8, D), 0) == 0, attn_gain, jnp.where(iota((8, D), 0) == 1, ffn_gain, 0.0)
    )
    gain_columns = sum(mul(part, select, TN) for part in thirds(both))
    grad_small[...] = (router_grad + gain_columns).astype(BF16)
    for push in pushes:
        push.wait_recv()
    for wait in late:
        wait()
    for stay in stays:
        stay.wait()
    link.drain()


def run_backward(*operands):
    anywhere = pl.BlockSpec(memory_space=pltpu.HBM)
    inside = pl.BlockSpec(memory_space=pltpu.VMEM)
    vmem, dma = pltpu.VMEM, pltpu.SemaphoreType.DMA
    shape = jax.ShapeDtypeStruct
    return pl.pallas_call(
        backward_kernel,
        name="backward",
        out_shape=(
            shape((COUNT, D), BF16),
            shape((D, WA), BF16),
            shape((D, D), BF16),
            shape((D, SMALL), BF16),
            shape((2, UP_HALF, 2 * FF), BF16),
            shape((2, FF, DOWN_PART), BF16),
            *(shape((4, COUNT // 2, HALF), BF16),) * 4,
        ),
        in_specs=[pl.BlockSpec(memory_space=pltpu.SMEM)]
        + [anywhere] * 2
        + [inside]
        + [anywhere] * 5
        + [inside] * 4
        + [anywhere] * 10,
        out_specs=(inside, anywhere, anywhere, inside) + (anywhere,) * 6,
        scratch_shapes=[
            vmem((COUNT, D), BF16),
            vmem((COUNT, D), BF16),
            vmem((COUNT, D), BF16),
            vmem((GROUP_ROWS, 512), BF16),
            vmem((COUNT, D), BF16),
            vmem((COUNT, D), F32),
            vmem((COUNT, D), BF16),
            vmem((D, WA), BF16),
            vmem((D, WB), BF16),
            vmem((4, COUNT, SLOTS), BF16),
            vmem((4, COUNT, SLOTS), BF16),
            vmem((PARTS, 8, 4, PART, HALF), BF16),
            vmem((PARTS, 8, 4, PART, HALF), BF16),
            vmem((3, COUNT, HALF), BF16),
            vmem((3, COUNT, HALF), BF16),
            vmem((4, COUNT, HALF), BF16),
            vmem((4, COUNT, HALF), BF16),
            vmem((2, DOWN_HALF, DOWN_PART), BF16),
            vmem((2, DOWN_HALF, DOWN_PART), BF16),
            vmem((8, 8, LANES), F32),
            vmem((3, 8, COUNT), F32),
            vmem((4, 8, COUNT), F32),
            vmem((GROUP_ROWS, COUNT), F32),
            vmem((HEADS_KV, HEAD_DIM, GROUP_ROWS), BF16),
            vmem((COUNT, D), F32),
            vmem((COUNT, D), F32),
            vmem((COUNT, D), BF16),
            vmem((COUNT, D), BF16),
            vmem((COUNT, WA), BF16),
            vmem((GROUP_ROWS, HEAD_DIM), F32),
            vmem((GROUP_ROWS, HEAD_DIM), F32),
            vmem((HEADS_KV, GROUP_ROWS, 256), BF16),
            vmem((HEADS_KV, 3, COUNT, 256), BF16),
            vmem((D, WA), BF16),
            dma((6 + 4 + 14 + 6 + 6 + 4 + 3,)),
            dma((6 + 4 + 14 + 6 + 6 + 4 + 3,)),
            dma((2 + 4 + 2,)),
            dma((16,)),
            pltpu.SemaphoreType.REGULAR,
        ],
        compiler_params=pltpu.CompilerParams(
            collective_id=4, has_side_effects=True, vmem_limit_bytes=60 * 1024 * 1024
        ),
        cost_estimate=pl.CostEstimate(
            flops=13_000_000_000, bytes_accessed=50_000_000, transcendentals=3_200_000
        ),
    )(*operands)


def finish_kernel(
    sum_a_in, sum_b_in, up_in, down_in, out_in, tokens_in,
    output, grad_tokens, grad_up, grad_down, grad_qkv, grad_out_t, grad_attn, grad_ffn, grad_router,
    sum_a, sum_b, up, down, out, tokens, load_sem, store_sem,
):
    pairs = (
        (up_in, up), (down_in, down), (out_in, out), (tokens_in, tokens),
        (sum_a_in, sum_a), (sum_b_in, sum_b),
    )
    loads = [
        pltpu.make_async_copy(src, dst, load_sem.at[i]) for i, (src, dst) in enumerate(pairs)
    ]
    for load in loads:
        load.start()
    pairs = ((up, grad_up), (down, grad_down), (out, output), (tokens, grad_tokens))
    stores = [
        pltpu.make_async_copy(src, dst, store_sem.at[i]) for i, (src, dst) in enumerate(pairs)
    ]
    for load, store in zip(loads, stores):
        load.wait()
        store.start()
    for load in loads[4:]:
        load.wait()
    grad_qkv[...] = sum_a[0:PIECE, :]
    grad_out_t[...] = sum_b[0:PIECE, 0:D]
    small = sum_b[0:PIECE, D:]
    grad_router[...] = small[:, 0:EXPERTS]
    diagonal = iota((PIECE, SMALL), 0) == iota((PIECE, SMALL), 1)
    for k, gain in enumerate((grad_attn, grad_ffn)):
        lanes = iota((PIECE, SMALL), 1) == EXPERTS + k
        column = jnp.sum(jnp.where(lanes, small, 0.0), axis=1, keepdims=True)
        row = jnp.sum(jnp.where(diagonal, column, 0.0), axis=0, keepdims=True)
        gain[...] = row[:, 0:PIECE]
    for store in stores:
        store.wait()


def finish(*operands):
    anywhere = pl.BlockSpec(memory_space=pltpu.HBM)
    inside = pl.BlockSpec(memory_space=pltpu.VMEM)
    shape, vmem, dma = jax.ShapeDtypeStruct, pltpu.VMEM, pltpu.SemaphoreType.DMA
    return pl.pallas_call(
        finish_kernel,
        name="finish",
        out_shape=(
            shape((COUNT, D), BF16),
            shape((COUNT, D), BF16),
            shape((UP_PART, 2 * FF), F32),
            shape((FF, DOWN_PART), F32),
            shape((PIECE, WA), F32),
            shape((PIECE, D), F32),
            shape((1, PIECE), F32),
            shape((1, PIECE), F32),
            shape((PIECE, EXPERTS), F32),
        ),
        in_specs=[anywhere] * 6,
        out_specs=(anywhere,) * 4 + (inside,) * 5,
        scratch_shapes=[
            vmem((PADDED, WA), F32),
            vmem((PADDED, WB), F32),
            vmem((UP_PART, 2 * FF), F32),
            vmem((FF, DOWN_PART), F32),
            vmem((COUNT, D), BF16),
            vmem((COUNT, D), BF16),
            dma((6,)),
            dma((4,)),
        ],
        compiler_params=pltpu.CompilerParams(vmem_limit_bytes=60 * 1024 * 1024),
    )(*operands)


def body(
    tokens, lengths, top_experts, w_qkv, w_out, gain_attn, gain_ffn, router, gate_up, down_proj, cotangent,
):
    half = HEAD_DIM // 2
    rates = rope_base ** (-(np.arange(HEAD_DIM, dtype=np.float32) % half) / half)
    full_a, full_b, named, hot_a, hot_b, dy_a, dy_b, cosd, sind = gather_weights(
        lengths, jnp.asarray(rates.astype(np.float32))[None], w_qkv, w_out.T, router,
        gain_attn[None], gain_ffn[None], top_experts.T, cotangent,
    )
    wq = full_a.reshape(D, WA)
    wb = full_b.reshape(D, WB)
    (
        queries, kv, attended, middle, normed, tops, totals, gates, nf_a, nf_b, dy_rows, tiles,
    ) = run_forward(
        lengths, tokens, wq, wb, named, cosd, sind, hot_a, hot_b, dy_a, dy_b
    )
    back_a, back_b, expert_out, up_local, down_local, tiles_back = run_experts(
        hot_a, hot_b, nf_a, nf_b, dy_rows, tiles, gate_up, down_proj
    )
    grad_tokens, grad_qkv, grad_out, grad_small, *passed_on = run_backward(
        lengths, tokens, cotangent, gates, queries, kv, attended, middle, normed, tops, totals,
        cosd, sind, wq, wb, hot_a, hot_b, back_a, back_b, expert_out, up_local, down_local,
        tiles_back,
    )
    sum_a, sum_b, up_sum, down_sum, output = scatter_sums(
        grad_qkv.reshape(4, 4, 2, BLOCK, WA),
        grad_out.reshape(4, 4, 2, BLOCK, D),
        grad_small.reshape(4, 4, 2, BLOCK, SMALL),
        up_local,
        down_local,
        *passed_on,
        middle,
    )
    (
        output, grad_tokens, up_sum, down_sum, grad_qkv, grad_out_t, grad_attn, grad_ffn, grad_router,
    ) = finish(sum_a, sum_b, up_sum, down_sum, output, grad_tokens)
    return (
        output,
        grad_tokens,
        grad_qkv,
        grad_out_t.T,
        grad_attn[0],
        grad_ffn[0],
        grad_router,
        up_sum[None],
        down_sum[None],
    )


def solution(mesh):
    return jax.shard_map(
        body,
        mesh=mesh,
        in_specs=(
            P(("expert", "shard"), None),
            P("expert", None),
            P(("expert", "shard"), None),
            P(("expert", "shard"), None),
            P(None, ("expert", "shard")),
            P(("expert", "shard")),
            P(("expert", "shard")),
            P(("expert", "shard"), None),
            P("expert", None, None),
            P("expert", None, None),
            P(("expert", "shard"), None),
        ),
        out_specs=(
            P(("expert", "shard"), None),
            P(("expert", "shard"), None),
            P(("expert", "shard"), None),
            P(None, ("expert", "shard")),
            P(("expert", "shard")),
            P(("expert", "shard")),
            P(("expert", "shard"), None),
            P("expert", "shard", None),
            P("expert", None, "shard"),
        ),
        check_vma=False,
    )
```

```python
import jax
import jax.numpy as jnp
import numpy as np
from jax import lax
from jax.experimental import pallas as pl
from jax.experimental.pallas import tpu as pltpu
from jax.sharding import PartitionSpec as P

D = 1536
HEADS_Q = 12
HEADS_KV = 2
HEAD_DIM = 128
FF = 768
TOP = 4
EXPERTS = 32
CAP = 48
WIDTH_Q = HEADS_Q * HEAD_DIM
WIDTH_KV = HEADS_KV * HEAD_DIM
REPEAT = HEADS_Q // HEADS_KV

norm_eps = 1e-06
rope_base = 1000000.0
MESH = pl.DeviceIdType.MESH
F32 = jnp.float32
BF16 = jnp.bfloat16

PIECE = 12
PADDED = 16
BLOCK = 48
WA = 2048
WB = 1664
SMALL = WB - D
JOB_A = 1920
JOB_B = WA + WB - JOB_A
QUARTER = WA // 4


def place():
    e = lax.axis_index("expert")
    return e // 8, (e // 2) % 4, e % 2, lax.axis_index("shard")


def device(y, z, c, x):
    return ((y * 4 + z) * 2 + c, x)


def greet(devices):
    barrier = pltpu.get_barrier_semaphore()
    for d in devices:
        pl.semaphore_signal(barrier, inc=1, device_id=d, device_id_type=MESH)
    pl.semaphore_wait(barrier, len(devices))


class Links:
    def __init__(self, send, recv):
        self.send, self.recv, self.made = send, recv, []

    def push(self, src, dst, where):
        i = len(self.made)
        copy = pltpu.make_async_remote_copy(
            src_ref=src,
            dst_ref=dst,
            send_sem=self.send.at[i],
            recv_sem=self.recv.at[i],
            device_id=where,
            device_id_type=MESH,
        )
        copy.start()
        self.made.append(copy)
        return copy

    def drain(self):
        for copy in self.made:
            copy.wait_send()


def neighbours(y, z, c, x):
    other = 1 - c
    return dict(
        x=[device(y, z, c, (x + d) % 4) for d in (1, 2, 3)],
        y=(device((y + 1) % 4, z, c, x), device((y + 3) % 4, z, c, x)),
        z=(device(y, (z + 1) % 4, c, x), device(y, (z + 3) % 4, c, x)),
        core=device(y, z, other, x),
    )


def everyone_near(near):
    return list(near["x"]) + list(near["y"]) + list(near["z"]) + [near["core"]]


def pick_rows(rows, columns, row_block, column_block):
    r = lax.broadcasted_iota(jnp.int32, (rows, columns), 0)
    q = lax.broadcasted_iota(jnp.int32, (rows, columns), 1)
    same = (r // row_block == q // column_block) & (r % row_block == q % column_block)
    return jnp.where(same, 1.0, 0.0).astype(BF16)


def faces(y, z, c, x):
    along_z, along_y = [], []
    for d in range(4):
        for k in range(2):
            core = c if k == 0 else 1 - c
            along_z.append((device(y, (z + d) % 4, core, x), (z + d) % 4, core))
            along_y.append((device((y + d) % 4, z, core, x), (y + d) % 4, core))
    return along_z, along_y


def cross(y, z, c, x):
    along_z, along_y = faces(y, z, c, x)
    return [f[0] for f in along_z[1:] + along_y[2:]]


def lines(y, z, c, x):
    return (
        [device((y + d) % 4, z, c, x) for d in (1, 2, 3)],
        [device(y, (z + d) % 4, c, x) for d in (1, 2, 3)],
    )


def route(top_experts, named, own_slot):
    experts = iota((EXPERTS, COUNT), 0)
    names = sum(jnp.where(top_experts[k : k + 1, :] == experts, 1.0, 0.0) for k in range(TOP))
    low = names.astype(BF16)
    earlier = hot(iota((COUNT, COUNT), 0) < iota((COUNT, COUNT), 1))
    own_slot[...] = jnp.where(names > 0, mul(low, earlier), -1.0).astype(BF16)
    named[...] = mul(low, hot(iota((EXPERTS, 128), 0) == iota((EXPERTS, 128), 1)), TN)


def rope(lengths, rates, cosd, sind, x):
    own = x * COUNT + iota((COUNT, 1), 0)
    first = lengths[0, 0]
    second = first + lengths[0, 1]
    third = second + lengths[0, 2]
    start = jnp.zeros((COUNT, 1), jnp.int32)
    for end in (first, second, third):
        start = jnp.where(own >= end, end, start)
    angles = (own - start).astype(F32) * rates[...]
    cosd[...] = jnp.cos(angles)
    sine = jnp.sin(angles)
    sind[...] = jnp.where(iota((COUNT, HEAD_DIM), 1) < HEAD_DIM // 2, -sine, sine)


def fill_pack(pack, w_qkv, w_out_t, router, gain_attn, gain_ffn):
    pack[...] = jnp.zeros_like(pack)
    pack[0:PIECE, 0:WA] = w_qkv[...]
    pack[0:PIECE, WA : WA + D] = w_out_t[...]
    small = mul(router[...], hot(iota((EXPERTS, SMALL), 0) == iota((EXPERTS, SMALL), 1)))
    diagonal = iota((PIECE, PIECE), 0) == iota((PIECE, PIECE), 1)
    for k, gain in enumerate((gain_attn, gain_ffn)):
        column = jnp.sum(jnp.where(diagonal, gain[...].astype(F32), 0.0), axis=1, keepdims=True)
        small = jnp.where(iota((PIECE, SMALL), 1) == EXPERTS + k, column, small)
    pack[0:PIECE, WA + D :] = small.astype(BF16)


def slot_hits(slot_of, hits, experts):
    p = iota((1, SLOTS), 1)
    q = p % PIECE_SLOTS
    wanted = ((p // PIECE_SLOTS) * PART + q % PART).astype(F32)
    local = q // PART
    expand = hot(iota((EXPERTS, SLOTS), 0) == experts(local))

    def step(s, carry):
        hits[s] = hot(mul(slot_of[s], expand, TN) == wanted)
        return carry

    lax.fori_loop(0, 4, step, 0)


def gather_kernel(
    lengths, rates, w_qkv, w_out_t, router, gain_attn, gain_ffn, top_experts, cotangent,
    full_a, full_b, named, hot_a, hot_b, dy_a, dy_b, cosd, sind,
    pack, xbuf, own_0, own_1, own_2, own_slot, slot_y, slot_z, send, recv, local,
):
    y, z, c, x = place()
    near = neighbours(y, z, c, x)
    line_y, line_z = lines(y, z, c, x)
    fill_pack(pack, w_qkv, w_out_t, router, gain_attn, gain_ffn)
    greet(everyone_near(near) + [line_y[1], line_z[1]])
    link = Links(send, recv)
    first = [link.push(pack, xbuf.at[x], near["x"][d]) for d in range(3)]
    xbuf[pl.ds(x, 1)] = pack[...][None]
    half_a, half_b = cotangent.at[:, pl.ds(0, HALF)], cotangent.at[:, pl.ds(HALF, HALF)]
    kept = [
        pltpu.make_async_copy(half_a, dy_a.at[y], local.at[2]),
        pltpu.make_async_copy(half_b, dy_b.at[z], local.at[3]),
    ]
    for copy in kept:
        copy.start()
    dys = [
        around(link, half_a, dy_a, y, *near["y"]),
        around(link, half_b, dy_b, z, *near["z"]),
    ]
    for copy in first:
        copy.wait_recv()
    select = pick_rows(BLOCK, 4 * PADDED, PIECE, PADDED)
    pieces = xbuf[...].reshape(4 * PADDED, WA + WB)
    quarter = pl.multiple_of(x * QUARTER, QUARTER)
    mine = xbuf[:, :, pl.ds(quarter, QUARTER)].reshape(4 * PADDED, QUARTER)
    own_0[...] = mul(select, mine).astype(BF16)
    own_1[...] = mul(select, pieces[:, WA : WA + HALF]).astype(BF16)
    own_2[...] = mul(select, pieces[:, WA + HALF :]).astype(BF16)
    spot = dict(y=y, z=z)
    jobs = [
        dict(own=own_0, full=full_a, off=quarter, half=QUARTER // 2, close="y", far="z", i=0),
        dict(own=own_1, full=full_b, off=0, half=HALF // 2, close="y", far="z", i=1),
        dict(own=own_2, full=full_b, off=HALF, half=512, close="z", far="y", i=4),
    ]

    def block_at(j, far, close, first=0, count=None):
        yy, zz = (far, close) if j["far"] == "y" else (close, far)
        count = j["own"].shape[1] if count is None else count
        lanes = j["off"] + first
        lanes = lanes if isinstance(lanes, int) else pl.multiple_of(lanes, 128)
        return j["full"].at[yy, zz, c, :, pl.ds(lanes, count)]

    def line_at(j, far, start=0, count=4):
        return block_at(j, far, pl.ds(start, count))

    for j in jobs:
        j["p"], j["q"] = spot[j["close"]], spot[j["far"]]
        here = block_at(j, j["q"], j["p"])
        plus, minus = near[j["close"]]
        j["up"] = link.push(j["own"], here, plus)
        j["down"] = link.push(j["own"], here, minus)
        j["core"] = []
        if j["full"] is full_b:
            j["core"].append(link.push(j["own"], here, near["core"]))
        j["local"] = pltpu.make_async_copy(j["own"], here, local.at[j["i"]])
        j["local"].start()
    route(top_experts, named, own_slot)
    slot_y[pl.ds(y, 1)] = own_slot[...][None]
    slot_z[pl.ds(z, 1)] = own_slot[...][None]
    slots = [link.push(own_slot, slot_y.at[y], peer) for peer in line_y]
    slots += [link.push(own_slot, slot_z.at[z], peer) for peer in line_z]
    for j in jobs:
        plus, minus = near[j["close"]]
        left, right = (j["p"] + 3) % 4, (j["p"] + 1) % 4
        j["up"].wait_recv()
        part = block_at(j, j["q"], left, 0, j["half"])
        j["up2"] = link.push(part, part, plus)
        j["down"].wait_recv()
        part = block_at(j, j["q"], right, j["half"], j["own"].shape[1] - j["half"])
        j["down2"] = link.push(part, part, minus)
        if j["full"] is full_b:
            for side in (left, right):
                block = block_at(j, j["q"], side)
                j["core"].append(link.push(block, block, near["core"]))

    around_x = {}

    def quarter_at(far, which, start=0, count=4):
        lanes = pl.ds(pl.multiple_of(which * QUARTER, QUARTER), QUARTER)
        return full_a.at[pl.ds(start, count), far, c, :, lanes]

    def x_start(name, far):
        block = quarter_at(far, x)
        around_x[name] = [
            far, link.push(block, block, near["x"][0]), link.push(block, block, near["x"][2])
        ]

    def x_forward(name):
        far, up, down = around_x[name]
        up.wait_recv()
        part = quarter_at(far, (x + 3) % 4, 0, 2)
        up = link.push(part, part, near["x"][0])
        down.wait_recv()
        part = quarter_at(far, (x + 1) % 4, 2, 2)
        around_x[name] = [far, up, link.push(part, part, near["x"][2])]

    def x_done(name):
        far, up, down = around_x[name]
        up.wait_recv()
        down.wait_recv()
        line = full_a.at[:, far, c]
        jobs[0]["core"].append(link.push(line, line, near["core"]))

    def far_start(j):
        j["up2"].wait_recv()
        j["down2"].wait_recv()
        block = block_at(j, j["q"], (j["p"] + 2) % 4)
        j["local"].wait()
        plus, minus = near[j["far"]]
        line = line_at(j, j["q"])
        j["up"] = link.push(line, line, plus)
        j["down"] = link.push(line, line, minus)
        if j["full"] is full_b:
            j["core"].append(link.push(block, block, near["core"]))
        else:
            x_start("own", j["q"])

    far_start(jobs[0])
    far_start(jobs[2])
    dys = dys[0]() + dys[1]()
    for copy in slots:
        copy.wait_recv()
    def far_next(j):
        plus, minus = near[j["far"]]
        left, right = (j["q"] + 3) % 4, (j["q"] + 1) % 4
        j["up"].wait_recv()
        part = line_at(j, left, 0, 2)
        j["up2"] = link.push(part, part, plus)
        j["down"].wait_recv()
        part = line_at(j, right, 2, 2)
        j["down2"] = link.push(part, part, minus)
        if j["full"] is full_b:
            for side in (left, right):
                block = line_at(j, side)
                j["core"].append(link.push(block, block, near["core"]))
        else:
            x_start("left", left)
            x_start("right", right)

    def far_end(j):
        opposite = (j["q"] + 2) % 4
        j["up2"].wait_recv()
        j["down2"].wait_recv()
        if j["full"] is full_b:
            block = line_at(j, opposite)
            j["core"].append(link.push(block, block, near["core"]))
        else:
            x_start("opposite", opposite)

    far_next(jobs[0])
    far_start(jobs[1])
    x_forward("own")
    far_end(jobs[0])
    far_next(jobs[2])
    x_done("own")
    x_forward("left")
    x_forward("right")
    slot_hits(slot_y, hot_a, lambda e: y * 8 + e)
    far_next(jobs[1])
    slot_hits(slot_z, hot_b, lambda e: (e // 2) * 8 + z * 2 + e % 2)
    far_end(jobs[2])
    x_done("left")
    x_done("right")
    x_forward("opposite")
    far_end(jobs[1])
    rope(lengths, rates, cosd, sind, x)
    x_done("opposite")
    for j in jobs:
        for copy in j["core"]:
            copy.wait_recv()
    for wait in dys:
        wait()
    for copy in kept:
        copy.wait()
    link.drain()


def gather_weights(*operands):
    inside = pl.BlockSpec(memory_space=pltpu.VMEM)
    anywhere = pl.BlockSpec(memory_space=pltpu.HBM)
    copies = 3 + 2 * 15 + 8 + 16 + 4 + 6 + 8
    return pl.pallas_call(
        gather_kernel,
        name="gather_weights",
        out_shape=(
            jax.ShapeDtypeStruct((4, 4, 2, BLOCK, WA), BF16),
            jax.ShapeDtypeStruct((4, 4, 2, BLOCK, WB), BF16),
            jax.ShapeDtypeStruct((COUNT, 128), F32),
            jax.ShapeDtypeStruct((4, COUNT, SLOTS), BF16),
            jax.ShapeDtypeStruct((4, COUNT, SLOTS), BF16),
            jax.ShapeDtypeStruct((4, COUNT, HALF), BF16),
            jax.ShapeDtypeStruct((4, COUNT, HALF), BF16),
            jax.ShapeDtypeStruct((COUNT, HEAD_DIM), F32),
            jax.ShapeDtypeStruct((COUNT, HEAD_DIM), F32),
        ),
        in_specs=[pl.BlockSpec(memory_space=pltpu.SMEM)] + [inside] * 8,
        out_specs=(anywhere,) * 2 + (inside,) * 3 + (anywhere,) * 2 + (inside,) * 2,
        scratch_shapes=[
            pltpu.VMEM((PADDED, WA + WB), BF16),
            pltpu.VMEM((4, PADDED, WA + WB), BF16),
            pltpu.VMEM((BLOCK, QUARTER), BF16),
            pltpu.VMEM((BLOCK, HALF), BF16),
            pltpu.VMEM((BLOCK, WB - HALF), BF16),
            pltpu.VMEM((EXPERTS, COUNT), BF16),
            pltpu.VMEM((4, EXPERTS, COUNT), BF16),
            pltpu.VMEM((4, EXPERTS, COUNT), BF16),
            pltpu.SemaphoreType.DMA((copies,)),
            pltpu.SemaphoreType.DMA((copies,)),
            pltpu.SemaphoreType.DMA((5,)),
        ],
        compiler_params=pltpu.CompilerParams(
            collective_id=0, has_side_effects=True, vmem_limit_bytes=60 * 1024 * 1024
        ),
        cost_estimate=pl.CostEstimate(flops=0, bytes_accessed=24_000_000, transcendentals=0),
    )(*operands)


def add_blocks(dst, far, start, count, sources):
    def step(i, carry):
        total = dst[far, start + i].astype(F32)
        for source in sources:
            total = total + source(i).astype(F32)
        dst[far, start + i] = total.astype(BF16)
        return carry

    lax.fori_loop(0, count, step, 0)


def scatter_kernel(
    ga, gb, gs, up_in, down_in, up_far, down_far, late_a, late_b, came_a, came_b, middle,
    out_a, out_b, up_out, down_out, output,
    core_a, core_b, mine_a, mine_b, one_a, one_b, two_a, two_b,
    half_a0, half_a1, half_b0, half_b1, last_a, last_b, xout, xin,
    ups, downs, up_got, up_land, mid, land_a, land_b,
    send, recv, local,
):
    y, z, c, x = place()
    near = neighbours(y, z, c, x)
    line_y, line_z = lines(y, z, c, x)
    greet(everyone_near(near) + [line_y[1], line_z[1]])
    link = Links(send, recv)
    other = 1 - c
    jobs = [
        dict(src=[(lambda f, s: ga.at[f, :, s, :, pl.ds(0, JOB_A)], 0, JOB_A)], core=core_a, mine=mine_a, one=one_a, two=two_a,
             halves=(half_a0, half_a1), last=last_a, far="y", close="z", q=y, p=z,
             width=JOB_A, half=1024, lane=0, i=0),
        dict(src=[
                 (lambda f, s: ga.at[:, f, s, :, pl.ds(JOB_A, WA - JOB_A)], 0, WA - JOB_A),
                 (lambda f, s: gb.at[:, f, s], WA - JOB_A, D),
                 (lambda f, s: gs.at[:, f, s], WA - JOB_A + D, SMALL),
             ],
             core=core_b, mine=mine_b, one=one_b, two=two_b,
             halves=(half_b0, half_b1), last=last_b, far="z", close="y", q=z, p=y,
             width=JOB_B, half=896, lane=JOB_A, i=1),
    ]
    slots = 0
    for step in (2, 3, 1, 0):
        for j in jobs:
            f = (j["q"] + step) % 4
            j[step] = []
            for source, lane, width in j["src"]:
                lanes = pl.ds(lane, width)
                pushed = link.push(
                    source(f, other), j["core"].at[f, :, :, lanes], near["core"]
                )
                kept = pltpu.make_async_copy(
                    source(f, c), j["mine"].at[f, :, :, lanes], local.at[slots]
                )
                slots += 1
                kept.start()
                j[step].append((pushed, kept))

    first, second = pl.ds(0, COUNT // 2), pl.ds(COUNT // 2, COUNT // 2)
    fetches = [(up_far, up_got)]
    for i, d in enumerate((3, 1, 0)):
        up_rows = pl.ds(pl.multiple_of(((x + d) % 4) * UP_PART, UP_PART), UP_PART)
        fetches.append((up_in.at[up_rows], ups.at[i]))
    lanes = pl.ds(pl.multiple_of(x * DOWN_PART, 128), DOWN_PART)
    fetches += [
        (down_in.at[:, lanes], downs.at[0]),
        (down_far, downs.at[pl.ds(1, 2)]),
        (middle, mid),
        (came_a, land_a.at[:, first]),
        (came_b, land_b.at[:, first]),
        (late_a.at[y], land_a.at[y, second]),
        (late_b.at[z], land_b.at[z, second]),
    ]
    fetches = [
        pltpu.make_async_copy(src, dst, local.at[slots + i]) for i, (src, dst) in enumerate(fetches)
    ]
    for fetch in fetches:
        fetch.start()
    for fetch in fetches[:4]:
        fetch.wait()
    sides = []
    for i, peer in enumerate((near["x"][2], near["x"][0])):
        up_rows = slice(i * UP_HALF, (i + 1) * UP_HALF)
        ups[i, up_rows, :] = (ups[i, up_rows, :].astype(F32) + up_got[i].astype(F32)).astype(BF16)
        sides.append(link.push(ups.at[i], up_land.at[i], peer))

    def ready(j, step):
        for pushed, kept in j[step]:
            pushed.wait_recv()
            kept.wait()

    for j in jobs:
        f = (j["q"] + 2) % 4
        ready(j, 2)
        mine = j["mine"]
        add_blocks(j["core"], f, 0, 4, [lambda i, f=f, m=mine: m[f, i]])
        plus, minus = near[j["far"]]
        j["down"] = link.push(j["core"].at[f, pl.ds(0, 2)], j["one"].at[0], minus)
        j["up"] = link.push(j["core"].at[f, pl.ds(2, 2)], j["one"].at[1], plus)
    for j in jobs:
        plus, minus = near[j["far"]]
        mine, one = j["mine"], j["one"]
        f = (j["q"] + 3) % 4
        ready(j, 3)
        add_blocks(j["core"], f, 2, 2, [lambda i, f=f, m=mine: m[f, i + 2]])
        j["down"].wait_recv()
        add_blocks(
            j["core"], f, 0, 2, [lambda i, f=f, m=mine: m[f, i], lambda i, o=one: o[0, i]]
        )
        j["down2"] = link.push(j["core"].at[f], j["two"].at[0], minus)
        f = (j["q"] + 1) % 4
        ready(j, 1)
        add_blocks(j["core"], f, 0, 2, [lambda i, f=f, m=mine: m[f, i]])
        j["up"].wait_recv()
        add_blocks(
            j["core"], f, 2, 2, [lambda i, f=f, m=mine: m[f, i + 2], lambda i, o=one: o[1, i]]
        )
        j["up2"] = link.push(j["core"].at[f], j["two"].at[1], plus)
    for j in jobs:
        mine, two = j["mine"], j["two"]
        f = j["q"]
        ready(j, 0)
        j["down2"].wait_recv()
        j["up2"].wait_recv()
        add_blocks(
            j["core"], f, 0, 4,
            [lambda i, f=f, m=mine: m[f, i], lambda i, t=two: t[0, i], lambda i, t=two: t[1, i]],
        )
        plus, minus = near[j["close"]]
        g = (j["p"] + 2) % 4
        h, w = j["half"], j["width"]
        j["down"] = link.push(j["core"].at[f, g, :, pl.ds(0, h)], j["halves"][0], minus)
        j["up"] = link.push(j["core"].at[f, g, :, pl.ds(h, w - h)], j["halves"][1], plus)
    for j in jobs:
        plus, minus = near[j["close"]]
        f, h, w, core = j["q"], j["half"], j["width"], j["core"]
        g = (j["p"] + 3) % 4
        j["down"].wait_recv()
        core[f, g, :, 0:h] = (
            core[f, g, :, 0:h].astype(F32) + j["halves"][0][...].astype(F32)
        ).astype(BF16)
        j["down2"] = link.push(core.at[f, g], j["last"].at[0], minus)
        g = (j["p"] + 1) % 4
        j["up"].wait_recv()
        core[f, g, :, h:w] = (
            core[f, g, :, h:w].astype(F32) + j["halves"][1][...].astype(F32)
        ).astype(BF16)
        j["up2"] = link.push(core.at[f, g], j["last"].at[1], plus)
    late = []
    for src, dst, me, line in ((late_a, land_a, y, line_y), (late_b, land_b, z, line_z)):
        for d in (1, 2, 3):
            late.append(link.push(src.at[(me + d) % 4], dst.at[me, second], line[d - 1]))
    select = pick_rows(4 * PADDED, BLOCK, PADDED, PIECE)
    for j in jobs:
        f, g = j["q"], j["p"]
        j["down2"].wait_recv()
        j["up2"].wait_recv()
        total = (
            j["core"][f, g].astype(F32)
            + j["last"][0].astype(F32)
            + j["last"][1].astype(F32)
        ).astype(BF16)
        spread = jnp.dot(select, total, preferred_element_type=F32).astype(BF16)
        xout[:, :, j["lane"] : j["lane"] + j["width"]] = spread.reshape(4, PADDED, j["width"])
    final = [
        link.push(xout.at[(x + d) % 4], xin.at[d - 1], near["x"][d - 1]) for d in (1, 2, 3)
    ]
    for copy in final:
        copy.wait_recv()
    mine = xout[x].astype(F32)
    for d in range(3):
        mine = mine + xin[d].astype(F32)
    out_a[...] = mine[:, :WA]
    out_b[...] = mine[:, WA:]
    for push in sides:
        push.wait_recv()
    up_out[...] = ups[2].astype(F32) + up_land[0].astype(F32) + up_land[1].astype(F32)
    for fetch in fetches[4:]:
        fetch.wait()
    down_out[...] = downs[0].astype(F32) + downs[1].astype(F32) + downs[2].astype(F32)
    for push in late:
        push.wait_recv()
    for half, landed in enumerate((land_a, land_b)):
        lanes = slice(half * HALF, (half + 1) * HALF)
        total = mid[:, lanes]
        for s in range(4):
            total = total + landed[s].astype(F32)
        output[:, lanes] = total.astype(BF16)
    link.drain()


def scatter_sums(*operands):
    copies = 2 * (4 + 4 + 4) + 8 + 3 + 6 + 2
    vmem = pltpu.VMEM
    scratch = []
    for shape in ((4, 4), (4, 4), (2, 2), (2, 4)):
        scratch += [vmem((*shape, BLOCK, JOB_A), BF16), vmem((*shape, BLOCK, JOB_B), BF16)]
    scratch += [
        vmem((BLOCK, 1024), BF16),
        vmem((BLOCK, JOB_A - 1024), BF16),
        vmem((BLOCK, 896), BF16),
        vmem((BLOCK, JOB_B - 896), BF16),
        vmem((2, BLOCK, JOB_A), BF16),
        vmem((2, BLOCK, JOB_B), BF16),
        vmem((4, PADDED, WA + WB), BF16),
        vmem((3, PADDED, WA + WB), BF16),
        vmem((3, UP_PART, 2 * FF), BF16),
        vmem((3, FF, DOWN_PART), BF16),
        vmem((2, UP_HALF, 2 * FF), BF16),
        vmem((2, UP_PART, 2 * FF), BF16),
        vmem((COUNT, D), F32),
        vmem((4, COUNT, HALF), BF16),
        vmem((4, COUNT, HALF), BF16),
        pltpu.SemaphoreType.DMA((copies,)),
        pltpu.SemaphoreType.DMA((copies,)),
        pltpu.SemaphoreType.DMA((16 + 11,)),
    ]
    return pl.pallas_call(
        scatter_kernel,
        name="scatter_sums",
        out_shape=(
            jax.ShapeDtypeStruct((PADDED, WA), F32),
            jax.ShapeDtypeStruct((PADDED, WB), F32),
            jax.ShapeDtypeStruct((UP_PART, 2 * FF), F32),
            jax.ShapeDtypeStruct((FF, DOWN_PART), F32),
            jax.ShapeDtypeStruct((COUNT, D), BF16),
        ),
        in_specs=[pl.BlockSpec(memory_space=pltpu.HBM)] * 12,
        out_specs=(pl.BlockSpec(memory_space=pltpu.VMEM),) * 5,
        scratch_shapes=scratch,
        compiler_params=pltpu.CompilerParams(
            collective_id=1, has_side_effects=True, vmem_limit_bytes=60 * 1024 * 1024
        ),
        cost_estimate=pl.CostEstimate(flops=0, bytes_accessed=24_000_000, transcendentals=0),
    )(*operands)


ROWS = EXPERTS * CAP
TILE = 256
PARTS = 3
PART = CAP // PARTS
SLOTS = 8 * CAP
PIECE_SLOTS = 8 * PART
PIECE_ROWS = EXPERTS * PART
HALF = D // 2
LANES = 128
SCALE = HEAD_DIM ** (-0.5)
GROUP_ROWS = 1024
COUNT = 256
NT = (((1,), (1,)), ((), ()))
TN = (((0,), (0,)), ((), ()))


def mul(a, b, dims=None):
    if dims is None:
        return jnp.dot(a, b, preferred_element_type=F32)
    return lax.dot_general(a, b, dims, preferred_element_type=F32)


def thirds(v):
    high = v.astype(BF16)
    rest = v - high.astype(F32)
    middle = rest.astype(BF16)
    return high, middle, (rest - middle.astype(F32)).astype(BF16)


def exact(v, one_hot, dims=None):
    return sum(mul(part, one_hot, dims) for part in thirds(v))


def exact_right(one_hot, v):
    return sum(mul(one_hot, part, NT) for part in thirds(v))


def iota(shape, axis):
    return lax.broadcasted_iota(jnp.int32, shape, axis)


def hot(same):
    return jnp.where(same, 1.0, 0.0).astype(BF16)


class Moves(Links):
    def __init__(self, send, recv, local):
        super().__init__(send, recv)
        self.local, self.kept = local, 0

    def keep(self, src, dst):
        copy = pltpu.make_async_copy(src, dst, self.local.at[self.kept])
        self.kept += 1
        copy.start()
        return copy

    def send_or_keep(self, i, src, dst, where):
        if i == 0:
            return self.keep(src, dst).wait
        return self.push(src, dst, where).wait_recv


def to_slots(hits, rows, stage, piece):
    columns = slice(piece * PIECE_SLOTS, (piece + 1) * PIECE_SLOTS)
    for s in range(4):
        taken = mul(hits[s, :, columns], rows[s], TN).astype(BF16)
        stage[piece, :, s] = taken.reshape(8, PART, taken.shape[1])


def deliver(moves, at, stage_a, stage_b, rows, split, piece):
    y, z, c, x = at
    along_z, along_y = faces(y, z, c, x)
    width = rows.shape[4]
    waits = []
    for i, (where, zt, ct) in enumerate(along_z):
        dst = rows.at[piece, z, pl.ds(c * 4, 4), :, pl.ds(0, split)]
        waits.append(moves.send_or_keep(i, stage_a.at[piece, zt * 2 + ct], dst, where))
    for i, (where, yt, ct) in enumerate(along_y):
        dst = rows.at[piece, :, c * 4 + y, :, pl.ds(split, width - split)]
        waits.append(moves.send_or_keep(i, stage_b.at[piece, yt * 2 + ct], dst, where))
    return waits


def give_back(moves, at, rows, back_a, back_b, split, piece):
    y, z, c, x = at
    along_z, along_y = faces(y, z, c, x)
    width = rows.shape[4]
    waits = []
    for i, (where, zt, ct) in enumerate(along_z):
        src = rows.at[piece, zt, pl.ds(ct * 4, 4), :, pl.ds(0, split)]
        dst = back_a.at[piece, z * 2 + c, :, :, pl.ds(0, split)]
        waits.append(moves.send_or_keep(i, src, dst, where))
    for i, (where, yt, ct) in enumerate(along_y):
        src = rows.at[piece, :, ct * 4 + yt, :, pl.ds(split, width - split)]
        dst = back_b.at[piece, y * 2 + c, :, :, pl.ds(0, width - split)]
        waits.append(moves.send_or_keep(i, src, dst, where))
    return waits


def slot_fold():
    p = iota((LANES, SLOTS), 1)
    return hot((p // PIECE_SLOTS) * PART + p % PART == iota((LANES, SLOTS), 0))


def slot_owner():
    return (iota((8, SLOTS), 1) % PIECE_SLOTS) // PART == iota((8, SLOTS), 0)


def add_up(hits, back, s, width):
    rows = back[:, :, s, :, 0:width].reshape(SLOTS, width)
    return mul(hits[s], rows).astype(BF16)


def around(link, own, land, me, plus, minus):
    up = link.push(own, land.at[me], plus)
    down = link.push(own, land.at[me], minus)

    def forward():
        half = COUNT // 2
        up.wait_recv()
        block = land.at[(me + 3) % 4, pl.ds(0, half)]
        waits = [link.push(block, block, plus).wait_recv]
        down.wait_recv()
        block = land.at[(me + 1) % 4, pl.ds(half, half)]
        return waits + [link.push(block, block, minus).wait_recv]

    return forward


def gelu_parts(g):
    inner = 0.7978845608 * (g + 0.044715 * g * g * g)
    th = jnp.tanh(inner)
    half = 0.5 * (1.0 + th)
    slope = half + 0.5 * g * (1.0 - th * th) * (0.7978845608 * (1.0 + 0.134145 * g * g))
    return g * half, slope


def experts_kernel(
    hot_a_in, hot_b_in, nf_a_in, nf_b_in, dy_in, tiles_in, gate_up, down,
    back_a, back_b, out, up_out, down_out, tiles_back,
    hot_a, hot_b, nf_a, nf_b, stage_a, stage_b, rows, dy,
    gu, dn, raw, mixed, ghid, grow, eo, up_grad, down_grad, tiles, slope_tiles,
    send, recv, local, load_sem,
):
    at = place()
    y, z, c, x = at
    me = (y * 4 + z) * 2 + c
    loads = [
        pltpu.make_async_copy(src, dst, load_sem.at[i])
        for i, (src, dst) in enumerate(
            (
                (hot_a_in, hot_a), (nf_a_in, nf_a), (hot_b_in, hot_b), (nf_b_in, nf_b),
                (dy_in, dy), (down.at[0], dn), (gate_up.at[0], gu), (tiles_in, tiles),
            )
        )
    ]
    for load in loads:
        load.start()
    greet(cross(*at))
    moves = Moves(send, recv, local)
    for load in loads[:4]:
        load.wait()
    waits = []
    for piece in range(PARTS):
        to_slots(hot_a, nf_a, stage_a, piece)
        to_slots(hot_b, nf_b, stage_b, piece)
        waits.append(deliver(moves, at, stage_a, stage_b, rows, HALF, piece))
    for load in loads[4:]:
        load.wait()

    def raw_tile(j, carry):
        lanes = pl.ds(pl.multiple_of(j * TILE, TILE), TILE)
        raw[:, lanes] = mul(dy[...].reshape(ROWS, D), dn[lanes, :], NT)
        return carry

    lax.fori_loop(0, FF // TILE, raw_tile, 0, unroll=True)
    back_waits = []
    slope_tiles[...] = jnp.zeros_like(slope_tiles)
    for piece in range(PARTS):
        for wait in waits[piece]:
            wait()
        block = slice(piece * PIECE_ROWS, (piece + 1) * PIECE_ROWS)
        slot = piece * PART + iota((PIECE_ROWS, LANES), 0) % PART
        held = iota((PIECE_ROWS, LANES), 1) == slot
        spread = jnp.broadcast_to(tiles[:, 0:4, :][:, :, None, :], (8, 4, PART, LANES))
        spread = spread.reshape(PIECE_ROWS, LANES)
        gate = jnp.sum(jnp.where(held, spread, 0.0), axis=1, keepdims=True)

        def hidden_tile(j, slope_sum, piece=piece, block=block, gate=gate):
            lanes = pl.ds(pl.multiple_of(j * TILE, TILE), TILE)
            upper = pl.ds(pl.multiple_of(FF + j * TILE, TILE), TILE)
            g = mul(rows[piece].reshape(PIECE_ROWS, D), gu[:, lanes])
            act, slope = gelu_parts(g)
            u = mul(rows[piece].reshape(PIECE_ROWS, D), gu[:, upper])
            m = raw[block, lanes]
            both = act * u
            mixed[block, lanes] = (both * gate).astype(BF16)
            slope_sum = slope_sum + jnp.sum(both * m, axis=1, keepdims=True)
            m = m * gate
            ghid[block, lanes] = (m * u * slope).astype(BF16)
            ghid[block, upper] = (m * act).astype(BF16)
            return slope_sum

        slopes = lax.fori_loop(
            0, FF // TILE, hidden_tile, jnp.zeros((PIECE_ROWS, 1), F32), unroll=True
        )
        slopes = jnp.where(held, slopes, 0.0).reshape(8, 4, PART, LANES)
        slope_tiles[:, 0:4, :] += jnp.sum(slopes, axis=2)

        def rows_tile(j, carry, piece=piece, block=block):
            lanes = pl.ds(pl.multiple_of(j * TILE, TILE), TILE)
            part = mul(ghid[block, :], gu[lanes, :], NT).astype(BF16)
            grow[piece, :, :, :, lanes] = part.reshape(4, 8, PART, TILE)
            return carry

        lax.fori_loop(0, D // TILE, rows_tile, 0, unroll=True)
        back_waits += give_back(moves, at, grow, back_a, back_b, HALF, piece)

    along_z, _ = faces(*at)
    back_waits += [
        moves.send_or_keep(i, slope_tiles.at[zt * 2 + ct], tiles_back.at[z * 2 + c], where)
        for i, (where, zt, ct) in enumerate(along_z)
    ]

    def out_tile(j, carry):
        lanes = pl.ds(pl.multiple_of(j * TILE, TILE), TILE)
        part = mul(mixed[...], dn[:, lanes]).astype(BF16)
        eo[:, :, :, :, lanes] = part.reshape(PARTS, 4, 8, PART, TILE)
        return carry

    lax.fori_loop(0, D // TILE, out_tile, 0, unroll=2)
    back_waits.append(moves.keep(eo, out).wait)

    def up_tile(j, carry):
        lanes = pl.ds(pl.multiple_of(j * TILE, TILE), TILE)
        part = mul(rows[:, :, :, :, lanes].reshape(ROWS, TILE), ghid[...], TN)
        up_grad[lanes, :] = part.astype(BF16)
        return carry

    lax.fori_loop(0, D // TILE, up_tile, 0, unroll=2)
    back_waits.append(moves.keep(up_grad, up_out).wait)

    def down_tile(j, carry):
        lanes = pl.ds(pl.multiple_of(j * TILE, TILE), TILE)
        part = mul(mixed[:, lanes], dy[...].reshape(ROWS, D), TN)
        down_grad[lanes, :] = part.astype(BF16)
        return carry

    lax.fori_loop(0, FF // TILE, down_tile, 0, unroll=True)
    back_waits.append(moves.keep(down_grad, down_out).wait)
    for wait in back_waits:
        wait()
    moves.drain()


def run_experts(*operands):
    anywhere = pl.BlockSpec(memory_space=pltpu.HBM)
    vmem, dma = pltpu.VMEM, pltpu.SemaphoreType.DMA
    outs = (
        (PARTS, 8, 4, PART, HALF),
        (PARTS, 8, 4, PART, HALF),
        (PARTS, 4, 8, PART, D),
        (D, 2 * FF),
        (FF, D),
    )
    held = (
        (4, COUNT, SLOTS),
        (4, COUNT, SLOTS),
        (4, COUNT, HALF),
        (4, COUNT, HALF),
        (PARTS, 8, 4, PART, HALF),
        (PARTS, 8, 4, PART, HALF),
        (PARTS, 4, 8, PART, D),
        (PARTS, 4, 8, PART, D),
        (D, 2 * FF),
        (FF, D),
        None,
        (ROWS, FF),
        (ROWS, 2 * FF),
        (PARTS, 4, 8, PART, D),
        (PARTS, 4, 8, PART, D),
        (D, 2 * FF),
        (FF, D),
    )
    return pl.pallas_call(
        experts_kernel,
        name="experts",
        out_shape=tuple(jax.ShapeDtypeStruct(shape, BF16) for shape in outs)
        + (jax.ShapeDtypeStruct((8, 8, LANES), F32),),
        in_specs=[anywhere] * 8,
        out_specs=(anywhere,) * 6,
        scratch_shapes=[vmem(shape, BF16) if shape else vmem((ROWS, FF), F32) for shape in held]
        + [vmem((8, 8, LANES), F32)] * 2
        + [dma((84 + 7,)), dma((84 + 7,)), dma((15 + 1,)), dma((8,))],
        compiler_params=pltpu.CompilerParams(
            collective_id=2, has_side_effects=True, vmem_limit_bytes=60 * 1024 * 1024
        ),
        cost_estimate=pl.CostEstimate(
            flops=33_000_000_000, bytes_accessed=60_000_000, transcendentals=1_200_000
        ),
    )(*operands)


UP_PART = D // 4
UP_HALF = UP_PART // 2
DOWN_PART = D // 4
DOWN_HALF = FF // 2


def read_gains(small):
    select = hot(iota((8, SMALL), 1) == iota((8, SMALL), 0) + EXPERTS)
    select = jnp.where(iota((8, SMALL), 0) < 2, select, jnp.zeros_like(select))
    return mul(select, small, NT), select


def fill_bias(lengths, bias, x):
    first = lengths[0, 0]
    second = first + lengths[0, 1]
    third = second + lengths[0, 2]
    own = x * COUNT + iota((1, COUNT), 1)
    own_seg = sum(jnp.where(own >= end, 1, 0) for end in (first, second, third))

    def step(i, carry):
        base = pl.multiple_of(i * COUNT, COUNT)
        key = base + iota((COUNT, 1), 0)
        key_seg = sum(jnp.where(key >= end, 1, 0) for end in (first, second, third))
        allowed = (key_seg == own_seg) & (key <= own)
        bias[pl.ds(base, COUNT), :] = jnp.where(allowed, 0.0, -1e30)
        return carry

    lax.fori_loop(0, GROUP_ROWS // COUNT, step, 0)


def turn(v, cosd, sind):
    return v * cosd + pltpu.roll(v, HEAD_DIM // 2, 1) * sind


def forward_kernel(
    lengths, tokens, wq_in, wb_in, named, cosd, sind, hot_a_in, hot_b_in, dy_a_in, dy_b_in,
    q_out, kv_out, attended_out, middle_out, normed_out, tops, totals, gates_out,
    nf_a, nf_b, dy_rows, tiles_out,
    wq, wb, kv, own_kv, bias, vt, q, attended, middle, normed, nf,
    hot_a, hot_b, dy_a, dy_b, stage_a, stage_b, own_gates, gates_y, tiles, send, recv, local, load_sem,
):
    at = place()
    y, z, c, x = at
    line_y, line_z = lines(y, z, c, x)
    peers = [device(y, z, c, (x + d) % 4) for d in (1, 2, 3)]
    pairs = (
        (wb_in.at[:, pl.ds(D, SMALL)], wb.at[:, pl.ds(D, SMALL)]),
        (wq_in.at[:, pl.ds(D, 512)], wq.at[:, pl.ds(D, 512)]),
        (hot_a_in, hot_a), (dy_a_in, dy_a), (hot_b_in, hot_b), (dy_b_in, dy_b),
        (wq_in.at[:, pl.ds(0, D)], wq.at[:, pl.ds(0, D)]),
        (wb_in.at[:, pl.ds(0, D)], wb.at[:, pl.ds(0, D)]),
    )
    loads = [
        pltpu.make_async_copy(src, dst, load_sem.at[i]) for i, (src, dst) in enumerate(pairs)
    ]
    for load in loads:
        load.start()
    greet(cross(*at) + peers)
    moves = Moves(send, recv, local)
    loads[0].wait()
    small = wb[:, D:]
    gains, _ = read_gains(small)
    xf = tokens[...].astype(F32)
    inverse = lax.rsqrt(jnp.mean(xf * xf, axis=1, keepdims=True) + norm_eps)
    normed[...] = (xf * inverse * gains[0:1, :]).astype(BF16)
    loads[1].wait()
    part = mul(normed[...], wq[:, D : D + 512])
    for g in range(HEADS_KV):
        key = turn(part[:, g * 128 : (g + 1) * 128], cosd[...], sind[...])
        own_kv[:, g * 256 : g * 256 + 128] = key.astype(BF16)
        own_kv[:, g * 256 + 128 : (g + 1) * 256] = part[:, 256 + g * 128 : 384 + g * 128].astype(BF16)
    rows = pl.ds(pl.multiple_of(x * COUNT, COUNT), COUNT)
    pushes = []
    for g in range(HEADS_KV):
        lanes = pl.ds(g * 256, 256)
        pushes.append(
            [moves.push(own_kv.at[:, lanes], kv.at[rows, lanes], peer) for peer in peers]
        )
    kv[rows, :] = own_kv[...]
    for load in loads[2:6]:
        load.wait()
    for piece in range(PARTS):
        to_slots(hot_a, dy_a, stage_a, piece)
        to_slots(hot_b, dy_b, stage_b, piece)
    dy_waits = deliver(moves, at, stage_a, stage_b, dy_rows, HALF, slice(None))
    fill_bias(lengths, bias, x)
    loads[6].wait()

    def query_tile(j, carry):
        lanes = pl.ds(pl.multiple_of(j * 256, 256), 256)
        part = mul(normed[...], wq[:, lanes])
        q[:, lanes] = jnp.concatenate(
            [turn(part[:, h * 128 : (h + 1) * 128], cosd[...], sind[...]) for h in range(2)],
            axis=1,
        ).astype(BF16)
        return carry

    lax.fori_loop(0, D // 256, query_tile, 0, unroll=True)

    logits = jnp.where(named[...] > 0, mul(tokens[...], small), -jnp.inf)
    weight = jnp.exp(logits - jnp.max(logits, axis=1, keepdims=True))
    gates = weight / jnp.sum(weight, axis=1, keepdims=True)
    gates_out[...] = gates
    flat = exact_right(hot(iota((EXPERTS, LANES), 0) == iota((EXPERTS, LANES), 1)), gates)
    own_gates[...] = flat.reshape(4, 8, COUNT)
    gates_y[pl.ds(y, 1)] = own_gates[pl.ds(y, 1)]
    gate_pushes = [
        moves.push(own_gates.at[(y + d) % 4], gates_y.at[y], line_y[d - 1]) for d in (1, 2, 3)
    ]

    stays = [moves.keep(q, q_out), moves.keep(normed, normed_out)]
    for g in range(HEADS_KV):
        for push in pushes[g]:
            push.wait_recv()
        vt[g] = kv[:, g * 256 + 128 : (g + 1) * 256].T

        def head(i, carry, g=g):
            h = g * REPEAT + i
            lanes = pl.ds(pl.multiple_of(h * HEAD_DIM, HEAD_DIM), HEAD_DIM)
            s = mul(kv[:, g * 256 : g * 256 + 128], q[:, lanes], NT) * SCALE + bias[...]
            top = jnp.max(s, axis=0, keepdims=True)
            p = jnp.exp(s - top)
            total = jnp.sum(p, axis=0, keepdims=True)
            tops[pl.ds(h, 1), :] = top
            totals[pl.ds(h, 1), :] = total
            low = (p * (1.0 / total)).astype(BF16)
            attended[:, lanes] = mul(vt[g], low).T.astype(BF16)
            return carry

        lax.fori_loop(0, REPEAT, head, 0, unroll=3)

    stays.append(moves.keep(kv, kv_out))
    loads[7].wait()

    def out_tile(j, carry):
        lanes = pl.ds(pl.multiple_of(j * 256, 256), 256)
        middle[:, lanes] = tokens[:, lanes].astype(F32) + mul(attended[...], wb[lanes, 0:D], NT)
        return carry

    lax.fori_loop(0, D // 256, out_tile, 0, unroll=True)
    m = middle[...]
    inverse = lax.rsqrt(jnp.mean(m * m, axis=1, keepdims=True) + norm_eps)
    stays += [moves.keep(attended, attended_out), moves.keep(middle, middle_out)]
    nf[...] = (m * inverse * gains[1:2, :]).astype(BF16)
    half_a, half_b = nf.at[:, pl.ds(0, HALF)], nf.at[:, pl.ds(HALF, HALF)]
    last = [
        around(moves, half_a, nf_a, y, line_y[0], line_y[2]),
        around(moves, half_b, nf_b, z, line_z[0], line_z[2]),
    ]
    stays += [moves.keep(half_a, nf_a.at[y]), moves.keep(half_b, nf_b.at[z])]
    for push in gate_pushes:
        push.wait_recv()
    tiles[...] = jnp.zeros_like(tiles)
    owner = hot(slot_owner())
    for s in range(4):
        spread = exact(gates_y[s], owner, TN) * hot_a[s].astype(F32)
        row = jnp.sum(spread, axis=0, keepdims=True)
        tile = exact(jnp.where(slot_owner(), row, 0.0), slot_fold(), NT)
        tiles[:, s : s + 1, :] = tile[:, None, :]
    along_z, _ = faces(*at)
    dy_waits += [
        moves.send_or_keep(i, tiles.at[zt * 2 + ct], tiles_out.at[z * 2 + c], where)
        for i, (where, zt, ct) in enumerate(along_z)
    ]
    for wait in last[0]() + last[1]():
        wait()
    for stay in stays:
        stay.wait()
    for wait in dy_waits:
        wait()
    moves.drain()


def run_forward(*operands):
    anywhere = pl.BlockSpec(memory_space=pltpu.HBM)
    inside = pl.BlockSpec(memory_space=pltpu.VMEM)
    vmem, dma = pltpu.VMEM, pltpu.SemaphoreType.DMA
    shape = jax.ShapeDtypeStruct
    return pl.pallas_call(
        forward_kernel,
        name="forward",
        out_shape=(
            shape((COUNT, D), BF16),
            shape((GROUP_ROWS, 512), BF16),
            shape((COUNT, D), BF16),
            shape((COUNT, D), F32),
            shape((COUNT, D), BF16),
            shape((16, COUNT), F32),
            shape((16, COUNT), F32),
            shape((COUNT, 128), F32),
            shape((4, COUNT, HALF), BF16),
            shape((4, COUNT, HALF), BF16),
            shape((PARTS, 4, 8, PART, D), BF16),
            shape((8, 8, LANES), F32),
        ),
        in_specs=[pl.BlockSpec(memory_space=pltpu.SMEM), inside, anywhere, anywhere]
        + [inside] * 3
        + [anywhere] * 4,
        out_specs=(anywhere,) * 5 + (inside,) * 3 + (anywhere,) * 4,
        scratch_shapes=[
            vmem((D, WA), BF16),
            vmem((D, WB), BF16),
            vmem((GROUP_ROWS, 512), BF16),
            vmem((COUNT, 512), BF16),
            vmem((GROUP_ROWS, COUNT), F32),
            vmem((HEADS_KV, HEAD_DIM, GROUP_ROWS), BF16),
            vmem((COUNT, D), BF16),
            vmem((COUNT, D), BF16),
            vmem((COUNT, D), F32),
            vmem((COUNT, D), BF16),
            vmem((COUNT, D), BF16),
            vmem((4, COUNT, SLOTS), BF16),
            vmem((4, COUNT, SLOTS), BF16),
            vmem((4, COUNT, HALF), BF16),
            vmem((4, COUNT, HALF), BF16),
            *(vmem((PARTS, 8, 4, PART, HALF), BF16),) * 2,
            vmem((4, 8, COUNT), F32),
            vmem((4, 8, COUNT), F32),
            vmem((8, 8, LANES), F32),
            dma((6 + 14 + 8 + 3 + 7,)),
            dma((6 + 14 + 8 + 3 + 7,)),
            dma((2 + 7 + 1,)),
            dma((8,)),
        ],
        compiler_params=pltpu.CompilerParams(
            collective_id=3, has_side_effects=True, vmem_limit_bytes=60 * 1024 * 1024
        ),
        cost_estimate=pl.CostEstimate(
            flops=6_000_000_000, bytes_accessed=30_000_000, transcendentals=3_200_000
        ),
    )(*operands)


def norm_grad(values, gain, grad):
    inverse = lax.rsqrt(jnp.mean(values * values, axis=1, keepdims=True) + norm_eps)
    unit = values * inverse
    scaled = grad * gain
    drop = jnp.mean(scaled * unit, axis=1, keepdims=True)
    return inverse * (scaled - unit * drop), jnp.sum(grad * unit, axis=0, keepdims=True)


def backward_kernel(
    lengths, tokens_in, cotangent_in, gates, queries_in, kv_src, attended_in, middle_in, normed_in,
    tops, totals, cosd, sind, wq_in, wb_in, hot_a_in, hot_b_in,
    back_a_in, back_b_in, out_in, up_in, down_in, tiles_in,
    grad_tokens, grad_qkv_out, grad_out_out, grad_small, up_far, down_far,
    late_a, late_b, came_a, came_b,
    tokens, cotangent, queries, kv_in, attended, middle, normed,
    wq, wb, hot_a, hot_b, back_a, back_b,
    part_a, part_b, land_a, land_b, down_own, down_got,
    tiles, slopes, slopes_y,
    bias, kt, gn, gmid, gb, gatt, gp, dk, dv, leave, land, grad_qkv,
    send, recv, local, load_sem, empty,
):
    at = place()
    y, z, c, x = at
    line_y, line_z = lines(y, z, c, x)
    peers = [device(y, z, c, (x + d) % 4) for d in (1, 2, 3)]
    pairs = (
        (back_a_in, back_a), (hot_a_in, hot_a), (back_b_in, back_b), (hot_b_in, hot_b),
        (tiles_in, tiles),
        (kv_src, kv_in), (wb_in, wb), (middle_in, middle), (cotangent_in, cotangent),
        (queries_in, queries), (attended_in, attended), (tokens_in, tokens),
        (normed_in, normed), (wq_in, wq),
    )
    pairs += tuple(
        (
            down_in.at[
                pl.ds(half * DOWN_HALF, DOWN_HALF),
                pl.ds(pl.multiple_of(((x + d) % 4) * DOWN_PART, 128), DOWN_PART),
            ],
            down_own.at[half],
        )
        for half, d in ((0, 3), (1, 1))
    )
    loads = [
        pltpu.make_async_copy(src, dst, load_sem.at[i]) for i, (src, dst) in enumerate(pairs)
    ]
    for load in loads:
        load.start()
    greet(cross(*at) + peers)
    link = Moves(send, recv, local)
    for load in loads[:5]:
        load.wait()
    part_waits = []
    for hits, back, parts, land_here, me, line, width in (
        (hot_a, back_a, part_a, land_a, y, line_y, HALF),
        (hot_b, back_b, part_b, land_b, z, line_z, HALF),
    ):
        for d in (1, 2, 3):
            parts[d - 1] = add_up(hits, back, (me + d) % 4, width)
            push = link.push(parts.at[d - 1], land_here.at[me], line[d - 1])
            part_waits.append(push.wait_recv)
        land_here[pl.ds(me, 1)] = add_up(hits, back, me, width)[None]
    for peer in cross(*at):
        pl.semaphore_signal(empty, inc=1, device_id=peer, device_id_type=MESH)
    facing = (x + 2) % 4
    pushes, down_pushes = [], []
    for half, peer in ((0, peers[2]), (1, peers[0])):
        up_rows = pl.ds(pl.multiple_of(facing * UP_PART + half * UP_HALF, UP_HALF), UP_HALF)
        pushes.append(link.push(up_in.at[up_rows], up_far.at[half], peer))
        lanes = pl.ds(pl.multiple_of(facing * DOWN_PART, 128), DOWN_PART)
        down_rows = pl.ds(half * DOWN_HALF, DOWN_HALF)
        down_pushes.append(link.push(down_in.at[down_rows, lanes], down_got.at[half], peer))
    slope_pushes = []
    for d in (1, 2, 3, 0):
        source = (y + d) % 4
        chosen = iota((8, 8, LANES), 1) == source
        tile = jnp.sum(jnp.where(chosen, tiles[...], 0.0), axis=1)
        spread = jnp.where(slot_owner(), exact(tile, slot_fold()), 0.0)
        slope = exact(spread, hot_a[source], NT)
        if d == 0:
            slopes_y[pl.ds(y, 1)] = slope[None]
        else:
            slopes[d - 1] = slope
            slope_pushes.append(link.push(slopes.at[d - 1], slopes_y.at[y], line_y[d - 1]))
    fill_bias(lengths, bias, x)
    for load in loads[5:]:
        load.wait()
    for g in range(HEADS_KV):
        kt[g] = kv_in[:, g * 256 : g * 256 + 128].T
    def softmax(h, g):
        lanes = pl.ds(pl.multiple_of(h * HEAD_DIM, HEAD_DIM), HEAD_DIM)
        s = mul(kv_in[:, g * 256 : g * 256 + 128], queries[:, lanes], NT) * SCALE + bias[...]
        p = jnp.exp(s - tops[pl.ds(h, 1), :]) * (1.0 / totals[pl.ds(h, 1), :])
        p = p.astype(BF16)
        for k in range(8):
            grad_qkv[lanes, k * 256 : (k + 1) * 256] = p[k * 128 : (k + 1) * 128, :]

    for g in range(HEADS_KV):

        def softmax_step(i, carry, g=g):
            softmax(g * REPEAT + i, g)
            return carry

        lax.fori_loop(0, REPEAT, softmax_step, 0, unroll=2)

    for push in slope_pushes:
        push.wait_recv()
    same = hot(iota((EXPERTS, LANES), 0) == iota((EXPERTS, LANES), 1))
    gate_grad = exact(slopes_y[...].reshape(EXPERTS, COUNT), same, TN)
    weighted = gates[...] * gate_grad
    logit_grad = weighted - gates[...] * jnp.sum(weighted, axis=1, keepdims=True)
    parts = thirds(logit_grad)
    router_grad = sum(mul(tokens[...], part, TN) for part in parts)
    for wait in part_waits:
        wait()
    pl.semaphore_wait(empty, 13)
    out_waits = give_back(link, at, out_in, back_a, back_b, HALF, slice(None))
    total = land_a[0].astype(F32)
    for s in range(1, 4):
        total = total + land_a[s].astype(F32)
    gn[:, 0:HALF] = total
    total = land_b[0].astype(F32)
    for s in range(1, 4):
        total = total + land_b[s].astype(F32)
    gn[:, HALF:] = total
    gains, select = read_gains(wb[:, D:])
    moved, ffn_gain = norm_grad(middle[...], gains[1:2, :], gn[...])
    gm = cotangent[...].astype(F32) + moved
    gmid[...] = gm
    gb[...] = gm.astype(BF16)

    def att_tile(j, carry):
        lanes = pl.ds(pl.multiple_of(j * 256, 256), 256)
        gatt[:, lanes] = mul(gb[...], wb[:, lanes]).astype(BF16)
        return carry

    lax.fori_loop(0, D // 256, att_tile, 0, unroll=True)
    kv_pushes = []
    for g in range(HEADS_KV):
        dk[...] = jnp.zeros_like(dk)
        dv[...] = jnp.zeros_like(dv)

        def head(i, carry, g=g):
            h = g * REPEAT + i
            lanes = pl.ds(pl.multiple_of(h * HEAD_DIM, HEAD_DIM), HEAD_DIM)
            low = jnp.concatenate(
                [grad_qkv[lanes, k * 256 : (k + 1) * 256] for k in range(8)], axis=0
            )
            p = low.astype(F32)
            dv[...] += mul(low, gatt[:, lanes])
            t = p * mul(kv_in[:, g * 256 + 128 : (g + 1) * 256], gatt[:, lanes], NT)
            ds = (t - p * jnp.sum(t, axis=0, keepdims=True)).astype(BF16)
            dk[...] += mul(ds, queries[:, lanes])
            dq = mul(kt[g], ds).T * SCALE
            gp[:, lanes] = turn(dq, cosd[...], -sind[...]).astype(BF16)
            return carry

        lax.fori_loop(0, REPEAT, head, 0, unroll=3)
        leave[g, :, 0:128] = (dk[...] * SCALE).astype(BF16)
        leave[g, :, 128:256] = dv[...].astype(BF16)
        for d in (1, 2, 3):
            away = pl.ds(pl.multiple_of(((x + d) % 4) * COUNT, COUNT), COUNT)
            kv_pushes.append(link.push(leave.at[g, away], land.at[g, d - 1], peers[d - 1]))

    def out_tile(j, carry):
        lanes = pl.ds(pl.multiple_of(j * 256, 256), 256)
        grad_qkv[lanes, 0:D] = mul(gb[:, lanes], attended[...], TN).astype(BF16)
        return carry

    lax.fori_loop(0, D // 256, out_tile, 0, unroll=True)

    out_kept = link.keep(grad_qkv.at[:, pl.ds(0, D)], grad_out_out)

    for push in down_pushes:
        push.wait_recv()
    for half, (peer, part) in enumerate(((peers[2], (x + 3) % 4), (peers[0], (x + 1) % 4))):
        down_own[half] = (down_own[half].astype(F32) + down_got[half].astype(F32)).astype(BF16)
        lanes = pl.ds(pl.multiple_of(part * DOWN_PART, 128), DOWN_PART)
        here, rest = (pl.ds(k * DOWN_HALF, DOWN_HALF) for k in (half, 1 - half))
        pushes.append(link.push(down_own.at[half], down_far.at[half, here], peer))
        pushes.append(link.push(down_in.at[rest, lanes], down_far.at[half, rest], peer))

    small = wb[:, D:]

    for wait in out_waits:
        wait()
    first, second, lanes = pl.ds(0, COUNT // 2), pl.ds(COUNT // 2, COUNT // 2), pl.ds(0, HALF)
    late, stays = [], []
    ends = (
        (hot_a, back_a, land_a, came_a, late_a, y, line_y),
        (hot_b, back_b, land_b, came_b, late_b, z, line_z),
    )
    for d in (2, 1, 3, 0):
        for hits, back, summed, came, left, me, line in ends:
            s = (me + d) % 4
            summed[pl.ds(s, 1), :, 0:HALF] = add_up(hits, back, s, HALF)[None]
            if d == 0:
                stays.append(link.keep(summed.at[me, first, lanes], came.at[me]))
                stays.append(link.keep(summed.at[:, second, lanes], left))
            else:
                push = link.push(summed.at[s, first, lanes], came.at[me], line[d - 1])
                late.append(push.wait_recv)
    for push in kv_pushes:
        push.wait_recv()
    mine = pl.ds(pl.multiple_of(x * COUNT, COUNT), COUNT)
    for g in range(HEADS_KV):
        total = leave[g, mine, :].astype(F32)
        for d in range(3):
            total = total + land[g, d].astype(F32)
        gp[:, D + g * 128 : D + (g + 1) * 128] = turn(
            total[:, 0:128], cosd[...], -sind[...]
        ).astype(BF16)
        gp[:, D + 256 + g * 128 : D + 384 + g * 128] = total[:, 128:256].astype(BF16)
    out_kept.wait()

    def qkv_tile(j, carry):
        lanes = pl.ds(pl.multiple_of(j * 256, 256), 256)
        grad_qkv[lanes, :] = mul(normed[:, lanes], gp[...], TN).astype(BF16)
        gn[:, lanes] = mul(gp[...], wq[lanes, :], NT)
        return carry

    lax.fori_loop(0, D // 256, qkv_tile, 0, unroll=True)
    stays.append(link.keep(grad_qkv, grad_qkv_out))
    moved, attn_gain = norm_grad(tokens[...].astype(F32), gains[0:1, :], gn[...])
    from_router = sum(mul(part, small, NT) for part in parts)
    grad_tokens[...] = (gmid[...] + moved + from_router).astype(BF16)
    both = jnp.where(
        iota((8, D), 0) == 0, attn_gain, jnp.where(iota((8, D), 0) == 1, ffn_gain, 0.0)
    )
    gain_columns = sum(mul(part, select, TN) for part in thirds(both))
    grad_small[...] = (router_grad + gain_columns).astype(BF16)
    for push in pushes:
        push.wait_recv()
    for wait in late:
        wait()
    for stay in stays:
        stay.wait()
    link.drain()


def run_backward(*operands):
    anywhere = pl.BlockSpec(memory_space=pltpu.HBM)
    inside = pl.BlockSpec(memory_space=pltpu.VMEM)
    vmem, dma = pltpu.VMEM, pltpu.SemaphoreType.DMA
    shape = jax.ShapeDtypeStruct
    return pl.pallas_call(
        backward_kernel,
        name="backward",
        out_shape=(
            shape((COUNT, D), BF16),
            shape((D, WA), BF16),
            shape((D, D), BF16),
            shape((D, SMALL), BF16),
            shape((2, UP_HALF, 2 * FF), BF16),
            shape((2, FF, DOWN_PART), BF16),
            *(shape((4, COUNT // 2, HALF), BF16),) * 4,
        ),
        in_specs=[pl.BlockSpec(memory_space=pltpu.SMEM)]
        + [anywhere] * 2
        + [inside]
        + [anywhere] * 5
        + [inside] * 4
        + [anywhere] * 10,
        out_specs=(inside, anywhere, anywhere, inside) + (anywhere,) * 6,
        scratch_shapes=[
            vmem((COUNT, D), BF16),
            vmem((COUNT, D), BF16),
            vmem((COUNT, D), BF16),
            vmem((GROUP_ROWS, 512), BF16),
            vmem((COUNT, D), BF16),
            vmem((COUNT, D), F32),
            vmem((COUNT, D), BF16),
            vmem((D, WA), BF16),
            vmem((D, WB), BF16),
            vmem((4, COUNT, SLOTS), BF16),
            vmem((4, COUNT, SLOTS), BF16),
            vmem((PARTS, 8, 4, PART, HALF), BF16),
            vmem((PARTS, 8, 4, PART, HALF), BF16),
            vmem((3, COUNT, HALF), BF16),
            vmem((3, COUNT, HALF), BF16),
            vmem((4, COUNT, HALF), BF16),
            vmem((4, COUNT, HALF), BF16),
            vmem((2, DOWN_HALF, DOWN_PART), BF16),
            vmem((2, DOWN_HALF, DOWN_PART), BF16),
            vmem((8, 8, LANES), F32),
            vmem((3, 8, COUNT), F32),
            vmem((4, 8, COUNT), F32),
            vmem((GROUP_ROWS, COUNT), F32),
            vmem((HEADS_KV, HEAD_DIM, GROUP_ROWS), BF16),
            vmem((COUNT, D), F32),
            vmem((COUNT, D), F32),
            vmem((COUNT, D), BF16),
            vmem((COUNT, D), BF16),
            vmem((COUNT, WA), BF16),
            vmem((GROUP_ROWS, HEAD_DIM), F32),
            vmem((GROUP_ROWS, HEAD_DIM), F32),
            vmem((HEADS_KV, GROUP_ROWS, 256), BF16),
            vmem((HEADS_KV, 3, COUNT, 256), BF16),
            vmem((D, WA), BF16),
            dma((6 + 4 + 14 + 6 + 6 + 4 + 3,)),
            dma((6 + 4 + 14 + 6 + 6 + 4 + 3,)),
            dma((2 + 4 + 2,)),
            dma((16,)),
            pltpu.SemaphoreType.REGULAR,
        ],
        compiler_params=pltpu.CompilerParams(
            collective_id=4, has_side_effects=True, vmem_limit_bytes=60 * 1024 * 1024
        ),
        cost_estimate=pl.CostEstimate(
            flops=13_000_000_000, bytes_accessed=50_000_000, transcendentals=3_200_000
        ),
    )(*operands)


def finish_kernel(
    sum_a_in, sum_b_in, up_in, down_in, out_in, tokens_in,
    output, grad_tokens, grad_up, grad_down, grad_qkv, grad_out_t, grad_attn, grad_ffn, grad_router,
    sum_a, sum_b, up, down, out, tokens, load_sem, store_sem,
):
    pairs = (
        (up_in, up), (down_in, down), (out_in, out), (tokens_in, tokens),
        (sum_a_in, sum_a), (sum_b_in, sum_b),
    )
    loads = [
        pltpu.make_async_copy(src, dst, load_sem.at[i]) for i, (src, dst) in enumerate(pairs)
    ]
    for load in loads:
        load.start()
    pairs = ((up, grad_up), (down, grad_down), (out, output), (tokens, grad_tokens))
    stores = [
        pltpu.make_async_copy(src, dst, store_sem.at[i]) for i, (src, dst) in enumerate(pairs)
    ]
    for load, store in zip(loads, stores):
        load.wait()
        store.start()
    for load in loads[4:]:
        load.wait()
    grad_qkv[...] = sum_a[0:PIECE, :]
    grad_out_t[...] = sum_b[0:PIECE, 0:D]
    small = sum_b[0:PIECE, D:]
    grad_router[...] = small[:, 0:EXPERTS]
    diagonal = iota((PIECE, SMALL), 0) == iota((PIECE, SMALL), 1)
    for k, gain in enumerate((grad_attn, grad_ffn)):
        lanes = iota((PIECE, SMALL), 1) == EXPERTS + k
        column = jnp.sum(jnp.where(lanes, small, 0.0), axis=1, keepdims=True)
        row = jnp.sum(jnp.where(diagonal, column, 0.0), axis=0, keepdims=True)
        gain[...] = row[:, 0:PIECE]
    for store in stores:
        store.wait()


def finish(*operands):
    anywhere = pl.BlockSpec(memory_space=pltpu.HBM)
    inside = pl.BlockSpec(memory_space=pltpu.VMEM)
    shape, vmem, dma = jax.ShapeDtypeStruct, pltpu.VMEM, pltpu.SemaphoreType.DMA
    return pl.pallas_call(
        finish_kernel,
        name="finish",
        out_shape=(
            shape((COUNT, D), BF16),
            shape((COUNT, D), BF16),
            shape((UP_PART, 2 * FF), F32),
            shape((FF, DOWN_PART), F32),
            shape((PIECE, WA), F32),
            shape((PIECE, D), F32),
            shape((1, PIECE), F32),
            shape((1, PIECE), F32),
            shape((PIECE, EXPERTS), F32),
        ),
        in_specs=[anywhere] * 6,
        out_specs=(anywhere,) * 4 + (inside,) * 5,
        scratch_shapes=[
            vmem((PADDED, WA), F32),
            vmem((PADDED, WB), F32),
            vmem((UP_PART, 2 * FF), F32),
            vmem((FF, DOWN_PART), F32),
            vmem((COUNT, D), BF16),
            vmem((COUNT, D), BF16),
            dma((6,)),
            dma((4,)),
        ],
        compiler_params=pltpu.CompilerParams(vmem_limit_bytes=60 * 1024 * 1024),
    )(*operands)


def body(
    tokens, lengths, top_experts, w_qkv, w_out, gain_attn, gain_ffn, router, gate_up, down_proj, cotangent,
):
    half = HEAD_DIM // 2
    rates = rope_base ** (-(np.arange(HEAD_DIM, dtype=np.float32) % half) / half)
    full_a, full_b, named, hot_a, hot_b, dy_a, dy_b, cosd, sind = gather_weights(
        lengths, jnp.asarray(rates.astype(np.float32))[None], w_qkv, w_out.T, router,
        gain_attn[None], gain_ffn[None], top_experts.T, cotangent,
    )
    wq = full_a.reshape(D, WA)
    wb = full_b.reshape(D, WB)
    (
        queries, kv, attended, middle, normed, tops, totals, gates, nf_a, nf_b, dy_rows, tiles,
    ) = run_forward(
        lengths, tokens, wq, wb, named, cosd, sind, hot_a, hot_b, dy_a, dy_b
    )
    back_a, back_b, expert_out, up_local, down_local, tiles_back = run_experts(
        hot_a, hot_b, nf_a, nf_b, dy_rows, tiles, gate_up, down_proj
    )
    grad_tokens, grad_qkv, grad_out, grad_small, *passed_on = run_backward(
        lengths, tokens, cotangent, gates, queries, kv, attended, middle, normed, tops, totals,
        cosd, sind, wq, wb, hot_a, hot_b, back_a, back_b, expert_out, up_local, down_local,
        tiles_back,
    )
    sum_a, sum_b, up_sum, down_sum, output = scatter_sums(
        grad_qkv.reshape(4, 4, 2, BLOCK, WA),
        grad_out.reshape(4, 4, 2, BLOCK, D),
        grad_small.reshape(4, 4, 2, BLOCK, SMALL),
        up_local,
        down_local,
        *passed_on,
        middle,
    )
    (
        output, grad_tokens, up_sum, down_sum, grad_qkv, grad_out_t, grad_attn, grad_ffn, grad_router,
    ) = finish(sum_a, sum_b, up_sum, down_sum, output, grad_tokens)
    return (
        output,
        grad_tokens,
        grad_qkv,
        grad_out_t.T,
        grad_attn[0],
        grad_ffn[0],
        grad_router,
        up_sum[None],
        down_sum[None],
    )


def solution(mesh):
    return jax.shard_map(
        body,
        mesh=mesh,
        in_specs=(
            P(("expert", "shard"), None),
            P("expert", None),
            P(("expert", "shard"), None),
            P(("expert", "shard"), None),
            P(None, ("expert", "shard")),
            P(("expert", "shard")),
            P(("expert", "shard")),
            P(("expert", "shard"), None),
            P("expert", None, None),
            P("expert", None, None),
            P(("expert", "shard"), None),
        ),
        out_specs=(
            P(("expert", "shard"), None),
            P(("expert", "shard"), None),
            P(("expert", "shard"), None),
            P(None, ("expert", "shard")),
            P(("expert", "shard")),
            P(("expert", "shard")),
            P(("expert", "shard"), None),
            P("expert", "shard", None),
            P("expert", None, "shard"),
        ),
        check_vma=False,
    )
```
